32 devices in a mesh: batch: 2 (over x), space: 16 (over z, y, core).
Axes of the slice: x: 2, y: 2, z: 4, core: 2. Of those that a mesh axis runs over, the one named last changes fastest.
Arguments:
- snapshots: bfloat16 [2, 64, 32, 1024], P('batch', None, 'space'), may hold values from -6 to 6
- cotangent: bfloat16 [2, 64, 32, 1024], P('batch', None, 'space'), may hold values from -6 to 6
- mode_weight: bfloat16 [16, 16, 24, 64, 64], P('batch', 'space'), may hold values from -0.75 to 0.75
- conv_weight: bfloat16 [3, 3, 3, 64, 64], replicated, may hold values from -0.15625 to 0.15625
Outputs:
- activated: bfloat16 [2, 64, 32, 1024], P('batch', None, 'space')
- input_gradient: bfloat16 [2, 64, 32, 1024], P('batch', None, 'space')
- mode_gradient: float32 [16, 16, 24, 64, 64], P('batch', 'space')
- conv_gradient: float32 [3, 3, 3, 64, 64], replicated
The draws below stay inside these ranges and needn't reach their ends.
All inputs are finite; a program needn't handle non-finite values.
Results may differ from the reference program's by a relative error of at most 0.02.
Values may be sent and summed in bfloat16 or wider, within the bound.
No kernel may reach another device: no remote copies, remote signals or barrier semaphores. Data moves between devices by JAX's collectives and lax.ppermute only.
A program may use at most 128 MiB of HBM per device.

```python
import math
import jax
import jax.numpy as jnp
from jax import lax

C = 64
KX = 8
KY = 8
KZ = 12
NX = 32
NY = 32
PX = 16
PY = 16
PZ = 24
NZ = 32
PLANE = 1024
SNAPS = 2


def shard_levels(rng, dims, cuts, least, top_value):
    loudness, own = 1.0, jax.random.fold_in(rng, 6)
    for axis_at, parts in cuts:
        steps = jnp.exp(jax.random.uniform(jax.random.fold_in(own, axis_at), (parts,), jnp.float32, least / len(cuts), top_value / len(cuts)))
        loudness = loudness * jnp.repeat(steps, dims[axis_at] // parts).reshape([-1 if axis == axis_at else 1 for axis in range(len(dims))])
    return loudness


def gaussian(stream_key, extent, scale, most, cuts=(), kind=jnp.bfloat16):
    result = jax.random.normal(stream_key, extent, jnp.float32) * scale
    if len(cuts) > 0:
        result = shard_levels(stream_key, extent, cuts, -0.22, 0.18) * result
    return jnp.clip(result, min=-most, max=most).astype(kind)


def setup_inputs(seed: int = 0) -> dict:
    arg_keys = jax.random.split(jax.random.key(seed), 5)
    snapshots = gaussian(arg_keys[0], (SNAPS, C, NZ, PLANE), 1.0, 6.0, ((0, 2), (2, 16)))
    cotangent = gaussian(arg_keys[1], (SNAPS, C, NZ, PLANE), 1.0, 6.0, ((0, 2), (2, 16)))
    mode_weight = gaussian(arg_keys[2], (PX, PY, PZ, C, C), C ** -0.5, 0.75, ((0, 2), (1, 16)))
    conv_weight = gaussian(arg_keys[3], (3, 3, 3, C, C), (27 * C) ** -0.5, 0.15625)
    return dict(snapshots=snapshots, cotangent=cotangent, mode_weight=mode_weight, conv_weight=conv_weight)


inv_root_two = 1.0 / math.sqrt(2.0)
inv_root_two_pi = 1.0 / math.sqrt(2.0 * math.pi)

def basis_rows(half_count, length):
    row_index = lax.broadcasted_iota(jnp.int32, (2 * half_count, length), 0)
    cell_index = lax.broadcasted_iota(jnp.int32, (2 * half_count, length), 1)
    frequency = jnp.where(row_index < half_count, row_index, row_index - half_count + 1)
    phases = (frequency * cell_index % length).astype(jnp.float32) * (2.0 * math.pi / length)
    return jnp.where(row_index < half_count, jnp.cos(phases), jnp.sin(phases))

def make_tables(count_x, count_y, count_z, length_x, length_y, length_z):
    across = basis_rows(count_x, length_x)
    along_y = basis_rows(count_y, length_y)
    depth_rows = basis_rows(count_z, length_z)
    modes_x = 2 * count_x
    modes_y = 2 * count_y
    outer_table = (across[:, None, :, None] * along_y[None, :, None, :]).reshape(modes_x * modes_y, length_x * length_y)
    plane_analysis = (outer_table * (2.0 / math.sqrt(length_x * length_y))).astype(jnp.bfloat16)
    plane_synthesis = (outer_table.T * (2.0 / math.sqrt(modes_x * modes_y))).astype(jnp.bfloat16)
    depth_analysis = (depth_rows * math.sqrt(2.0 / length_z)).astype(jnp.bfloat16)
    depth_synthesis = (depth_rows.T * math.sqrt(2.0 / (2 * count_z))).astype(jnp.bfloat16)
    return (plane_analysis, plane_synthesis, depth_analysis, depth_synthesis)

def highest_einsum(formula, left, right):
    return jnp.einsum(formula, left.astype(jnp.float32), right.astype(jnp.float32), precision=lax.Precision.HIGHEST)

def stencil(padded, kernel):
    channels = padded.shape[0]
    depth_cells = padded.shape[1] - 2
    summed = jnp.zeros((kernel.shape[4], depth_cells * NX * NY), jnp.float32)
    for offset_x in range(3):
        for offset_y in range(3):
            window = padded[:, :, offset_x:offset_x + NX, offset_y:offset_y + NY]
            stacked = jnp.stack([window[:, offset_z:offset_z + depth_cells] for offset_z in range(3)], 0)
            stacked = stacked.reshape(3, channels, depth_cells * NX * NY).astype(jnp.float32)
            summed = summed + lax.dot_general(kernel[:, offset_x, offset_y].astype(jnp.float32), stacked, (((0, 1), (0, 1)), ((), ())), precision=lax.Precision.HIGHEST)
    return summed

def kernel_terms(padded, pre_flat):
    channels = padded.shape[0]
    depth_cells = padded.shape[1] - 2
    pieces = []
    for offset_x in range(3):
        row_pieces = []
        for offset_y in range(3):
            window = padded[:, :, offset_x:offset_x + NX, offset_y:offset_y + NY]
            stacked = jnp.stack([window[:, offset_z:offset_z + depth_cells] for offset_z in range(3)], 0)
            stacked = stacked.reshape(3, channels, depth_cells * NX * NY).astype(jnp.float32)
            row_pieces.append(lax.dot_general(stacked, pre_flat.astype(jnp.float32), (((2,), (1,)), ((), ())), precision=lax.Precision.HIGHEST))
        pieces.append(jnp.stack(row_pieces, 1))
    return jnp.stack(pieces, 1)

def widen(field):
    channels, depth_cells, plane = field.shape
    return jnp.pad(field.reshape(channels, depth_cells, NX, NY), ((0, 0), (1, 1), (1, 1), (1, 1)))

def one_snapshot(tables, mode_weight, conv_weight, snapshot, cotangent):
    plane_analysis, plane_synthesis, depth_analysis, depth_synthesis = tables
    channels, depth_len, plane = snapshot.shape
    modes_x = 2 * KX
    modes_y = 2 * KY
    plane_coef = lax.dot_general(snapshot.reshape(channels * depth_len, plane), plane_analysis, (((1,), (1,)), ((), ())), preferred_element_type=jnp.float32)
    plane_coef = plane_coef.astype(jnp.bfloat16).reshape(channels, depth_len, modes_x, modes_y)
    coef = highest_einsum('czxy,pz->cpxy', plane_coef, depth_analysis).astype(jnp.bfloat16)
    mixed = highest_einsum('ipxy,xypio->opxy', coef, mode_weight).astype(jnp.bfloat16)
    depth_back = highest_einsum('opxy,zp->ozxy', mixed, depth_synthesis).astype(jnp.bfloat16)
    spectral = lax.dot_general(depth_back.reshape(channels * depth_len, modes_x * modes_y), plane_synthesis, (((1,), (1,)), ((), ())), preferred_element_type=jnp.float32)
    padded = widen(snapshot)
    pre = spectral.reshape(channels, depth_len * plane) + stencil(padded, conv_weight)
    normal_cdf = 0.5 * (1.0 + lax.erf(pre * inv_root_two))
    density = jnp.exp(-0.5 * pre * pre) * inv_root_two_pi
    activated = (pre * normal_cdf).astype(jnp.bfloat16).reshape(channels, depth_len, plane)
    pre_grad = (cotangent.reshape(channels, depth_len * plane).astype(jnp.float32) * (normal_cdf + pre * density)).astype(jnp.bfloat16)
    back_plane = jnp.dot(pre_grad.reshape(channels * depth_len, plane), plane_synthesis, preferred_element_type=jnp.float32)
    back_plane = back_plane.astype(jnp.bfloat16).reshape(channels, depth_len, modes_x, modes_y)
    mixed_grad = highest_einsum('ozxy,zp->opxy', back_plane, depth_synthesis).astype(jnp.bfloat16)
    weight_term = highest_einsum('ipxy,opxy->xypio', coef, mixed_grad)
    coef_grad = highest_einsum('opxy,xypio->ipxy', mixed_grad, mode_weight).astype(jnp.bfloat16)
    depth_grad = highest_einsum('ipxy,pz->izxy', coef_grad, depth_analysis).astype(jnp.bfloat16)
    spectral_grad = jnp.dot(depth_grad.reshape(channels * depth_len, modes_x * modes_y), plane_analysis, preferred_element_type=jnp.float32)
    flipped = jnp.transpose(conv_weight[::-1, ::-1, ::-1], (0, 1, 2, 4, 3))
    local_grad = stencil(widen(pre_grad.reshape(channels, depth_len, plane)), flipped)
    input_gradient = (spectral_grad.reshape(channels, depth_len * plane) + local_grad).astype(jnp.bfloat16).reshape(channels, depth_len, plane)
    kernel_term = kernel_terms(padded, pre_grad)
    return (activated, input_gradient, weight_term, kernel_term)

def reference(snapshots, cotangent, mode_weight, conv_weight):
    tables = make_tables(KX, KY, KZ, NX, NY, NZ)

    def advance(carry, inputs):
        weight_sum, kernel_sum = carry
        activated, input_gradient, weight_term, kernel_term = one_snapshot(tables, mode_weight, conv_weight, inputs[0], inputs[1])
        return ((weight_sum + weight_term, kernel_sum + kernel_term), (activated, input_gradient))
    start_sums = (jnp.zeros(mode_weight.shape, jnp.float32), jnp.zeros(conv_weight.shape, jnp.float32))
    (mode_gradient, kernel_sum), (activated, input_gradient) = lax.scan(advance, start_sums, (snapshots, cotangent))
    conv_gradient = kernel_sum / math.sqrt(SNAPS * NZ * PLANE)
    return (activated, input_gradient, mode_gradient, conv_gradient)
```

```python
import functools
import math

import jax
import jax.numpy as jnp
import ml_dtypes
import numpy as np
from jax import lax
from jax.experimental import pallas as pl
from jax.experimental.pallas import tpu as pltpu
from jax.sharding import PartitionSpec as P

KX = 8
KY = 8
KZ = 12
NX = 32
NY = 32
CELLS = NX * NY
LANES = 128
GROUP = 8
OFFSETS = 27
TERM_ROWS = 1024

F32 = jnp.float32
BF16 = jnp.bfloat16
inv_root_two = 1.0 / math.sqrt(2.0)
inv_root_two_pi = 1.0 / math.sqrt(2.0 * math.pi)


def basis_rows(half_count, length):
    row = np.arange(2 * half_count)[:, None]
    cell = np.arange(length)[None, :]
    frequency = np.where(row < half_count, row, row - half_count + 1)
    phases = (frequency * cell % length).astype(np.float32) * np.float32(2.0 * math.pi / length)
    return np.where(row < half_count, np.cos(phases), np.sin(phases)).astype(np.float32)


def plane_tables(batches, slabs):
    outer = (basis_rows(KX, NX)[:, None, :, None] * basis_rows(KY, NY)[None, :, None, :]).reshape(
        2 * KX, 2 * KY, CELLS
    )
    outer = outer.reshape(batches, 2 * KX // batches, slabs, 2 * KY // slabs, CELLS)
    outer = outer.transpose(0, 2, 1, 3, 4).reshape(4 * KX * KY, CELLS)
    analysis = (outer * np.float32(2.0 / math.sqrt(CELLS))).astype(ml_dtypes.bfloat16)
    synthesis = (outer * np.float32(2.0 / math.sqrt(4 * KX * KY))).astype(ml_dtypes.bfloat16)
    return analysis, synthesis


def depth_tables(batches, slabs, layers, modes):
    rows = basis_rows(KZ, slabs * layers)
    analysis = (rows * np.float32(math.sqrt(2.0 / (slabs * layers)))).astype(ml_dtypes.bfloat16)
    synthesis = (rows * np.float32(math.sqrt(2.0 / (2 * KZ)))).astype(ml_dtypes.bfloat16)

    def spread(table):
        table = table.astype(np.float32).reshape(2 * KZ, slabs, layers)
        full = np.einsum("psz,bc,mn->mpbzcsn", table, np.eye(batches), np.eye(modes))
        return full.reshape(modes * 2 * KZ * batches, layers * batches * slabs * modes)

    def gathered(table):
        return spread(table).astype(ml_dtypes.bfloat16)

    def scattered(table):
        full = spread(table)
        count = full.shape[0]
        full = full.reshape(count, layers, -1).transpose(2, 1, 0)
        return full.reshape(-1, layers * count).astype(ml_dtypes.bfloat16)

    return gathered(analysis), scattered(synthesis), gathered(synthesis), scattered(analysis)


def interleave_table(channels, layers):
    table = np.zeros((channels, layers, layers, channels), np.float32)
    for layer in range(layers):
        table[np.arange(channels), layer, layer, np.arange(channels)] = 1.0
    return table.reshape(channels * layers, channels * layers).astype(ml_dtypes.bfloat16)


def dot(left, right, contract=(1, 0)):
    return lax.dot_general(
        left, right, (((contract[0],), (contract[1],)), ((), ())), preferred_element_type=F32
    )


def low_lanes(rows):
    return lax.broadcasted_iota(jnp.int32, (rows, LANES), 1) < LANES // 2


def swap_halves(values):
    return pltpu.roll(values, LANES // 2, 1)


def doubled(values):
    low = low_lanes(values.shape[0])
    swapped = swap_halves(values)
    return jnp.concatenate(
        [jnp.where(low, values, swapped), jnp.where(low, swapped, values)], axis=0
    )


def halved(values):
    low = low_lanes(values.shape[0])
    return jnp.concatenate([jnp.where(low, values, 0.0), jnp.where(low, 0.0, values)], axis=0)


def edge_layers(cells_first):
    top = cells_first[: CELLS // 2]
    bottom = cells_first[CELLS // 2 :]
    low = low_lanes(CELLS // 2)
    first = jnp.where(low, top, swap_halves(bottom))
    last = jnp.where(low, swap_halves(top), bottom)
    return first.astype(BF16), last.astype(BF16)


def beside_layers(before, after):
    before = before.astype(F32)
    after = after.astype(F32)
    low = low_lanes(CELLS // 2)
    top = jnp.where(low, before, swap_halves(after))
    bottom = jnp.where(low, swap_halves(before), after)
    return jnp.concatenate([top, bottom], axis=0).astype(BF16)


def y_cells(rows):
    return lax.broadcasted_iota(jnp.int32, (rows, LANES), 0) % NY


def from_below(values):
    return jnp.where(y_cells(values.shape[0]) == 0, 0.0, pltpu.roll(values, 1, 0))


def from_above(values):
    rows = values.shape[0]
    return jnp.where(y_cells(rows) == NY - 1, 0.0, pltpu.roll(values, rows - 1, 0))


def pad_cells(padded, own, beside):
    width = own.shape[1] + beside.shape[1]
    padded[0:NY, :] = jnp.zeros((NY, width), BF16)
    padded[NY + CELLS : 2 * NY + CELLS, :] = jnp.zeros((NY, width), BF16)
    padded[NY : NY + CELLS, 0 : own.shape[1]] = own
    padded[NY : NY + CELLS, own.shape[1] :] = beside


BLOCK_OF_DEPTH = {-1: 2, 0: 0, 1: 1, 2: 3}
STEP = 256


def stencil(padded, table, transposed, store):
    for start in range(0, CELLS, STEP):
        total = None
        for b in range(3):
            cells = padded[start + NY * b : start + NY * b + STEP, :]
            term = dot(cells, table[b], (1, 1) if transposed else (1, 0))
            total = term if total is None else total + term
        result = (
            from_below(total[:, 0:LANES])
            + total[:, LANES : 2 * LANES]
            + from_above(total[:, 2 * LANES :])
        )
        store(start, result)


def banded_forward(weights, table):
    half = LANES // 2
    for b in range(3):
        for c in range(3):
            for depth, block in BLOCK_OF_DEPTH.items():
                parts = []
                for out in range(2):
                    a = depth - out + 1
                    if 0 <= a < 3:
                        parts.append(weights[a * 9 + b * 3 + c])
                    else:
                        parts.append(jnp.zeros((half, half), BF16))
                table[b, block * half : (block + 1) * half, c * LANES : (c + 1) * LANES] = (
                    jnp.concatenate(parts, axis=1)
                )


def banded_backward(weights, table):
    half = LANES // 2
    for b in range(3):
        for c in range(3):
            for out in range(2):
                for pair in ((0, 1), (-1, 2)):
                    parts = []
                    for depth in pair:
                        a = depth - out + 1
                        if 0 <= a < 3:
                            parts.append(weights[(2 - a) * 9 + (2 - b) * 3 + 2 - c])
                        else:
                            parts.append(jnp.zeros((half, half), BF16))
                    row = c * LANES + out * half
                    column = BLOCK_OF_DEPTH[pair[0]] * half
                    table[b, row : row + half, column : column + LANES] = jnp.concatenate(
                        parts, axis=1
                    )


def analyse_kernel(field, turn, analysis, cells_out, coef_out, first_out, last_out):
    cells = dot(field[...], turn[...], (0, 0))
    rounded = cells.astype(BF16)
    coef_out[...] = dot(analysis[...], rounded).astype(BF16)
    cells_out[...] = rounded
    first, last = edge_layers(cells)
    first_out[...] = first
    last_out[...] = last


def local_kernel(
    cells, before, after, cotangent, turn, weights, local_out, lanes_out, cotangent_out, padded, table
):
    banded_forward(weights, table)
    beside = beside_layers(before[...], after[...])
    pad_cells(padded, cells[...], beside)

    def store(start, result):
        local_out[start : start + STEP, :] = result

    stencil(padded, table, False, store)
    whole = jnp.concatenate([cells[...].astype(F32), beside.astype(F32)], axis=1)
    lanes_out[...] = whole.T.astype(BF16)
    cotangent_out[...] = dot(cotangent[...], turn[...], (0, 0))


def diagonal_mask(rows, snaps):
    width = GROUP * LANES // 2
    row = lax.broadcasted_iota(jnp.int32, (rows, width), 0)
    lane = lax.broadcasted_iota(jnp.int32, (rows, width), 1)
    return (row // snaps) % GROUP == lane // (LANES // 2)


def mix_kernel(snaps, received, gather, weights, scatter, back_out, diagonal_out):
    both = doubled(received[...].astype(F32)).astype(BF16)
    coef = dot(gather[...], both)
    count = coef.shape[0]
    wide = jnp.concatenate([coef] * (GROUP // 2), axis=1)
    diagonal_out[...] = jnp.where(diagonal_mask(count, snaps), wide, 0.0).astype(BF16)
    rows = GROUP * snaps
    depth = GROUP * LANES // 2
    mixed = jnp.concatenate(
        [
            dot(
                diagonal_out[g * rows : (g + 1) * rows, :],
                weights[g * depth : (g + 1) * depth, :],
            )
            for g in range(count // rows)
        ],
        axis=0,
    )
    mixed = halved(jnp.concatenate([mixed, mixed], axis=1)).astype(BF16)
    back_out[...] = dot(scatter[...], mixed).astype(BF16)


def activate_kernel(
    terms_in_slab,
    received,
    synthesis,
    synthesis_rows,
    local,
    cotangent,
    lanes,
    activated_out,
    grad_out,
    first_out,
    last_out,
    back_out,
    terms_out,
    spread,
):
    pre = dot(synthesis[...], received[...]) + local[...]
    cdf = 0.5 * (1.0 + lax.erf(pre * inv_root_two))
    density = jnp.exp(-0.5 * pre * pre) * inv_root_two_pi
    activated_out[...] = (pre * cdf).astype(BF16)
    grad = (cotangent[...] * (cdf + pre * density)).astype(BF16)
    grad_out[...] = grad
    back = dot(synthesis_rows[...], grad)
    grad = grad.astype(F32)
    first, last = edge_layers(grad)
    first_out[...] = first
    last_out[...] = last
    spread[0:NY, :] = jnp.zeros((NY, 3 * LANES), BF16)
    spread[NY + CELLS : 2 * NY + CELLS, :] = jnp.zeros((NY, 3 * LANES), BF16)
    spread[NY : NY + CELLS, 0:LANES] = from_above(grad).astype(BF16)
    spread[NY : NY + CELLS, LANES : 2 * LANES] = grad.astype(BF16)
    spread[NY : NY + CELLS, 2 * LANES :] = from_below(grad).astype(BF16)
    half = LANES // 2
    low = low_lanes(half)
    twice = {}
    for b in range(3):
        product = dot(lanes[...], spread[NY * (2 - b) : NY * (2 - b) + CELLS, :])
        for c in range(3):
            for a in range(3):
                blocks = [BLOCK_OF_DEPTH[out + a - 1] * half for out in range(2)]
                columns = slice(c * LANES, (c + 1) * LANES)
                both = jnp.where(
                    low,
                    product[blocks[0] : blocks[0] + half, columns],
                    product[blocks[1] : blocks[1] + half, columns],
                )
                twice[a * 9 + b * 3 + c] = both + swap_halves(both)
    pairs = []
    for k in range(0, OFFSETS, 2):
        pairs.append(jnp.where(low, twice[k], twice.get(k + 1, 0.0)))
    pairs.append(jnp.zeros((TERM_ROWS - half * len(pairs), LANES), F32))
    terms = jnp.concatenate(pairs, axis=0)
    if terms_in_slab:
        slab_store(back_out, back, terms)
    else:
        back_out[...] = back.astype(BF16)
        terms_out[...] = terms.astype(BF16)


def slab_store(slab, modes, terms):
    owners = slab.shape[0]
    modes = modes.reshape(owners, 8, LANES)
    slab[:, 0:16, :] = jnp.concatenate([modes, jnp.zeros_like(modes)], axis=1).astype(BF16)
    slab[:, 16:, :] = terms.reshape(owners, -1, LANES).astype(BF16)


def slab_modes(slab):
    owners = slab.shape[0]
    return slab[:, 0:16, :].astype(F32)[:, 0:8, :].reshape(owners * 8, LANES)


def unmix_kernel(snaps, scale, received, terms, gather, weights, scatter, grad_out, mixed_out, sums_out):
    in_slab = terms is None
    modes = slab_modes(received) if in_slab else received[...].astype(F32)
    mixed = dot(gather[...], doubled(modes).astype(BF16)).astype(BF16)
    mixed_out[...] = mixed
    count = mixed.shape[0]
    rows = GROUP * snaps
    depth = GROUP * LANES // 2
    own = diagonal_mask(rows, snaps)
    narrow = mixed[:, 0 : LANES // 2]
    pieces = []
    for g in range(count // rows):
        full = dot(
            narrow[g * rows : (g + 1) * rows, :], weights[g * depth : (g + 1) * depth, :], (1, 1)
        )
        full = jnp.where(own, full, 0.0)
        pieces.append(sum(full[:, k : k + LANES] for k in range(0, depth, LANES)))
    coef = jnp.concatenate(pieces, axis=0)
    coef = coef + swap_halves(coef)
    grad = dot(scatter[...], halved(coef).astype(BF16))
    if in_slab:
        owners = received.shape[0]
        sums = jnp.sum(received[:, 16:, :].astype(F32), axis=0) * scale
        share = sums.shape[0]
        slab_store(
            grad_out, grad, jnp.broadcast_to(sums[None], (owners, share, LANES)).reshape(-1, LANES)
        )
    else:
        grad_out[...] = grad.astype(BF16)
        sums_out[...] = jnp.sum(terms[...].astype(F32), axis=0) * scale


def weight_kernel(snaps, diagonal, mixed, out):
    rows = GROUP * snaps
    depth = GROUP * LANES // 2
    half = LANES // 2
    for g in range(diagonal.shape[0] // rows):
        span = slice(g * rows, (g + 1) * rows)
        out[g * depth : (g + 1) * depth, :] = dot(diagonal[span, :], mixed[span, 0:half], (0, 0))


def output_kernel(cells, turn, out):
    out[...] = dot(turn[...], cells[...], (1, 1)).astype(BF16)


def local_grad_kernel(grad, before, after, weights, out, padded, table):
    banded_backward(weights, table)
    pad_cells(padded, grad[...], beside_layers(before[...], after[...]))

    def store(start, result):
        out[start : start + STEP, :] = result

    stencil(padded, table, True, store)


def finish_kernel(received, sums, synthesis, local, turn, grad_out, stencil_out):
    in_slab = sums is None
    modes = slab_modes(received).astype(BF16) if in_slab else received[...]
    cells = (dot(synthesis[...], modes) + local[...]).astype(BF16)
    grad_out[...] = dot(turn[...], cells, (1, 1)).astype(BF16)
    if in_slab:
        terms = received[:, 16:, :].astype(F32).reshape(TERM_ROWS, LANES)
    else:
        terms = sums[...].astype(F32)
    half = LANES // 2
    for k in range(OFFSETS):
        row = (k // 2) * half
        lane = (k % 2) * half
        stencil_out[k] = terms[row : row + half, lane : lane + half]


def shape(dims, dtype):
    return jax.ShapeDtypeStruct(dims, dtype)


def run(body, outs, *operands, scratch=(), flops=0):
    given = [operand for operand in operands if operand is not None]

    def kernel(*refs):
        refs = list(refs)
        filled = [None if operand is None else refs.pop(0) for operand in operands]
        kept = [None if out is None else refs.pop(0) for out in outs]
        body(*filled, *kept, *refs)

    made = [out for out in outs if out is not None]
    size = sum(x.size * x.dtype.itemsize for x in (*given, *made))
    results = pl.pallas_call(
        kernel,
        out_shape=made,
        in_specs=[pl.BlockSpec(memory_space=pltpu.VMEM)] * len(given),
        out_specs=[pl.BlockSpec(memory_space=pltpu.VMEM)] * len(made),
        scratch_shapes=list(scratch),
        compiler_params=pltpu.CompilerParams(vmem_limit_bytes=40 * 1024 * 1024),
        cost_estimate=pl.CostEstimate(flops=flops, bytes_accessed=size, transcendentals=0),
        name=body.__name__ if hasattr(body, "__name__") else body.func.__name__,
    )(*given)
    results = list(results)
    return [None if out is None else results.pop(0) for out in outs]


def exchange(values):
    return lax.all_to_all(values, ("batch", "space"), split_axis=0, concat_axis=0, tiled=True)


def neighbours(first, last):
    ends = lax.axis_size("space") - 1
    before = lax.ppermute(last, "space", [(i, i + 1) for i in range(ends)])
    after = lax.ppermute(first, "space", [(i + 1, i) for i in range(ends)])
    return before, after


def shards(snapshots, cotangent, mode_weight, conv_weight):
    batches = lax.axis_size("batch")
    slabs = lax.axis_size("space")
    devices = batches * slabs
    _, channels, layers, plane = snapshots.shape
    modes = mode_weight.shape[0] * mode_weight.shape[1]
    half = LANES // 2
    assert channels == half and layers == 2 and plane == CELLS
    plane_rows = devices * modes
    count = modes * 2 * KZ * batches
    in_slab = modes == 8 and devices * 32 == TERM_ROWS

    analysis, synthesis = plane_tables(batches, slabs)
    gather, scatter, gather_back, scatter_back = depth_tables(batches, slabs, layers, modes)
    turn = interleave_table(channels, layers)

    weights = mode_weight.reshape(modes * 2 * KZ * channels, channels)
    taps = conv_weight.reshape(OFFSETS, channels, channels)
    field = snapshots.reshape(channels * layers, plane)
    outer = cotangent.reshape(channels * layers, plane)
    wide = shape((CELLS, LANES), BF16)
    edge = shape((CELLS // 2, LANES), BF16)
    plane_modes = shape((plane_rows, LANES), BF16)
    padded = pltpu.VMEM((CELLS + 2 * NY, 2 * LANES), BF16)

    def send(values):
        return exchange(values.reshape(devices, modes, LANES)).reshape(plane_rows, LANES)

    cells, coef, first, last = run(
        analyse_kernel, [wide, plane_modes, edge, edge], field, turn, analysis, flops=10**8
    )
    coef = send(coef)
    before, after = neighbours(first, last)
    local, lanes, outer_cells = run(
        local_kernel,
        [shape((CELLS, LANES), F32), shape((2 * LANES, CELLS), BF16), shape((CELLS, LANES), F32)],
        cells,
        before,
        after,
        outer,
        turn,
        taps,
        scratch=[padded, pltpu.VMEM((3, 2 * LANES, 3 * LANES), BF16)],
        flops=7 * 10**8,
    )
    back, diagonal = run(
        functools.partial(mix_kernel, batches),
        [plane_modes, shape((count, GROUP * half), BF16)],
        coef,
        gather,
        weights,
        scatter,
        flops=4 * 10**8,
    )
    back = send(back)
    slab = shape((devices, 16 + TERM_ROWS // devices, LANES), BF16)
    activated, grad, first, last, back, terms = run(
        functools.partial(activate_kernel, in_slab),
        [
            wide,
            wide,
            edge,
            edge,
            slab if in_slab else plane_modes,
            None if in_slab else shape((TERM_ROWS, LANES), BF16),
        ],
        back,
        np.ascontiguousarray(synthesis.T),
        synthesis,
        local,
        outer_cells,
        lanes,
        scratch=[pltpu.VMEM((CELLS + 2 * NY, 3 * LANES), BF16)],
        flops=10**9,
    )
    if in_slab:
        back = exchange(back)
    else:
        back = send(back)
        terms = exchange(terms.reshape(devices, TERM_ROWS // devices, LANES))
    before, after = neighbours(first, last)
    (activated,) = run(
        output_kernel, [shape((channels * layers, plane), BF16)], activated, turn, flops=10**8
    )
    (local,) = run(
        local_grad_kernel,
        [shape((CELLS, LANES), F32)],
        grad,
        before,
        after,
        taps,
        scratch=[padded, pltpu.VMEM((3, 3 * LANES, 2 * LANES), BF16)],
        flops=7 * 10**8,
    )
    scale = 1.0 / math.sqrt(batches * slabs * layers * plane)
    grad_modes, mixed_grad, sums = run(
        functools.partial(unmix_kernel, batches, scale),
        [
            slab if in_slab else plane_modes,
            shape((count, LANES), BF16),
            None if in_slab else shape((TERM_ROWS // devices, LANES), F32),
        ],
        back,
        None if in_slab else terms,
        gather_back,
        weights,
        scatter_back,
        flops=4 * 10**8,
    )
    if in_slab:
        grad_modes = exchange(grad_modes)
    else:
        grad_modes = send(grad_modes)
        sums = lax.all_gather(sums, ("batch", "space"), axis=0, tiled=True)
    (mode_gradient,) = run(
        functools.partial(weight_kernel, batches),
        [shape((modes * 2 * KZ * channels, channels), F32)],
        diagonal,
        mixed_grad,
        flops=4 * 10**8,
    )
    input_gradient, conv_gradient = run(
        finish_kernel,
        [shape((channels * layers, plane), BF16), shape((OFFSETS, channels, channels), F32)],
        grad_modes,
        sums,
        np.ascontiguousarray(analysis.T),
        local,
        turn,
        flops=10**8,
    )
    return (
        activated.reshape(snapshots.shape),
        input_gradient.reshape(snapshots.shape),
        mode_gradient.reshape(mode_weight.shape),
        conv_gradient.reshape(conv_weight.shape),
    )


def solution(mesh):
    in_specs = (
        P("batch", None, "space", None),
        P("batch", None, "space", None),
        P("batch", "space", None, None, None),
        P(),
    )
    out_specs = (
        P("batch", None, "space", None),
        P("batch", None, "space", None),
        P("batch", "space", None, None, None),
        P(),
    )
    return jax.shard_map(shards, mesh=mesh, in_specs=in_specs, out_specs=out_specs, check_vma=False)
```

```python
import functools
import math

import jax
import jax.numpy as jnp
import ml_dtypes
import numpy as np
from jax import lax
from jax.experimental import pallas as pl
from jax.experimental.pallas import tpu as pltpu
from jax.sharding import PartitionSpec as P

KX = 8
KY = 8
KZ = 12
NX = 32
NY = 32
CELLS = NX * NY
LANES = 128
GROUP = 8
OFFSETS = 27
TERM_ROWS = 1024

F32 = jnp.float32
BF16 = jnp.bfloat16
inv_root_two = 1.0 / math.sqrt(2.0)
inv_root_two_pi = 1.0 / math.sqrt(2.0 * math.pi)


def basis_rows(half_count, length):
    row = np.arange(2 * half_count)[:, None]
    cell = np.arange(length)[None, :]
    frequency = np.where(row < half_count, row, row - half_count + 1)
    phases = (frequency * cell % length).astype(np.float32) * np.float32(2.0 * math.pi / length)
    return np.where(row < half_count, np.cos(phases), np.sin(phases)).astype(np.float32)


def plane_tables(batches, slabs):
    outer = (basis_rows(KX, NX)[:, None, :, None] * basis_rows(KY, NY)[None, :, None, :]).reshape(
        2 * KX, 2 * KY, CELLS
    )
    outer = outer.reshape(batches, 2 * KX // batches, slabs, 2 * KY // slabs, CELLS)
    outer = outer.transpose(0, 2, 1, 3, 4).reshape(4 * KX * KY, CELLS)
    analysis = (outer * np.float32(2.0 / math.sqrt(CELLS))).astype(ml_dtypes.bfloat16)
    synthesis = (outer * np.float32(2.0 / math.sqrt(4 * KX * KY))).astype(ml_dtypes.bfloat16)
    return analysis, synthesis


def depth_tables(batches, slabs, layers, modes):
    rows = basis_rows(KZ, slabs * layers)
    analysis = (rows * np.float32(math.sqrt(2.0 / (slabs * layers)))).astype(ml_dtypes.bfloat16)
    synthesis = (rows * np.float32(math.sqrt(2.0 / (2 * KZ)))).astype(ml_dtypes.bfloat16)

    def spread(table):
        table = table.astype(np.float32).reshape(2 * KZ, slabs, layers)
        full = np.einsum("psz,bc,mn->mpbzcsn", table, np.eye(batches), np.eye(modes))
        return full.reshape(modes * 2 * KZ * batches, layers * batches * slabs * modes)

    def gathered(table):
        return spread(table).astype(ml_dtypes.bfloat16)

    def scattered(table):
        full = spread(table)
        count = full.shape[0]
        full = full.reshape(count, layers, -1).transpose(2, 1, 0)
        return full.reshape(-1, layers * count).astype(ml_dtypes.bfloat16)

    return gathered(analysis), scattered(synthesis), gathered(synthesis), scattered(analysis)


def interleave_table(channels, layers):
    table = np.zeros((channels, layers, layers, channels), np.float32)
    for layer in range(layers):
        table[np.arange(channels), layer, layer, np.arange(channels)] = 1.0
    return table.reshape(channels * layers, channels * layers).astype(ml_dtypes.bfloat16)


def dot(left, right, contract=(1, 0)):
    return lax.dot_general(
        left, right, (((contract[0],), (contract[1],)), ((), ())), preferred_element_type=F32
    )


def low_lanes(rows):
    return lax.broadcasted_iota(jnp.int32, (rows, LANES), 1) < LANES // 2


def swap_halves(values):
    return pltpu.roll(values, LANES // 2, 1)


def doubled(values):
    low = low_lanes(values.shape[0])
    swapped = swap_halves(values)
    return jnp.concatenate(
        [jnp.where(low, values, swapped), jnp.where(low, swapped, values)], axis=0
    )


def halved(values):
    low = low_lanes(values.shape[0])
    return jnp.concatenate([jnp.where(low, values, 0.0), jnp.where(low, 0.0, values)], axis=0)


def edge_layers(cells_first):
    top = cells_first[: CELLS // 2]
    bottom = cells_first[CELLS // 2 :]
    low = low_lanes(CELLS // 2)
    first = jnp.where(low, top, swap_halves(bottom))
    last = jnp.where(low, swap_halves(top), bottom)
    return first.astype(BF16), last.astype(BF16)


def beside_layers(before, after):
    before = before.astype(F32)
    after = after.astype(F32)
    low = low_lanes(CELLS // 2)
    top = jnp.where(low, before, swap_halves(after))
    bottom = jnp.where(low, swap_halves(before), after)
    return jnp.concatenate([top, bottom], axis=0).astype(BF16)


def y_cells(rows):
    return lax.broadcasted_iota(jnp.int32, (rows, LANES), 0) % NY


def from_below(values):
    return jnp.where(y_cells(values.shape[0]) == 0, 0.0, pltpu.roll(values, 1, 0))


def from_above(values):
    rows = values.shape[0]
    return jnp.where(y_cells(rows) == NY - 1, 0.0, pltpu.roll(values, rows - 1, 0))


def pad_cells(padded, own, beside):
    width = own.shape[1] + beside.shape[1]
    padded[0:NY, :] = jnp.zeros((NY, width), BF16)
    padded[NY + CELLS : 2 * NY + CELLS, :] = jnp.zeros((NY, width), BF16)
    padded[NY : NY + CELLS, 0 : own.shape[1]] = own
    padded[NY : NY + CELLS, own.shape[1] :] = beside


BLOCK_OF_DEPTH = {-1: 2, 0: 0, 1: 1, 2: 3}
STEP = 256


def stencil(padded, table, transposed, store):
    for start in range(0, CELLS, STEP):
        total = None
        for b in range(3):
            cells = padded[start + NY * b : start + NY * b + STEP, :]
            term = dot(cells, table[b], (1, 1) if transposed else (1, 0))
            total = term if total is None else total + term
        result = (
            from_below(total[:, 0:LANES])
            + total[:, LANES : 2 * LANES]
            + from_above(total[:, 2 * LANES :])
        )
        store(start, result)


def banded_forward(weights, table):
    half = LANES // 2
    for b in range(3):
        for c in range(3):
            for depth, block in BLOCK_OF_DEPTH.items():
                parts = []
                for out in range(2):
                    a = depth - out + 1
                    if 0 <= a < 3:
                        parts.append(weights[a * 9 + b * 3 + c])
                    else:
                        parts.append(jnp.zeros((half, half), BF16))
                table[b, block * half : (block + 1) * half, c * LANES : (c + 1) * LANES] = (
                    jnp.concatenate(parts, axis=1)
                )


def banded_backward(weights, table):
    half = LANES // 2
    for b in range(3):
        for c in range(3):
            for out in range(2):
                for pair in ((0, 1), (-1, 2)):
                    parts = []
                    for depth in pair:
                        a = depth - out + 1
                        if 0 <= a < 3:
                            parts.append(weights[(2 - a) * 9 + (2 - b) * 3 + 2 - c])
                        else:
                            parts.append(jnp.zeros((half, half), BF16))
                    row = c * LANES + out * half
                    column = BLOCK_OF_DEPTH[pair[0]] * half
                    table[b, row : row + half, column : column + LANES] = jnp.concatenate(
                        parts, axis=1
                    )


def analyse_kernel(field, turn, analysis, cells_out, coef_out, first_out, last_out):
    cells = dot(field[...], turn[...], (0, 0))
    rounded = cells.astype(BF16)
    coef_out[...] = dot(analysis[...], rounded).astype(BF16)
    cells_out[...] = rounded
    first, last = edge_layers(cells)
    first_out[...] = first
    last_out[...] = last


def local_kernel(
    cells, before, after, cotangent, turn, weights, local_out, lanes_out, cotangent_out, padded, table
):
    banded_forward(weights, table)
    beside = beside_layers(before[...], after[...])
    pad_cells(padded, cells[...], beside)

    def store(start, result):
        local_out[start : start + STEP, :] = result

    stencil(padded, table, False, store)
    whole = jnp.concatenate([cells[...].astype(F32), beside.astype(F32)], axis=1)
    lanes_out[...] = whole.T.astype(BF16)
    cotangent_out[...] = dot(cotangent[...], turn[...], (0, 0)).astype(BF16)


def diagonal_mask(rows, snaps):
    width = GROUP * LANES // 2
    row = lax.broadcasted_iota(jnp.int32, (rows, width), 0)
    lane = lax.broadcasted_iota(jnp.int32, (rows, width), 1)
    return (row // snaps) % GROUP == lane // (LANES // 2)


def mix_kernel(snaps, received, gather, weights, scatter, back_out, diagonal_out):
    both = doubled(received[...].astype(F32)).astype(BF16)
    coef = dot(gather[...], both)
    count = coef.shape[0]
    wide = jnp.concatenate([coef] * (GROUP // 2), axis=1)
    diagonal_out[...] = jnp.where(diagonal_mask(count, snaps), wide, 0.0).astype(BF16)
    rows = GROUP * snaps
    depth = GROUP * LANES // 2
    mixed = jnp.concatenate(
        [
            dot(
                diagonal_out[g * rows : (g + 1) * rows, :],
                weights[g * depth : (g + 1) * depth, :],
            )
            for g in range(count // rows)
        ],
        axis=0,
    )
    mixed = halved(jnp.concatenate([mixed, mixed], axis=1)).astype(BF16)
    back_out[...] = dot(scatter[...], mixed).astype(BF16)


def activate_kernel(
    terms_in_slab,
    received,
    synthesis,
    synthesis_rows,
    local,
    cotangent,
    lanes,
    activated_out,
    grad_out,
    first_out,
    last_out,
    back_out,
    terms_out,
    spread,
):
    pre = dot(synthesis[...], received[...]) + local[...]
    cdf = 0.5 * (1.0 + lax.erf(pre * inv_root_two))
    density = jnp.exp(-0.5 * pre * pre) * inv_root_two_pi
    activated_out[...] = (pre * cdf).astype(BF16)
    grad = (cotangent[...].astype(F32) * (cdf + pre * density)).astype(BF16)
    grad_out[...] = grad
    back = dot(synthesis_rows[...], grad)
    grad = grad.astype(F32)
    first, last = edge_layers(grad)
    first_out[...] = first
    last_out[...] = last
    spread[0:NY, :] = jnp.zeros((NY, 3 * LANES), BF16)
    spread[NY + CELLS : 2 * NY + CELLS, :] = jnp.zeros((NY, 3 * LANES), BF16)
    spread[NY : NY + CELLS, 0:LANES] = from_above(grad).astype(BF16)
    spread[NY : NY + CELLS, LANES : 2 * LANES] = grad.astype(BF16)
    spread[NY : NY + CELLS, 2 * LANES :] = from_below(grad).astype(BF16)
    half = LANES // 2
    low = low_lanes(half)
    twice = {}
    for b in range(3):
        product = dot(lanes[...], spread[NY * (2 - b) : NY * (2 - b) + CELLS, :])
        for c in range(3):
            for a in range(3):
                blocks = [BLOCK_OF_DEPTH[out + a - 1] * half for out in range(2)]
                columns = slice(c * LANES, (c + 1) * LANES)
                both = jnp.where(
                    low,
                    product[blocks[0] : blocks[0] + half, columns],
                    product[blocks[1] : blocks[1] + half, columns],
                )
                twice[a * 9 + b * 3 + c] = both + swap_halves(both)
    pairs = []
    for k in range(0, OFFSETS, 2):
        pairs.append(jnp.where(low, twice[k], twice.get(k + 1, 0.0)))
    pairs.append(jnp.zeros((TERM_ROWS - half * len(pairs), LANES), F32))
    terms = jnp.concatenate(pairs, axis=0)
    if terms_in_slab:
        slab_store(back_out, back, terms)
    else:
        back_out[...] = back.astype(BF16)
        terms_out[...] = terms.astype(BF16)


def slab_store(slab, modes, terms):
    owners = slab.shape[0]
    modes = modes.reshape(owners, 8, LANES)
    terms = terms.reshape(owners, -1, LANES)
    slab[...] = jnp.concatenate([modes, terms], axis=1).astype(BF16)


def slab_load(slab):
    whole = slab[...].astype(F32)
    return whole[:, 0:8, :].reshape(-1, LANES), whole[:, 8:, :]


def unmix_kernel(snaps, scale, received, terms, gather, weights, scatter, grad_out, mixed_out, sums_out):
    in_slab = terms is None
    if in_slab:
        modes, terms = slab_load(received)
    else:
        modes, terms = received[...].astype(F32), terms[...].astype(F32)
    mixed = dot(gather[...], doubled(modes).astype(BF16)).astype(BF16)
    mixed_out[...] = mixed
    count = mixed.shape[0]
    rows = GROUP * snaps
    depth = GROUP * LANES // 2
    own = diagonal_mask(rows, snaps)
    narrow = mixed[:, 0 : LANES // 2]
    sums = jnp.sum(terms, axis=0) * scale
    pieces = []
    for g in range(count // rows):
        full = dot(
            narrow[g * rows : (g + 1) * rows, :], weights[g * depth : (g + 1) * depth, :], (1, 1)
        )
        full = jnp.where(own, full, 0.0)
        pieces.append(sum(full[:, k : k + LANES] for k in range(0, depth, LANES)))
    coef = jnp.concatenate(pieces, axis=0)
    coef = coef + swap_halves(coef)
    grad = dot(scatter[...], halved(coef).astype(BF16))
    if in_slab:
        owners = received.shape[0]
        share = sums.shape[0]
        slab_store(
            grad_out, grad, jnp.broadcast_to(sums[None], (owners, share, LANES)).reshape(-1, LANES)
        )
    else:
        grad_out[...] = grad.astype(BF16)
        sums_out[...] = sums


def weight_kernel(snaps, diagonal, mixed, out):
    rows = GROUP * snaps
    depth = GROUP * LANES // 2
    half = LANES // 2
    for g in range(diagonal.shape[0] // rows):
        span = slice(g * rows, (g + 1) * rows)
        out[g * depth : (g + 1) * depth, :] = dot(diagonal[span, :], mixed[span, 0:half], (0, 0))


def output_kernel(cells, turn, out):
    out[...] = dot(turn[...], cells[...], (1, 1)).astype(BF16)


def local_grad_kernel(grad, before, after, weights, out, padded, table):
    banded_backward(weights, table)
    pad_cells(padded, grad[...], beside_layers(before[...], after[...]))

    def store(start, result):
        out[start : start + STEP, :] = result

    stencil(padded, table, True, store)


def finish_kernel(received, sums, synthesis, local, turn, grad_out, stencil_out):
    in_slab = sums is None
    if in_slab:
        modes, terms = slab_load(received)
        terms = terms.reshape(TERM_ROWS, LANES)
    else:
        modes, terms = received[...], sums[...].astype(F32)
    cells = (dot(synthesis[...], modes.astype(BF16)) + local[...]).astype(BF16)
    grad_out[...] = dot(turn[...], cells, (1, 1)).astype(BF16)
    half = LANES // 2
    for k in range(OFFSETS):
        row = (k // 2) * half
        lane = (k % 2) * half
        stencil_out[k] = terms[row : row + half, lane : lane + half]


def shape(dims, dtype):
    return jax.ShapeDtypeStruct(dims, dtype)


class Staged:
    def __init__(self, source, buffer, semaphore):
        self.copy = pltpu.make_async_copy(source, buffer, semaphore)
        self.buffer = buffer
        self.copy.start()
        self.ready = False

    def load(self):
        if not self.ready:
            self.copy.wait()
            self.ready = True
        return self.buffer

    def __getitem__(self, index):
        return self.load()[index]

    @property
    def shape(self):
        return self.buffer.shape


class Sent:
    def __init__(self, target, buffer, semaphore):
        self.copy = pltpu.make_async_copy(buffer, target, semaphore)
        self.buffer = buffer

    def __setitem__(self, index, value):
        self.buffer[index] = value
        self.copy.start()

    @property
    def shape(self):
        return self.buffer.shape


def run(body, outs, *operands, staged=(), sent=(), after=(), scratch=(), flops=0):
    given = [k for k, operand in enumerate(operands) if operand is not None]
    made = [k for k, out in enumerate(outs) if out is not None]
    staged = [k for k in given if k in staged]
    sent = [k for k in made if k in sent]

    def kernel(*refs):
        refs = list(refs)

        def take(count):
            taken = refs[:count]
            del refs[:count]
            return taken

        filled = dict(zip(given, take(len(given))))
        take(len(after))
        kept = dict(zip(made, take(len(made))))
        own = take(len(scratch))
        for place, (k, buffer) in enumerate(zip(staged, take(len(staged)))):
            filled[k] = Staged(filled[k], buffer, refs[-1].at[place])
        for place, (k, buffer) in enumerate(zip(sent, take(len(sent)))):
            kept[k] = Sent(kept[k], buffer, refs[-1].at[len(staged) + place])
        body(
            *[filled.get(k) for k in range(len(operands))],
            *[kept.get(k) for k in range(len(outs))],
            *own,
        )
        for k in staged:
            filled[k].load()
        for k in sent:
            kept[k].copy.wait()

    arrays = [operands[k] for k in given]
    results = [outs[k] for k in made]
    size = sum(x.size * x.dtype.itemsize for x in (*arrays, *results))
    in_vmem = pl.BlockSpec(memory_space=pltpu.VMEM)
    anywhere = pl.BlockSpec(memory_space=pl.ANY)
    in_hbm = pl.BlockSpec(memory_space=pltpu.HBM)
    buffers = [operands[k] for k in staged] + [outs[k] for k in sent]
    buffers = [pltpu.VMEM(x.shape, x.dtype) for x in buffers]
    if buffers:
        buffers.append(pltpu.SemaphoreType.DMA((len(buffers),)))
    results = pl.pallas_call(
        kernel,
        out_shape=results,
        in_specs=[in_hbm if k in staged else in_vmem for k in given] + [anywhere] * len(after),
        out_specs=[in_hbm if k in sent else in_vmem for k in made],
        scratch_shapes=[*scratch, *buffers],
        compiler_params=pltpu.CompilerParams(vmem_limit_bytes=24 * 1024 * 1024),
        cost_estimate=pl.CostEstimate(flops=flops, bytes_accessed=size, transcendentals=0),
        name=body.__name__ if hasattr(body, "__name__") else body.func.__name__,
    )(*arrays, *after)
    results = dict(zip(made, results))
    return [results.get(k) for k in range(len(outs))]


def exchange(values):
    return lax.all_to_all(values, ("batch", "space"), split_axis=0, concat_axis=0, tiled=True)


def neighbours(first, last):
    ends = lax.axis_size("space") - 1
    before = lax.ppermute(last, "space", [(i, i + 1) for i in range(ends)])
    after = lax.ppermute(first, "space", [(i + 1, i) for i in range(ends)])
    return before, after


def shards(snapshots, cotangent, mode_weight, conv_weight):
    batches = lax.axis_size("batch")
    slabs = lax.axis_size("space")
    devices = batches * slabs
    _, channels, layers, plane = snapshots.shape
    modes = mode_weight.shape[0] * mode_weight.shape[1]
    half = LANES // 2
    assert channels == half and layers == 2 and plane == CELLS
    plane_rows = devices * modes
    count = modes * 2 * KZ * batches
    in_slab = modes == 8 and devices * 32 == TERM_ROWS

    analysis, synthesis = plane_tables(batches, slabs)
    gather, scatter, gather_back, scatter_back = depth_tables(batches, slabs, layers, modes)
    turn = interleave_table(channels, layers)

    weights = mode_weight.reshape(modes * 2 * KZ * channels, channels)
    taps = conv_weight.reshape(OFFSETS, channels, channels)
    field = snapshots.reshape(channels * layers, plane)
    outer = cotangent.reshape(channels * layers, plane)
    wide = shape((CELLS, LANES), BF16)
    edge = shape((CELLS // 2, LANES), BF16)
    plane_modes = shape((plane_rows, LANES), BF16)
    padded = pltpu.VMEM((CELLS + 2 * NY, 2 * LANES), BF16)

    def send(values):
        return exchange(values.reshape(devices, modes, LANES)).reshape(plane_rows, LANES)

    cells, coef, first, last = run(
        analyse_kernel,
        [wide, plane_modes, edge, edge],
        field,
        turn,
        analysis,
        staged=(1, 2),
        sent=(1, 2, 3),
        flops=10**8,
    )
    coef = send(coef)
    before, after = neighbours(first, last)
    local, lanes, outer_cells = run(
        local_kernel,
        [shape((CELLS, LANES), F32), shape((2 * LANES, CELLS), BF16), wide],
        cells,
        before,
        after,
        outer,
        turn,
        taps,
        staged=(4, 5),
        scratch=[padded, pltpu.VMEM((3, 2 * LANES, 3 * LANES), BF16)],
        flops=7 * 10**8,
    )
    back, diagonal = run(
        functools.partial(mix_kernel, batches),
        [plane_modes, shape((count, GROUP * half), BF16)],
        coef,
        gather,
        weights,
        scatter,
        staged=(1, 2, 3),
        sent=(0,),
        flops=4 * 10**8,
    )
    back = send(back)
    slab = shape((devices, 8 + TERM_ROWS // devices, LANES), BF16)
    activated, grad, first, last, back, terms = run(
        functools.partial(activate_kernel, in_slab),
        [
            wide,
            wide,
            edge,
            edge,
            slab if in_slab else plane_modes,
            None if in_slab else shape((TERM_ROWS, LANES), BF16),
        ],
        back,
        np.ascontiguousarray(synthesis.T),
        synthesis,
        local,
        outer_cells,
        lanes,
        staged=(1, 2),
        sent=(2, 3, 4),
        scratch=[pltpu.VMEM((CELLS + 2 * NY, 3 * LANES), BF16)],
        flops=10**9,
    )
    if in_slab:
        back = exchange(back)
    else:
        back = send(back)
        terms = exchange(terms.reshape(devices, TERM_ROWS // devices, LANES))
    before, after = neighbours(first, last)
    (activated,) = run(
        output_kernel,
        [shape((channels * layers, plane), BF16)],
        activated,
        turn,
        staged=(1,),
        flops=10**8,
    )
    scale = 1.0 / math.sqrt(batches * slabs * layers * plane)
    grad_modes, mixed_grad, sums = run(
        functools.partial(unmix_kernel, batches, scale),
        [
            slab if in_slab else plane_modes,
            shape((count, LANES), BF16),
            None if in_slab else shape((TERM_ROWS // devices, LANES), F32),
        ],
        back,
        None if in_slab else terms,
        gather_back,
        weights,
        scatter_back,
        staged=(2, 3, 4),
        sent=(0,),
        after=(before, after, activated),
        flops=4 * 10**8,
    )
    if in_slab:
        grad_modes = exchange(grad_modes)
    else:
        grad_modes = send(grad_modes)
        sums = lax.all_gather(sums, ("batch", "space"), axis=0, tiled=True)
    (local,) = run(
        local_grad_kernel,
        [shape((CELLS, LANES), F32)],
        grad,
        before,
        after,
        taps,
        staged=(3,),
        scratch=[padded, pltpu.VMEM((3, 3 * LANES, 2 * LANES), BF16)],
        flops=7 * 10**8,
    )
    (mode_gradient,) = run(
        functools.partial(weight_kernel, batches),
        [shape((modes * 2 * KZ * channels, channels), F32)],
        diagonal,
        mixed_grad,
        flops=4 * 10**8,
    )
    input_gradient, conv_gradient = run(
        finish_kernel,
        [shape((channels * layers, plane), BF16), shape((OFFSETS, channels, channels), F32)],
        grad_modes,
        sums,
        np.ascontiguousarray(analysis.T),
        local,
        turn,
        staged=(2, 4),
        flops=10**8,
    )
    return (
        activated.reshape(snapshots.shape),
        input_gradient.reshape(snapshots.shape),
        mode_gradient.reshape(mode_weight.shape),
        conv_gradient.reshape(conv_weight.shape),
    )


def solution(mesh):
    in_specs = (
        P("batch", None, "space", None),
        P("batch", None, "space", None),
        P("batch", "space", None, None, None),
        P(),
    )
    out_specs = (
        P("batch", None, "space", None),
        P("batch", None, "space", None),
        P("batch", "space", None, None, None),
        P(),
    )
    return jax.shard_map(shards, mesh=mesh, in_specs=in_specs, out_specs=out_specs, check_vma=False)
```

```python
import functools
import math

import jax
import jax.numpy as jnp
import ml_dtypes
import numpy as np
from jax import lax
from jax.experimental import pallas as pl
from jax.experimental.pallas import tpu as pltpu
from jax.sharding import PartitionSpec as P

KX = 8
KY = 8
KZ = 12
NX = 32
NY = 32
CELLS = NX * NY
LANES = 128
GROUP = 8
OFFSETS = 27
TERM_ROWS = 1024
VMEM_BYTES = 65000 * 1024

F32 = jnp.float32
BF16 = jnp.bfloat16
inv_root_two = 1.0 / math.sqrt(2.0)
inv_root_two_pi = 1.0 / math.sqrt(2.0 * math.pi)


def basis_rows(half_count, length):
    row = np.arange(2 * half_count)[:, None]
    cell = np.arange(length)[None, :]
    frequency = np.where(row < half_count, row, row - half_count + 1)
    phases = (frequency * cell % length).astype(np.float32) * np.float32(2.0 * math.pi / length)
    return np.where(row < half_count, np.cos(phases), np.sin(phases)).astype(np.float32)


def plane_tables(batches, slabs):
    outer = (basis_rows(KX, NX)[:, None, :, None] * basis_rows(KY, NY)[None, :, None, :]).reshape(
        2 * KX, 2 * KY, CELLS
    )
    outer = outer.reshape(batches, 2 * KX // batches, slabs, 2 * KY // slabs, CELLS)
    outer = outer.transpose(0, 2, 1, 3, 4).reshape(4 * KX * KY, CELLS)
    analysis = (outer * np.float32(2.0 / math.sqrt(CELLS))).astype(ml_dtypes.bfloat16)
    synthesis = (outer * np.float32(2.0 / math.sqrt(4 * KX * KY))).astype(ml_dtypes.bfloat16)
    return analysis, synthesis


def depth_tables(batches, slabs, layers, modes):
    rows = basis_rows(KZ, slabs * layers)
    analysis = (rows * np.float32(math.sqrt(2.0 / (slabs * layers)))).astype(ml_dtypes.bfloat16)
    synthesis = (rows * np.float32(math.sqrt(2.0 / (2 * KZ)))).astype(ml_dtypes.bfloat16)

    def spread(table):
        table = table.astype(np.float32).reshape(2 * KZ, slabs, layers)
        full = np.einsum("psz,bc,mn->mpbzcsn", table, np.eye(batches), np.eye(modes))
        return full.reshape(modes * 2 * KZ * batches, layers * batches * slabs * modes)

    def gathered(table):
        return spread(table).astype(ml_dtypes.bfloat16)

    def scattered(table):
        full = spread(table)
        count = full.shape[0]
        full = full.reshape(count, layers, -1).transpose(2, 1, 0)
        return full.reshape(-1, layers * count).astype(ml_dtypes.bfloat16)

    return gathered(analysis), scattered(synthesis), gathered(synthesis), scattered(analysis)


def interleave_table(channels, layers):
    table = np.zeros((channels, layers, layers, channels), np.float32)
    for layer in range(layers):
        table[np.arange(channels), layer, layer, np.arange(channels)] = 1.0
    return table.reshape(channels * layers, channels * layers).astype(ml_dtypes.bfloat16)


def dot(left, right, contract=(1, 0)):
    return lax.dot_general(
        left, right, (((contract[0],), (contract[1],)), ((), ())), preferred_element_type=F32
    )


def low_lanes(rows):
    return lax.broadcasted_iota(jnp.int32, (rows, LANES), 1) < LANES // 2


def swap_halves(values):
    return pltpu.roll(values, LANES // 2, 1)


def doubled(values):
    low = low_lanes(values.shape[0])
    swapped = swap_halves(values)
    return jnp.concatenate(
        [jnp.where(low, values, swapped), jnp.where(low, swapped, values)], axis=0
    )


def halved(values):
    low = low_lanes(values.shape[0])
    return jnp.concatenate([jnp.where(low, values, 0.0), jnp.where(low, 0.0, values)], axis=0)


def edge_layers(cells_first):
    top = cells_first[: CELLS // 2]
    bottom = cells_first[CELLS // 2 :]
    low = low_lanes(CELLS // 2)
    first = jnp.where(low, top, swap_halves(bottom))
    last = jnp.where(low, swap_halves(top), bottom)
    return first.astype(BF16), last.astype(BF16)


def beside_layers(before, after):
    before = before.astype(F32)
    after = after.astype(F32)
    low = low_lanes(CELLS // 2)
    top = jnp.where(low, before, swap_halves(after))
    bottom = jnp.where(low, swap_halves(before), after)
    return jnp.concatenate([top, bottom], axis=0).astype(BF16)


def y_cells(rows):
    return lax.broadcasted_iota(jnp.int32, (rows, LANES), 0) % NY


def from_below(values):
    return jnp.where(y_cells(values.shape[0]) == 0, 0.0, pltpu.roll(values, 1, 0))


def from_above(values):
    rows = values.shape[0]
    return jnp.where(y_cells(rows) == NY - 1, 0.0, pltpu.roll(values, rows - 1, 0))


def pad_cells(padded, own, beside):
    width = own.shape[1] + beside.shape[1]
    padded[0:NY, :] = jnp.zeros((NY, width), BF16)
    padded[NY + CELLS : 2 * NY + CELLS, :] = jnp.zeros((NY, width), BF16)
    padded[NY : NY + CELLS, 0 : own.shape[1]] = own
    padded[NY : NY + CELLS, own.shape[1] :] = beside


BLOCK_OF_DEPTH = {-1: 2, 0: 0, 1: 1, 2: 3}
STEP = 256


def stencil(padded, table, transposed, store):
    for start in range(0, CELLS, STEP):
        total = None
        for b in range(3):
            cells = padded[start + NY * b : start + NY * b + STEP, :]
            term = dot(cells, table[b], (1, 1) if transposed else (1, 0))
            total = term if total is None else total + term
        result = (
            from_below(total[:, 0:LANES])
            + total[:, LANES : 2 * LANES]
            + from_above(total[:, 2 * LANES :])
        )
        store(start, result)


def banded_forward(weights, table):
    half = LANES // 2
    for b in range(3):
        for c in range(3):
            for depth, block in BLOCK_OF_DEPTH.items():
                parts = []
                for out in range(2):
                    a = depth - out + 1
                    if 0 <= a < 3:
                        parts.append(weights[a * 9 + b * 3 + c])
                    else:
                        parts.append(jnp.zeros((half, half), BF16))
                table[b, block * half : (block + 1) * half, c * LANES : (c + 1) * LANES] = (
                    jnp.concatenate(parts, axis=1)
                )


def banded_backward(weights, table):
    half = LANES // 2
    for b in range(3):
        for c in range(3):
            for out in range(2):
                for pair in ((0, 1), (-1, 2)):
                    parts = []
                    for depth in pair:
                        a = depth - out + 1
                        if 0 <= a < 3:
                            parts.append(weights[(2 - a) * 9 + (2 - b) * 3 + 2 - c])
                        else:
                            parts.append(jnp.zeros((half, half), BF16))
                    row = c * LANES + out * half
                    column = BLOCK_OF_DEPTH[pair[0]] * half
                    table[b, row : row + half, column : column + LANES] = jnp.concatenate(
                        parts, axis=1
                    )


def analyse_kernel(field, turn, analysis, cells_out, coef_out, first_out, last_out):
    cells = dot(field[...], turn[...], (0, 0))
    rounded = cells.astype(BF16)
    coef_out[...] = dot(analysis[...], rounded).astype(BF16)
    cells_out[...] = rounded
    first, last = edge_layers(cells)
    first_out[...] = first
    last_out[...] = last


def local_kernel(
    cells, before, after, cotangent, turn, weights, local_out, lanes_out, cotangent_out, padded, table
):
    banded_forward(weights, table)
    beside = beside_layers(before[...], after[...])
    pad_cells(padded, cells[...], beside)

    def store(start, result):
        local_out[start : start + STEP, :] = result

    stencil(padded, table, False, store)
    whole = jnp.concatenate([cells[...].astype(F32), beside.astype(F32)], axis=1)
    lanes_out[...] = whole.T.astype(BF16)
    cotangent_out[...] = dot(cotangent[...], turn[...], (0, 0)).astype(BF16)


def diagonal_mask(rows, snaps):
    width = GROUP * LANES // 2
    row = lax.broadcasted_iota(jnp.int32, (rows, width), 0)
    lane = lax.broadcasted_iota(jnp.int32, (rows, width), 1)
    return (row // snaps) % GROUP == lane // (LANES // 2)


def mix_kernel(snaps, received, gather, weights, scatter, back_out, diagonal_out):
    both = doubled(received[...].astype(F32)).astype(BF16)
    coef = dot(gather[...], both)
    count = coef.shape[0]
    wide = jnp.concatenate([coef] * (GROUP // 2), axis=1)
    diagonal_out[...] = jnp.where(diagonal_mask(count, snaps), wide, 0.0).astype(BF16)
    rows = GROUP * snaps
    depth = GROUP * LANES // 2
    mixed = jnp.concatenate(
        [
            dot(
                diagonal_out[g * rows : (g + 1) * rows, :],
                weights[g * depth : (g + 1) * depth, :],
            )
            for g in range(count // rows)
        ],
        axis=0,
    )
    mixed = halved(jnp.concatenate([mixed, mixed], axis=1)).astype(BF16)
    back_out[...] = dot(scatter[...], mixed).astype(BF16)


def activate_kernel(
    terms_in_slab,
    received,
    synthesis,
    synthesis_rows,
    local,
    cotangent,
    lanes,
    activated_out,
    grad_out,
    first_out,
    last_out,
    back_out,
    terms_out,
    spread,
):
    pre = dot(synthesis[...], received[...]) + local[...]
    cdf = 0.5 * (1.0 + lax.erf(pre * inv_root_two))
    density = jnp.exp(-0.5 * pre * pre) * inv_root_two_pi
    activated_out[...] = (pre * cdf).astype(BF16)
    grad = (cotangent[...].astype(F32) * (cdf + pre * density)).astype(BF16)
    grad_out[...] = grad
    back = dot(synthesis_rows[...], grad)
    grad = grad.astype(F32)
    first, last = edge_layers(grad)
    first_out[...] = first
    last_out[...] = last
    spread[0:NY, :] = jnp.zeros((NY, 3 * LANES), BF16)
    spread[NY + CELLS : 2 * NY + CELLS, :] = jnp.zeros((NY, 3 * LANES), BF16)
    spread[NY : NY + CELLS, 0:LANES] = from_above(grad).astype(BF16)
    spread[NY : NY + CELLS, LANES : 2 * LANES] = grad.astype(BF16)
    spread[NY : NY + CELLS, 2 * LANES :] = from_below(grad).astype(BF16)
    half = LANES // 2
    low = low_lanes(half)
    twice = {}
    for b in range(3):
        product = dot(lanes[...], spread[NY * (2 - b) : NY * (2 - b) + CELLS, :])
        for c in range(3):
            for a in range(3):
                blocks = [BLOCK_OF_DEPTH[out + a - 1] * half for out in range(2)]
                columns = slice(c * LANES, (c + 1) * LANES)
                both = jnp.where(
                    low,
                    product[blocks[0] : blocks[0] + half, columns],
                    product[blocks[1] : blocks[1] + half, columns],
                )
                twice[a * 9 + b * 3 + c] = both + swap_halves(both)
    pairs = []
    for k in range(0, OFFSETS, 2):
        pairs.append(jnp.where(low, twice[k], twice.get(k + 1, 0.0)))
    pairs.append(jnp.zeros((TERM_ROWS - half * len(pairs), LANES), F32))
    terms = jnp.concatenate(pairs, axis=0)
    if terms_in_slab:
        slab_store(back_out, back, terms)
    else:
        back_out[...] = back.astype(BF16)
        terms_out[...] = terms.astype(BF16)


def slab_store(slab, modes, terms):
    owners = slab.shape[0]
    modes = modes.reshape(owners, 8, LANES)
    terms = terms.reshape(owners, -1, LANES)
    slab[...] = jnp.concatenate([modes, terms], axis=1).astype(BF16)


def slab_load(slab):
    whole = slab[...].astype(F32)
    return whole[:, 0:8, :].reshape(-1, LANES), whole[:, 8:, :]


def unmix_kernel(snaps, scale, received, terms, gather, weights, scatter, grad_out, mixed_out, sums_out):
    in_slab = terms is None
    if in_slab:
        modes, terms = slab_load(received)
    else:
        modes, terms = received[...].astype(F32), terms[...].astype(F32)
    mixed = dot(gather[...], doubled(modes).astype(BF16)).astype(BF16)
    mixed_out[...] = mixed
    count = mixed.shape[0]
    rows = GROUP * snaps
    depth = GROUP * LANES // 2
    own = diagonal_mask(rows, snaps)
    narrow = mixed[:, 0 : LANES // 2]
    sums = jnp.sum(terms, axis=0) * scale
    pieces = []
    for g in range(count // rows):
        full = dot(
            narrow[g * rows : (g + 1) * rows, :], weights[g * depth : (g + 1) * depth, :], (1, 1)
        )
        full = jnp.where(own, full, 0.0)
        pieces.append(sum(full[:, k : k + LANES] for k in range(0, depth, LANES)))
    coef = jnp.concatenate(pieces, axis=0)
    coef = coef + swap_halves(coef)
    grad = dot(scatter[...], halved(coef).astype(BF16))
    if in_slab:
        owners = received.shape[0]
        share = sums.shape[0]
        slab_store(
            grad_out, grad, jnp.broadcast_to(sums[None], (owners, share, LANES)).reshape(-1, LANES)
        )
    else:
        grad_out[...] = grad.astype(BF16)
        sums_out[...] = sums


def weight_kernel(snaps, diagonal, mixed, out):
    rows = GROUP * snaps
    depth = GROUP * LANES // 2
    half = LANES // 2
    for g in range(diagonal.shape[0] // rows):
        span = slice(g * rows, (g + 1) * rows)
        out[g * depth : (g + 1) * depth, :] = dot(diagonal[span, :], mixed[span, 0:half], (0, 0))


def output_kernel(cells, turn, out):
    out[...] = dot(turn[...], cells[...], (1, 1)).astype(BF16)


def local_grad_kernel(grad, before, after, weights, out, padded, table):
    banded_backward(weights, table)
    pad_cells(padded, grad[...], beside_layers(before[...], after[...]))

    def store(start, result):
        out[start : start + STEP, :] = result

    stencil(padded, table, True, store)


def finish_kernel(received, sums, synthesis, local, turn, grad_out, stencil_out):
    in_slab = sums is None
    if in_slab:
        modes, terms = slab_load(received)
        terms = terms.reshape(TERM_ROWS, LANES)
    else:
        modes, terms = received[...], sums[...].astype(F32)
    cells = (dot(synthesis[...], modes.astype(BF16)) + local[...]).astype(BF16)
    grad_out[...] = dot(turn[...], cells, (1, 1)).astype(BF16)
    half = LANES // 2
    for k in range(OFFSETS):
        row = (k // 2) * half
        lane = (k % 2) * half
        stencil_out[k] = terms[row : row + half, lane : lane + half]


def shape(dims, dtype):
    return jax.ShapeDtypeStruct(dims, dtype)


class Staged:
    def __init__(self, source, buffer, semaphore):
        self.copy = pltpu.make_async_copy(source, buffer, semaphore)
        self.buffer = buffer
        self.copy.start()
        self.ready = False

    def load(self):
        if not self.ready:
            self.copy.wait()
            self.ready = True
        return self.buffer

    def __getitem__(self, index):
        return self.load()[index]

    @property
    def shape(self):
        return self.buffer.shape


class Sent:
    def __init__(self, target, buffer, semaphore):
        self.copy = pltpu.make_async_copy(buffer, target, semaphore)
        self.buffer = buffer

    def __setitem__(self, index, value):
        self.buffer[index] = value
        self.copy.start()

    @property
    def shape(self):
        return self.buffer.shape


def run(body, outs, *operands, staged=(), sent=(), after=(), scratch=(), flops=0):
    given = [k for k, operand in enumerate(operands) if operand is not None]
    made = [k for k, out in enumerate(outs) if out is not None]
    staged = [k for k in given if k in staged]
    sent = [k for k in made if k in sent]

    def kernel(*refs):
        refs = list(refs)

        def take(count):
            taken = refs[:count]
            del refs[:count]
            return taken

        filled = dict(zip(given, take(len(given))))
        take(len(after))
        kept = dict(zip(made, take(len(made))))
        own = take(len(scratch))
        for place, (k, buffer) in enumerate(zip(staged, take(len(staged)))):
            filled[k] = Staged(filled[k], buffer, refs[-1].at[place])
        for place, (k, buffer) in enumerate(zip(sent, take(len(sent)))):
            kept[k] = Sent(kept[k], buffer, refs[-1].at[len(staged) + place])
        body(
            *[filled.get(k) for k in range(len(operands))],
            *[kept.get(k) for k in range(len(outs))],
            *own,
        )
        for k in staged:
            filled[k].load()
        for k in sent:
            kept[k].copy.wait()

    arrays = [operands[k] for k in given]
    results = [outs[k] for k in made]
    size = sum(x.size * x.dtype.itemsize for x in (*arrays, *results))
    in_vmem = pl.BlockSpec(memory_space=pltpu.VMEM)
    anywhere = pl.BlockSpec(memory_space=pl.ANY)
    in_hbm = pl.BlockSpec(memory_space=pltpu.HBM)
    buffers = [operands[k] for k in staged] + [outs[k] for k in sent]
    buffers = [pltpu.VMEM(x.shape, x.dtype) for x in buffers]
    if buffers:
        buffers.append(pltpu.SemaphoreType.DMA((len(buffers),)))
    results = pl.pallas_call(
        kernel,
        out_shape=results,
        in_specs=[in_hbm if k in staged else in_vmem for k in given] + [anywhere] * len(after),
        out_specs=[in_hbm if k in sent else in_vmem for k in made],
        scratch_shapes=[*scratch, *buffers],
        compiler_params=pltpu.CompilerParams(vmem_limit_bytes=VMEM_BYTES),
        cost_estimate=pl.CostEstimate(flops=flops, bytes_accessed=size, transcendentals=0),
        name=body.__name__ if hasattr(body, "__name__") else body.func.__name__,
    )(*arrays, *after)
    results = dict(zip(made, results))
    return [results.get(k) for k in range(len(outs))]


def exchange(values):
    return lax.all_to_all(values, ("batch", "space"), split_axis=0, concat_axis=0, tiled=True)


def neighbours(first, last):
    ends = lax.axis_size("space") - 1
    before = lax.ppermute(last, "space", [(i, i + 1) for i in range(ends)])
    after = lax.ppermute(first, "space", [(i + 1, i) for i in range(ends)])
    return before, after


def shards(snapshots, cotangent, mode_weight, conv_weight):
    batches = lax.axis_size("batch")
    slabs = lax.axis_size("space")
    devices = batches * slabs
    _, channels, layers, plane = snapshots.shape
    modes = mode_weight.shape[0] * mode_weight.shape[1]
    half = LANES // 2
    assert channels == half and layers == 2 and plane == CELLS
    plane_rows = devices * modes
    count = modes * 2 * KZ * batches
    in_slab = modes == 8 and devices * 32 == TERM_ROWS

    analysis, synthesis = plane_tables(batches, slabs)
    gather, scatter, gather_back, scatter_back = depth_tables(batches, slabs, layers, modes)
    turn = interleave_table(channels, layers)

    weights = mode_weight.reshape(modes * 2 * KZ * channels, channels)
    taps = conv_weight.reshape(OFFSETS, channels, channels)
    field = snapshots.reshape(channels * layers, plane)
    outer = cotangent.reshape(channels * layers, plane)
    wide = shape((CELLS, LANES), BF16)
    edge = shape((CELLS // 2, LANES), BF16)
    plane_modes = shape((plane_rows, LANES), BF16)
    padded = pltpu.VMEM((CELLS + 2 * NY, 2 * LANES), BF16)

    def send(values):
        return exchange(values.reshape(devices, modes, LANES)).reshape(plane_rows, LANES)

    cells, coef, first, last = run(
        analyse_kernel,
        [wide, plane_modes, edge, edge],
        field,
        turn,
        analysis,
        staged=(0, 1, 2),
        sent=(0, 1, 2, 3),
        flops=10**8,
    )
    coef = send(coef)
    before, after = neighbours(first, last)
    local, lanes, outer_cells = run(
        local_kernel,
        [shape((CELLS, LANES), F32), shape((2 * LANES, CELLS), BF16), wide],
        cells,
        before,
        after,
        outer,
        turn,
        taps,
        staged=(0, 1, 2, 3, 4, 5),
        sent=(1, 2),
        scratch=[padded, pltpu.VMEM((3, 2 * LANES, 3 * LANES), BF16)],
        flops=7 * 10**8,
    )
    back, diagonal = run(
        functools.partial(mix_kernel, batches),
        [plane_modes, shape((count, GROUP * half), BF16)],
        coef,
        gather,
        weights,
        scatter,
        staged=(1, 2, 3),
        sent=(0,),
        flops=4 * 10**8,
    )
    back = send(back)
    slab = shape((devices, 8 + TERM_ROWS // devices, LANES), BF16)
    activated, grad, first, last, back, terms = run(
        functools.partial(activate_kernel, in_slab),
        [
            wide,
            wide,
            edge,
            edge,
            slab if in_slab else plane_modes,
            None if in_slab else shape((TERM_ROWS, LANES), BF16),
        ],
        back,
        np.ascontiguousarray(synthesis.T),
        synthesis,
        local,
        outer_cells,
        lanes,
        staged=(1, 2, 3, 4, 5),
        sent=(0, 1, 2, 3, 4),
        scratch=[pltpu.VMEM((CELLS + 2 * NY, 3 * LANES), BF16)],
        flops=10**9,
    )
    if in_slab:
        back = exchange(back)
    else:
        back = send(back)
        terms = exchange(terms.reshape(devices, TERM_ROWS // devices, LANES))
    before, after = neighbours(first, last)
    (activated,) = run(
        output_kernel,
        [shape((channels * layers, plane), BF16)],
        activated,
        turn,
        staged=(0, 1),
        sent=(0,),
        flops=10**8,
    )
    scale = 1.0 / math.sqrt(batches * slabs * layers * plane)
    grad_modes, mixed_grad, sums = run(
        functools.partial(unmix_kernel, batches, scale),
        [
            slab if in_slab else plane_modes,
            shape((count, LANES), BF16),
            None if in_slab else shape((TERM_ROWS // devices, LANES), F32),
        ],
        back,
        None if in_slab else terms,
        gather_back,
        weights,
        scatter_back,
        staged=(2, 3, 4),
        sent=(0, 1),
        after=(before, after, activated),
        flops=4 * 10**8,
    )
    if in_slab:
        grad_modes = exchange(grad_modes)
    else:
        grad_modes = send(grad_modes)
        sums = lax.all_gather(sums, ("batch", "space"), axis=0, tiled=True)
    (local,) = run(
        local_grad_kernel,
        [shape((CELLS, LANES), F32)],
        grad,
        before,
        after,
        taps,
        staged=(0, 1, 2, 3),
        scratch=[padded, pltpu.VMEM((3, 3 * LANES, 2 * LANES), BF16)],
        flops=7 * 10**8,
    )
    (mode_gradient,) = run(
        functools.partial(weight_kernel, batches),
        [shape((modes * 2 * KZ * channels, channels), F32)],
        diagonal,
        mixed_grad,
        staged=(0, 1),
        flops=4 * 10**8,
    )
    input_gradient, conv_gradient = run(
        finish_kernel,
        [shape((channels * layers, plane), BF16), shape((OFFSETS, channels, channels), F32)],
        grad_modes,
        sums,
        np.ascontiguousarray(analysis.T),
        local,
        turn,
        staged=(2, 3, 4),
        sent=(0,),
        flops=10**8,
    )
    return (
        activated.reshape(snapshots.shape),
        input_gradient.reshape(snapshots.shape),
        mode_gradient.reshape(mode_weight.shape),
        conv_gradient.reshape(conv_weight.shape),
    )


def solution(mesh):
    in_specs = (
        P("batch", None, "space", None),
        P("batch", None, "space", None),
        P("batch", "space", None, None, None),
        P(),
    )
    out_specs = (
        P("batch", None, "space", None),
        P("batch", None, "space", None),
        P("batch", "space", None, None, None),
        P(),
    )
    return jax.shard_map(shards, mesh=mesh, in_specs=in_specs, out_specs=out_specs, check_vma=False)
```

```python
import functools
import math

import jax
import jax.numpy as jnp
import ml_dtypes
import numpy as np
from jax import lax
from jax.experimental import pallas as pl
from jax.experimental.pallas import tpu as pltpu
from jax.sharding import PartitionSpec as P

KX = 8
KY = 8
KZ = 12
NX = 32
NY = 32
CELLS = NX * NY
LANES = 128
GROUP = 8
OFFSETS = 27
TERM_ROWS = 1024
VMEM_BYTES = 63000 * 1024

F32 = jnp.float32
BF16 = jnp.bfloat16
inv_root_two = 1.0 / math.sqrt(2.0)
inv_root_two_pi = 1.0 / math.sqrt(2.0 * math.pi)


def basis_rows(half_count, length):
    row = np.arange(2 * half_count)[:, None]
    cell = np.arange(length)[None, :]
    frequency = np.where(row < half_count, row, row - half_count + 1)
    phases = (frequency * cell % length).astype(np.float32) * np.float32(2.0 * math.pi / length)
    return np.where(row < half_count, np.cos(phases), np.sin(phases)).astype(np.float32)


def plane_tables(batches, slabs):
    outer = (basis_rows(KX, NX)[:, None, :, None] * basis_rows(KY, NY)[None, :, None, :]).reshape(
        2 * KX, 2 * KY, CELLS
    )
    outer = outer.reshape(batches, 2 * KX // batches, slabs, 2 * KY // slabs, CELLS)
    outer = outer.transpose(0, 2, 1, 3, 4).reshape(4 * KX * KY, CELLS)
    analysis = (outer * np.float32(2.0 / math.sqrt(CELLS))).astype(ml_dtypes.bfloat16)
    synthesis = (outer * np.float32(2.0 / math.sqrt(4 * KX * KY))).astype(ml_dtypes.bfloat16)
    return analysis, synthesis


def depth_tables(batches, slabs, layers, modes):
    rows = basis_rows(KZ, slabs * layers)
    analysis = (rows * np.float32(math.sqrt(2.0 / (slabs * layers)))).astype(ml_dtypes.bfloat16)
    synthesis = (rows * np.float32(math.sqrt(2.0 / (2 * KZ)))).astype(ml_dtypes.bfloat16)

    def spread(table):
        table = table.astype(np.float32).reshape(2 * KZ, slabs, layers)
        full = np.einsum("psz,bc,mn->mpbzcsn", table, np.eye(batches), np.eye(modes))
        return full.reshape(modes * 2 * KZ * batches, layers * batches * slabs * modes)

    def gathered(table):
        return spread(table).astype(ml_dtypes.bfloat16)

    def scattered(table):
        full = spread(table)
        count = full.shape[0]
        full = full.reshape(count, layers, -1).transpose(2, 1, 0)
        return full.reshape(-1, layers * count).astype(ml_dtypes.bfloat16)

    return gathered(analysis), scattered(synthesis), gathered(synthesis), scattered(analysis)


def interleave_table(channels, layers):
    table = np.zeros((channels, layers, layers, channels), np.float32)
    for layer in range(layers):
        table[np.arange(channels), layer, layer, np.arange(channels)] = 1.0
    return table.reshape(channels * layers, channels * layers).astype(ml_dtypes.bfloat16)


class Piece:
    def __init__(self, row, column, values):
        self.index = (slice(row, row + values.shape[0]), slice(column, column + values.shape[1]))
        self.shape = values.shape
        self.dtype = BF16
        self.values = values


def join_tables(batches, slabs, layers, modes, channels):
    analysis, synthesis = plane_tables(batches, slabs)
    gather, scatter, gather_back, scatter_back = depth_tables(batches, slabs, layers, modes)
    turn = interleave_table(channels, layers)
    parts = {}
    rows = [0]

    def shelf(**named):
        column = 0
        for name, values in named.items():
            parts[name] = Piece(rows[0], column, values)
            column += values.shape[1]
        rows[0] += max(values.shape[0] for values in named.values())

    shelf(analysis=analysis)
    shelf(synthesis=synthesis)
    shelf(
        synthesis_cells=synthesis.T,
        analysis_cells=analysis.T,
        gather=np.concatenate([gather, gather_back], axis=0),
    )
    both = parts.pop("gather")
    first, column = both.index[0].start, both.index[1].start
    parts["gather"] = Piece(first, column, gather)
    parts["gather_back"] = Piece(first + gather.shape[0], column, gather_back)
    shelf(scatter=scatter, turn=turn)
    shelf(scatter_back=scatter_back)
    joined = np.zeros((rows[0], 1024), ml_dtypes.bfloat16)
    for part in parts.values():
        joined[part.index] = part.values
    return joined, parts


def dot(left, right, contract=(1, 0)):
    return lax.dot_general(
        left, right, (((contract[0],), (contract[1],)), ((), ())), preferred_element_type=F32
    )


def low_lanes(rows):
    return lax.broadcasted_iota(jnp.int32, (rows, LANES), 1) < LANES // 2


def swap_halves(values):
    return pltpu.roll(values, LANES // 2, 1)


def doubled(values):
    low = low_lanes(values.shape[0])
    swapped = swap_halves(values)
    return jnp.concatenate(
        [jnp.where(low, values, swapped), jnp.where(low, swapped, values)], axis=0
    )


def halved(values):
    low = low_lanes(values.shape[0])
    return jnp.concatenate([jnp.where(low, values, 0.0), jnp.where(low, 0.0, values)], axis=0)


def edge_layers(cells_first):
    top = cells_first[: CELLS // 2]
    bottom = cells_first[CELLS // 2 :]
    low = low_lanes(CELLS // 2)
    first = jnp.where(low, top, swap_halves(bottom))
    last = jnp.where(low, swap_halves(top), bottom)
    return first.astype(BF16), last.astype(BF16)


def beside_layers(before, after):
    before = before.astype(F32)
    after = after.astype(F32)
    low = low_lanes(CELLS // 2)
    top = jnp.where(low, before, swap_halves(after))
    bottom = jnp.where(low, swap_halves(before), after)
    return jnp.concatenate([top, bottom], axis=0).astype(BF16)


def y_cells(rows):
    return lax.broadcasted_iota(jnp.int32, (rows, LANES), 0) % NY


def from_below(values):
    return jnp.where(y_cells(values.shape[0]) == 0, 0.0, pltpu.roll(values, 1, 0))


def from_above(values):
    rows = values.shape[0]
    return jnp.where(y_cells(rows) == NY - 1, 0.0, pltpu.roll(values, rows - 1, 0))


def pad_cells(padded, own, beside):
    width = own.shape[1] + beside.shape[1]
    padded[0:NY, :] = jnp.zeros((NY, width), BF16)
    padded[NY + CELLS : 2 * NY + CELLS, :] = jnp.zeros((NY, width), BF16)
    padded[NY : NY + CELLS, 0 : own.shape[1]] = own
    padded[NY : NY + CELLS, own.shape[1] :] = beside


BLOCK_OF_DEPTH = {-1: 2, 0: 0, 1: 1, 2: 3}
STEP = 256


def stencil(padded, table, transposed, store):
    for start in range(0, CELLS, STEP):
        total = None
        for b in range(3):
            cells = padded[start + NY * b : start + NY * b + STEP, :]
            term = dot(cells, table[b], (1, 1) if transposed else (1, 0))
            total = term if total is None else total + term
        result = (
            from_below(total[:, 0:LANES])
            + total[:, LANES : 2 * LANES]
            + from_above(total[:, 2 * LANES :])
        )
        store(start, result)


def banded_forward(weights, table):
    half = LANES // 2
    for b in range(3):
        for c in range(3):
            for depth, block in BLOCK_OF_DEPTH.items():
                parts = []
                for out in range(2):
                    a = depth - out + 1
                    if 0 <= a < 3:
                        parts.append(weights[a * 9 + b * 3 + c])
                    else:
                        parts.append(jnp.zeros((half, half), BF16))
                table[b, block * half : (block + 1) * half, c * LANES : (c + 1) * LANES] = (
                    jnp.concatenate(parts, axis=1)
                )


def banded_backward(weights, table):
    half = LANES // 2
    for b in range(3):
        for c in range(3):
            for out in range(2):
                for pair in ((0, 1), (-1, 2)):
                    parts = []
                    for depth in pair:
                        a = depth - out + 1
                        if 0 <= a < 3:
                            parts.append(weights[(2 - a) * 9 + (2 - b) * 3 + 2 - c])
                        else:
                            parts.append(jnp.zeros((half, half), BF16))
                    row = c * LANES + out * half
                    column = BLOCK_OF_DEPTH[pair[0]] * half
                    table[b, row : row + half, column : column + LANES] = jnp.concatenate(
                        parts, axis=1
                    )


def analyse_kernel(field, turn, analysis, cells_out, coef_out, first_out, last_out):
    cells = dot(field[...], turn[...], (0, 0))
    rounded = cells.astype(BF16)
    coef_out[...] = dot(analysis[...], rounded).astype(BF16)
    cells_out[...] = rounded
    first, last = edge_layers(cells)
    first_out[...] = first
    last_out[...] = last


def local_kernel(
    cells, before, after, cotangent, turn, weights, local_out, lanes_out, cotangent_out, padded, table
):
    banded_forward(weights, table)
    beside = beside_layers(before[...], after[...])
    pad_cells(padded, cells[...], beside)

    def store(start, result):
        local_out[start : start + STEP, :] = result

    stencil(padded, table, False, store)
    whole = jnp.concatenate([cells[...].astype(F32), beside.astype(F32)], axis=1)
    lanes_out[...] = whole.T.astype(BF16)
    cotangent_out[...] = dot(cotangent[...], turn[...], (0, 0)).astype(BF16)


def diagonal_mask(rows, snaps):
    width = GROUP * LANES // 2
    row = lax.broadcasted_iota(jnp.int32, (rows, width), 0)
    lane = lax.broadcasted_iota(jnp.int32, (rows, width), 1)
    return (row // snaps) % GROUP == lane // (LANES // 2)


def mix_kernel(snaps, received, gather, weights, scatter, back_out, diagonal_out):
    both = doubled(received[...].astype(F32)).astype(BF16)
    coef = dot(gather[...], both)
    count = coef.shape[0]
    wide = jnp.concatenate([coef] * (GROUP // 2), axis=1)
    diagonal_out[...] = jnp.where(diagonal_mask(count, snaps), wide, 0.0).astype(BF16)
    rows = GROUP * snaps
    depth = GROUP * LANES // 2
    mixed = jnp.concatenate(
        [
            dot(
                diagonal_out[g * rows : (g + 1) * rows, :],
                weights[g * depth : (g + 1) * depth, :],
            )
            for g in range(count // rows)
        ],
        axis=0,
    )
    mixed = halved(jnp.concatenate([mixed, mixed], axis=1)).astype(BF16)
    back_out[...] = dot(scatter[...], mixed).astype(BF16)


def activate_kernel(
    terms_in_slab,
    received,
    synthesis,
    synthesis_rows,
    local,
    cotangent,
    lanes,
    activated_out,
    grad_out,
    first_out,
    last_out,
    back_out,
    terms_out,
    spread,
):
    pre = dot(synthesis[...], received[...]) + local[...]
    cdf = 0.5 * (1.0 + lax.erf(pre * inv_root_two))
    density = jnp.exp(-0.5 * pre * pre) * inv_root_two_pi
    activated_out[...] = (pre * cdf).astype(BF16)
    grad = (cotangent[...].astype(F32) * (cdf + pre * density)).astype(BF16)
    grad_out[...] = grad
    back = dot(synthesis_rows[...], grad)
    grad = grad.astype(F32)
    first, last = edge_layers(grad)
    first_out[...] = first
    last_out[...] = last
    spread[0:NY, :] = jnp.zeros((NY, 3 * LANES), BF16)
    spread[NY + CELLS : 2 * NY + CELLS, :] = jnp.zeros((NY, 3 * LANES), BF16)
    spread[NY : NY + CELLS, 0:LANES] = from_above(grad).astype(BF16)
    spread[NY : NY + CELLS, LANES : 2 * LANES] = grad.astype(BF16)
    spread[NY : NY + CELLS, 2 * LANES :] = from_below(grad).astype(BF16)
    half = LANES // 2
    low = low_lanes(half)
    twice = {}
    for b in range(3):
        product = dot(lanes[...], spread[NY * (2 - b) : NY * (2 - b) + CELLS, :])
        for c in range(3):
            for a in range(3):
                blocks = [BLOCK_OF_DEPTH[out + a - 1] * half for out in range(2)]
                columns = slice(c * LANES, (c + 1) * LANES)
                both = jnp.where(
                    low,
                    product[blocks[0] : blocks[0] + half, columns],
                    product[blocks[1] : blocks[1] + half, columns],
                )
                twice[a * 9 + b * 3 + c] = both + swap_halves(both)
    pairs = []
    for k in range(0, OFFSETS, 2):
        pairs.append(jnp.where(low, twice[k], twice.get(k + 1, 0.0)))
    pairs.append(jnp.zeros((TERM_ROWS - half * len(pairs), LANES), F32))
    terms = jnp.concatenate(pairs, axis=0)
    if terms_in_slab:
        slab_store(back_out, back, terms)
    else:
        back_out[...] = back.astype(BF16)
        terms_out[...] = terms.astype(BF16)


def slab_store(slab, modes, terms):
    owners = slab.shape[0]
    modes = modes.reshape(owners, 8, LANES)
    terms = terms.reshape(owners, -1, LANES)
    slab[...] = jnp.concatenate([modes, terms], axis=1).astype(BF16)


def slab_load(slab):
    whole = slab[...].astype(F32)
    return whole[:, 0:8, :].reshape(-1, LANES), whole[:, 8:, :]


def unmix_kernel(snaps, scale, received, terms, gather, weights, scatter, grad_out, mixed_out, sums_out):
    in_slab = terms is None
    if in_slab:
        modes, terms = slab_load(received)
    else:
        modes, terms = received[...].astype(F32), terms[...].astype(F32)
    mixed = dot(gather[...], doubled(modes).astype(BF16)).astype(BF16)
    mixed_out[...] = mixed
    count = mixed.shape[0]
    rows = GROUP * snaps
    depth = GROUP * LANES // 2
    own = diagonal_mask(rows, snaps)
    narrow = mixed[:, 0 : LANES // 2]
    sums = jnp.sum(terms, axis=0) * scale
    pieces = []
    for g in range(count // rows):
        full = dot(
            narrow[g * rows : (g + 1) * rows, :], weights[g * depth : (g + 1) * depth, :], (1, 1)
        )
        full = jnp.where(own, full, 0.0)
        pieces.append(sum(full[:, k : k + LANES] for k in range(0, depth, LANES)))
    coef = jnp.concatenate(pieces, axis=0)
    coef = coef + swap_halves(coef)
    grad = dot(scatter[...], halved(coef).astype(BF16))
    if in_slab:
        owners = received.shape[0]
        share = sums.shape[0]
        slab_store(
            grad_out, grad, jnp.broadcast_to(sums[None], (owners, share, LANES)).reshape(-1, LANES)
        )
    else:
        grad_out[...] = grad.astype(BF16)
        sums_out[...] = sums


def weight_kernel(snaps, diagonal, mixed, out):
    rows = GROUP * snaps
    depth = GROUP * LANES // 2
    half = LANES // 2
    for g in range(diagonal.shape[0] // rows):
        span = slice(g * rows, (g + 1) * rows)
        out[g * depth : (g + 1) * depth, :] = dot(diagonal[span, :], mixed[span, 0:half], (0, 0))


def output_kernel(cells, turn, out):
    out[...] = dot(turn[...], cells[...], (1, 1)).astype(BF16)


def local_grad_kernel(grad, before, after, weights, out, padded, table):
    banded_backward(weights, table)
    pad_cells(padded, grad[...], beside_layers(before[...], after[...]))

    def store(start, result):
        out[start : start + STEP, :] = result

    stencil(padded, table, True, store)


def finish_kernel(received, sums, synthesis, local, turn, grad_out, stencil_out):
    in_slab = sums is None
    if in_slab:
        modes, terms = slab_load(received)
        terms = terms.reshape(TERM_ROWS, LANES)
    else:
        modes, terms = received[...], sums[...].astype(F32)
    cells = (dot(synthesis[...], modes.astype(BF16)) + local[...]).astype(BF16)
    grad_out[...] = dot(turn[...], cells, (1, 1)).astype(BF16)
    half = LANES // 2
    for k in range(OFFSETS):
        row = (k // 2) * half
        lane = (k % 2) * half
        stencil_out[k] = terms[row : row + half, lane : lane + half]


def shape(dims, dtype):
    return jax.ShapeDtypeStruct(dims, dtype)


class Staged:
    def __init__(self, source, buffer, semaphore):
        self.copy = pltpu.make_async_copy(source, buffer, semaphore)
        self.buffer = buffer
        self.copy.start()
        self.ready = False

    def load(self):
        if not self.ready:
            self.copy.wait()
            self.ready = True
        return self.buffer

    def __getitem__(self, index):
        return self.load()[index]

    @property
    def shape(self):
        return self.buffer.shape


class Sent:
    def __init__(self, target, buffer, semaphore):
        self.copy = pltpu.make_async_copy(buffer, target, semaphore)
        self.buffer = buffer

    def __setitem__(self, index, value):
        self.buffer[index] = value
        self.copy.start()

    @property
    def shape(self):
        return self.buffer.shape


def run(body, outs, *operands, tables=None, staged=(), sent=(), after=(), scratch=(), flops=0):
    pieces = [k for k, operand in enumerate(operands) if isinstance(operand, Piece)]
    given = [k for k, operand in enumerate(operands) if operand is not None and k not in pieces]
    made = [k for k, out in enumerate(outs) if out is not None]
    staged = [k for k in range(len(operands)) if k in pieces or (k in given and k in staged)]
    sent = [k for k in made if k in sent]

    def kernel(*refs):
        refs = list(refs)

        def take(count):
            taken = refs[:count]
            del refs[:count]
            return taken

        filled = dict(zip(given, take(len(given))))
        if pieces:
            joined = take(1)[0]
            for k in pieces:
                filled[k] = joined.at[operands[k].index]
        take(len(after))
        kept = dict(zip(made, take(len(made))))
        own = take(len(scratch))
        for place, (k, buffer) in enumerate(zip(staged, take(len(staged)))):
            filled[k] = Staged(filled[k], buffer, refs[-1].at[place])
        for place, (k, buffer) in enumerate(zip(sent, take(len(sent)))):
            kept[k] = Sent(kept[k], buffer, refs[-1].at[len(staged) + place])
        body(
            *[filled.get(k) for k in range(len(operands))],
            *[kept.get(k) for k in range(len(outs))],
            *own,
        )
        for k in staged:
            filled[k].load()
        for k in sent:
            kept[k].copy.wait()

    arrays = [operands[k] for k in given]
    results = [outs[k] for k in made]
    size = sum(x.size * x.dtype.itemsize for x in (*arrays, *results))
    in_vmem = pl.BlockSpec(memory_space=pltpu.VMEM)
    anywhere = pl.BlockSpec(memory_space=pl.ANY)
    in_hbm = pl.BlockSpec(memory_space=pltpu.HBM)
    buffers = [operands[k] for k in staged] + [outs[k] for k in sent]
    buffers = [pltpu.VMEM(x.shape, x.dtype) for x in buffers]
    if buffers:
        buffers.append(pltpu.SemaphoreType.DMA((len(buffers),)))
    results = pl.pallas_call(
        kernel,
        out_shape=results,
        in_specs=[in_hbm if k in staged else in_vmem for k in given]
        + [in_hbm] * len(pieces[:1])
        + [anywhere] * len(after),
        out_specs=[in_hbm if k in sent else in_vmem for k in made],
        scratch_shapes=[*scratch, *buffers],
        compiler_params=pltpu.CompilerParams(vmem_limit_bytes=VMEM_BYTES),
        cost_estimate=pl.CostEstimate(flops=flops, bytes_accessed=size, transcendentals=0),
        name=body.__name__ if hasattr(body, "__name__") else body.func.__name__,
    )(*arrays, *([tables] if pieces else []), *after)
    results = dict(zip(made, results))
    return [results.get(k) for k in range(len(outs))]


def exchange(values):
    return lax.all_to_all(values, ("batch", "space"), split_axis=0, concat_axis=0, tiled=True)


def neighbours(first, last):
    ends = lax.axis_size("space") - 1
    before = lax.ppermute(last, "space", [(i, i + 1) for i in range(ends)])
    after = lax.ppermute(first, "space", [(i + 1, i) for i in range(ends)])
    return before, after


def shards(snapshots, cotangent, mode_weight, conv_weight):
    batches = lax.axis_size("batch")
    slabs = lax.axis_size("space")
    devices = batches * slabs
    _, channels, layers, plane = snapshots.shape
    modes = mode_weight.shape[0] * mode_weight.shape[1]
    half = LANES // 2
    assert channels == half and layers == 2 and plane == CELLS
    plane_rows = devices * modes
    count = modes * 2 * KZ * batches
    in_slab = modes == 8 and devices * 32 == TERM_ROWS

    tables, parts = join_tables(batches, slabs, layers, modes, channels)
    call = functools.partial(run, tables=tables)
    weights = mode_weight.reshape(modes * 2 * KZ * channels, channels)
    taps = conv_weight.reshape(OFFSETS, channels, channels)
    field = snapshots.reshape(channels * layers, plane)
    outer = cotangent.reshape(channels * layers, plane)
    wide = shape((CELLS, LANES), BF16)
    edge = shape((CELLS // 2, LANES), BF16)
    plane_modes = shape((plane_rows, LANES), BF16)
    padded = pltpu.VMEM((CELLS + 2 * NY, 2 * LANES), BF16)

    def send(values):
        return exchange(values.reshape(devices, modes, LANES)).reshape(plane_rows, LANES)

    cells, coef, first, last = call(
        analyse_kernel,
        [wide, plane_modes, edge, edge],
        field,
        parts["turn"],
        parts["analysis"],
        sent=(1, 2, 3),
        flops=10**8,
    )
    coef = send(coef)
    before, after = neighbours(first, last)
    local, lanes, outer_cells = call(
        local_kernel,
        [shape((CELLS, LANES), F32), shape((2 * LANES, CELLS), BF16), wide],
        cells,
        before,
        after,
        outer,
        parts["turn"],
        taps,
        staged=(5,),
        scratch=[padded, pltpu.VMEM((3, 2 * LANES, 3 * LANES), BF16)],
        flops=7 * 10**8,
    )
    back, diagonal = call(
        functools.partial(mix_kernel, batches),
        [plane_modes, shape((count, GROUP * half), BF16)],
        coef,
        parts["gather"],
        weights,
        parts["scatter"],
        staged=(2,),
        sent=(0,),
        flops=4 * 10**8,
    )
    back = send(back)
    slab = shape((devices, 8 + TERM_ROWS // devices, LANES), BF16)
    activated, grad, first, last, back, terms = call(
        functools.partial(activate_kernel, in_slab),
        [
            wide,
            wide,
            edge,
            edge,
            slab if in_slab else plane_modes,
            None if in_slab else shape((TERM_ROWS, LANES), BF16),
        ],
        back,
        parts["synthesis_cells"],
        parts["synthesis"],
        local,
        outer_cells,
        lanes,
        sent=(2, 3, 4),
        scratch=[pltpu.VMEM((CELLS + 2 * NY, 3 * LANES), BF16)],
        flops=10**9,
    )
    if in_slab:
        back = exchange(back)
    else:
        back = send(back)
        terms = exchange(terms.reshape(devices, TERM_ROWS // devices, LANES))
    before, after = neighbours(first, last)
    (activated,) = call(
        output_kernel,
        [shape((channels * layers, plane), BF16)],
        activated,
        parts["turn"],
        flops=10**8,
    )
    back, before, after, activated = lax.optimization_barrier((back, before, after, activated))
    scale = 1.0 / math.sqrt(batches * slabs * layers * plane)
    grad_modes, mixed_grad, sums = call(
        functools.partial(unmix_kernel, batches, scale),
        [
            slab if in_slab else plane_modes,
            shape((count, LANES), BF16),
            None if in_slab else shape((TERM_ROWS // devices, LANES), F32),
        ],
        back,
        None if in_slab else terms,
        parts["gather_back"],
        weights,
        parts["scatter_back"],
        staged=(3,),
        sent=(0,),
        flops=4 * 10**8,
    )
    if in_slab:
        grad_modes = exchange(grad_modes)
    else:
        grad_modes = send(grad_modes)
        sums = lax.all_gather(sums, ("batch", "space"), axis=0, tiled=True)
    (local,) = call(
        local_grad_kernel,
        [shape((CELLS, LANES), F32)],
        grad,
        before,
        after,
        taps,
        staged=(3,),
        scratch=[padded, pltpu.VMEM((3, 3 * LANES, 2 * LANES), BF16)],
        flops=7 * 10**8,
    )
    (mode_gradient,) = call(
        functools.partial(weight_kernel, batches),
        [shape((modes * 2 * KZ * channels, channels), F32)],
        diagonal,
        mixed_grad,
        flops=4 * 10**8,
    )
    input_gradient, conv_gradient = call(
        finish_kernel,
        [shape((channels * layers, plane), BF16), shape((OFFSETS, channels, channels), F32)],
        grad_modes,
        sums,
        parts["analysis_cells"],
        local,
        parts["turn"],
        flops=10**8,
    )
    return (
        activated.reshape(snapshots.shape),
        input_gradient.reshape(snapshots.shape),
        mode_gradient.reshape(mode_weight.shape),
        conv_gradient.reshape(conv_weight.shape),
    )


def solution(mesh):
    in_specs = (
        P("batch", None, "space", None),
        P("batch", None, "space", None),
        P("batch", "space", None, None, None),
        P(),
    )
    out_specs = (
        P("batch", None, "space", None),
        P("batch", None, "space", None),
        P("batch", "space", None, None, None),
        P(),
    )
    return jax.shard_map(shards, mesh=mesh, in_specs=in_specs, out_specs=out_specs, check_vma=False)
```

```python
import functools
import math

import jax
import jax.numpy as jnp
import ml_dtypes
import numpy as np
from jax import lax
from jax.experimental import pallas as pl
from jax.experimental.pallas import tpu as pltpu
from jax.sharding import PartitionSpec as P

KX = 8
KY = 8
KZ = 12
NX = 32
NY = 32
CELLS = NX * NY
LANES = 128
GROUP = 8
OFFSETS = 27
TERM_ROWS = 1024
VMEM_BYTES = 40 * 1024 * 1024

F32 = jnp.float32
BF16 = jnp.bfloat16
inv_root_two = 1.0 / math.sqrt(2.0)
inv_root_two_pi = 1.0 / math.sqrt(2.0 * math.pi)


def basis_rows(half_count, length):
    row = np.arange(2 * half_count)[:, None]
    cell = np.arange(length)[None, :]
    frequency = np.where(row < half_count, row, row - half_count + 1)
    phases = (frequency * cell % length).astype(np.float32) * np.float32(2.0 * math.pi / length)
    return np.where(row < half_count, np.cos(phases), np.sin(phases)).astype(np.float32)


def plane_tables(batches, slabs):
    outer = (basis_rows(KX, NX)[:, None, :, None] * basis_rows(KY, NY)[None, :, None, :]).reshape(
        2 * KX, 2 * KY, CELLS
    )
    outer = outer.reshape(batches, 2 * KX // batches, slabs, 2 * KY // slabs, CELLS)
    outer = outer.transpose(0, 2, 1, 3, 4).reshape(4 * KX * KY, CELLS)
    analysis = (outer * np.float32(2.0 / math.sqrt(CELLS))).astype(ml_dtypes.bfloat16)
    synthesis = (outer * np.float32(2.0 / math.sqrt(4 * KX * KY))).astype(ml_dtypes.bfloat16)
    return analysis, synthesis


def depth_tables(batches, slabs, layers, modes):
    rows = basis_rows(KZ, slabs * layers)
    analysis = (rows * np.float32(math.sqrt(2.0 / (slabs * layers)))).astype(ml_dtypes.bfloat16)
    synthesis = (rows * np.float32(math.sqrt(2.0 / (2 * KZ)))).astype(ml_dtypes.bfloat16)

    def spread(table):
        table = table.astype(np.float32).reshape(2 * KZ, slabs, layers)
        full = np.einsum("psz,bc,mn->mpbzcsn", table, np.eye(batches), np.eye(modes))
        return full.reshape(modes * 2 * KZ * batches, layers * batches * slabs * modes)

    def gathered(table):
        return spread(table).astype(ml_dtypes.bfloat16)

    def scattered(table):
        full = spread(table)
        count = full.shape[0]
        full = full.reshape(count, layers, -1).transpose(2, 1, 0)
        return full.reshape(-1, layers * count).astype(ml_dtypes.bfloat16)

    return gathered(analysis), scattered(synthesis), gathered(synthesis), scattered(analysis)


def interleave_table(channels, layers):
    table = np.zeros((channels, layers, layers, channels), np.float32)
    for layer in range(layers):
        table[np.arange(channels), layer, layer, np.arange(channels)] = 1.0
    return table.reshape(channels * layers, channels * layers).astype(ml_dtypes.bfloat16)


def dot(left, right, contract=(1, 0)):
    return lax.dot_general(
        left, right, (((contract[0],), (contract[1],)), ((), ())), preferred_element_type=F32
    )


def low_lanes(rows):
    return lax.broadcasted_iota(jnp.int32, (rows, LANES), 1) < LANES // 2


def swap_halves(values):
    return pltpu.roll(values, LANES // 2, 1)


def doubled(values):
    low = low_lanes(values.shape[0])
    swapped = swap_halves(values)
    return jnp.concatenate(
        [jnp.where(low, values, swapped), jnp.where(low, swapped, values)], axis=0
    )


def halved(values):
    low = low_lanes(values.shape[0])
    return jnp.concatenate([jnp.where(low, values, 0.0), jnp.where(low, 0.0, values)], axis=0)


def edge_layers(cells_first):
    top = cells_first[: CELLS // 2]
    bottom = cells_first[CELLS // 2 :]
    low = low_lanes(CELLS // 2)
    first = jnp.where(low, top, swap_halves(bottom))
    last = jnp.where(low, swap_halves(top), bottom)
    return first.astype(BF16), last.astype(BF16)


def beside_layers(before, after):
    before = before.astype(F32)
    after = after.astype(F32)
    low = low_lanes(CELLS // 2)
    top = jnp.where(low, before, swap_halves(after))
    bottom = jnp.where(low, swap_halves(before), after)
    return jnp.concatenate([top, bottom], axis=0).astype(BF16)


def y_cells(rows):
    return lax.broadcasted_iota(jnp.int32, (rows, LANES), 0) % NY


def from_below(values):
    return jnp.where(y_cells(values.shape[0]) == 0, 0.0, pltpu.roll(values, 1, 0))


def from_above(values):
    rows = values.shape[0]
    return jnp.where(y_cells(rows) == NY - 1, 0.0, pltpu.roll(values, rows - 1, 0))


def pad_cells(padded, own, beside):
    width = own.shape[1] + beside.shape[1]
    padded[0:NY, :] = jnp.zeros((NY, width), BF16)
    padded[NY + CELLS : 2 * NY + CELLS, :] = jnp.zeros((NY, width), BF16)
    padded[NY : NY + CELLS, 0 : own.shape[1]] = own
    padded[NY : NY + CELLS, own.shape[1] :] = beside


BLOCK_OF_DEPTH = {-1: 2, 0: 0, 1: 1, 2: 3}
STEP = 256


def stencil(padded, table, transposed, store):
    for start in range(0, CELLS, STEP):
        total = None
        for b in range(3):
            cells = padded[start + NY * b : start + NY * b + STEP, :]
            term = dot(cells, table[b], (1, 1) if transposed else (1, 0))
            total = term if total is None else total + term
        result = (
            from_below(total[:, 0:LANES])
            + total[:, LANES : 2 * LANES]
            + from_above(total[:, 2 * LANES :])
        )
        store(start, result)


def banded_forward(weights, table):
    half = LANES // 2
    for b in range(3):
        for c in range(3):
            for depth, block in BLOCK_OF_DEPTH.items():
                parts = []
                for out in range(2):
                    a = depth - out + 1
                    if 0 <= a < 3:
                        parts.append(weights[a * 9 + b * 3 + c])
                    else:
                        parts.append(jnp.zeros((half, half), BF16))
                table[b, block * half : (block + 1) * half, c * LANES : (c + 1) * LANES] = (
                    jnp.concatenate(parts, axis=1)
                )


def banded_backward(weights, table):
    half = LANES // 2
    for b in range(3):
        for c in range(3):
            for out in range(2):
                for pair in ((0, 1), (-1, 2)):
                    parts = []
                    for depth in pair:
                        a = depth - out + 1
                        if 0 <= a < 3:
                            parts.append(weights[(2 - a) * 9 + (2 - b) * 3 + 2 - c])
                        else:
                            parts.append(jnp.zeros((half, half), BF16))
                    row = c * LANES + out * half
                    column = BLOCK_OF_DEPTH[pair[0]] * half
                    table[b, row : row + half, column : column + LANES] = jnp.concatenate(
                        parts, axis=1
                    )


def analyse_kernel(field, turn, analysis, cells_out, coef_out, first_out, last_out):
    cells = dot(field[...], turn[...], (0, 0))
    rounded = cells.astype(BF16)
    coef_out[...] = dot(analysis[...], rounded).astype(BF16)
    cells_out[...] = rounded
    first, last = edge_layers(cells)
    first_out[...] = first
    last_out[...] = last


def local_kernel(
    cells, before, after, cotangent, turn, weights, local_out, lanes_out, cotangent_out, padded, table
):
    banded_forward(weights, table)
    beside = beside_layers(before[...], after[...])
    pad_cells(padded, cells[...], beside)

    def store(start, result):
        local_out[start : start + STEP, :] = result

    stencil(padded, table, False, store)
    whole = jnp.concatenate([cells[...].astype(F32), beside.astype(F32)], axis=1)
    lanes_out[...] = whole.T.astype(BF16)
    cotangent_out[...] = dot(cotangent[...], turn[...], (0, 0)).astype(BF16)


def pack_kernel(weights, out):
    rows = GROUP * LANES // 4
    for g in range(out.shape[0] // rows):
        first = weights[2 * g * rows : (2 * g + 1) * rows, :]
        second = weights[(2 * g + 1) * rows : (2 * g + 2) * rows, :]
        out[g * rows : (g + 1) * rows, :] = jnp.concatenate([first, second], axis=1)


def mode_in_group(rows, lanes, snaps):
    return (lax.broadcasted_iota(jnp.int32, (rows, lanes), 0) // snaps) % GROUP


def own_block(rows, snaps):
    width = GROUP * LANES // 4
    lane = lax.broadcasted_iota(jnp.int32, (rows, width), 1)
    return mode_in_group(rows, width, snaps) % (GROUP // 2) == lane // (LANES // 2)


def own_half(rows, snaps):
    return (mode_in_group(rows, LANES, snaps) < GROUP // 2) == low_lanes(rows)


def mix_kernel(snaps, received, gather, weights, scatter, back_out, diagonal_out):
    both = doubled(received[...].astype(F32)).astype(BF16)
    coef = dot(gather[...], both)
    count = coef.shape[0]
    wide = jnp.concatenate([coef] * (GROUP // 4), axis=1)
    diagonal_out[...] = jnp.where(own_block(count, snaps), wide, 0.0).astype(BF16)
    rows = GROUP * snaps
    depth = GROUP * LANES // 4
    mixed = jnp.concatenate(
        [
            dot(
                diagonal_out[g * rows : (g + 1) * rows, :],
                weights[g * depth : (g + 1) * depth, :],
            )
            for g in range(count // rows)
        ],
        axis=0,
    )
    mixed = jnp.where(own_half(count, snaps), mixed, swap_halves(mixed))
    back_out[...] = dot(scatter[...], halved(mixed).astype(BF16)).astype(BF16)


def activate_kernel(
    terms_in_slab,
    received,
    synthesis,
    synthesis_rows,
    local,
    cotangent,
    lanes,
    activated_out,
    grad_out,
    first_out,
    last_out,
    back_out,
    terms_out,
    spread,
):
    pre = dot(synthesis[...], received[...]) + local[...]
    cdf = 0.5 * (1.0 + lax.erf(pre * inv_root_two))
    density = jnp.exp(-0.5 * pre * pre) * inv_root_two_pi
    activated_out[...] = (pre * cdf).astype(BF16)
    grad = (cotangent[...].astype(F32) * (cdf + pre * density)).astype(BF16)
    grad_out[...] = grad
    back = dot(synthesis_rows[...], grad)
    grad = grad.astype(F32)
    first, last = edge_layers(grad)
    first_out[...] = first
    last_out[...] = last
    spread[0:NY, :] = jnp.zeros((NY, 3 * LANES), BF16)
    spread[NY + CELLS : 2 * NY + CELLS, :] = jnp.zeros((NY, 3 * LANES), BF16)
    spread[NY : NY + CELLS, 0:LANES] = from_above(grad).astype(BF16)
    spread[NY : NY + CELLS, LANES : 2 * LANES] = grad.astype(BF16)
    spread[NY : NY + CELLS, 2 * LANES :] = from_below(grad).astype(BF16)
    half = LANES // 2
    low = low_lanes(half)
    twice = {}
    for b in range(3):
        product = dot(lanes[...], spread[NY * (2 - b) : NY * (2 - b) + CELLS, :])
        for c in range(3):
            for a in range(3):
                blocks = [BLOCK_OF_DEPTH[out + a - 1] * half for out in range(2)]
                columns = slice(c * LANES, (c + 1) * LANES)
                both = jnp.where(
                    low,
                    product[blocks[0] : blocks[0] + half, columns],
                    product[blocks[1] : blocks[1] + half, columns],
                )
                twice[a * 9 + b * 3 + c] = both + swap_halves(both)
    pairs = []
    for k in range(0, OFFSETS, 2):
        pairs.append(jnp.where(low, twice[k], twice.get(k + 1, 0.0)))
    pairs.append(jnp.zeros((TERM_ROWS - half * len(pairs), LANES), F32))
    terms = jnp.concatenate(pairs, axis=0)
    if terms_in_slab:
        slab_store(back_out, back, terms)
    else:
        back_out[...] = back.astype(BF16)
        terms_out[...] = terms.astype(BF16)


def slab_store(slab, modes, terms):
    owners = slab.shape[0]
    modes = modes.reshape(owners, 8, LANES)
    terms = terms.reshape(owners, -1, LANES)
    slab[...] = jnp.concatenate([modes, terms], axis=1).astype(BF16)


def slab_load(slab):
    whole = slab[...].astype(F32)
    return whole[:, 0:8, :].reshape(-1, LANES), whole[:, 8:, :]


def unmix_kernel(snaps, scale, received, terms, gather, weights, scatter, grad_out, mixed_out, sums_out):
    in_slab = terms is None
    if in_slab:
        modes, terms = slab_load(received)
    else:
        modes, terms = received[...].astype(F32), terms[...].astype(F32)
    mixed = dot(gather[...], doubled(modes).astype(BF16))
    mixed_out[...] = mixed.astype(BF16)
    count = mixed.shape[0]
    rows = GROUP * snaps
    depth = GROUP * LANES // 4
    sums = jnp.sum(terms, axis=0) * scale
    own = own_block(rows, snaps)
    placed = jnp.where(own_half(count, snaps), mixed, 0.0).astype(BF16)
    pieces = []
    for g in range(count // rows):
        full = dot(
            placed[g * rows : (g + 1) * rows, :], weights[g * depth : (g + 1) * depth, :], (1, 1)
        )
        full = jnp.where(own, full, 0.0)
        pieces.append(sum(full[:, k : k + LANES] for k in range(0, depth, LANES)))
    coef = jnp.concatenate(pieces, axis=0)
    coef = coef + swap_halves(coef)
    grad = dot(scatter[...], halved(coef).astype(BF16))
    if in_slab:
        owners = received.shape[0]
        share = sums.shape[0]
        slab_store(
            grad_out, grad, jnp.broadcast_to(sums[None], (owners, share, LANES)).reshape(-1, LANES)
        )
    else:
        grad_out[...] = grad.astype(BF16)
        sums_out[...] = sums


def weight_kernel(snaps, diagonal, mixed, out):
    rows = GROUP * snaps
    depth = GROUP * LANES // 4
    half = LANES // 2
    first = mode_in_group(rows, depth, snaps) < GROUP // 2
    for g in range(diagonal.shape[0] // rows):
        span = slice(g * rows, (g + 1) * rows)
        blocks = diagonal[span, :].astype(F32)
        blocks = [jnp.where(first, blocks, 0.0), jnp.where(first, 0.0, blocks)]
        blocks = jnp.concatenate(blocks, axis=1).astype(BF16)
        out[2 * g * depth : 2 * (g + 1) * depth, :] = dot(blocks, mixed[span, 0:half], (0, 0))


def output_kernel(cells, turn, out):
    out[...] = dot(turn[...], cells[...], (1, 1)).astype(BF16)


def local_grad_kernel(grad, before, after, weights, out, padded, table):
    banded_backward(weights, table)
    pad_cells(padded, grad[...], beside_layers(before[...], after[...]))

    def store(start, result):
        out[start : start + STEP, :] = result

    stencil(padded, table, True, store)


def finish_kernel(received, sums, synthesis, local, turn, grad_out, stencil_out):
    in_slab = sums is None
    if in_slab:
        modes, terms = slab_load(received)
        terms = terms.reshape(TERM_ROWS, LANES)
    else:
        modes, terms = received[...], sums[...].astype(F32)
    cells = (dot(synthesis[...], modes.astype(BF16)) + local[...]).astype(BF16)
    grad_out[...] = dot(turn[...], cells, (1, 1)).astype(BF16)
    half = LANES // 2
    for k in range(OFFSETS):
        row = (k // 2) * half
        lane = (k % 2) * half
        stencil_out[k] = terms[row : row + half, lane : lane + half]


def shape(dims, dtype):
    return jax.ShapeDtypeStruct(dims, dtype)


class Sent:
    def __init__(self, target, buffer, semaphore):
        self.copy = pltpu.make_async_copy(buffer, target, semaphore)
        self.buffer = buffer

    def __setitem__(self, index, value):
        self.buffer[index] = value
        self.copy.start()

    @property
    def shape(self):
        return self.buffer.shape


def run(body, outs, *operands, sent=(), scratch=(), flops=0):
    given = [k for k, operand in enumerate(operands) if operand is not None]
    made = [k for k, out in enumerate(outs) if out is not None]
    sent = [k for k in made if k in sent]

    def kernel(*refs):
        refs = list(refs)

        def take(count):
            taken = refs[:count]
            del refs[:count]
            return taken

        filled = dict(zip(given, take(len(given))))
        kept = dict(zip(made, take(len(made))))
        own = take(len(scratch))
        for place, (k, buffer) in enumerate(zip(sent, take(len(sent)))):
            kept[k] = Sent(kept[k], buffer, refs[-1].at[place])
        body(
            *[filled.get(k) for k in range(len(operands))],
            *[kept.get(k) for k in range(len(outs))],
            *own,
        )
        for k in sent:
            kept[k].copy.wait()

    arrays = [operands[k] for k in given]
    results = [outs[k] for k in made]
    size = sum(x.size * x.dtype.itemsize for x in (*arrays, *results))
    in_vmem = pl.BlockSpec(memory_space=pltpu.VMEM)
    in_hbm = pl.BlockSpec(memory_space=pltpu.HBM)
    buffers = [pltpu.VMEM(outs[k].shape, outs[k].dtype) for k in sent]
    if buffers:
        buffers.append(pltpu.SemaphoreType.DMA((len(buffers),)))
    results = pl.pallas_call(
        kernel,
        out_shape=results,
        in_specs=[in_vmem] * len(given),
        out_specs=[in_hbm if k in sent else in_vmem for k in made],
        scratch_shapes=[*scratch, *buffers],
        compiler_params=pltpu.CompilerParams(vmem_limit_bytes=VMEM_BYTES),
        cost_estimate=pl.CostEstimate(flops=flops, bytes_accessed=size, transcendentals=0),
        name=body.__name__ if hasattr(body, "__name__") else body.func.__name__,
    )(*arrays)
    results = dict(zip(made, results))
    return [results.get(k) for k in range(len(outs))]


def exchange(values):
    return lax.all_to_all(values, ("batch", "space"), split_axis=0, concat_axis=0, tiled=True)


def neighbours(first, last):
    ends = lax.axis_size("space") - 1
    before = lax.ppermute(last, "space", [(i, i + 1) for i in range(ends)])
    after = lax.ppermute(first, "space", [(i + 1, i) for i in range(ends)])
    return before, after


def shards(snapshots, cotangent, mode_weight, conv_weight):
    batches = lax.axis_size("batch")
    slabs = lax.axis_size("space")
    devices = batches * slabs
    _, channels, layers, plane = snapshots.shape
    modes = mode_weight.shape[0] * mode_weight.shape[1]
    half = LANES // 2
    assert channels == half and layers == 2 and plane == CELLS
    plane_rows = devices * modes
    count = modes * 2 * KZ * batches
    in_slab = modes == 8 and devices * 32 == TERM_ROWS

    analysis, synthesis = plane_tables(batches, slabs)
    gather, scatter, gather_back, scatter_back = depth_tables(batches, slabs, layers, modes)
    turn = interleave_table(channels, layers)
    weights = mode_weight.reshape(modes * 2 * KZ * channels, channels)
    taps = conv_weight.reshape(OFFSETS, channels, channels)
    field = snapshots.reshape(channels * layers, plane)
    outer = cotangent.reshape(channels * layers, plane)
    wide = shape((CELLS, LANES), BF16)
    edge = shape((CELLS // 2, LANES), BF16)
    plane_modes = shape((plane_rows, LANES), BF16)
    padded = pltpu.VMEM((CELLS + 2 * NY, 2 * LANES), BF16)

    def send(values):
        return exchange(values.reshape(devices, modes, LANES)).reshape(plane_rows, LANES)

    cells, coef, first, last = run(
        analyse_kernel,
        [wide, plane_modes, edge, edge],
        field,
        turn,
        analysis,
        sent=(1, 2, 3),
        flops=10**8,
    )
    weights, coef = lax.optimization_barrier((weights, coef))
    coef = send(coef)
    (weights,) = run(pack_kernel, [shape((weights.shape[0] // 2, LANES), BF16)], weights)
    before, after = neighbours(first, last)
    local, lanes, outer_cells = run(
        local_kernel,
        [shape((CELLS, LANES), F32), shape((2 * LANES, CELLS), BF16), wide],
        cells,
        before,
        after,
        outer,
        turn,
        taps,
        scratch=[padded, pltpu.VMEM((3, 2 * LANES, 3 * LANES), BF16)],
        flops=7 * 10**8,
    )
    back, diagonal = run(
        functools.partial(mix_kernel, batches),
        [plane_modes, shape((count, GROUP * half // 2), BF16)],
        coef,
        gather,
        weights,
        scatter,
        sent=(0,),
        flops=4 * 10**8,
    )
    back = send(back)
    slab = shape((devices, 8 + TERM_ROWS // devices, LANES), BF16)
    activated, grad, first, last, back, terms = run(
        functools.partial(activate_kernel, in_slab),
        [
            wide,
            wide,
            edge,
            edge,
            slab if in_slab else plane_modes,
            None if in_slab else shape((TERM_ROWS, LANES), BF16),
        ],
        back,
        np.ascontiguousarray(synthesis.T),
        synthesis,
        local,
        outer_cells,
        lanes,
        sent=(2, 3, 4),
        scratch=[pltpu.VMEM((CELLS + 2 * NY, 3 * LANES), BF16)],
        flops=10**9,
    )
    if in_slab:
        back = exchange(back)
    else:
        back = send(back)
        terms = exchange(terms.reshape(devices, TERM_ROWS // devices, LANES))
    before, after = neighbours(first, last)
    (activated,) = run(
        output_kernel,
        [shape((channels * layers, plane), BF16)],
        activated,
        turn,
        flops=10**8,
    )
    back, before, after, activated = lax.optimization_barrier((back, before, after, activated))
    scale = 1.0 / math.sqrt(batches * slabs * layers * plane)
    grad_modes, mixed_grad, sums = run(
        functools.partial(unmix_kernel, batches, scale),
        [
            slab if in_slab else plane_modes,
            shape((count, LANES), BF16),
            None if in_slab else shape((TERM_ROWS // devices, LANES), F32),
        ],
        back,
        None if in_slab else terms,
        gather_back,
        weights,
        scatter_back,
        sent=(0,),
        flops=4 * 10**8,
    )
    if in_slab:
        grad_modes = exchange(grad_modes)
    else:
        grad_modes = send(grad_modes)
        sums = lax.all_gather(sums, ("batch", "space"), axis=0, tiled=True)
    (local,) = run(
        local_grad_kernel,
        [shape((CELLS, LANES), F32)],
        grad,
        before,
        after,
        taps,
        scratch=[padded, pltpu.VMEM((3, 3 * LANES, 2 * LANES), BF16)],
        flops=7 * 10**8,
    )
    (mode_gradient,) = run(
        functools.partial(weight_kernel, batches),
        [shape((modes * 2 * KZ * channels, channels), F32)],
        diagonal,
        mixed_grad,
        flops=4 * 10**8,
    )
    input_gradient, conv_gradient = run(
        finish_kernel,
        [shape((channels * layers, plane), BF16), shape((OFFSETS, channels, channels), F32)],
        grad_modes,
        sums,
        np.ascontiguousarray(analysis.T),
        local,
        turn,
        flops=10**8,
    )
    return (
        activated.reshape(snapshots.shape),
        input_gradient.reshape(snapshots.shape),
        mode_gradient.reshape(mode_weight.shape),
        conv_gradient.reshape(conv_weight.shape),
    )


def solution(mesh):
    in_specs = (
        P("batch", None, "space", None),
        P("batch", None, "space", None),
        P("batch", "space", None, None, None),
        P(),
    )
    out_specs = (
        P("batch", None, "space", None),
        P("batch", None, "space", None),
        P("batch", "space", None, None, None),
        P(),
    )
    return jax.shard_map(shards, mesh=mesh, in_specs=in_specs, out_specs=out_specs, check_vma=False)
```

```python
import functools
import math

import jax
import jax.numpy as jnp
import ml_dtypes
import numpy as np
from jax import lax
from jax.experimental import pallas as pl
from jax.experimental.pallas import tpu as pltpu
from jax.sharding import PartitionSpec as P

KX = 8
KY = 8
KZ = 12
NX = 32
NY = 32
CELLS = NX * NY
LANES = 128
GROUP = 8
OFFSETS = 27
TERM_ROWS = 1024
VMEM_BYTES = 40 * 1024 * 1024
WHOLE_VMEM = 65000 * 1024

F32 = jnp.float32
BF16 = jnp.bfloat16
inv_root_two = 1.0 / math.sqrt(2.0)
inv_root_two_pi = 1.0 / math.sqrt(2.0 * math.pi)


def basis_rows(half_count, length):
    row = np.arange(2 * half_count)[:, None]
    cell = np.arange(length)[None, :]
    frequency = np.where(row < half_count, row, row - half_count + 1)
    phases = (frequency * cell % length).astype(np.float32) * np.float32(2.0 * math.pi / length)
    return np.where(row < half_count, np.cos(phases), np.sin(phases)).astype(np.float32)


def plane_tables(batches, slabs):
    outer = (basis_rows(KX, NX)[:, None, :, None] * basis_rows(KY, NY)[None, :, None, :]).reshape(
        2 * KX, 2 * KY, CELLS
    )
    outer = outer.reshape(batches, 2 * KX // batches, slabs, 2 * KY // slabs, CELLS)
    outer = outer.transpose(0, 2, 1, 3, 4).reshape(4 * KX * KY, CELLS)
    analysis = (outer * np.float32(2.0 / math.sqrt(CELLS))).astype(ml_dtypes.bfloat16)
    synthesis = (outer * np.float32(2.0 / math.sqrt(4 * KX * KY))).astype(ml_dtypes.bfloat16)
    return analysis, synthesis


def depth_tables(batches, slabs, layers, modes):
    rows = basis_rows(KZ, slabs * layers)
    analysis = (rows * np.float32(math.sqrt(2.0 / (slabs * layers)))).astype(ml_dtypes.bfloat16)
    synthesis = (rows * np.float32(math.sqrt(2.0 / (2 * KZ)))).astype(ml_dtypes.bfloat16)

    def spread(table):
        table = table.astype(np.float32).reshape(2 * KZ, slabs, layers)
        full = np.einsum("psz,bc,mn->mpbzcsn", table, np.eye(batches), np.eye(modes))
        return full.reshape(modes * 2 * KZ * batches, layers * batches * slabs * modes)

    def gathered(table):
        return spread(table).astype(ml_dtypes.bfloat16)

    def scattered(table):
        full = spread(table)
        count = full.shape[0]
        full = full.reshape(count, layers, -1).transpose(2, 1, 0)
        return full.reshape(-1, layers * count).astype(ml_dtypes.bfloat16)

    return gathered(analysis), scattered(synthesis), gathered(synthesis), scattered(analysis)


def dot(left, right, contract=(1, 0)):
    return lax.dot_general(
        left, right, (((contract[0],), (contract[1],)), ((), ())), preferred_element_type=F32
    )


def turn_table():
    row = lax.broadcasted_iota(jnp.int32, (LANES, LANES), 0)
    column = lax.broadcasted_iota(jnp.int32, (LANES, LANES), 1)
    return jnp.where(column == row % 2 * (LANES // 2) + row // 2, 1.0, 0.0).astype(BF16)


def to_cells(field):
    return dot(field.reshape(LANES, CELLS), turn_table(), (0, 0))


def to_field(cells):
    return dot(turn_table(), cells, (1, 1)).astype(BF16).reshape(LANES // 2, 2, CELLS)


def low_lanes(rows):
    return lax.broadcasted_iota(jnp.int32, (rows, LANES), 1) < LANES // 2


def swap_halves(values):
    return pltpu.roll(values, LANES // 2, 1)


def doubled(values):
    low = low_lanes(values.shape[0])
    swapped = swap_halves(values)
    return jnp.concatenate(
        [jnp.where(low, values, swapped), jnp.where(low, swapped, values)], axis=0
    )


def halved(values):
    low = low_lanes(values.shape[0])
    return jnp.concatenate([jnp.where(low, values, 0.0), jnp.where(low, 0.0, values)], axis=0)


def edge_layers(cells_first):
    top = cells_first[: CELLS // 2]
    bottom = cells_first[CELLS // 2 :]
    low = low_lanes(CELLS // 2)
    first = jnp.where(low, top, swap_halves(bottom))
    last = jnp.where(low, swap_halves(top), bottom)
    return first.astype(BF16), last.astype(BF16)


def beside_layers(before, after):
    before = before.astype(F32)
    after = after.astype(F32)
    low = low_lanes(CELLS // 2)
    top = jnp.where(low, before, swap_halves(after))
    bottom = jnp.where(low, swap_halves(before), after)
    return jnp.concatenate([top, bottom], axis=0).astype(BF16)


def y_cells(rows):
    return lax.broadcasted_iota(jnp.int32, (rows, LANES), 0) % NY


def from_below(values):
    return jnp.where(y_cells(values.shape[0]) == 0, 0.0, pltpu.roll(values, 1, 0))


def from_above(values):
    rows = values.shape[0]
    return jnp.where(y_cells(rows) == NY - 1, 0.0, pltpu.roll(values, rows - 1, 0))


def pad_cells(padded, own, beside):
    width = own.shape[1] + beside.shape[1]
    padded[0:NY, :] = jnp.zeros((NY, width), BF16)
    padded[NY + CELLS : 2 * NY + CELLS, :] = jnp.zeros((NY, width), BF16)
    padded[NY : NY + CELLS, 0 : own.shape[1]] = own
    padded[NY : NY + CELLS, own.shape[1] :] = beside


BLOCK_OF_DEPTH = {-1: 2, 0: 0, 1: 1, 2: 3}
STEP = 256


def stencil(padded, table, transposed, store):
    for start in range(0, CELLS, STEP):
        total = None
        for b in range(3):
            cells = padded[start + NY * b : start + NY * b + STEP, :]
            term = dot(cells, table[b], (1, 1) if transposed else (1, 0))
            total = term if total is None else total + term
        result = (
            from_below(total[:, 0:LANES])
            + total[:, LANES : 2 * LANES]
            + from_above(total[:, 2 * LANES :])
        )
        store(start, result)


def banded_forward(weights, table):
    half = LANES // 2
    for b in range(3):
        for c in range(3):
            for depth, block in BLOCK_OF_DEPTH.items():
                parts = []
                for out in range(2):
                    a = depth - out + 1
                    if 0 <= a < 3:
                        parts.append(weights[a * 9 + b * 3 + c])
                    else:
                        parts.append(jnp.zeros((half, half), BF16))
                table[b, block * half : (block + 1) * half, c * LANES : (c + 1) * LANES] = (
                    jnp.concatenate(parts, axis=1)
                )


def banded_backward(weights, table):
    half = LANES // 2
    for b in range(3):
        for c in range(3):
            for out in range(2):
                for pair in ((0, 1), (-1, 2)):
                    parts = []
                    for depth in pair:
                        a = depth - out + 1
                        if 0 <= a < 3:
                            parts.append(weights[(2 - a) * 9 + (2 - b) * 3 + 2 - c])
                        else:
                            parts.append(jnp.zeros((half, half), BF16))
                    row = c * LANES + out * half
                    column = BLOCK_OF_DEPTH[pair[0]] * half
                    table[b, row : row + half, column : column + LANES] = jnp.concatenate(
                        parts, axis=1
                    )


def analyse_kernel(field, analysis, cells_out, coef_out, first_out, last_out):
    cells = to_cells(field[...])
    rounded = cells.astype(BF16)
    coef_out[...] = dot(analysis[...], rounded).astype(BF16)
    cells_out[...] = rounded
    first, last = edge_layers(cells)
    first_out[...] = first
    last_out[...] = last


def local_kernel(
    cells, before, after, cotangent, weights, local_out, lanes_out, cotangent_out, padded, table
):
    banded_forward(weights, table)
    beside = beside_layers(before[...], after[...])
    pad_cells(padded, cells[...], beside)

    def store(start, result):
        local_out[start : start + STEP, :] = result

    stencil(padded, table, False, store)
    whole = jnp.concatenate([cells[...].astype(F32), beside.astype(F32)], axis=1)
    lanes_out[...] = whole.T.astype(BF16)
    cotangent_out[...] = to_cells(cotangent[...]).astype(BF16)


def pack_kernel(weights, out):
    rows = GROUP * LANES // 4
    for g in range(out.shape[0] // rows):
        first = weights[2 * g * rows : (2 * g + 1) * rows, :]
        second = weights[(2 * g + 1) * rows : (2 * g + 2) * rows, :]
        out[g * rows : (g + 1) * rows, :] = jnp.concatenate([first, second], axis=1)


def mode_in_group(rows, lanes, snaps):
    return (lax.broadcasted_iota(jnp.int32, (rows, lanes), 0) // snaps) % GROUP


def own_block(rows, snaps):
    width = GROUP * LANES // 4
    lane = lax.broadcasted_iota(jnp.int32, (rows, width), 1)
    return mode_in_group(rows, width, snaps) % (GROUP // 2) == lane // (LANES // 2)


def own_half(rows, snaps):
    return (mode_in_group(rows, LANES, snaps) < GROUP // 2) == low_lanes(rows)


def mix_kernel(snaps, received, gather, weights, scatter, back_out, diagonal_out):
    both = doubled(received[...].astype(F32)).astype(BF16)
    coef = dot(gather[...], both)
    count = coef.shape[0]
    wide = jnp.concatenate([coef] * (GROUP // 4), axis=1)
    diagonal_out[...] = jnp.where(own_block(count, snaps), wide, 0.0).astype(BF16)
    rows = GROUP * snaps
    depth = GROUP * LANES // 4
    mixed = jnp.concatenate(
        [
            dot(
                diagonal_out[g * rows : (g + 1) * rows, :],
                weights[g * depth : (g + 1) * depth, :],
            )
            for g in range(count // rows)
        ],
        axis=0,
    )
    mixed = jnp.where(own_half(count, snaps), mixed, swap_halves(mixed))
    back_out[...] = dot(scatter[...], halved(mixed).astype(BF16)).astype(BF16)


def activate_kernel(
    terms_in_slab,
    received,
    synthesis,
    synthesis_rows,
    local,
    cotangent,
    lanes,
    activated_out,
    grad_out,
    first_out,
    last_out,
    back_out,
    terms_out,
    spread,
):
    pre = dot(synthesis[...], received[...]) + local[...]
    cdf = 0.5 * (1.0 + lax.erf(pre * inv_root_two))
    density = jnp.exp(-0.5 * pre * pre) * inv_root_two_pi
    activated_out[...] = (pre * cdf).astype(BF16)
    grad = (cotangent[...].astype(F32) * (cdf + pre * density)).astype(BF16)
    grad_out[...] = grad
    back = dot(synthesis_rows[...], grad)
    grad = grad.astype(F32)
    first, last = edge_layers(grad)
    first_out[...] = first
    last_out[...] = last
    spread[0:NY, :] = jnp.zeros((NY, 3 * LANES), BF16)
    spread[NY + CELLS : 2 * NY + CELLS, :] = jnp.zeros((NY, 3 * LANES), BF16)
    spread[NY : NY + CELLS, 0:LANES] = from_above(grad).astype(BF16)
    spread[NY : NY + CELLS, LANES : 2 * LANES] = grad.astype(BF16)
    spread[NY : NY + CELLS, 2 * LANES :] = from_below(grad).astype(BF16)
    half = LANES // 2
    low = low_lanes(half)
    twice = {}
    for b in range(3):
        product = dot(lanes[...], spread[NY * (2 - b) : NY * (2 - b) + CELLS, :])
        for c in range(3):
            for a in range(3):
                blocks = [BLOCK_OF_DEPTH[out + a - 1] * half for out in range(2)]
                columns = slice(c * LANES, (c + 1) * LANES)
                both = jnp.where(
                    low,
                    product[blocks[0] : blocks[0] + half, columns],
                    product[blocks[1] : blocks[1] + half, columns],
                )
                twice[a * 9 + b * 3 + c] = both + swap_halves(both)
    pairs = []
    for k in range(0, OFFSETS, 2):
        pairs.append(jnp.where(low, twice[k], twice.get(k + 1, 0.0)))
    pairs.append(jnp.zeros((TERM_ROWS - half * len(pairs), LANES), F32))
    terms = jnp.concatenate(pairs, axis=0)
    if terms_in_slab:
        slab_store(back_out, back, terms)
    else:
        back_out[...] = back.astype(BF16)
        terms_out[...] = terms.astype(BF16)


def slab_store(slab, modes, terms):
    owners = slab.shape[0]
    modes = modes.reshape(owners, 8, LANES)
    terms = terms.reshape(owners, -1, LANES)
    slab[...] = jnp.concatenate([modes, terms], axis=1).astype(BF16)


def slab_load(slab):
    whole = slab[...].astype(F32)
    return whole[:, 0:8, :].reshape(-1, LANES), whole[:, 8:, :]


def unmix_kernel(snaps, scale, received, terms, gather, weights, scatter, grad_out, mixed_out, sums_out):
    in_slab = terms is None
    if in_slab:
        modes, terms = slab_load(received)
    else:
        modes, terms = received[...].astype(F32), terms[...].astype(F32)
    mixed = dot(gather[...], doubled(modes).astype(BF16))
    mixed_out[...] = mixed.astype(BF16)
    count = mixed.shape[0]
    rows = GROUP * snaps
    depth = GROUP * LANES // 4
    sums = jnp.sum(terms, axis=0) * scale
    own = own_block(rows, snaps)
    placed = jnp.where(own_half(count, snaps), mixed, 0.0).astype(BF16)
    pieces = []
    for g in range(count // rows):
        full = dot(
            placed[g * rows : (g + 1) * rows, :], weights[g * depth : (g + 1) * depth, :], (1, 1)
        )
        full = jnp.where(own, full, 0.0)
        pieces.append(sum(full[:, k : k + LANES] for k in range(0, depth, LANES)))
    coef = jnp.concatenate(pieces, axis=0)
    coef = coef + swap_halves(coef)
    grad = dot(scatter[...], halved(coef).astype(BF16))
    if in_slab:
        owners = received.shape[0]
        share = sums.shape[0]
        slab_store(
            grad_out, grad, jnp.broadcast_to(sums[None], (owners, share, LANES)).reshape(-1, LANES)
        )
    else:
        grad_out[...] = grad.astype(BF16)
        sums_out[...] = sums


def weight_kernel(snaps, diagonal, mixed, out):
    rows = GROUP * snaps
    depth = GROUP * LANES // 4
    half = LANES // 2
    first = mode_in_group(rows, depth, snaps) < GROUP // 2
    for g in range(diagonal.shape[0] // rows):
        span = slice(g * rows, (g + 1) * rows)
        blocks = diagonal[span, :].astype(F32)
        blocks = [jnp.where(first, blocks, 0.0), jnp.where(first, 0.0, blocks)]
        blocks = jnp.concatenate(blocks, axis=1).astype(BF16)
        out[2 * g * depth : 2 * (g + 1) * depth, :] = dot(blocks, mixed[span, 0:half], (0, 0))


def output_kernel(cells, out):
    out[...] = to_field(cells[...])


def local_grad_kernel(grad, before, after, weights, out, padded, table):
    banded_backward(weights, table)
    pad_cells(padded, grad[...], beside_layers(before[...], after[...]))

    def store(start, result):
        out[start : start + STEP, :] = result

    stencil(padded, table, True, store)


def finish_kernel(received, sums, synthesis, local, grad_out, stencil_out):
    in_slab = sums is None
    if in_slab:
        modes, terms = slab_load(received)
        terms = terms.reshape(TERM_ROWS, LANES)
    else:
        modes, terms = received[...], sums[...].astype(F32)
    cells = (dot(synthesis[...], modes.astype(BF16)) + local[...]).astype(BF16)
    grad_out[...] = to_field(cells)
    half = LANES // 2
    for k in range(OFFSETS):
        row = (k // 2) * half
        lane = (k % 2) * half
        stencil_out[k] = terms[row : row + half, lane : lane + half]


def shape(dims, dtype):
    return jax.ShapeDtypeStruct(dims, dtype)


class Staged:
    def __init__(self, source, buffer, semaphore):
        self.copy = pltpu.make_async_copy(source, buffer, semaphore)
        self.buffer = buffer
        self.copy.start()
        self.ready = False

    def load(self):
        if not self.ready:
            self.copy.wait()
            self.ready = True

    def __getitem__(self, index):
        self.load()
        return self.buffer[index]


class Sent:
    def __init__(self, target, buffer, semaphore):
        self.copy = pltpu.make_async_copy(buffer, target, semaphore)
        self.buffer = buffer

    def __setitem__(self, index, value):
        self.buffer[index] = value
        self.copy.start()

    @property
    def shape(self):
        return self.buffer.shape


def run(body, outs, *operands, staged=(), sent=(), scratch=(), flops=0, limit=VMEM_BYTES):
    given = [k for k, operand in enumerate(operands) if operand is not None]
    made = [k for k, out in enumerate(outs) if out is not None]
    sent = [k for k in made if k in sent]

    def kernel(*refs):
        refs = list(refs)

        def take(count):
            taken = refs[:count]
            del refs[:count]
            return taken

        filled = dict(zip(given, take(len(given))))
        kept = dict(zip(made, take(len(made))))
        own = take(len(scratch))
        for place, (k, buffer) in enumerate(zip(staged, take(len(staged)))):
            filled[k] = Staged(filled[k], buffer, refs[-1].at[place])
        for place, (k, buffer) in enumerate(zip(sent, take(len(sent)))):
            kept[k] = Sent(kept[k], buffer, refs[-1].at[len(staged) + place])
        body(
            *[filled.get(k) for k in range(len(operands))],
            *[kept.get(k) for k in range(len(outs))],
            *own,
        )
        for k in staged:
            filled[k].load()
        for k in sent:
            kept[k].copy.wait()

    arrays = [operands[k] for k in given]
    results = [outs[k] for k in made]
    size = sum(x.size * x.dtype.itemsize for x in (*arrays, *results))
    in_vmem = pl.BlockSpec(memory_space=pltpu.VMEM)
    in_hbm = pl.BlockSpec(memory_space=pltpu.HBM)
    buffers = [operands[k] for k in staged] + [outs[k] for k in sent]
    buffers = [pltpu.VMEM(x.shape, x.dtype) for x in buffers]
    if buffers:
        buffers.append(pltpu.SemaphoreType.DMA((len(buffers),)))
    results = pl.pallas_call(
        kernel,
        out_shape=results,
        in_specs=[in_hbm if k in staged else in_vmem for k in given],
        out_specs=[in_hbm if k in sent else in_vmem for k in made],
        scratch_shapes=[*scratch, *buffers],
        compiler_params=pltpu.CompilerParams(vmem_limit_bytes=limit),
        cost_estimate=pl.CostEstimate(flops=flops, bytes_accessed=size, transcendentals=0),
        name=body.__name__ if hasattr(body, "__name__") else body.func.__name__,
    )(*arrays)
    results = dict(zip(made, results))
    return [results.get(k) for k in range(len(outs))]


def exchange(values):
    return lax.all_to_all(values, ("batch", "space"), split_axis=0, concat_axis=0, tiled=True)


def neighbours(first, last):
    ends = lax.axis_size("space") - 1
    before = lax.ppermute(last, "space", [(i, i + 1) for i in range(ends)])
    after = lax.ppermute(first, "space", [(i + 1, i) for i in range(ends)])
    return before, after


def shards(snapshots, cotangent, mode_weight, conv_weight):
    batches = lax.axis_size("batch")
    slabs = lax.axis_size("space")
    devices = batches * slabs
    _, channels, layers, plane = snapshots.shape
    modes = mode_weight.shape[0] * mode_weight.shape[1]
    half = LANES // 2
    assert channels == half and layers == 2 and plane == CELLS
    plane_rows = devices * modes
    count = modes * 2 * KZ * batches
    in_slab = modes == 8 and devices * 32 == TERM_ROWS

    analysis, synthesis = plane_tables(batches, slabs)
    gather, scatter, gather_back, scatter_back = depth_tables(batches, slabs, layers, modes)
    weights = mode_weight.reshape(modes * 2 * KZ * channels, channels)
    taps = conv_weight.reshape(OFFSETS, channels, channels)
    field = shape((channels, layers, plane), BF16)
    wide = shape((CELLS, LANES), BF16)
    edge = shape((CELLS // 2, LANES), BF16)
    plane_modes = shape((plane_rows, LANES), BF16)
    padded = pltpu.VMEM((CELLS + 2 * NY, 2 * LANES), BF16)

    def send(values):
        return exchange(values.reshape(devices, modes, LANES)).reshape(plane_rows, LANES)

    cells, coef, first, last = run(
        analyse_kernel,
        [wide, plane_modes, edge, edge],
        snapshots.reshape(field.shape),
        analysis,
        staged=(0, 1),
        sent=(0, 1, 2, 3),
        limit=WHOLE_VMEM,
        flops=10**8,
    )
    packed = shape((weights.shape[0] // 2, LANES), BF16)
    weights, coef = lax.optimization_barrier((weights, coef))
    coef = send(coef)
    (packed_weights,) = run(pack_kernel, [packed], weights)
    before, after = neighbours(first, last)
    local, lanes, outer_cells = run(
        local_kernel,
        [shape((CELLS, LANES), F32), shape((2 * LANES, CELLS), BF16), wide],
        cells,
        before,
        after,
        cotangent.reshape(field.shape),
        taps,
        scratch=[padded, pltpu.VMEM((3, 2 * LANES, 3 * LANES), BF16)],
        flops=7 * 10**8,
    )
    back, diagonal = run(
        functools.partial(mix_kernel, batches),
        [plane_modes, shape((count, GROUP * half // 2), BF16)],
        coef,
        gather,
        packed_weights,
        scatter,
        sent=(0,),
        flops=4 * 10**8,
    )
    back = send(back)
    slab = shape((devices, 8 + TERM_ROWS // devices, LANES), BF16)
    activated, grad, first, last, back, terms = run(
        functools.partial(activate_kernel, in_slab),
        [
            wide,
            wide,
            edge,
            edge,
            slab if in_slab else plane_modes,
            None if in_slab else shape((TERM_ROWS, LANES), BF16),
        ],
        back,
        np.ascontiguousarray(synthesis.T),
        synthesis,
        local,
        outer_cells,
        lanes,
        sent=(0, 1, 2, 3, 4),
        scratch=[pltpu.VMEM((CELLS + 2 * NY, 3 * LANES), BF16)],
        flops=10**9,
    )
    weights, back = lax.optimization_barrier((weights, back))
    (packed_weights,) = run(pack_kernel, [packed], weights)
    if in_slab:
        back = exchange(back)
    else:
        back = send(back)
        terms = exchange(terms.reshape(devices, TERM_ROWS // devices, LANES))
    before, after = neighbours(first, last)
    (activated,) = run(
        output_kernel,
        [field],
        activated,
        flops=10**8,
    )
    back, before, after, activated, packed_weights = lax.optimization_barrier(
        (back, before, after, activated, packed_weights)
    )
    scale = 1.0 / math.sqrt(batches * slabs * layers * plane)
    grad_modes, mixed_grad, sums = run(
        functools.partial(unmix_kernel, batches, scale),
        [
            slab if in_slab else plane_modes,
            shape((count, LANES), BF16),
            None if in_slab else shape((TERM_ROWS // devices, LANES), F32),
        ],
        back,
        None if in_slab else terms,
        gather_back,
        packed_weights,
        scatter_back,
        sent=(0,),
        flops=4 * 10**8,
    )
    if in_slab:
        grad_modes = exchange(grad_modes)
    else:
        grad_modes = send(grad_modes)
        sums = lax.all_gather(sums, ("batch", "space"), axis=0, tiled=True)
    (local,) = run(
        local_grad_kernel,
        [shape((CELLS, LANES), F32)],
        grad,
        before,
        after,
        taps,
        scratch=[padded, pltpu.VMEM((3, 3 * LANES, 2 * LANES), BF16)],
        flops=7 * 10**8,
    )
    (mode_gradient,) = run(
        functools.partial(weight_kernel, batches),
        [shape((modes * 2 * KZ * channels, channels), F32)],
        diagonal,
        mixed_grad,
        flops=4 * 10**8,
    )
    input_gradient, conv_gradient = run(
        finish_kernel,
        [field, shape((OFFSETS, channels, channels), F32)],
        grad_modes,
        sums,
        np.ascontiguousarray(analysis.T),
        local,
        flops=10**8,
    )
    return (
        activated.reshape(snapshots.shape),
        input_gradient.reshape(snapshots.shape),
        mode_gradient.reshape(mode_weight.shape),
        conv_gradient.reshape(conv_weight.shape),
    )


def solution(mesh):
    in_specs = (
        P("batch", None, "space", None),
        P("batch", None, "space", None),
        P("batch", "space", None, None, None),
        P(),
    )
    out_specs = (
        P("batch", None, "space", None),
        P("batch", None, "space", None),
        P("batch", "space", None, None, None),
        P(),
    )
    return jax.shard_map(shards, mesh=mesh, in_specs=in_specs, out_specs=out_specs, check_vma=False)
```

```python
import functools
import math

import jax
import jax.numpy as jnp
import ml_dtypes
import numpy as np
from jax import lax
from jax.experimental import pallas as pl
from jax.experimental.pallas import tpu as pltpu
from jax.sharding import PartitionSpec as P

KX = 8
KY = 8
KZ = 12
NX = 32
NY = 32
CELLS = NX * NY
LANES = 128
GROUP = 8
OFFSETS = 27
TERM_ROWS = 1024
VMEM_BYTES = 40 * 1024 * 1024
LOADER_VMEM = 60 * 1024 * 1024
WHOLE_VMEM = 65000 * 1024
HBM_ROWS = 20480
TABLE_ROWS = 2560

F32 = jnp.float32
BF16 = jnp.bfloat16
inv_root_two = 1.0 / math.sqrt(2.0)
inv_root_two_pi = 1.0 / math.sqrt(2.0 * math.pi)


def basis_rows(half_count, length):
    row = np.arange(2 * half_count)[:, None]
    cell = np.arange(length)[None, :]
    frequency = np.where(row < half_count, row, row - half_count + 1)
    phases = (frequency * cell % length).astype(np.float32) * np.float32(2.0 * math.pi / length)
    return np.where(row < half_count, np.cos(phases), np.sin(phases)).astype(np.float32)


def plane_tables(batches, slabs):
    outer = (basis_rows(KX, NX)[:, None, :, None] * basis_rows(KY, NY)[None, :, None, :]).reshape(
        2 * KX, 2 * KY, CELLS
    )
    outer = outer.reshape(batches, 2 * KX // batches, slabs, 2 * KY // slabs, CELLS)
    outer = outer.transpose(0, 2, 1, 3, 4).reshape(4 * KX * KY, CELLS)
    analysis = (outer * np.float32(2.0 / math.sqrt(CELLS))).astype(ml_dtypes.bfloat16)
    synthesis = (outer * np.float32(2.0 / math.sqrt(4 * KX * KY))).astype(ml_dtypes.bfloat16)
    return analysis, synthesis


def depth_tables(batches, slabs, layers, modes):
    rows = basis_rows(KZ, slabs * layers)
    analysis = (rows * np.float32(math.sqrt(2.0 / (slabs * layers)))).astype(ml_dtypes.bfloat16)
    synthesis = (rows * np.float32(math.sqrt(2.0 / (2 * KZ)))).astype(ml_dtypes.bfloat16)

    def spread(table):
        table = table.astype(np.float32).reshape(2 * KZ, slabs, layers)
        full = np.einsum("psz,bc,mn->mpbzcsn", table, np.eye(batches), np.eye(modes))
        return full.reshape(modes * 2 * KZ * batches, layers * batches * slabs * modes)

    def gathered(table):
        return spread(table).astype(ml_dtypes.bfloat16)

    def scattered(table):
        full = spread(table)
        count = full.shape[0]
        full = full.reshape(count, layers, -1).transpose(2, 1, 0)
        return full.reshape(-1, layers * count).astype(ml_dtypes.bfloat16)

    return gathered(analysis), scattered(synthesis), gathered(synthesis), scattered(analysis)


class Piece:
    def __init__(self, row, column, values):
        self.index = (slice(row, row + values.shape[0]), slice(column, column + values.shape[1]))
        self.values = values


def join_tables(batches, slabs, layers, modes):
    analysis, synthesis = plane_tables(batches, slabs)
    gather, scatter, gather_back, scatter_back = depth_tables(batches, slabs, layers, modes)
    parts = {}
    rows = [0]

    def shelf(**named):
        column = 0
        for name, values in named.items():
            parts[name] = Piece(rows[0], column, values)
            column += values.shape[1]
        rows[0] += max(values.shape[0] for values in named.values())

    shelf(analysis=analysis)
    shelf(synthesis=synthesis)
    shelf(
        synthesis_cells=synthesis.T,
        analysis_cells=analysis.T,
        gather=np.concatenate([gather, gather_back], axis=0),
    )
    both = parts.pop("gather")
    first, column = both.index[0].start, both.index[1].start
    parts["gather"] = Piece(first, column, gather)
    parts["gather_back"] = Piece(first + gather.shape[0], column, gather_back)
    shelf(scatter=scatter)
    shelf(scatter_back=scatter_back)
    joined = np.zeros((max(rows[0], TABLE_ROWS), 1024), ml_dtypes.bfloat16)
    for part in parts.values():
        joined[part.index] = part.values
    return joined, parts


def dot(left, right, contract=(1, 0)):
    return lax.dot_general(
        left, right, (((contract[0],), (contract[1],)), ((), ())), preferred_element_type=F32
    )


def turn_table():
    row = lax.broadcasted_iota(jnp.int32, (LANES, LANES), 0)
    column = lax.broadcasted_iota(jnp.int32, (LANES, LANES), 1)
    return jnp.where(column == row % 2 * (LANES // 2) + row // 2, 1.0, 0.0).astype(BF16)


def to_cells(field):
    return dot(field.reshape(LANES, CELLS), turn_table(), (0, 0))


def to_field(cells):
    return dot(turn_table(), cells, (1, 1)).astype(BF16).reshape(LANES // 2, 2, CELLS)


def low_lanes(rows):
    return lax.broadcasted_iota(jnp.int32, (rows, LANES), 1) < LANES // 2


def swap_halves(values):
    return pltpu.roll(values, LANES // 2, 1)


def doubled(values):
    low = low_lanes(values.shape[0])
    swapped = swap_halves(values)
    return jnp.concatenate(
        [jnp.where(low, values, swapped), jnp.where(low, swapped, values)], axis=0
    )


def halved(values):
    low = low_lanes(values.shape[0])
    return jnp.concatenate([jnp.where(low, values, 0.0), jnp.where(low, 0.0, values)], axis=0)


def edge_layers(cells_first):
    top = cells_first[: CELLS // 2]
    bottom = cells_first[CELLS // 2 :]
    low = low_lanes(CELLS // 2)
    first = jnp.where(low, top, swap_halves(bottom))
    last = jnp.where(low, swap_halves(top), bottom)
    return first.astype(BF16), last.astype(BF16)


def beside_layers(before, after):
    before = before.astype(F32)
    after = after.astype(F32)
    low = low_lanes(CELLS // 2)
    top = jnp.where(low, before, swap_halves(after))
    bottom = jnp.where(low, swap_halves(before), after)
    return jnp.concatenate([top, bottom], axis=0).astype(BF16)


def y_cells(rows):
    return lax.broadcasted_iota(jnp.int32, (rows, LANES), 0) % NY


def from_below(values):
    return jnp.where(y_cells(values.shape[0]) == 0, 0.0, pltpu.roll(values, 1, 0))


def from_above(values):
    rows = values.shape[0]
    return jnp.where(y_cells(rows) == NY - 1, 0.0, pltpu.roll(values, rows - 1, 0))


def pad_cells(padded, own, beside):
    width = own.shape[1] + beside.shape[1]
    padded[0:NY, :] = jnp.zeros((NY, width), BF16)
    padded[NY + CELLS : 2 * NY + CELLS, :] = jnp.zeros((NY, width), BF16)
    padded[NY : NY + CELLS, 0 : own.shape[1]] = own
    padded[NY : NY + CELLS, own.shape[1] :] = beside


BLOCK_OF_DEPTH = {-1: 2, 0: 0, 1: 1, 2: 3}
STEP = 256


def stencil(padded, table, transposed, store):
    for start in range(0, CELLS, STEP):
        total = None
        for b in range(3):
            cells = padded[start + NY * b : start + NY * b + STEP, :]
            term = dot(cells, table[b], (1, 1) if transposed else (1, 0))
            total = term if total is None else total + term
        result = (
            from_below(total[:, 0:LANES])
            + total[:, LANES : 2 * LANES]
            + from_above(total[:, 2 * LANES :])
        )
        store(start, result)


def banded_forward(weights, table):
    half = LANES // 2
    for b in range(3):
        for c in range(3):
            for depth, block in BLOCK_OF_DEPTH.items():
                parts = []
                for out in range(2):
                    a = depth - out + 1
                    if 0 <= a < 3:
                        parts.append(weights[a * 9 + b * 3 + c])
                    else:
                        parts.append(jnp.zeros((half, half), BF16))
                table[b, block * half : (block + 1) * half, c * LANES : (c + 1) * LANES] = (
                    jnp.concatenate(parts, axis=1)
                )


def banded_backward(weights, table):
    half = LANES // 2
    for b in range(3):
        for c in range(3):
            for out in range(2):
                for pair in ((0, 1), (-1, 2)):
                    parts = []
                    for depth in pair:
                        a = depth - out + 1
                        if 0 <= a < 3:
                            parts.append(weights[(2 - a) * 9 + (2 - b) * 3 + 2 - c])
                        else:
                            parts.append(jnp.zeros((half, half), BF16))
                    row = c * LANES + out * half
                    column = BLOCK_OF_DEPTH[pair[0]] * half
                    table[b, row : row + half, column : column + LANES] = jnp.concatenate(
                        parts, axis=1
                    )


def analyse_kernel(field, analysis, cells_out, coef_out, first_out, last_out):
    cells = to_cells(field[...])
    rounded = cells.astype(BF16)
    coef_out[...] = dot(analysis[...], rounded).astype(BF16)
    cells_out[...] = rounded
    first, last = edge_layers(cells)
    first_out[...] = first
    last_out[...] = last


def local_kernel(
    cells, before, after, cotangent, weights, local_out, lanes_out, cotangent_out, padded, table
):
    banded_forward(weights, table)
    beside = beside_layers(before[...], after[...])
    pad_cells(padded, cells[...], beside)

    def store(start, result):
        local_out[start : start + STEP, :] = result

    stencil(padded, table, False, store)
    whole = jnp.concatenate([cells[...].astype(F32), beside.astype(F32)], axis=1)
    lanes_out[...] = whole.T.astype(BF16)
    cotangent_out[...] = to_cells(cotangent[...]).astype(BF16)


def pack_kernel(weights, out, kept):
    rows = GROUP * LANES // 4
    for g in range(out.shape[0] // rows):
        first = weights[2 * g * rows : (2 * g + 1) * rows, :]
        second = weights[(2 * g + 1) * rows : (2 * g + 2) * rows, :]
        out[g * rows : (g + 1) * rows, :] = jnp.concatenate([first, second], axis=1)
    kept[...] = out[...]


def mode_in_group(rows, lanes, snaps):
    return (lax.broadcasted_iota(jnp.int32, (rows, lanes), 0) // snaps) % GROUP


def own_block(rows, snaps):
    width = GROUP * LANES // 4
    lane = lax.broadcasted_iota(jnp.int32, (rows, width), 1)
    return mode_in_group(rows, width, snaps) % (GROUP // 2) == lane // (LANES // 2)


def own_half(rows, snaps):
    return (mode_in_group(rows, LANES, snaps) < GROUP // 2) == low_lanes(rows)


def mix_kernel(snaps, received, gather, weights, scatter, back_out, diagonal_out):
    both = doubled(received[...].astype(F32)).astype(BF16)
    coef = dot(gather[...], both)
    count = coef.shape[0]
    wide = jnp.concatenate([coef] * (GROUP // 4), axis=1)
    diagonal_out[...] = jnp.where(own_block(count, snaps), wide, 0.0).astype(BF16)
    rows = GROUP * snaps
    depth = GROUP * LANES // 4
    mixed = jnp.concatenate(
        [
            dot(
                diagonal_out[g * rows : (g + 1) * rows, :],
                weights[g * depth : (g + 1) * depth, :],
            )
            for g in range(count // rows)
        ],
        axis=0,
    )
    mixed = jnp.where(own_half(count, snaps), mixed, swap_halves(mixed))
    back_out[...] = dot(scatter[...], halved(mixed).astype(BF16)).astype(BF16)


def activate_kernel(
    terms_in_slab,
    received,
    synthesis,
    synthesis_rows,
    local,
    cotangent,
    lanes,
    activated_out,
    grad_out,
    first_out,
    last_out,
    back_out,
    terms_out,
    spread,
):
    pre = dot(synthesis[...], received[...]) + local[...]
    cdf = 0.5 * (1.0 + lax.erf(pre * inv_root_two))
    density = jnp.exp(-0.5 * pre * pre) * inv_root_two_pi
    activated_out[...] = (pre * cdf).astype(BF16)
    grad = (cotangent[...].astype(F32) * (cdf + pre * density)).astype(BF16)
    grad_out[...] = grad
    back = dot(synthesis_rows[...], grad)
    grad = grad.astype(F32)
    first, last = edge_layers(grad)
    first_out[...] = first
    last_out[...] = last
    spread[0:NY, :] = jnp.zeros((NY, 3 * LANES), BF16)
    spread[NY + CELLS : 2 * NY + CELLS, :] = jnp.zeros((NY, 3 * LANES), BF16)
    spread[NY : NY + CELLS, 0:LANES] = from_above(grad).astype(BF16)
    spread[NY : NY + CELLS, LANES : 2 * LANES] = grad.astype(BF16)
    spread[NY : NY + CELLS, 2 * LANES :] = from_below(grad).astype(BF16)
    half = LANES // 2
    low = low_lanes(half)
    twice = {}
    for b in range(3):
        product = dot(lanes[...], spread[NY * (2 - b) : NY * (2 - b) + CELLS, :])
        for c in range(3):
            for a in range(3):
                blocks = [BLOCK_OF_DEPTH[out + a - 1] * half for out in range(2)]
                columns = slice(c * LANES, (c + 1) * LANES)
                both = jnp.where(
                    low,
                    product[blocks[0] : blocks[0] + half, columns],
                    product[blocks[1] : blocks[1] + half, columns],
                )
                twice[a * 9 + b * 3 + c] = both + swap_halves(both)
    pairs = []
    for k in range(0, OFFSETS, 2):
        pairs.append(jnp.where(low, twice[k], twice.get(k + 1, 0.0)))
    pairs.append(jnp.zeros((TERM_ROWS - half * len(pairs), LANES), F32))
    terms = jnp.concatenate(pairs, axis=0)
    if terms_in_slab:
        slab_store(back_out, back, terms)
    else:
        back_out[...] = back.astype(BF16)
        terms_out[...] = terms.astype(BF16)


def slab_store(slab, modes, terms):
    owners = slab.shape[0]
    modes = modes.reshape(owners, 8, LANES)
    terms = terms.reshape(owners, -1, LANES)
    slab[...] = jnp.concatenate([modes, terms], axis=1).astype(BF16)


def slab_load(slab):
    whole = slab[...].astype(F32)
    return whole[:, 0:8, :].reshape(-1, LANES), whole[:, 8:, :]


def unmix_kernel(snaps, scale, received, terms, gather, weights, scatter, grad_out, mixed_out, sums_out):
    in_slab = terms is None
    if in_slab:
        modes, terms = slab_load(received)
    else:
        modes, terms = received[...].astype(F32), terms[...].astype(F32)
    mixed = dot(gather[...], doubled(modes).astype(BF16))
    mixed_out[...] = mixed.astype(BF16)
    count = mixed.shape[0]
    rows = GROUP * snaps
    depth = GROUP * LANES // 4
    sums = jnp.sum(terms, axis=0) * scale
    own = own_block(rows, snaps)
    placed = jnp.where(own_half(count, snaps), mixed, 0.0).astype(BF16)
    pieces = []
    for g in range(count // rows):
        full = dot(
            placed[g * rows : (g + 1) * rows, :], weights[g * depth : (g + 1) * depth, :], (1, 1)
        )
        full = jnp.where(own, full, 0.0)
        pieces.append(sum(full[:, k : k + LANES] for k in range(0, depth, LANES)))
    coef = jnp.concatenate(pieces, axis=0)
    coef = coef + swap_halves(coef)
    grad = dot(scatter[...], halved(coef).astype(BF16))
    if in_slab:
        owners = received.shape[0]
        share = sums.shape[0]
        slab_store(
            grad_out, grad, jnp.broadcast_to(sums[None], (owners, share, LANES)).reshape(-1, LANES)
        )
    else:
        grad_out[...] = grad.astype(BF16)
        sums_out[...] = sums


def weight_kernel(snaps, diagonal, mixed, out):
    rows = GROUP * snaps
    depth = GROUP * LANES // 4
    half = LANES // 2
    first = mode_in_group(rows, depth, snaps) < GROUP // 2
    for g in range(diagonal.shape[0] // rows):
        span = slice(g * rows, (g + 1) * rows)
        blocks = diagonal[span, :].astype(F32)
        blocks = [jnp.where(first, blocks, 0.0), jnp.where(first, 0.0, blocks)]
        blocks = jnp.concatenate(blocks, axis=1).astype(BF16)
        out[2 * g * depth : 2 * (g + 1) * depth, :] = dot(blocks, mixed[span, 0:half], (0, 0))


def output_kernel(cells, out):
    out[...] = to_field(cells[...])


def local_grad_kernel(grad, before, after, weights, out, padded, table):
    banded_backward(weights, table)
    pad_cells(padded, grad[...], beside_layers(before[...], after[...]))

    def store(start, result):
        out[start : start + STEP, :] = result

    stencil(padded, table, True, store)


def finish_kernel(received, sums, synthesis, local, grad_out, stencil_out):
    in_slab = sums is None
    if in_slab:
        modes, terms = slab_load(received)
        terms = terms.reshape(TERM_ROWS, LANES)
    else:
        modes, terms = received[...], sums[...].astype(F32)
    cells = (dot(synthesis[...], modes.astype(BF16)) + local[...]).astype(BF16)
    grad_out[...] = to_field(cells)
    half = LANES // 2
    for k in range(OFFSETS):
        row = (k // 2) * half
        lane = (k % 2) * half
        stencil_out[k] = terms[row : row + half, lane : lane + half]


def part_shape(source, index):
    dims = [part.stop - part.start for part in index]
    return jax.ShapeDtypeStruct((*dims, *source.shape[len(dims) :]), source.dtype)


def shape(dims, dtype):
    return jax.ShapeDtypeStruct(dims, dtype)


class Staged:
    def __init__(self, source, buffer, semaphore):
        self.copy = pltpu.make_async_copy(source, buffer, semaphore)
        self.buffer = buffer
        self.copy.start()
        self.ready = False

    def load(self):
        if not self.ready:
            self.copy.wait()
            self.ready = True

    def __getitem__(self, index):
        self.load()
        return self.buffer[index]


class Sent:
    def __init__(self, target, buffer, semaphore):
        self.copy = pltpu.make_async_copy(buffer, target, semaphore)
        self.buffer = buffer

    def __setitem__(self, index, value):
        self.buffer[index] = value
        self.copy.start()

    def __getitem__(self, index):
        return self.buffer[index]

    @property
    def shape(self):
        return self.buffer.shape


def run(
    body, outs, *operands, staged=(), sent=(), loads=(), scratch=(), flops=0, limit=VMEM_BYTES
):
    given = [k for k, operand in enumerate(operands) if operand is not None]
    made = [k for k, out in enumerate(outs) if out is not None]
    sent = {k: sent[k] if isinstance(sent, dict) else None for k in made if k in sent}
    copies = len(staged) + len(sent)

    def kernel(*refs):
        refs = list(refs)

        def take(count):
            taken = refs[:count]
            del refs[:count]
            return taken

        filled = dict(zip(given, take(len(given))))
        sources = take(len(loads))
        kept = dict(zip(made, take(len(made))))
        loaded = [
            pltpu.make_async_copy(source.at[index], target, refs[-1].at[copies + place])
            for place, (source, (_, index), target) in enumerate(
                zip(sources, loads, take(len(loads)))
            )
        ]
        for copy in loaded:
            copy.start()
        own = take(len(scratch))
        for place, (k, buffer) in enumerate(zip(staged, take(len(staged)))):
            filled[k] = Staged(filled[k], buffer, refs[-1].at[place])
        for place, (k, buffer) in enumerate(zip(sent, take(len(sent)))):
            target = kept[k].at[0 : buffer.shape[0]] if outs[k].shape != buffer.shape else kept[k]
            kept[k] = Sent(target, buffer, refs[-1].at[len(staged) + place])
        body(
            *[filled.get(k) for k in range(len(operands))],
            *[kept.get(k) for k in range(len(outs))],
            *own,
        )
        for k in staged:
            filled[k].load()
        for k in sent:
            kept[k].copy.wait()
        for copy in loaded:
            copy.wait()

    arrays = [operands[k] for k in given]
    results = [outs[k] for k in made]
    size = sum(x.size * x.dtype.itemsize for x in (*arrays, *results))
    in_vmem = pl.BlockSpec(memory_space=pltpu.VMEM)
    in_hbm = pl.BlockSpec(memory_space=pltpu.HBM)
    buffers = [pltpu.VMEM(operands[k].shape, operands[k].dtype) for k in staged]
    for k in sent:
        rows = sent[k] or outs[k].shape[0]
        buffers.append(pltpu.VMEM((rows, *outs[k].shape[1:]), outs[k].dtype))
    if copies + len(loads) > 0:
        buffers.append(pltpu.SemaphoreType.DMA((copies + len(loads),)))
    results += [part_shape(source, index) for source, index in loads]
    results = pl.pallas_call(
        kernel,
        out_shape=results,
        in_specs=[in_hbm if k in staged else in_vmem for k in given] + [in_hbm] * len(loads),
        out_specs=[in_hbm if k in sent else in_vmem for k in made] + [in_vmem] * len(loads),
        scratch_shapes=[*scratch, *buffers],
        compiler_params=pltpu.CompilerParams(vmem_limit_bytes=limit),
        cost_estimate=pl.CostEstimate(flops=flops, bytes_accessed=size, transcendentals=0),
        name=body.__name__ if hasattr(body, "__name__") else body.func.__name__,
    )(*arrays, *[source for source, _ in loads])
    loaded = list(results[len(made) :])
    results = dict(zip(made, results))
    return [results.get(k) for k in range(len(outs))] + loaded


def exchange(values):
    return lax.all_to_all(values, ("batch", "space"), split_axis=0, concat_axis=0, tiled=True)


def neighbours(first, last):
    ends = lax.axis_size("space") - 1
    before = lax.ppermute(last, "space", [(i, i + 1) for i in range(ends)])
    after = lax.ppermute(first, "space", [(i + 1, i) for i in range(ends)])
    return before, after


def shards(snapshots, cotangent, mode_weight, conv_weight):
    batches = lax.axis_size("batch")
    slabs = lax.axis_size("space")
    devices = batches * slabs
    _, channels, layers, plane = snapshots.shape
    modes = mode_weight.shape[0] * mode_weight.shape[1]
    half = LANES // 2
    assert channels == half and layers == 2 and plane == CELLS
    plane_rows = devices * modes
    count = modes * 2 * KZ * batches
    in_slab = modes == 8 and devices * 32 == TERM_ROWS

    tables, parts = join_tables(batches, slabs, layers, modes)
    tables = jnp.asarray(tables)

    def table(name):
        return tables, parts[name].index

    weights = mode_weight.reshape(modes * 2 * KZ * channels, channels)
    taps = conv_weight.reshape(OFFSETS, channels, channels)
    field = shape((channels, layers, plane), BF16)
    wide = shape((CELLS, LANES), BF16)
    edge = shape((CELLS // 2, LANES), BF16)
    plane_modes = shape((plane_rows, LANES), BF16)
    padded = pltpu.VMEM((CELLS + 2 * NY, 2 * LANES), BF16)

    def send(values):
        return exchange(values.reshape(devices, modes, LANES)).reshape(plane_rows, LANES)

    cells, coef, first, last = run(
        analyse_kernel,
        [wide, plane_modes, edge, edge],
        snapshots.reshape(field.shape),
        parts["analysis"].values,
        staged=(0, 1),
        sent=(0, 1, 2, 3),
        limit=WHOLE_VMEM,
        flops=10**8,
    )
    packed = shape((weights.shape[0] // 2, LANES), BF16)
    weights, coef = lax.optimization_barrier((weights, coef))
    coef = send(coef)
    packed_rows = packed.shape[0]
    packed_weights, kept_weights, gather, scatter = run(
        pack_kernel,
        [packed, shape((max(packed_rows, HBM_ROWS), LANES), BF16)],
        weights,
        sent={1: packed_rows},
        loads=[table("gather"), table("scatter")],
        limit=LOADER_VMEM,
    )
    before, after = neighbours(first, last)
    local, lanes, outer_cells, synthesis_cells, synthesis = run(
        local_kernel,
        [shape((CELLS, LANES), F32), shape((2 * LANES, CELLS), BF16), wide],
        cells,
        before,
        after,
        cotangent.reshape(field.shape),
        taps,
        loads=[table("synthesis_cells"), table("synthesis")],
        limit=LOADER_VMEM,
        scratch=[padded, pltpu.VMEM((3, 2 * LANES, 3 * LANES), BF16)],
        flops=7 * 10**8,
    )
    back, diagonal = run(
        functools.partial(mix_kernel, batches),
        [plane_modes, shape((count, GROUP * half // 2), BF16)],
        coef,
        gather,
        packed_weights,
        scatter,
        sent=(0, 1),
        flops=4 * 10**8,
    )
    back = send(back)
    slab = shape((devices, 8 + TERM_ROWS // devices, LANES), BF16)
    activated, grad, first, last, back, terms = run(
        functools.partial(activate_kernel, in_slab),
        [
            wide,
            wide,
            edge,
            edge,
            slab if in_slab else plane_modes,
            None if in_slab else shape((TERM_ROWS, LANES), BF16),
        ],
        back,
        synthesis_cells,
        synthesis,
        local,
        outer_cells,
        lanes,
        sent=(0, 1, 2, 3, 4),
        scratch=[pltpu.VMEM((CELLS + 2 * NY, 3 * LANES), BF16)],
        flops=10**9,
    )
    if in_slab:
        back = exchange(back)
    else:
        back = send(back)
        terms = exchange(terms.reshape(devices, TERM_ROWS // devices, LANES))
    before, after = neighbours(first, last)
    activated, packed_weights, gather_back, scatter_back = run(
        output_kernel,
        [field],
        activated,
        loads=[
            (kept_weights, (slice(0, packed_rows),)),
            table("gather_back"),
            table("scatter_back"),
        ],
        limit=LOADER_VMEM,
        flops=10**8,
    )
    back, before, after = lax.optimization_barrier((back, before, after))
    scale = 1.0 / math.sqrt(batches * slabs * layers * plane)
    grad_modes, mixed_grad, sums = run(
        functools.partial(unmix_kernel, batches, scale),
        [
            slab if in_slab else plane_modes,
            shape((count, LANES), BF16),
            None if in_slab else shape((TERM_ROWS // devices, LANES), F32),
        ],
        back,
        None if in_slab else terms,
        gather_back,
        packed_weights,
        scatter_back,
        sent=(0,),
        flops=4 * 10**8,
    )
    if in_slab:
        grad_modes = exchange(grad_modes)
    else:
        grad_modes = send(grad_modes)
        sums = lax.all_gather(sums, ("batch", "space"), axis=0, tiled=True)
    local, analysis_cells = run(
        local_grad_kernel,
        [shape((CELLS, LANES), F32)],
        grad,
        before,
        after,
        taps,
        loads=[table("analysis_cells")],
        limit=LOADER_VMEM,
        scratch=[padded, pltpu.VMEM((3, 3 * LANES, 2 * LANES), BF16)],
        flops=7 * 10**8,
    )
    (mode_gradient,) = run(
        functools.partial(weight_kernel, batches),
        [shape((modes * 2 * KZ * channels, channels), F32)],
        diagonal,
        mixed_grad,
        flops=4 * 10**8,
    )
    input_gradient, conv_gradient = run(
        finish_kernel,
        [field, shape((OFFSETS, channels, channels), F32)],
        grad_modes,
        sums,
        analysis_cells,
        local,
        flops=10**8,
    )
    return (
        activated.reshape(snapshots.shape),
        input_gradient.reshape(snapshots.shape),
        mode_gradient.reshape(mode_weight.shape),
        conv_gradient.reshape(conv_weight.shape),
    )


def solution(mesh):
    in_specs = (
        P("batch", None, "space", None),
        P("batch", None, "space", None),
        P("batch", "space", None, None, None),
        P(),
    )
    out_specs = (
        P("batch", None, "space", None),
        P("batch", None, "space", None),
        P("batch", "space", None, None, None),
        P(),
    )
    return jax.shard_map(shards, mesh=mesh, in_specs=in_specs, out_specs=out_specs, check_vma=False)
```

```python
import functools
import math

import jax
import jax.numpy as jnp
import ml_dtypes
import numpy as np
from jax import lax
from jax.experimental import pallas as pl
from jax.experimental.pallas import tpu as pltpu
from jax.sharding import PartitionSpec as P

KX = 8
KY = 8
KZ = 12
NX = 32
NY = 32
CELLS = NX * NY
LANES = 128
GROUP = 8
OFFSETS = 27
TERM_ROWS = 1024
VMEM_BYTES = 40 * 1024 * 1024
WHOLE_VMEM = 65000 * 1024
HBM_ROWS = 163840

F32 = jnp.float32
BF16 = jnp.bfloat16
inv_root_two = 1.0 / math.sqrt(2.0)
inv_root_two_pi = 1.0 / math.sqrt(2.0 * math.pi)


def basis_rows(half_count, length):
    row = np.arange(2 * half_count)[:, None]
    cell = np.arange(length)[None, :]
    frequency = np.where(row < half_count, row, row - half_count + 1)
    phases = (frequency * cell % length).astype(np.float32) * np.float32(2.0 * math.pi / length)
    return np.where(row < half_count, np.cos(phases), np.sin(phases)).astype(np.float32)


def plane_tables(batches, slabs):
    outer = (basis_rows(KX, NX)[:, None, :, None] * basis_rows(KY, NY)[None, :, None, :]).reshape(
        2 * KX, 2 * KY, CELLS
    )
    outer = outer.reshape(batches, 2 * KX // batches, slabs, 2 * KY // slabs, CELLS)
    outer = outer.transpose(0, 2, 1, 3, 4).reshape(4 * KX * KY, CELLS)
    analysis = (outer * np.float32(2.0 / math.sqrt(CELLS))).astype(ml_dtypes.bfloat16)
    synthesis = (outer * np.float32(2.0 / math.sqrt(4 * KX * KY))).astype(ml_dtypes.bfloat16)
    return analysis, synthesis


def depth_tables(slabs, layers, modes):
    rows = basis_rows(KZ, slabs * layers)
    analysis = (rows * np.float32(math.sqrt(2.0 / (slabs * layers)))).astype(ml_dtypes.bfloat16)
    synthesis = (rows * np.float32(math.sqrt(2.0 / (2 * KZ)))).astype(ml_dtypes.bfloat16)

    def spread(table, order):
        table = table.astype(np.float32).reshape(2 * KZ, slabs, layers)
        full = np.einsum("psz,mn->" + order, table, np.eye(modes, dtype=np.float32))
        return full.astype(ml_dtypes.bfloat16)

    def gathered(table):
        return spread(table, "mpzsn").reshape(modes * 2 * KZ, layers * slabs * modes)

    def scattered(table):
        return spread(table, "snzmp").reshape(slabs * modes, layers * modes * 2 * KZ)

    return gathered(analysis), scattered(synthesis), gathered(synthesis), scattered(analysis)


def dot(left, right, contract=(1, 0)):
    return lax.dot_general(
        left, right, (((contract[0],), (contract[1],)), ((), ())), preferred_element_type=F32
    )


def turn_table():
    row = lax.broadcasted_iota(jnp.int32, (LANES, LANES), 0)
    column = lax.broadcasted_iota(jnp.int32, (LANES, LANES), 1)
    return jnp.where(column == row % 2 * (LANES // 2) + row // 2, 1.0, 0.0).astype(BF16)


def to_cells(field):
    return dot(field.reshape(LANES, CELLS), turn_table(), (0, 0))


def to_field(cells):
    return dot(turn_table(), cells, (1, 1)).astype(BF16).reshape(LANES // 2, 2, CELLS)


def low_lanes(rows):
    return lax.broadcasted_iota(jnp.int32, (rows, LANES), 1) < LANES // 2


def swap_halves(values):
    return pltpu.roll(values, LANES // 2, 1)


def doubled(values):
    low = low_lanes(values.shape[0])
    swapped = swap_halves(values)
    return jnp.concatenate(
        [jnp.where(low, values, swapped), jnp.where(low, swapped, values)], axis=0
    )


def halved(values):
    low = low_lanes(values.shape[0])
    return jnp.concatenate([jnp.where(low, values, 0.0), jnp.where(low, 0.0, values)], axis=0)


def edge_layers(cells_first):
    top = cells_first[: CELLS // 2]
    bottom = cells_first[CELLS // 2 :]
    low = low_lanes(CELLS // 2)
    first = jnp.where(low, top, swap_halves(bottom))
    last = jnp.where(low, swap_halves(top), bottom)
    return first.astype(BF16), last.astype(BF16)


def beside_layers(before, after):
    before = before.astype(F32)
    after = after.astype(F32)
    low = low_lanes(CELLS // 2)
    top = jnp.where(low, before, swap_halves(after))
    bottom = jnp.where(low, swap_halves(before), after)
    return jnp.concatenate([top, bottom], axis=0).astype(BF16)


def y_cells(rows):
    return lax.broadcasted_iota(jnp.int32, (rows, LANES), 0) % NY


def from_below(values):
    return jnp.where(y_cells(values.shape[0]) == 0, 0.0, pltpu.roll(values, 1, 0))


def from_above(values):
    rows = values.shape[0]
    return jnp.where(y_cells(rows) == NY - 1, 0.0, pltpu.roll(values, rows - 1, 0))


def pad_cells(padded, own, beside):
    width = own.shape[1] + beside.shape[1]
    padded[0:NY, :] = jnp.zeros((NY, width), BF16)
    padded[NY + CELLS : 2 * NY + CELLS, :] = jnp.zeros((NY, width), BF16)
    padded[NY : NY + CELLS, 0 : own.shape[1]] = own
    padded[NY : NY + CELLS, own.shape[1] :] = beside


BLOCK_OF_DEPTH = {-1: 2, 0: 0, 1: 1, 2: 3}
STEP = 256


def stencil(padded, table, transposed, store):
    for start in range(0, CELLS, STEP):
        total = None
        for b in range(3):
            cells = padded[start + NY * b : start + NY * b + STEP, :]
            term = dot(cells, table[b], (1, 1) if transposed else (1, 0))
            total = term if total is None else total + term
        result = (
            from_below(total[:, 0:LANES])
            + total[:, LANES : 2 * LANES]
            + from_above(total[:, 2 * LANES :])
        )
        store(start, result)


def banded_forward(weights, table):
    half = LANES // 2
    for b in range(3):
        for c in range(3):
            for depth, block in BLOCK_OF_DEPTH.items():
                parts = []
                for out in range(2):
                    a = depth - out + 1
                    if 0 <= a < 3:
                        parts.append(weights[a * 9 + b * 3 + c])
                    else:
                        parts.append(jnp.zeros((half, half), BF16))
                table[b, block * half : (block + 1) * half, c * LANES : (c + 1) * LANES] = (
                    jnp.concatenate(parts, axis=1)
                )


def banded_backward(weights, table):
    half = LANES // 2
    for b in range(3):
        for c in range(3):
            for out in range(2):
                for pair in ((0, 1), (-1, 2)):
                    parts = []
                    for depth in pair:
                        a = depth - out + 1
                        if 0 <= a < 3:
                            parts.append(weights[(2 - a) * 9 + (2 - b) * 3 + 2 - c])
                        else:
                            parts.append(jnp.zeros((half, half), BF16))
                    row = c * LANES + out * half
                    column = BLOCK_OF_DEPTH[pair[0]] * half
                    table[b, row : row + half, column : column + LANES] = jnp.concatenate(
                        parts, axis=1
                    )


def analyse_kernel(field, analysis, cells_out, coef_out, first_out, last_out):
    cells = to_cells(field[...])
    rounded = cells.astype(BF16)
    coef_out[...] = dot(analysis[...], rounded).astype(BF16)
    cells_out[...] = rounded
    first, last = edge_layers(cells)
    first_out[...] = first
    last_out[...] = last


def local_kernel(
    cells, before, after, cotangent, weights, local_out, lanes_out, cotangent_out, padded, table
):
    banded_forward(weights, table)
    beside = beside_layers(before[...], after[...])
    pad_cells(padded, cells[...], beside)

    def store(start, result):
        local_out[start : start + STEP, :] = result

    stencil(padded, table, False, store)
    whole = jnp.concatenate([cells[...].astype(F32), beside.astype(F32)], axis=1)
    lanes_out[...] = whole.T.astype(BF16)
    cotangent_out[...] = to_cells(cotangent[...]).astype(BF16)


def pack_kernel(weights, out, kept):
    rows = GROUP * LANES // 4
    for g in range(out.shape[0] // rows):
        first = weights[2 * g * rows : (2 * g + 1) * rows, :]
        second = weights[(2 * g + 1) * rows : (2 * g + 2) * rows, :]
        out[g * rows : (g + 1) * rows, :] = jnp.concatenate([first, second], axis=1)
    kept[...] = out[...]


def mode_in_group(rows, lanes):
    return lax.broadcasted_iota(jnp.int32, (rows, lanes), 0) % GROUP


def own_block(rows):
    width = GROUP * LANES // 4
    lane = lax.broadcasted_iota(jnp.int32, (rows, width), 1)
    return mode_in_group(rows, width) % (GROUP // 2) == lane // (LANES // 2)


def own_half(rows):
    return (mode_in_group(rows, LANES) < GROUP // 2) == low_lanes(rows)


def to_depth(modes, table, snaps):
    rows = modes.shape[0] // snaps
    both = [doubled(modes[b * rows : (b + 1) * rows]) for b in range(snaps)]
    result = dot(table, jnp.concatenate(both, axis=1).astype(BF16))
    return jnp.concatenate(
        [
            result[g : g + GROUP, b * LANES : (b + 1) * LANES]
            for g in range(0, result.shape[0], GROUP)
            for b in range(snaps)
        ],
        axis=0,
    )


def from_depth(modes, table, snaps):
    count = modes.shape[0] // GROUP
    both = []
    for b in range(snaps):
        own = [modes[g * GROUP : (g + 1) * GROUP] for g in range(b, count, snaps)]
        both.append(halved(jnp.concatenate(own, axis=0)))
    result = dot(table, jnp.concatenate(both, axis=1).astype(BF16))
    return jnp.concatenate(
        [result[:, b * LANES : (b + 1) * LANES] for b in range(snaps)], axis=0
    )


def mix_kernel(snaps, received, gather, weights, scatter, back_out, diagonal_out):
    coef = to_depth(received[...].astype(F32), gather[...], snaps)
    count = coef.shape[0]
    wide = jnp.concatenate([coef] * (GROUP // 4), axis=1)
    diagonal = jnp.where(own_block(count), wide, 0.0).astype(BF16)
    diagonal_out[...] = diagonal
    rows = GROUP * snaps
    depth = GROUP * LANES // 4
    mixed = jnp.concatenate(
        [
            dot(diagonal[g * rows : (g + 1) * rows, :], weights[g * depth : (g + 1) * depth, :])
            for g in range(count // rows)
        ],
        axis=0,
    )
    mixed = jnp.where(own_half(count), mixed, swap_halves(mixed))
    back_out[...] = from_depth(mixed, scatter[...], snaps).astype(BF16)


def activate_kernel(
    terms_in_slab,
    received,
    synthesis,
    synthesis_rows,
    local,
    cotangent,
    lanes,
    activated_out,
    grad_out,
    first_out,
    last_out,
    back_out,
    terms_out,
    spread,
):
    pre = dot(synthesis[...], received[...]) + local[...]
    cdf = 0.5 * (1.0 + lax.erf(pre * inv_root_two))
    density = jnp.exp(-0.5 * pre * pre) * inv_root_two_pi
    activated_out[...] = (pre * cdf).astype(BF16)
    grad = (cotangent[...].astype(F32) * (cdf + pre * density)).astype(BF16)
    grad_out[...] = grad
    back = dot(synthesis_rows[...], grad)
    grad = grad.astype(F32)
    first, last = edge_layers(grad)
    first_out[...] = first
    last_out[...] = last
    spread[0:NY, :] = jnp.zeros((NY, 3 * LANES), BF16)
    spread[NY + CELLS : 2 * NY + CELLS, :] = jnp.zeros((NY, 3 * LANES), BF16)
    spread[NY : NY + CELLS, 0:LANES] = from_above(grad).astype(BF16)
    spread[NY : NY + CELLS, LANES : 2 * LANES] = grad.astype(BF16)
    spread[NY : NY + CELLS, 2 * LANES :] = from_below(grad).astype(BF16)
    half = LANES // 2
    low = low_lanes(half)
    twice = {}
    for b in range(3):
        product = dot(lanes[...], spread[NY * (2 - b) : NY * (2 - b) + CELLS, :])
        for c in range(3):
            for a in range(3):
                blocks = [BLOCK_OF_DEPTH[out + a - 1] * half for out in range(2)]
                columns = slice(c * LANES, (c + 1) * LANES)
                both = jnp.where(
                    low,
                    product[blocks[0] : blocks[0] + half, columns],
                    product[blocks[1] : blocks[1] + half, columns],
                )
                twice[a * 9 + b * 3 + c] = both + swap_halves(both)
    pairs = []
    for k in range(0, OFFSETS, 2):
        pairs.append(jnp.where(low, twice[k], twice.get(k + 1, 0.0)))
    pairs.append(jnp.zeros((TERM_ROWS - half * len(pairs), LANES), F32))
    terms = jnp.concatenate(pairs, axis=0)
    if terms_in_slab:
        slab_store(back_out, back, terms)
    else:
        back_out[...] = back.astype(BF16)
        terms_out[...] = terms.astype(BF16)


def slab_store(slab, modes, terms):
    owners = slab.shape[0]
    modes = modes.reshape(owners, 8, LANES)
    terms = terms.reshape(owners, -1, LANES)
    slab[...] = jnp.concatenate([modes, terms], axis=1).astype(BF16)


def slab_load(slab):
    whole = slab[...].astype(F32)
    return whole[:, 0:8, :].reshape(-1, LANES), whole[:, 8:, :]


def unmix_kernel(snaps, scale, received, terms, gather, weights, scatter, grad_out, mixed_out, sums_out):
    in_slab = terms is None
    if in_slab:
        modes, terms = slab_load(received)
    else:
        modes, terms = received[...].astype(F32), terms[...].astype(F32)
    mixed = to_depth(modes, gather[...], snaps)
    mixed_out[...] = mixed.astype(BF16)
    count = mixed.shape[0]
    rows = GROUP * snaps
    depth = GROUP * LANES // 4
    sums = jnp.sum(terms, axis=0) * scale
    own = own_block(rows)
    placed = jnp.where(own_half(count), mixed, 0.0).astype(BF16)
    pieces = []
    for g in range(count // rows):
        full = dot(
            placed[g * rows : (g + 1) * rows, :], weights[g * depth : (g + 1) * depth, :], (1, 1)
        )
        full = jnp.where(own, full, 0.0)
        pieces.append(sum(full[:, k : k + LANES] for k in range(0, depth, LANES)))
    coef = jnp.concatenate(pieces, axis=0)
    coef = coef + swap_halves(coef)
    grad = from_depth(coef, scatter[...], snaps)
    if in_slab:
        owners = received.shape[0]
        share = sums.shape[0]
        slab_store(
            grad_out, grad, jnp.broadcast_to(sums[None], (owners, share, LANES)).reshape(-1, LANES)
        )
    else:
        grad_out[...] = grad.astype(BF16)
        sums_out[...] = sums


def weight_kernel(snaps, diagonal, mixed, out):
    rows = GROUP * snaps
    depth = GROUP * LANES // 4
    half = LANES // 2
    first = mode_in_group(rows, depth) < GROUP // 2
    for g in range(diagonal.shape[0] // rows):
        span = slice(g * rows, (g + 1) * rows)
        blocks = diagonal[span, :].astype(F32)
        blocks = [jnp.where(first, blocks, 0.0), jnp.where(first, 0.0, blocks)]
        blocks = jnp.concatenate(blocks, axis=1).astype(BF16)
        out[2 * g * depth : 2 * (g + 1) * depth, :] = dot(blocks, mixed[span, 0:half], (0, 0))


def output_kernel(cells, out):
    out[...] = to_field(cells[...])


def local_grad_kernel(grad, before, after, weights, out, padded, table):
    banded_backward(weights, table)
    pad_cells(padded, grad[...], beside_layers(before[...], after[...]))

    def store(start, result):
        out[start : start + STEP, :] = result

    stencil(padded, table, True, store)


def finish_kernel(received, sums, synthesis, local, grad_out, stencil_out):
    in_slab = sums is None
    if in_slab:
        modes, terms = slab_load(received)
        terms = terms.reshape(TERM_ROWS, LANES)
    else:
        modes, terms = received[...], sums[...].astype(F32)
    cells = (dot(synthesis[...], modes.astype(BF16)) + local[...]).astype(BF16)
    grad_out[...] = to_field(cells)
    half = LANES // 2
    for k in range(OFFSETS):
        row = (k // 2) * half
        lane = (k % 2) * half
        stencil_out[k] = terms[row : row + half, lane : lane + half]


def shape(dims, dtype):
    return jax.ShapeDtypeStruct(dims, dtype)


class Staged:
    def __init__(self, source, buffer, semaphore):
        self.copy = pltpu.make_async_copy(source, buffer, semaphore)
        self.buffer = buffer
        self.copy.start()
        self.ready = False

    def load(self):
        if not self.ready:
            self.copy.wait()
            self.ready = True

    def __getitem__(self, index):
        self.load()
        return self.buffer[index]


class Sent:
    def __init__(self, target, buffer, semaphore):
        self.copy = pltpu.make_async_copy(buffer, target, semaphore)
        self.buffer = buffer

    def __setitem__(self, index, value):
        self.buffer[index] = value
        self.copy.start()

    def __getitem__(self, index):
        return self.buffer[index]

    @property
    def shape(self):
        return self.buffer.shape


def run(body, outs, *operands, staged=(), sent=(), scratch=(), flops=0, limit=VMEM_BYTES):
    given = [k for k, operand in enumerate(operands) if operand is not None]
    made = [k for k, out in enumerate(outs) if out is not None]

    def rows_of(chosen, places, arrays):
        chosen = {k: chosen[k] if isinstance(chosen, dict) else None for k in places if k in chosen}
        return {k: rows or arrays[k].shape[0] for k, rows in chosen.items()}

    staged = rows_of(staged, given, operands)
    sent = rows_of(sent, made, outs)

    def kernel(*refs):
        refs = list(refs)

        def take(count):
            taken = refs[:count]
            del refs[:count]
            return taken

        def part(ref, rows):
            return ref if ref.shape[0] == rows else ref.at[0:rows]

        filled = dict(zip(given, take(len(given))))
        kept = dict(zip(made, take(len(made))))
        own = take(len(scratch))
        for place, (k, buffer) in enumerate(zip(staged, take(len(staged)))):
            filled[k] = Staged(part(filled[k], staged[k]), buffer, refs[-1].at[place])
        for place, (k, buffer) in enumerate(zip(sent, take(len(sent)))):
            kept[k] = Sent(part(kept[k], sent[k]), buffer, refs[-1].at[len(staged) + place])
        body(
            *[filled.get(k) for k in range(len(operands))],
            *[kept.get(k) for k in range(len(outs))],
            *own,
        )
        for k in staged:
            filled[k].load()
        for k in sent:
            kept[k].copy.wait()

    arrays = [operands[k] for k in given]
    results = [outs[k] for k in made]
    size = sum(x.size * x.dtype.itemsize for x in (*arrays, *results))
    in_vmem = pl.BlockSpec(memory_space=pltpu.VMEM)
    in_hbm = pl.BlockSpec(memory_space=pltpu.HBM)
    buffers = [(operands[k], rows) for k, rows in staged.items()]
    buffers += [(outs[k], rows) for k, rows in sent.items()]
    buffers = [pltpu.VMEM((rows, *x.shape[1:]), x.dtype) for x, rows in buffers]
    if buffers:
        buffers.append(pltpu.SemaphoreType.DMA((len(buffers),)))
    results = pl.pallas_call(
        kernel,
        out_shape=results,
        in_specs=[in_hbm if k in staged else in_vmem for k in given],
        out_specs=[in_hbm if k in sent else in_vmem for k in made],
        scratch_shapes=[*scratch, *buffers],
        compiler_params=pltpu.CompilerParams(vmem_limit_bytes=limit),
        cost_estimate=pl.CostEstimate(flops=flops, bytes_accessed=size, transcendentals=0),
        name=body.__name__ if hasattr(body, "__name__") else body.func.__name__,
    )(*arrays)
    results = dict(zip(made, results))
    return [results.get(k) for k in range(len(outs))]


def exchange(values):
    return lax.all_to_all(values, ("batch", "space"), split_axis=0, concat_axis=0, tiled=True)


def neighbours(first, last):
    ends = lax.axis_size("space") - 1
    before = lax.ppermute(last, "space", [(i, i + 1) for i in range(ends)])
    after = lax.ppermute(first, "space", [(i + 1, i) for i in range(ends)])
    return before, after


def shards(snapshots, cotangent, mode_weight, conv_weight):
    batches = lax.axis_size("batch")
    slabs = lax.axis_size("space")
    devices = batches * slabs
    _, channels, layers, plane = snapshots.shape
    modes = mode_weight.shape[0] * mode_weight.shape[1]
    half = LANES // 2
    assert channels == half and layers == 2 and plane == CELLS
    plane_rows = devices * modes
    count = modes * 2 * KZ * batches
    in_slab = modes == 8 and devices * 32 == TERM_ROWS

    analysis, synthesis = plane_tables(batches, slabs)
    gather, scatter, gather_back, scatter_back = depth_tables(slabs, layers, modes)
    weights = mode_weight.reshape(modes * 2 * KZ * channels, channels)
    taps = conv_weight.reshape(OFFSETS, channels, channels)
    field = shape((channels, layers, plane), BF16)
    wide = shape((CELLS, LANES), BF16)
    edge = shape((CELLS // 2, LANES), BF16)
    plane_modes = shape((plane_rows, LANES), BF16)
    padded = pltpu.VMEM((CELLS + 2 * NY, 2 * LANES), BF16)

    def send(values):
        return exchange(values.reshape(devices, modes, LANES)).reshape(plane_rows, LANES)

    cells, coef, first, last = run(
        analyse_kernel,
        [wide, plane_modes, edge, edge],
        snapshots.reshape(field.shape),
        analysis,
        staged=(0, 1),
        sent=(0, 1, 2, 3),
        limit=WHOLE_VMEM,
        flops=10**8,
    )
    packed = shape((weights.shape[0] // 2, LANES), BF16)
    weights, coef = lax.optimization_barrier((weights, coef))
    coef = send(coef)
    packed_rows = packed.shape[0]
    packed_weights, kept_weights = run(
        pack_kernel,
        [packed, shape((max(packed_rows, HBM_ROWS), LANES), BF16)],
        weights,
        sent={1: packed_rows},
    )
    before, after = neighbours(first, last)
    local, lanes, outer_cells = run(
        local_kernel,
        [shape((CELLS, LANES), F32), shape((2 * LANES, CELLS), BF16), wide],
        cells,
        before,
        after,
        cotangent.reshape(field.shape),
        taps,
        scratch=[padded, pltpu.VMEM((3, 2 * LANES, 3 * LANES), BF16)],
        flops=7 * 10**8,
    )
    back, diagonal = run(
        functools.partial(mix_kernel, batches),
        [plane_modes, shape((count, GROUP * half // 2), BF16)],
        coef,
        gather,
        packed_weights,
        scatter,
        sent=(0, 1),
        flops=4 * 10**8,
    )
    back = send(back)
    slab = shape((devices, 8 + TERM_ROWS // devices, LANES), BF16)
    activated, grad, first, last, back, terms = run(
        functools.partial(activate_kernel, in_slab),
        [
            wide,
            wide,
            edge,
            edge,
            slab if in_slab else plane_modes,
            None if in_slab else shape((TERM_ROWS, LANES), BF16),
        ],
        back,
        np.ascontiguousarray(synthesis.T),
        synthesis,
        local,
        outer_cells,
        lanes,
        sent=(2, 3, 4),
        scratch=[pltpu.VMEM((CELLS + 2 * NY, 3 * LANES), BF16)],
        flops=10**9,
    )
    if in_slab:
        back = exchange(back)
    else:
        back = send(back)
        terms = exchange(terms.reshape(devices, TERM_ROWS // devices, LANES))
    before, after = neighbours(first, last)
    (activated,) = run(
        output_kernel,
        [field],
        activated,
        flops=10**8,
    )
    back, before, after, activated = lax.optimization_barrier((back, before, after, activated))
    scale = 1.0 / math.sqrt(batches * slabs * layers * plane)
    grad_modes, mixed_grad, sums = run(
        functools.partial(unmix_kernel, batches, scale),
        [
            slab if in_slab else plane_modes,
            shape((count, LANES), BF16),
            None if in_slab else shape((TERM_ROWS // devices, LANES), F32),
        ],
        back,
        None if in_slab else terms,
        gather_back,
        kept_weights,
        scatter_back,
        staged={3: packed_rows},
        sent=(0,),
        flops=4 * 10**8,
    )
    if in_slab:
        grad_modes = exchange(grad_modes)
    else:
        grad_modes = send(grad_modes)
        sums = lax.all_gather(sums, ("batch", "space"), axis=0, tiled=True)
    (local,) = run(
        local_grad_kernel,
        [shape((CELLS, LANES), F32)],
        grad,
        before,
        after,
        taps,
        scratch=[padded, pltpu.VMEM((3, 3 * LANES, 2 * LANES), BF16)],
        flops=7 * 10**8,
    )
    (mode_gradient,) = run(
        functools.partial(weight_kernel, batches),
        [shape((modes * 2 * KZ * channels, channels), F32)],
        diagonal,
        mixed_grad,
        flops=4 * 10**8,
    )
    input_gradient, conv_gradient = run(
        finish_kernel,
        [field, shape((OFFSETS, channels, channels), F32)],
        grad_modes,
        sums,
        np.ascontiguousarray(analysis.T),
        local,
        flops=10**8,
    )
    return (
        activated.reshape(snapshots.shape),
        input_gradient.reshape(snapshots.shape),
        mode_gradient.reshape(mode_weight.shape),
        conv_gradient.reshape(conv_weight.shape),
    )


def solution(mesh):
    in_specs = (
        P("batch", None, "space", None),
        P("batch", None, "space", None),
        P("batch", "space", None, None, None),
        P(),
    )
    out_specs = (
        P("batch", None, "space", None),
        P("batch", None, "space", None),
        P("batch", "space", None, None, None),
        P(),
    )
    return jax.shard_map(shards, mesh=mesh, in_specs=in_specs, out_specs=out_specs, check_vma=False)
```

```python
import functools
import math

import jax
import jax.numpy as jnp
import ml_dtypes
import numpy as np
from jax import lax
from jax.experimental import pallas as pl
from jax.experimental.pallas import tpu as pltpu
from jax.sharding import PartitionSpec as P

KX = 8
KY = 8
KZ = 12
NX = 32
NY = 32
CELLS = NX * NY
LANES = 128
GROUP = 8
OFFSETS = 27
TERM_ROWS = 1024
VMEM_BYTES = 40 * 1024 * 1024
WHOLE_VMEM = 65000 * 1024
HBM_BYTES = 100 * 1024 * 256

F32 = jnp.float32
BF16 = jnp.bfloat16
inv_root_two = 1.0 / math.sqrt(2.0)
inv_root_two_pi = 1.0 / math.sqrt(2.0 * math.pi)


def basis_rows(half_count, length):
    row = np.arange(2 * half_count)[:, None]
    cell = np.arange(length)[None, :]
    frequency = np.where(row < half_count, row, row - half_count + 1)
    phases = (frequency * cell % length).astype(np.float32) * np.float32(2.0 * math.pi / length)
    return np.where(row < half_count, np.cos(phases), np.sin(phases)).astype(np.float32)


def plane_tables(batches, slabs):
    outer = (basis_rows(KX, NX)[:, None, :, None] * basis_rows(KY, NY)[None, :, None, :]).reshape(
        2 * KX, 2 * KY, CELLS
    )
    outer = outer.reshape(batches, 2 * KX // batches, slabs, 2 * KY // slabs, CELLS)
    outer = outer.transpose(0, 2, 1, 3, 4).reshape(4 * KX * KY, CELLS)
    analysis = (outer * np.float32(2.0 / math.sqrt(CELLS))).astype(ml_dtypes.bfloat16)
    synthesis = (outer * np.float32(2.0 / math.sqrt(4 * KX * KY))).astype(ml_dtypes.bfloat16)
    return analysis, synthesis


def depth_tables(slabs, layers, modes):
    rows = basis_rows(KZ, slabs * layers)
    analysis = (rows * np.float32(math.sqrt(2.0 / (slabs * layers)))).astype(ml_dtypes.bfloat16)
    synthesis = (rows * np.float32(math.sqrt(2.0 / (2 * KZ)))).astype(ml_dtypes.bfloat16)

    def spread(table, order):
        table = table.astype(np.float32).reshape(2 * KZ, slabs, layers)
        full = np.einsum("psz,mn->" + order, table, np.eye(modes, dtype=np.float32))
        return full.astype(ml_dtypes.bfloat16)

    def gathered(table):
        return spread(table, "mpzsn").reshape(modes * 2 * KZ, layers * slabs * modes)

    def scattered(table):
        return spread(table, "snzmp").reshape(slabs * modes, layers * modes * 2 * KZ)

    return gathered(analysis), scattered(synthesis), gathered(synthesis), scattered(analysis)


def dot(left, right, contract=(1, 0)):
    return lax.dot_general(
        left, right, (((contract[0],), (contract[1],)), ((), ())), preferred_element_type=F32
    )


def turn_table():
    row = lax.broadcasted_iota(jnp.int32, (LANES, LANES), 0)
    column = lax.broadcasted_iota(jnp.int32, (LANES, LANES), 1)
    return jnp.where(column == row % 2 * (LANES // 2) + row // 2, 1.0, 0.0).astype(BF16)


def to_cells(field):
    return dot(field.reshape(LANES, CELLS), turn_table(), (0, 0))


def to_field(cells):
    return dot(turn_table(), cells, (1, 1)).astype(BF16).reshape(LANES // 2, 2, CELLS)


def low_lanes(rows):
    return lax.broadcasted_iota(jnp.int32, (rows, LANES), 1) < LANES // 2


def swap_halves(values):
    return pltpu.roll(values, LANES // 2, 1)


def doubled(values):
    low = low_lanes(values.shape[0])
    swapped = swap_halves(values)
    return jnp.concatenate(
        [jnp.where(low, values, swapped), jnp.where(low, swapped, values)], axis=0
    )


def halved(values):
    low = low_lanes(values.shape[0])
    return jnp.concatenate([jnp.where(low, values, 0.0), jnp.where(low, 0.0, values)], axis=0)


def edge_layers(cells_first):
    top = cells_first[: CELLS // 2]
    bottom = cells_first[CELLS // 2 :]
    low = low_lanes(CELLS // 2)
    first = jnp.where(low, top, swap_halves(bottom))
    last = jnp.where(low, swap_halves(top), bottom)
    return first.astype(BF16), last.astype(BF16)


def beside_layers(before, after):
    before = before.astype(F32)
    after = after.astype(F32)
    low = low_lanes(CELLS // 2)
    top = jnp.where(low, before, swap_halves(after))
    bottom = jnp.where(low, swap_halves(before), after)
    return jnp.concatenate([top, bottom], axis=0).astype(BF16)


def y_cells(rows):
    return lax.broadcasted_iota(jnp.int32, (rows, LANES), 0) % NY


def from_below(values):
    return jnp.where(y_cells(values.shape[0]) == 0, 0.0, pltpu.roll(values, 1, 0))


def from_above(values):
    rows = values.shape[0]
    return jnp.where(y_cells(rows) == NY - 1, 0.0, pltpu.roll(values, rows - 1, 0))


def pad_cells(padded, own, beside):
    width = own.shape[1] + beside.shape[1]
    padded[0:NY, :] = jnp.zeros((NY, width), BF16)
    padded[NY + CELLS : 2 * NY + CELLS, :] = jnp.zeros((NY, width), BF16)
    padded[NY : NY + CELLS, 0 : own.shape[1]] = own
    padded[NY : NY + CELLS, own.shape[1] :] = beside


BLOCK_OF_DEPTH = {-1: 2, 0: 0, 1: 1, 2: 3}
STEP = 256


def stencil(padded, table, transposed, store):
    for start in range(0, CELLS, STEP):
        total = None
        for b in range(3):
            cells = padded[start + NY * b : start + NY * b + STEP, :]
            term = dot(cells, table[b], (1, 1) if transposed else (1, 0))
            total = term if total is None else total + term
        result = (
            from_below(total[:, 0:LANES])
            + total[:, LANES : 2 * LANES]
            + from_above(total[:, 2 * LANES :])
        )
        store(start, result)


def banded_forward(weights, table):
    half = LANES // 2
    for b in range(3):
        for c in range(3):
            for depth, block in BLOCK_OF_DEPTH.items():
                parts = []
                for out in range(2):
                    a = depth - out + 1
                    if 0 <= a < 3:
                        parts.append(weights[a * 9 + b * 3 + c])
                    else:
                        parts.append(jnp.zeros((half, half), BF16))
                table[b, block * half : (block + 1) * half, c * LANES : (c + 1) * LANES] = (
                    jnp.concatenate(parts, axis=1)
                )


def banded_backward(weights, table):
    half = LANES // 2
    for b in range(3):
        for c in range(3):
            for out in range(2):
                for pair in ((0, 1), (-1, 2)):
                    parts = []
                    for depth in pair:
                        a = depth - out + 1
                        if 0 <= a < 3:
                            parts.append(weights[(2 - a) * 9 + (2 - b) * 3 + 2 - c])
                        else:
                            parts.append(jnp.zeros((half, half), BF16))
                    row = c * LANES + out * half
                    column = BLOCK_OF_DEPTH[pair[0]] * half
                    table[b, row : row + half, column : column + LANES] = jnp.concatenate(
                        parts, axis=1
                    )


def analyse_kernel(field, analysis, cells_out, coef_out, first_out, last_out):
    cells = to_cells(field[...])
    rounded = cells.astype(BF16)
    coef_out[...] = dot(analysis[...], rounded).astype(BF16)
    cells_out[...] = rounded
    first, last = edge_layers(cells)
    first_out[...] = first
    last_out[...] = last


def local_kernel(
    cells, before, after, cotangent, weights, local_out, lanes_out, cotangent_out, padded, table
):
    banded_forward(weights, table)
    beside = beside_layers(before[...], after[...])
    pad_cells(padded, cells[...], beside)

    def store(start, result):
        local_out[start : start + STEP, :] = result

    stencil(padded, table, False, store)
    whole = jnp.concatenate([cells[...].astype(F32), beside.astype(F32)], axis=1)
    lanes_out[...] = whole.T.astype(BF16)
    cotangent_out[...] = to_cells(cotangent[...]).astype(BF16)


def pack_kernel(weights, out):
    rows = GROUP * LANES // 4
    for g in range(out.shape[0] // rows):
        first = weights[2 * g * rows : (2 * g + 1) * rows, :]
        second = weights[(2 * g + 1) * rows : (2 * g + 2) * rows, :]
        out[g * rows : (g + 1) * rows, :] = jnp.concatenate([first, second], axis=1)


def mode_in_group(rows, lanes):
    return lax.broadcasted_iota(jnp.int32, (rows, lanes), 0) % GROUP


def own_block(rows):
    width = GROUP * LANES // 4
    lane = lax.broadcasted_iota(jnp.int32, (rows, width), 1)
    return mode_in_group(rows, width) % (GROUP // 2) == lane // (LANES // 2)


def own_half(rows):
    return (mode_in_group(rows, LANES) < GROUP // 2) == low_lanes(rows)


def to_depth(modes, table, snaps):
    rows = modes.shape[0] // snaps
    both = [doubled(modes[b * rows : (b + 1) * rows]) for b in range(snaps)]
    result = dot(table, jnp.concatenate(both, axis=1).astype(BF16))
    return jnp.concatenate(
        [
            result[g : g + GROUP, b * LANES : (b + 1) * LANES]
            for g in range(0, result.shape[0], GROUP)
            for b in range(snaps)
        ],
        axis=0,
    )


def from_depth(modes, table, snaps):
    count = modes.shape[0] // GROUP
    both = []
    for b in range(snaps):
        own = [modes[g * GROUP : (g + 1) * GROUP] for g in range(b, count, snaps)]
        both.append(halved(jnp.concatenate(own, axis=0)))
    result = dot(table, jnp.concatenate(both, axis=1).astype(BF16))
    return jnp.concatenate(
        [result[:, b * LANES : (b + 1) * LANES] for b in range(snaps)], axis=0
    )


def mix_kernel(snaps, received, gather, weights, scatter, back_out, diagonal_out):
    coef = to_depth(received[...].astype(F32), gather[...], snaps)
    count = coef.shape[0]
    wide = jnp.concatenate([coef] * (GROUP // 4), axis=1)
    diagonal = jnp.where(own_block(count), wide, 0.0).astype(BF16)
    diagonal_out[...] = diagonal
    rows = GROUP * snaps
    depth = GROUP * LANES // 4
    mixed = jnp.concatenate(
        [
            dot(diagonal[g * rows : (g + 1) * rows, :], weights[g * depth : (g + 1) * depth, :])
            for g in range(count // rows)
        ],
        axis=0,
    )
    mixed = jnp.where(own_half(count), mixed, swap_halves(mixed))
    back_out[...] = from_depth(mixed, scatter[...], snaps).astype(BF16)


def activate_kernel(
    terms_in_slab,
    received,
    synthesis,
    synthesis_rows,
    local,
    cotangent,
    lanes,
    activated_out,
    grad_out,
    first_out,
    last_out,
    back_out,
    terms_out,
    spread,
):
    pre = dot(synthesis[...], received[...]) + local[...]
    cdf = 0.5 * (1.0 + lax.erf(pre * inv_root_two))
    density = jnp.exp(-0.5 * pre * pre) * inv_root_two_pi
    activated_out[...] = (pre * cdf).astype(BF16)
    grad = (cotangent[...].astype(F32) * (cdf + pre * density)).astype(BF16)
    grad_out[...] = grad
    back = dot(synthesis_rows[...], grad)
    grad = grad.astype(F32)
    first, last = edge_layers(grad)
    first_out[...] = first
    last_out[...] = last
    spread[0:NY, :] = jnp.zeros((NY, 3 * LANES), BF16)
    spread[NY + CELLS : 2 * NY + CELLS, :] = jnp.zeros((NY, 3 * LANES), BF16)
    spread[NY : NY + CELLS, 0:LANES] = from_above(grad).astype(BF16)
    spread[NY : NY + CELLS, LANES : 2 * LANES] = grad.astype(BF16)
    spread[NY : NY + CELLS, 2 * LANES :] = from_below(grad).astype(BF16)
    half = LANES // 2
    low = low_lanes(half)
    twice = {}
    for b in range(3):
        product = dot(lanes[...], spread[NY * (2 - b) : NY * (2 - b) + CELLS, :])
        for c in range(3):
            for a in range(3):
                blocks = [BLOCK_OF_DEPTH[out + a - 1] * half for out in range(2)]
                columns = slice(c * LANES, (c + 1) * LANES)
                both = jnp.where(
                    low,
                    product[blocks[0] : blocks[0] + half, columns],
                    product[blocks[1] : blocks[1] + half, columns],
                )
                twice[a * 9 + b * 3 + c] = both + swap_halves(both)
    pairs = []
    for k in range(0, OFFSETS, 2):
        pairs.append(jnp.where(low, twice[k], twice.get(k + 1, 0.0)))
    pairs.append(jnp.zeros((TERM_ROWS - half * len(pairs), LANES), F32))
    terms = jnp.concatenate(pairs, axis=0)
    if terms_in_slab:
        slab_store(back_out, back, terms)
    else:
        back_out[...] = back.astype(BF16)
        terms_out[...] = terms.astype(BF16)


def slab_store(slab, modes, terms):
    owners = slab.shape[0]
    modes = modes.reshape(owners, 8, LANES)
    terms = terms.reshape(owners, -1, LANES)
    slab[...] = jnp.concatenate([modes, terms], axis=1).astype(BF16)


def slab_load(slab):
    whole = slab[...].astype(F32)
    return whole[:, 0:8, :].reshape(-1, LANES), whole[:, 8:, :]


def unmix_kernel(snaps, scale, received, terms, gather, weights, scatter, grad_out, mixed_out, sums_out):
    in_slab = terms is None
    if in_slab:
        modes, terms = slab_load(received)
    else:
        modes, terms = received[...].astype(F32), terms[...].astype(F32)
    mixed = to_depth(modes, gather[...], snaps)
    mixed_out[...] = mixed.astype(BF16)
    count = mixed.shape[0]
    rows = GROUP * snaps
    depth = GROUP * LANES // 4
    sums = jnp.sum(terms, axis=0) * scale
    own = own_block(rows)
    placed = jnp.where(own_half(count), mixed, 0.0).astype(BF16)
    pieces = []
    for g in range(count // rows):
        full = dot(
            placed[g * rows : (g + 1) * rows, :], weights[g * depth : (g + 1) * depth, :], (1, 1)
        )
        full = jnp.where(own, full, 0.0)
        pieces.append(sum(full[:, k : k + LANES] for k in range(0, depth, LANES)))
    coef = jnp.concatenate(pieces, axis=0)
    coef = coef + swap_halves(coef)
    grad = from_depth(coef, scatter[...], snaps)
    if in_slab:
        owners = received.shape[0]
        share = sums.shape[0]
        slab_store(
            grad_out, grad, jnp.broadcast_to(sums[None], (owners, share, LANES)).reshape(-1, LANES)
        )
    else:
        grad_out[...] = grad.astype(BF16)
        sums_out[...] = sums


def weight_kernel(snaps, diagonal, mixed, out):
    rows = GROUP * snaps
    depth = GROUP * LANES // 4
    half = LANES // 2
    first = mode_in_group(rows, depth) < GROUP // 2
    for g in range(diagonal.shape[0] // rows):
        span = slice(g * rows, (g + 1) * rows)
        blocks = diagonal[span, :].astype(F32)
        blocks = [jnp.where(first, blocks, 0.0), jnp.where(first, 0.0, blocks)]
        blocks = jnp.concatenate(blocks, axis=1).astype(BF16)
        out[2 * g * depth : 2 * (g + 1) * depth, :] = dot(blocks, mixed[span, 0:half], (0, 0))


def output_kernel(cells, out):
    out[...] = to_field(cells[...])


def local_grad_kernel(grad, before, after, weights, out, padded, table):
    banded_backward(weights, table)
    pad_cells(padded, grad[...], beside_layers(before[...], after[...]))

    def store(start, result):
        out[start : start + STEP, :] = result

    stencil(padded, table, True, store)


def finish_kernel(received, sums, synthesis, local, grad_out, stencil_out):
    in_slab = sums is None
    if in_slab:
        modes, terms = slab_load(received)
        terms = terms.reshape(TERM_ROWS, LANES)
    else:
        modes, terms = received[...], sums[...].astype(F32)
    cells = (dot(synthesis[...], modes.astype(BF16)) + local[...]).astype(BF16)
    grad_out[...] = to_field(cells)
    half = LANES // 2
    for k in range(OFFSETS):
        row = (k // 2) * half
        lane = (k % 2) * half
        stencil_out[k] = terms[row : row + half, lane : lane + half]


def shape(dims, dtype):
    return jax.ShapeDtypeStruct(dims, dtype)


class Staged:
    def __init__(self, source, buffer, semaphore):
        self.copy = pltpu.make_async_copy(source, buffer, semaphore)
        self.buffer = buffer
        self.copy.start()
        self.ready = False

    def load(self):
        if not self.ready:
            self.copy.wait()
            self.ready = True

    def __getitem__(self, index):
        self.load()
        return self.buffer[index]


class Sent:
    def __init__(self, target, buffer, semaphore):
        self.copy = pltpu.make_async_copy(buffer, target, semaphore)
        self.buffer = buffer

    def __setitem__(self, index, value):
        self.buffer[index] = value
        self.copy.start()

    def __getitem__(self, index):
        return self.buffer[index]

    @property
    def shape(self):
        return self.buffer.shape


def run(
    body, outs, *operands, staged=(), sent=(), moved=(), scratch=(), flops=0, limit=VMEM_BYTES
):
    given = [k for k, operand in enumerate(operands) if operand is not None]
    made = [k for k, out in enumerate(outs) if out is not None]

    def rows_of(chosen, places, arrays):
        chosen = {k: chosen[k] if isinstance(chosen, dict) else None for k in places if k in chosen}
        return {k: rows or arrays[k].shape[0] for k, rows in chosen.items()}

    staged = rows_of(staged, given, operands)
    sent = rows_of(sent, made, outs)

    def kernel(*refs):
        refs = list(refs)

        def take(count):
            taken = refs[:count]
            del refs[:count]
            return taken

        def part(ref, rows):
            return ref if ref.shape[0] == rows else ref.at[0:rows]

        filled = dict(zip(given, take(len(given))))
        kept = dict(zip(made, take(len(made))))
        own = take(len(scratch))
        copies = [
            pltpu.make_async_copy(
                filled.pop(k),
                part(kept.pop(out), operands[k].shape[0]),
                refs[-1].at[len(staged) + len(sent) + place],
            )
            for place, (k, out) in enumerate(dict(moved).items())
        ]
        for place, (k, buffer) in enumerate(zip(staged, take(len(staged)))):
            filled[k] = Staged(part(filled[k], staged[k]), buffer, refs[-1].at[place])
        for place, (k, buffer) in enumerate(zip(sent, take(len(sent)))):
            kept[k] = Sent(part(kept[k], sent[k]), buffer, refs[-1].at[len(staged) + place])
        for copy in copies:
            copy.start()
        body(
            *[filled.get(k) for k in range(len(operands)) if k not in dict(moved)],
            *[kept.get(k) for k in range(len(outs)) if k not in dict(moved).values()],
            *own,
        )
        for k in staged:
            filled[k].load()
        for k in sent:
            kept[k].copy.wait()
        for copy in copies:
            copy.wait()

    arrays = [operands[k] for k in given]
    results = [outs[k] for k in made]
    size = sum(x.size * x.dtype.itemsize for x in (*arrays, *results))
    in_vmem = pl.BlockSpec(memory_space=pltpu.VMEM)
    in_hbm = pl.BlockSpec(memory_space=pltpu.HBM)
    buffers = [(operands[k], rows) for k, rows in staged.items()]
    buffers += [(outs[k], rows) for k, rows in sent.items()]
    buffers = [pltpu.VMEM((rows, *x.shape[1:]), x.dtype) for x, rows in buffers]
    if len(buffers) + len(moved) > 0:
        buffers.append(pltpu.SemaphoreType.DMA((len(buffers) + len(moved),)))
    results = pl.pallas_call(
        kernel,
        out_shape=results,
        in_specs=[in_hbm if k in staged or k in moved else in_vmem for k in given],
        out_specs=[in_hbm if k in sent or k in dict(moved).values() else in_vmem for k in made],
        scratch_shapes=[*scratch, *buffers],
        compiler_params=pltpu.CompilerParams(vmem_limit_bytes=limit),
        cost_estimate=pl.CostEstimate(flops=flops, bytes_accessed=size, transcendentals=0),
        name=body.__name__ if hasattr(body, "__name__") else body.func.__name__,
    )(*arrays)
    results = dict(zip(made, results))
    return [results.get(k) for k in range(len(outs))]


def exchange(values):
    return lax.all_to_all(values, ("batch", "space"), split_axis=0, concat_axis=0, tiled=True)


def neighbours(first, last):
    ends = lax.axis_size("space") - 1
    before = lax.ppermute(last, "space", [(i, i + 1) for i in range(ends)])
    after = lax.ppermute(first, "space", [(i + 1, i) for i in range(ends)])
    return before, after


def shards(snapshots, cotangent, mode_weight, conv_weight):
    batches = lax.axis_size("batch")
    slabs = lax.axis_size("space")
    devices = batches * slabs
    _, channels, layers, plane = snapshots.shape
    modes = mode_weight.shape[0] * mode_weight.shape[1]
    half = LANES // 2
    assert channels == half and layers == 2 and plane == CELLS
    plane_rows = devices * modes
    count = modes * 2 * KZ * batches
    in_slab = modes == 8 and devices * 32 == TERM_ROWS

    analysis, synthesis = plane_tables(batches, slabs)
    gather, scatter, gather_back, scatter_back = depth_tables(slabs, layers, modes)
    weights = mode_weight.reshape(modes * 2 * KZ * channels, channels)
    taps = conv_weight.reshape(OFFSETS, channels, channels)
    field = shape((channels, layers, plane), BF16)
    wide = shape((CELLS, LANES), BF16)
    edge = shape((CELLS // 2, LANES), BF16)
    plane_modes = shape((plane_rows, LANES), BF16)
    padded = pltpu.VMEM((CELLS + 2 * NY, 2 * LANES), BF16)

    def send(values):
        return exchange(values.reshape(devices, modes, LANES)).reshape(plane_rows, LANES)

    cells, coef, first, last, weights = run(
        analyse_kernel,
        [wide, plane_modes, edge, edge, shape((HBM_BYTES // (2 * LANES), channels), BF16)],
        snapshots.reshape(field.shape),
        analysis,
        weights,
        staged=(0, 1),
        sent=(0, 1, 2, 3),
        moved={2: 4},
        limit=WHOLE_VMEM,
        flops=10**8,
    )
    rows = count * channels // batches

    def pack(weights, first):
        weights, first = lax.optimization_barrier((weights, first))
        packed = shape((rows // 2, LANES), BF16)
        return run(pack_kernel, [packed], weights, staged={0: rows})[0], first

    packed_weights, coef = pack(weights, coef)
    coef = send(coef)
    before, after = neighbours(first, last)
    local, lanes, outer_cells = run(
        local_kernel,
        [shape((CELLS, LANES), F32), shape((HBM_BYTES // (2 * CELLS), CELLS), BF16), wide],
        cells,
        before,
        after,
        cotangent.reshape(field.shape),
        taps,
        sent={1: 2 * LANES},
        scratch=[padded, pltpu.VMEM((3, 2 * LANES, 3 * LANES), BF16)],
        flops=7 * 10**8,
    )
    back, diagonal = run(
        functools.partial(mix_kernel, batches),
        [plane_modes, shape((count, GROUP * half // 2), BF16)],
        coef,
        gather,
        packed_weights,
        scatter,
        sent=(0, 1),
        flops=4 * 10**8,
    )
    back = send(back)
    slab = shape((devices, 8 + TERM_ROWS // devices, LANES), BF16)
    activated, grad, first, last, back, terms = run(
        functools.partial(activate_kernel, in_slab),
        [
            wide,
            shape((HBM_BYTES // (2 * LANES), LANES), BF16),
            edge,
            edge,
            slab if in_slab else plane_modes,
            None if in_slab else shape((TERM_ROWS, LANES), BF16),
        ],
        back,
        np.ascontiguousarray(synthesis.T),
        synthesis,
        local,
        outer_cells,
        lanes,
        staged={5: 2 * LANES},
        sent={1: CELLS, 2: None, 3: None, 4: None},
        scratch=[pltpu.VMEM((CELLS + 2 * NY, 3 * LANES), BF16)],
        flops=10**9,
    )
    packed_weights, back = pack(weights, back)
    if in_slab:
        back = exchange(back)
    else:
        back = send(back)
        terms = exchange(terms.reshape(devices, TERM_ROWS // devices, LANES))
    before, after = neighbours(first, last)
    (activated,) = run(
        output_kernel,
        [field],
        activated,
        flops=10**8,
    )
    back, before, after, activated, packed_weights = lax.optimization_barrier(
        (back, before, after, activated, packed_weights)
    )
    scale = 1.0 / math.sqrt(batches * slabs * layers * plane)
    grad_modes, mixed_grad, sums = run(
        functools.partial(unmix_kernel, batches, scale),
        [
            slab if in_slab else plane_modes,
            shape((count, LANES), BF16),
            None if in_slab else shape((TERM_ROWS // devices, LANES), F32),
        ],
        back,
        None if in_slab else terms,
        gather_back,
        packed_weights,
        scatter_back,
        sent=(0,),
        flops=4 * 10**8,
    )
    if in_slab:
        grad_modes = exchange(grad_modes)
    else:
        grad_modes = send(grad_modes)
        sums = lax.all_gather(sums, ("batch", "space"), axis=0, tiled=True)
    (local,) = run(
        local_grad_kernel,
        [shape((CELLS, LANES), F32)],
        grad,
        before,
        after,
        taps,
        staged={0: CELLS},
        scratch=[padded, pltpu.VMEM((3, 3 * LANES, 2 * LANES), BF16)],
        flops=7 * 10**8,
    )
    (mode_gradient,) = run(
        functools.partial(weight_kernel, batches),
        [shape((modes * 2 * KZ * channels, channels), F32)],
        diagonal,
        mixed_grad,
        flops=4 * 10**8,
    )
    input_gradient, conv_gradient = run(
        finish_kernel,
        [field, shape((OFFSETS, channels, channels), F32)],
        grad_modes,
        sums,
        np.ascontiguousarray(analysis.T),
        local,
        flops=10**8,
    )
    return (
        activated.reshape(snapshots.shape),
        input_gradient.reshape(snapshots.shape),
        mode_gradient.reshape(mode_weight.shape),
        conv_gradient.reshape(conv_weight.shape),
    )


def solution(mesh):
    in_specs = (
        P("batch", None, "space", None),
        P("batch", None, "space", None),
        P("batch", "space", None, None, None),
        P(),
    )
    out_specs = (
        P("batch", None, "space", None),
        P("batch", None, "space", None),
        P("batch", "space", None, None, None),
        P(),
    )
    return jax.shard_map(shards, mesh=mesh, in_specs=in_specs, out_specs=out_specs, check_vma=False)
```

```python
import functools
import math

import jax
import jax.numpy as jnp
import ml_dtypes
import numpy as np
from jax import lax
from jax.experimental import pallas as pl
from jax.experimental.pallas import tpu as pltpu
from jax.sharding import PartitionSpec as P

KX = 8
KY = 8
KZ = 12
NX = 32
NY = 32
CELLS = NX * NY
LANES = 128
GROUP = 8
OFFSETS = 27
TERM_ROWS = 1024
VMEM_BYTES = 40 * 1024 * 1024
WHOLE_VMEM = 65000 * 1024
HBM_BYTES = 100 * 1024 * 256

F32 = jnp.float32
BF16 = jnp.bfloat16
inv_root_two = 1.0 / math.sqrt(2.0)
inv_root_two_pi = 1.0 / math.sqrt(2.0 * math.pi)


def basis_rows(half_count, length):
    row = np.arange(2 * half_count)[:, None]
    cell = np.arange(length)[None, :]
    frequency = np.where(row < half_count, row, row - half_count + 1)
    phases = (frequency * cell % length).astype(np.float32) * np.float32(2.0 * math.pi / length)
    return np.where(row < half_count, np.cos(phases), np.sin(phases)).astype(np.float32)


def plane_tables(batches, slabs):
    outer = (basis_rows(KX, NX)[:, None, :, None] * basis_rows(KY, NY)[None, :, None, :]).reshape(
        2 * KX, 2 * KY, CELLS
    )
    outer = outer.reshape(batches, 2 * KX // batches, slabs, 2 * KY // slabs, CELLS)
    outer = outer.transpose(0, 2, 1, 3, 4).reshape(4 * KX * KY, CELLS)
    analysis = (outer * np.float32(2.0 / math.sqrt(CELLS))).astype(ml_dtypes.bfloat16)
    synthesis = (outer * np.float32(2.0 / math.sqrt(4 * KX * KY))).astype(ml_dtypes.bfloat16)
    return analysis, synthesis


def depth_tables(slabs, layers, modes):
    rows = basis_rows(KZ, slabs * layers)
    analysis = (rows * np.float32(math.sqrt(2.0 / (slabs * layers)))).astype(ml_dtypes.bfloat16)
    synthesis = (rows * np.float32(math.sqrt(2.0 / (2 * KZ)))).astype(ml_dtypes.bfloat16)

    def spread(table, order):
        table = table.astype(np.float32).reshape(2 * KZ, slabs, layers)
        full = np.einsum("psz,mn->" + order, table, np.eye(modes, dtype=np.float32))
        return full.astype(ml_dtypes.bfloat16)

    def gathered(table):
        return spread(table, "mpzsn").reshape(modes * 2 * KZ, layers * slabs * modes)

    def scattered(table):
        return spread(table, "snzmp").reshape(slabs * modes, layers * modes * 2 * KZ)

    return gathered(analysis), scattered(synthesis), gathered(synthesis), scattered(analysis)


def dot(left, right, contract=(1, 0)):
    return lax.dot_general(
        left, right, (((contract[0],), (contract[1],)), ((), ())), preferred_element_type=F32
    )


def turn_table():
    row = lax.broadcasted_iota(jnp.int32, (LANES, LANES), 0)
    column = lax.broadcasted_iota(jnp.int32, (LANES, LANES), 1)
    return jnp.where(column == row % 2 * (LANES // 2) + row // 2, 1.0, 0.0).astype(BF16)


def to_cells(field):
    return dot(field.reshape(LANES, CELLS), turn_table(), (0, 0))


def to_field(cells):
    return dot(turn_table(), cells, (1, 1)).astype(BF16).reshape(LANES // 2, 2, CELLS)


def low_lanes(rows):
    return lax.broadcasted_iota(jnp.int32, (rows, LANES), 1) < LANES // 2


def swap_halves(values):
    return pltpu.roll(values, LANES // 2, 1)


def doubled(values):
    low = low_lanes(values.shape[0])
    swapped = swap_halves(values)
    return jnp.concatenate(
        [jnp.where(low, values, swapped), jnp.where(low, swapped, values)], axis=0
    )


def halved(values):
    low = low_lanes(values.shape[0])
    return jnp.concatenate([jnp.where(low, values, 0.0), jnp.where(low, 0.0, values)], axis=0)


def edge_layers(cells_first):
    top = cells_first[: CELLS // 2]
    bottom = cells_first[CELLS // 2 :]
    low = low_lanes(CELLS // 2)
    first = jnp.where(low, top, swap_halves(bottom))
    last = jnp.where(low, swap_halves(top), bottom)
    return first.astype(BF16), last.astype(BF16)


def beside_layers(before, after):
    before = before.astype(F32)
    after = after.astype(F32)
    low = low_lanes(CELLS // 2)
    top = jnp.where(low, before, swap_halves(after))
    bottom = jnp.where(low, swap_halves(before), after)
    return jnp.concatenate([top, bottom], axis=0).astype(BF16)


def y_cells(rows):
    return lax.broadcasted_iota(jnp.int32, (rows, LANES), 0) % NY


def from_below(values):
    return jnp.where(y_cells(values.shape[0]) == 0, 0.0, pltpu.roll(values, 1, 0))


def from_above(values):
    rows = values.shape[0]
    return jnp.where(y_cells(rows) == NY - 1, 0.0, pltpu.roll(values, rows - 1, 0))


def pad_cells(padded, own, beside):
    width = own.shape[1] + beside.shape[1]
    padded[0:NY, :] = jnp.zeros((NY, width), BF16)
    padded[NY + CELLS : 2 * NY + CELLS, :] = jnp.zeros((NY, width), BF16)
    padded[NY : NY + CELLS, 0 : own.shape[1]] = own
    padded[NY : NY + CELLS, own.shape[1] :] = beside


BLOCK_OF_DEPTH = {-1: 2, 0: 0, 1: 1, 2: 3}
STEP = 256


def stencil(padded, table, transposed, store):
    for start in range(0, CELLS, STEP):
        total = None
        for b in range(3):
            cells = padded[start + NY * b : start + NY * b + STEP, :]
            term = dot(cells, table[b], (1, 1) if transposed else (1, 0))
            total = term if total is None else total + term
        result = (
            from_below(total[:, 0:LANES])
            + total[:, LANES : 2 * LANES]
            + from_above(total[:, 2 * LANES :])
        )
        store(start, result)


def banded_forward(weights, table):
    half = LANES // 2
    for b in range(3):
        for c in range(3):
            for depth, block in BLOCK_OF_DEPTH.items():
                parts = []
                for out in range(2):
                    a = depth - out + 1
                    if 0 <= a < 3:
                        parts.append(weights[a * 9 + b * 3 + c])
                    else:
                        parts.append(jnp.zeros((half, half), BF16))
                table[b, block * half : (block + 1) * half, c * LANES : (c + 1) * LANES] = (
                    jnp.concatenate(parts, axis=1)
                )


def banded_backward(weights, table):
    half = LANES // 2
    for b in range(3):
        for c in range(3):
            for out in range(2):
                for pair in ((0, 1), (-1, 2)):
                    parts = []
                    for depth in pair:
                        a = depth - out + 1
                        if 0 <= a < 3:
                            parts.append(weights[(2 - a) * 9 + (2 - b) * 3 + 2 - c])
                        else:
                            parts.append(jnp.zeros((half, half), BF16))
                    row = c * LANES + out * half
                    column = BLOCK_OF_DEPTH[pair[0]] * half
                    table[b, row : row + half, column : column + LANES] = jnp.concatenate(
                        parts, axis=1
                    )


def analyse_kernel(
    field, analysis, weights, cells_out, coef_out, first_out, last_out, packed_out
):
    cells = to_cells(field[...])
    rounded = cells.astype(BF16)
    coef_out[...] = dot(analysis[...], rounded).astype(BF16)
    cells_out[...] = rounded
    first, last = edge_layers(cells)
    first_out[...] = first
    last_out[...] = last
    weights.load()
    rows = GROUP * LANES // 4
    for g in range(packed_out.shape[0] // rows):
        pair = [weights[k * rows : (k + 1) * rows, :] for k in (2 * g, 2 * g + 1)]
        packed_out.buffer[g * rows : (g + 1) * rows, :] = jnp.concatenate(pair, axis=1)
    packed_out.copy.start()


def local_kernel(
    cells, before, after, cotangent, weights, local_out, lanes_out, cotangent_out, padded, table
):
    banded_forward(weights, table)
    beside = beside_layers(before[...], after[...])
    pad_cells(padded, cells[...], beside)

    def store(start, result):
        local_out[start : start + STEP, :] = result

    stencil(padded, table, False, store)
    whole = jnp.concatenate([cells[...].astype(F32), beside.astype(F32)], axis=1)
    lanes_out[...] = whole.T.astype(BF16)
    cotangent_out[...] = to_cells(cotangent[...]).astype(BF16)


def fetch_kernel():
    pass


def mode_in_group(rows, lanes):
    return lax.broadcasted_iota(jnp.int32, (rows, lanes), 0) % GROUP


def own_block(rows):
    width = GROUP * LANES // 4
    lane = lax.broadcasted_iota(jnp.int32, (rows, width), 1)
    return mode_in_group(rows, width) % (GROUP // 2) == lane // (LANES // 2)


def own_half(rows):
    return (mode_in_group(rows, LANES) < GROUP // 2) == low_lanes(rows)


def to_depth(modes, table, snaps):
    rows = modes.shape[0] // snaps
    both = [doubled(modes[b * rows : (b + 1) * rows]) for b in range(snaps)]
    result = dot(table, jnp.concatenate(both, axis=1).astype(BF16))
    return jnp.concatenate(
        [
            result[g : g + GROUP, b * LANES : (b + 1) * LANES]
            for g in range(0, result.shape[0], GROUP)
            for b in range(snaps)
        ],
        axis=0,
    )


def from_depth(modes, table, snaps):
    count = modes.shape[0] // GROUP
    both = []
    for b in range(snaps):
        own = [modes[g * GROUP : (g + 1) * GROUP] for g in range(b, count, snaps)]
        both.append(halved(jnp.concatenate(own, axis=0)))
    result = dot(table, jnp.concatenate(both, axis=1).astype(BF16))
    return jnp.concatenate(
        [result[:, b * LANES : (b + 1) * LANES] for b in range(snaps)], axis=0
    )


def mix_kernel(snaps, received, gather, weights, scatter, back_out, diagonal_out):
    coef = to_depth(received[...].astype(F32), gather[...], snaps)
    count = coef.shape[0]
    wide = jnp.concatenate([coef] * (GROUP // 4), axis=1)
    diagonal = jnp.where(own_block(count), wide, 0.0).astype(BF16)
    diagonal_out[...] = diagonal
    rows = GROUP * snaps
    depth = GROUP * LANES // 4
    mixed = jnp.concatenate(
        [
            dot(diagonal[g * rows : (g + 1) * rows, :], weights[g * depth : (g + 1) * depth, :])
            for g in range(count // rows)
        ],
        axis=0,
    )
    mixed = jnp.where(own_half(count), mixed, swap_halves(mixed))
    back_out[...] = from_depth(mixed, scatter[...], snaps).astype(BF16)


def activate_kernel(
    terms_in_slab,
    received,
    synthesis,
    synthesis_rows,
    local,
    cotangent,
    lanes,
    activated_out,
    grad_out,
    first_out,
    last_out,
    back_out,
    terms_out,
    spread,
):
    pre = dot(synthesis[...], received[...]) + local[...]
    cdf = 0.5 * (1.0 + lax.erf(pre * inv_root_two))
    density = jnp.exp(-0.5 * pre * pre) * inv_root_two_pi
    activated_out[...] = (pre * cdf).astype(BF16)
    grad = (cotangent[...].astype(F32) * (cdf + pre * density)).astype(BF16)
    grad_out[...] = grad
    back = dot(synthesis_rows[...], grad)
    grad = grad.astype(F32)
    first, last = edge_layers(grad)
    first_out[...] = first
    last_out[...] = last
    spread[0:NY, :] = jnp.zeros((NY, 3 * LANES), BF16)
    spread[NY + CELLS : 2 * NY + CELLS, :] = jnp.zeros((NY, 3 * LANES), BF16)
    spread[NY : NY + CELLS, 0:LANES] = from_above(grad).astype(BF16)
    spread[NY : NY + CELLS, LANES : 2 * LANES] = grad.astype(BF16)
    spread[NY : NY + CELLS, 2 * LANES :] = from_below(grad).astype(BF16)
    half = LANES // 2
    low = low_lanes(half)
    twice = {}
    for b in range(3):
        product = dot(lanes[...], spread[NY * (2 - b) : NY * (2 - b) + CELLS, :])
        for c in range(3):
            for a in range(3):
                blocks = [BLOCK_OF_DEPTH[out + a - 1] * half for out in range(2)]
                columns = slice(c * LANES, (c + 1) * LANES)
                both = jnp.where(
                    low,
                    product[blocks[0] : blocks[0] + half, columns],
                    product[blocks[1] : blocks[1] + half, columns],
                )
                twice[a * 9 + b * 3 + c] = both + swap_halves(both)
    pairs = []
    for k in range(0, OFFSETS, 2):
        pairs.append(jnp.where(low, twice[k], twice.get(k + 1, 0.0)))
    pairs.append(jnp.zeros((TERM_ROWS - half * len(pairs), LANES), F32))
    terms = jnp.concatenate(pairs, axis=0)
    if terms_in_slab:
        slab_store(back_out, back, terms)
    else:
        back_out[...] = back.astype(BF16)
        terms_out[...] = terms.astype(BF16)


def slab_store(slab, modes, terms):
    owners = slab.shape[0]
    modes = modes.reshape(owners, 8, LANES)
    terms = terms.reshape(owners, -1, LANES)
    slab[...] = jnp.concatenate([modes, terms], axis=1).astype(BF16)


def slab_load(slab):
    whole = slab[...].astype(F32)
    return whole[:, 0:8, :].reshape(-1, LANES), whole[:, 8:, :]


def unmix_kernel(snaps, scale, received, terms, gather, weights, scatter, grad_out, mixed_out, sums_out):
    in_slab = terms is None
    if in_slab:
        modes, terms = slab_load(received)
    else:
        modes, terms = received[...].astype(F32), terms[...].astype(F32)
    mixed = to_depth(modes, gather[...], snaps)
    mixed_out[...] = mixed.astype(BF16)
    count = mixed.shape[0]
    rows = GROUP * snaps
    depth = GROUP * LANES // 4
    sums = jnp.sum(terms, axis=0) * scale
    own = own_block(rows)
    placed = jnp.where(own_half(count), mixed, 0.0).astype(BF16)
    pieces = []
    for g in range(count // rows):
        full = dot(
            placed[g * rows : (g + 1) * rows, :], weights[g * depth : (g + 1) * depth, :], (1, 1)
        )
        full = jnp.where(own, full, 0.0)
        pieces.append(sum(full[:, k : k + LANES] for k in range(0, depth, LANES)))
    coef = jnp.concatenate(pieces, axis=0)
    coef = coef + swap_halves(coef)
    grad = from_depth(coef, scatter[...], snaps)
    if in_slab:
        owners = received.shape[0]
        share = sums.shape[0]
        slab_store(
            grad_out, grad, jnp.broadcast_to(sums[None], (owners, share, LANES)).reshape(-1, LANES)
        )
    else:
        grad_out[...] = grad.astype(BF16)
        sums_out[...] = sums


def weight_kernel(snaps, diagonal, mixed, out):
    rows = GROUP * snaps
    depth = GROUP * LANES // 4
    half = LANES // 2
    first = mode_in_group(rows, depth) < GROUP // 2
    for g in range(diagonal.shape[0] // rows):
        span = slice(g * rows, (g + 1) * rows)
        blocks = diagonal[span, :].astype(F32)
        blocks = [jnp.where(first, blocks, 0.0), jnp.where(first, 0.0, blocks)]
        blocks = jnp.concatenate(blocks, axis=1).astype(BF16)
        out[2 * g * depth : 2 * (g + 1) * depth, :] = dot(blocks, mixed[span, 0:half], (0, 0))


def output_kernel(cells, out):
    out[...] = to_field(cells[...])


def local_grad_kernel(grad, before, after, weights, out, padded, table):
    banded_backward(weights, table)
    pad_cells(padded, grad[...], beside_layers(before[...], after[...]))

    def store(start, result):
        out[start : start + STEP, :] = result

    stencil(padded, table, True, store)


def finish_kernel(received, sums, synthesis, local, grad_out, stencil_out):
    in_slab = sums is None
    if in_slab:
        modes, terms = slab_load(received)
        terms = terms.reshape(TERM_ROWS, LANES)
    else:
        modes, terms = received[...], sums[...].astype(F32)
    cells = (dot(synthesis[...], modes.astype(BF16)) + local[...]).astype(BF16)
    grad_out[...] = to_field(cells)
    half = LANES // 2
    for k in range(OFFSETS):
        row = (k // 2) * half
        lane = (k % 2) * half
        stencil_out[k] = terms[row : row + half, lane : lane + half]


def shape(dims, dtype):
    return jax.ShapeDtypeStruct(dims, dtype)


class Staged:
    def __init__(self, source, buffer, semaphore):
        self.copy = pltpu.make_async_copy(source, buffer, semaphore)
        self.buffer = buffer
        self.copy.start()
        self.ready = False

    def load(self):
        if not self.ready:
            self.copy.wait()
            self.ready = True

    def __getitem__(self, index):
        self.load()
        return self.buffer[index]


class Sent:
    def __init__(self, target, buffer, semaphore):
        self.copy = pltpu.make_async_copy(buffer, target, semaphore)
        self.buffer = buffer

    def __setitem__(self, index, value):
        self.buffer[index] = value
        self.copy.start()

    def __getitem__(self, index):
        return self.buffer[index]

    @property
    def shape(self):
        return self.buffer.shape


def run(
    body, outs, *operands, staged=(), sent=(), moved=(), scratch=(), flops=0, limit=VMEM_BYTES
):
    given = [k for k, operand in enumerate(operands) if operand is not None]
    made = [k for k, out in enumerate(outs) if out is not None]

    def rows_of(chosen, places, arrays):
        chosen = {k: chosen[k] if isinstance(chosen, dict) else None for k in places if k in chosen}
        return {k: rows or arrays[k].shape[0] for k, rows in chosen.items()}

    moved = dict(moved)
    staged = rows_of(staged, given, operands)
    sent = rows_of(sent, made, outs)

    def kernel(*refs):
        refs = list(refs)

        def take(count):
            taken = refs[:count]
            del refs[:count]
            return taken

        def part(ref, rows):
            return ref if ref.shape[0] == rows else ref.at[0:rows]

        filled = dict(zip(given, take(len(given))))
        kept = dict(zip(made, take(len(made))))
        own = take(len(scratch))
        copies = []
        for place, (k, out) in enumerate(moved.items()):
            source, target = filled.pop(k), kept.pop(out)
            rows = min(source.shape[0], target.shape[0])
            semaphore = refs[-1].at[len(staged) + len(sent) + place]
            copies.append(
                pltpu.make_async_copy(part(source, rows), part(target, rows), semaphore)
            )
        for place, (k, buffer) in enumerate(zip(staged, take(len(staged)))):
            filled[k] = Staged(part(filled[k], staged[k]), buffer, refs[-1].at[place])
        for place, (k, buffer) in enumerate(zip(sent, take(len(sent)))):
            kept[k] = Sent(part(kept[k], sent[k]), buffer, refs[-1].at[len(staged) + place])
        for copy in copies:
            copy.start()
        body(
            *[filled.get(k) for k in range(len(operands)) if k not in moved],
            *[kept.get(k) for k in range(len(outs)) if k not in moved.values()],
            *own,
        )
        for k in staged:
            filled[k].load()
        for k in sent:
            kept[k].copy.wait()
        for copy in copies:
            copy.wait()

    arrays = [operands[k] for k in given]
    results = [outs[k] for k in made]
    size = sum(x.size * x.dtype.itemsize for x in (*arrays, *results))
    in_vmem = pl.BlockSpec(memory_space=pltpu.VMEM)
    in_hbm = pl.BlockSpec(memory_space=pltpu.HBM)
    buffers = [(operands[k], rows) for k, rows in staged.items()]
    buffers += [(outs[k], rows) for k, rows in sent.items()]
    buffers = [pltpu.VMEM((rows, *x.shape[1:]), x.dtype) for x, rows in buffers]
    if len(buffers) + len(moved) > 0:
        buffers.append(pltpu.SemaphoreType.DMA((len(buffers) + len(moved),)))
    results = pl.pallas_call(
        kernel,
        out_shape=results,
        in_specs=[in_hbm if k in staged or k in moved else in_vmem for k in given],
        out_specs=[in_hbm if k in sent else in_vmem for k in made],
        scratch_shapes=[*scratch, *buffers],
        compiler_params=pltpu.CompilerParams(vmem_limit_bytes=limit),
        cost_estimate=pl.CostEstimate(flops=flops, bytes_accessed=size, transcendentals=0),
        name=body.__name__ if hasattr(body, "__name__") else body.func.__name__,
    )(*arrays)
    results = dict(zip(made, results))
    return [results.get(k) for k in range(len(outs))]


def exchange(values):
    return lax.all_to_all(values, ("batch", "space"), split_axis=0, concat_axis=0, tiled=True)


def neighbours(first, last):
    ends = lax.axis_size("space") - 1
    before = lax.ppermute(last, "space", [(i, i + 1) for i in range(ends)])
    after = lax.ppermute(first, "space", [(i + 1, i) for i in range(ends)])
    return before, after


def shards(snapshots, cotangent, mode_weight, conv_weight):
    batches = lax.axis_size("batch")
    slabs = lax.axis_size("space")
    devices = batches * slabs
    _, channels, layers, plane = snapshots.shape
    modes = mode_weight.shape[0] * mode_weight.shape[1]
    half = LANES // 2
    assert channels == half and layers == 2 and plane == CELLS
    plane_rows = devices * modes
    count = modes * 2 * KZ * batches
    in_slab = modes == 8 and devices * 32 == TERM_ROWS

    analysis, synthesis = plane_tables(batches, slabs)
    gather, scatter, gather_back, scatter_back = depth_tables(slabs, layers, modes)
    weights = mode_weight.reshape(modes * 2 * KZ * channels, channels)
    taps = conv_weight.reshape(OFFSETS, channels, channels)
    field = shape((channels, layers, plane), BF16)
    wide = shape((CELLS, LANES), BF16)
    edge = shape((CELLS // 2, LANES), BF16)
    plane_modes = shape((plane_rows, LANES), BF16)
    padded = pltpu.VMEM((CELLS + 2 * NY, 2 * LANES), BF16)

    def send(values):
        return exchange(values.reshape(devices, modes, LANES)).reshape(plane_rows, LANES)

    packed = shape((weights.shape[0] // 2, LANES), BF16)
    cells, coef, first, last, kept_weights = run(
        analyse_kernel,
        [wide, plane_modes, edge, edge, shape((HBM_BYTES // (2 * LANES), LANES), BF16)],
        snapshots.reshape(field.shape),
        analysis,
        weights,
        staged=(0, 1, 2),
        sent={0: None, 1: None, 2: None, 3: None, 4: packed.shape[0]},
        limit=WHOLE_VMEM,
        flops=10**8,
    )
    coef = send(coef)
    (packed_weights,) = run(fetch_kernel, [packed], kept_weights, moved={0: 0})
    before, after = neighbours(first, last)
    local, lanes, outer_cells = run(
        local_kernel,
        [shape((CELLS, LANES), F32), shape((HBM_BYTES // (2 * CELLS), CELLS), BF16), wide],
        cells,
        before,
        after,
        cotangent.reshape(field.shape),
        taps,
        sent={1: 2 * LANES},
        scratch=[padded, pltpu.VMEM((3, 2 * LANES, 3 * LANES), BF16)],
        flops=7 * 10**8,
    )
    back, diagonal = run(
        functools.partial(mix_kernel, batches),
        [plane_modes, shape((count, GROUP * half // 2), BF16)],
        coef,
        gather,
        packed_weights,
        scatter,
        sent=(0, 1),
        flops=4 * 10**8,
    )
    back = send(back)
    slab = shape((devices, 8 + TERM_ROWS // devices, LANES), BF16)
    activated, grad, first, last, back, terms = run(
        functools.partial(activate_kernel, in_slab),
        [
            wide,
            shape((HBM_BYTES // (2 * LANES), LANES), BF16),
            edge,
            edge,
            slab if in_slab else plane_modes,
            None if in_slab else shape((TERM_ROWS, LANES), BF16),
        ],
        back,
        np.ascontiguousarray(synthesis.T),
        synthesis,
        local,
        outer_cells,
        lanes,
        staged={5: 2 * LANES},
        sent={1: CELLS, 2: None, 3: None, 4: None},
        scratch=[pltpu.VMEM((CELLS + 2 * NY, 3 * LANES), BF16)],
        flops=10**9,
    )
    if in_slab:
        back = exchange(back)
    else:
        back = send(back)
        terms = exchange(terms.reshape(devices, TERM_ROWS // devices, LANES))
    before, after = neighbours(first, last)
    activated, packed_weights = run(
        output_kernel,
        [field, packed],
        activated,
        kept_weights,
        moved={1: 1},
        flops=10**8,
    )
    back, before, after, activated, packed_weights = lax.optimization_barrier(
        (back, before, after, activated, packed_weights)
    )
    scale = 1.0 / math.sqrt(batches * slabs * layers * plane)
    grad_modes, mixed_grad, sums = run(
        functools.partial(unmix_kernel, batches, scale),
        [
            slab if in_slab else plane_modes,
            shape((count, LANES), BF16),
            None if in_slab else shape((TERM_ROWS // devices, LANES), F32),
        ],
        back,
        None if in_slab else terms,
        gather_back,
        packed_weights,
        scatter_back,
        sent=(0,),
        flops=4 * 10**8,
    )
    if in_slab:
        grad_modes = exchange(grad_modes)
    else:
        grad_modes = send(grad_modes)
        sums = lax.all_gather(sums, ("batch", "space"), axis=0, tiled=True)
    (local,) = run(
        local_grad_kernel,
        [shape((CELLS, LANES), F32)],
        grad,
        before,
        after,
        taps,
        staged={0: CELLS},
        scratch=[padded, pltpu.VMEM((3, 3 * LANES, 2 * LANES), BF16)],
        flops=7 * 10**8,
    )
    (mode_gradient,) = run(
        functools.partial(weight_kernel, batches),
        [shape((modes * 2 * KZ * channels, channels), F32)],
        diagonal,
        mixed_grad,
        flops=4 * 10**8,
    )
    input_gradient, conv_gradient = run(
        finish_kernel,
        [field, shape((OFFSETS, channels, channels), F32)],
        grad_modes,
        sums,
        np.ascontiguousarray(analysis.T),
        local,
        flops=10**8,
    )
    return (
        activated.reshape(snapshots.shape),
        input_gradient.reshape(snapshots.shape),
        mode_gradient.reshape(mode_weight.shape),
        conv_gradient.reshape(conv_weight.shape),
    )


def solution(mesh):
    in_specs = (
        P("batch", None, "space", None),
        P("batch", None, "space", None),
        P("batch", "space", None, None, None),
        P(),
    )
    out_specs = (
        P("batch", None, "space", None),
        P("batch", None, "space", None),
        P("batch", "space", None, None, None),
        P(),
    )
    return jax.shard_map(shards, mesh=mesh, in_specs=in_specs, out_specs=out_specs, check_vma=False)
```

```python
import functools
import math

import jax
import jax.numpy as jnp
import ml_dtypes
import numpy as np
from jax import lax
from jax.experimental import pallas as pl
from jax.experimental.pallas import tpu as pltpu
from jax.sharding import PartitionSpec as P

KX = 8
KY = 8
KZ = 12
NX = 32
NY = 32
CELLS = NX * NY
LANES = 128
GROUP = 8
OFFSETS = 27
TERM_ROWS = 1024
CHUNKS = 3
VMEM_BYTES = 40 * 1024 * 1024
WHOLE_VMEM = 65000 * 1024
HBM_BYTES = 100 * 1024 * 256

F32 = jnp.float32
BF16 = jnp.bfloat16
inv_root_two = 1.0 / math.sqrt(2.0)
inv_root_two_pi = 1.0 / math.sqrt(2.0 * math.pi)


def basis_rows(half_count, length):
    row = np.arange(2 * half_count)[:, None]
    cell = np.arange(length)[None, :]
    frequency = np.where(row < half_count, row, row - half_count + 1)
    phases = (frequency * cell % length).astype(np.float32) * np.float32(2.0 * math.pi / length)
    return np.where(row < half_count, np.cos(phases), np.sin(phases)).astype(np.float32)


def plane_tables(batches, slabs):
    outer = (basis_rows(KX, NX)[:, None, :, None] * basis_rows(KY, NY)[None, :, None, :]).reshape(
        2 * KX, 2 * KY, CELLS
    )
    outer = outer.reshape(batches, 2 * KX // batches, slabs, 2 * KY // slabs, CELLS)
    outer = outer.transpose(0, 2, 1, 3, 4).reshape(4 * KX * KY, CELLS)
    analysis = (outer * np.float32(2.0 / math.sqrt(CELLS))).astype(ml_dtypes.bfloat16)
    synthesis = (outer * np.float32(2.0 / math.sqrt(4 * KX * KY))).astype(ml_dtypes.bfloat16)
    return analysis, synthesis


def depth_tables(slabs, layers, modes):
    rows = basis_rows(KZ, slabs * layers)
    analysis = (rows * np.float32(math.sqrt(2.0 / (slabs * layers)))).astype(ml_dtypes.bfloat16)
    synthesis = (rows * np.float32(math.sqrt(2.0 / (2 * KZ)))).astype(ml_dtypes.bfloat16)

    def spread(table, order):
        table = table.astype(np.float32).reshape(2 * KZ, slabs, layers)
        full = np.einsum("psz,mn->" + order, table, np.eye(modes, dtype=np.float32))
        return full.astype(ml_dtypes.bfloat16)

    def gathered(table):
        return spread(table, "mpzsn").reshape(modes * 2 * KZ, layers * slabs * modes)

    def scattered(table):
        return spread(table, "snzmp").reshape(slabs * modes, layers * modes * 2 * KZ)

    return gathered(analysis), scattered(synthesis), gathered(synthesis), scattered(analysis)


def dot(left, right, contract=(1, 0)):
    return lax.dot_general(
        left, right, (((contract[0],), (contract[1],)), ((), ())), preferred_element_type=F32
    )


def turn_table():
    row = lax.broadcasted_iota(jnp.int32, (LANES, LANES), 0)
    column = lax.broadcasted_iota(jnp.int32, (LANES, LANES), 1)
    return jnp.where(column == row % 2 * (LANES // 2) + row // 2, 1.0, 0.0).astype(BF16)


def to_cells(field):
    return dot(field.reshape(LANES, CELLS), turn_table(), (0, 0))


def to_field(cells):
    return dot(turn_table(), cells, (1, 1)).astype(BF16).reshape(LANES // 2, 2, CELLS)


def low_lanes(rows):
    return lax.broadcasted_iota(jnp.int32, (rows, LANES), 1) < LANES // 2


def swap_halves(values):
    return pltpu.roll(values, LANES // 2, 1)


def doubled(values):
    low = low_lanes(values.shape[0])
    swapped = swap_halves(values)
    return jnp.concatenate(
        [jnp.where(low, values, swapped), jnp.where(low, swapped, values)], axis=0
    )


def halved(values):
    low = low_lanes(values.shape[0])
    return jnp.concatenate([jnp.where(low, values, 0.0), jnp.where(low, 0.0, values)], axis=0)


def edge_layers(cells_first):
    top = cells_first[: CELLS // 2]
    bottom = cells_first[CELLS // 2 :]
    low = low_lanes(CELLS // 2)
    first = jnp.where(low, top, swap_halves(bottom))
    last = jnp.where(low, swap_halves(top), bottom)
    return first.astype(BF16), last.astype(BF16)


def beside_layers(before, after):
    before = before.astype(F32)
    after = after.astype(F32)
    low = low_lanes(CELLS // 2)
    top = jnp.where(low, before, swap_halves(after))
    bottom = jnp.where(low, swap_halves(before), after)
    return jnp.concatenate([top, bottom], axis=0).astype(BF16)


def y_cells(rows):
    return lax.broadcasted_iota(jnp.int32, (rows, LANES), 0) % NY


def from_below(values):
    return jnp.where(y_cells(values.shape[0]) == 0, 0.0, pltpu.roll(values, 1, 0))


def from_above(values):
    rows = values.shape[0]
    return jnp.where(y_cells(rows) == NY - 1, 0.0, pltpu.roll(values, rows - 1, 0))


def pad_cells(padded, own, beside):
    width = own.shape[1] + beside.shape[1]
    padded[0:NY, :] = jnp.zeros((NY, width), BF16)
    padded[NY + CELLS : 2 * NY + CELLS, :] = jnp.zeros((NY, width), BF16)
    padded[NY : NY + CELLS, 0 : own.shape[1]] = own
    padded[NY : NY + CELLS, own.shape[1] :] = beside


BLOCK_OF_DEPTH = {-1: 2, 0: 0, 1: 1, 2: 3}
STEP = 256


def stencil(padded, table, transposed, store):
    for start in range(0, CELLS, STEP):
        total = None
        for b in range(3):
            cells = padded[start + NY * b : start + NY * b + STEP, :]
            term = dot(cells, table[b], (1, 1) if transposed else (1, 0))
            total = term if total is None else total + term
        result = (
            from_below(total[:, 0:LANES])
            + total[:, LANES : 2 * LANES]
            + from_above(total[:, 2 * LANES :])
        )
        store(start, result)


def banded_forward(weights, table):
    half = LANES // 2
    for b in range(3):
        for c in range(3):
            for depth, block in BLOCK_OF_DEPTH.items():
                parts = []
                for out in range(2):
                    a = depth - out + 1
                    if 0 <= a < 3:
                        parts.append(weights[a * 9 + b * 3 + c])
                    else:
                        parts.append(jnp.zeros((half, half), BF16))
                table[b, block * half : (block + 1) * half, c * LANES : (c + 1) * LANES] = (
                    jnp.concatenate(parts, axis=1)
                )


def banded_backward(weights, table):
    half = LANES // 2
    for b in range(3):
        for c in range(3):
            for out in range(2):
                for pair in ((0, 1), (-1, 2)):
                    parts = []
                    for depth in pair:
                        a = depth - out + 1
                        if 0 <= a < 3:
                            parts.append(weights[(2 - a) * 9 + (2 - b) * 3 + 2 - c])
                        else:
                            parts.append(jnp.zeros((half, half), BF16))
                    row = c * LANES + out * half
                    column = BLOCK_OF_DEPTH[pair[0]] * half
                    table[b, row : row + half, column : column + LANES] = jnp.concatenate(
                        parts, axis=1
                    )


def analyse_kernel(field, analysis, *refs):
    weights = refs[:CHUNKS]
    cells_out, coef_out, first_out, last_out, packed_out, buffer, semaphores = refs[CHUNKS:]
    cells = to_cells(field[...])
    rounded = cells.astype(BF16)
    coef_out[...] = dot(analysis[...], rounded).astype(BF16)
    cells_out[...] = rounded
    first, last = edge_layers(cells)
    first_out[...] = first
    last_out[...] = last
    rows = GROUP * LANES // 4
    share = buffer.shape[0] // CHUNKS
    copies = []
    for place, part in enumerate(weights):
        for g in range(share // rows):
            pair = [part[k * rows : (k + 1) * rows, :] for k in (2 * g, 2 * g + 1)]
            row = place * share + g * rows
            buffer[row : row + rows, :] = jnp.concatenate(pair, axis=1)
        span = slice(place * share, (place + 1) * share)
        copies.append(
            pltpu.make_async_copy(buffer.at[span], packed_out.at[span], semaphores.at[place])
        )
        copies[-1].start()
    for copy in copies:
        copy.wait()


def local_kernel(
    cells, before, after, cotangent, weights, local_out, lanes_out, cotangent_out, padded, table
):
    banded_forward(weights, table)
    beside = beside_layers(before[...], after[...])
    pad_cells(padded, cells[...], beside)

    def store(start, result):
        local_out[start : start + STEP, :] = result

    stencil(padded, table, False, store)
    whole = jnp.concatenate([cells[...].astype(F32), beside.astype(F32)], axis=1)
    lanes_out[...] = whole.T.astype(BF16)
    cotangent_out[...] = to_cells(cotangent[...]).astype(BF16)


def fetch_kernel():
    pass


def mode_in_group(rows, lanes):
    return lax.broadcasted_iota(jnp.int32, (rows, lanes), 0) % GROUP


def own_block(rows):
    width = GROUP * LANES // 4
    lane = lax.broadcasted_iota(jnp.int32, (rows, width), 1)
    return mode_in_group(rows, width) % (GROUP // 2) == lane // (LANES // 2)


def own_half(rows):
    return (mode_in_group(rows, LANES) < GROUP // 2) == low_lanes(rows)


def to_depth(modes, table, snaps):
    rows = modes.shape[0] // snaps
    both = [doubled(modes[b * rows : (b + 1) * rows]) for b in range(snaps)]
    result = dot(table, jnp.concatenate(both, axis=1).astype(BF16))
    return jnp.concatenate(
        [
            result[g : g + GROUP, b * LANES : (b + 1) * LANES]
            for g in range(0, result.shape[0], GROUP)
            for b in range(snaps)
        ],
        axis=0,
    )


def from_depth(modes, table, snaps):
    count = modes.shape[0] // GROUP
    both = []
    for b in range(snaps):
        own = [modes[g * GROUP : (g + 1) * GROUP] for g in range(b, count, snaps)]
        both.append(halved(jnp.concatenate(own, axis=0)))
    result = dot(table, jnp.concatenate(both, axis=1).astype(BF16))
    return jnp.concatenate(
        [result[:, b * LANES : (b + 1) * LANES] for b in range(snaps)], axis=0
    )


def mix_kernel(snaps, received, gather, weights, scatter, back_out, diagonal_out):
    coef = to_depth(received[...].astype(F32), gather[...], snaps)
    count = coef.shape[0]
    wide = jnp.concatenate([coef] * (GROUP // 4), axis=1)
    diagonal = jnp.where(own_block(count), wide, 0.0).astype(BF16)
    diagonal_out[...] = diagonal
    rows = GROUP * snaps
    depth = GROUP * LANES // 4
    mixed = jnp.concatenate(
        [
            dot(diagonal[g * rows : (g + 1) * rows, :], weights[g * depth : (g + 1) * depth, :])
            for g in range(count // rows)
        ],
        axis=0,
    )
    mixed = jnp.where(own_half(count), mixed, swap_halves(mixed))
    back = from_depth(mixed, scatter[...], snaps).astype(BF16)
    back_out[...] = back.reshape(back_out.shape)


def activate_kernel(
    terms_in_slab,
    received,
    synthesis,
    synthesis_rows,
    local,
    cotangent,
    lanes,
    activated_out,
    grad_out,
    first_out,
    last_out,
    back_out,
    terms_out,
    spread,
):
    pre = dot(synthesis[...], received[...]) + local[...]
    cdf = 0.5 * (1.0 + lax.erf(pre * inv_root_two))
    density = jnp.exp(-0.5 * pre * pre) * inv_root_two_pi
    activated_out[...] = (pre * cdf).astype(BF16)
    grad = (cotangent[...].astype(F32) * (cdf + pre * density)).astype(BF16)
    grad_out[...] = grad
    back = dot(synthesis_rows[...], grad)
    grad = grad.astype(F32)
    first, last = edge_layers(grad)
    first_out[...] = first
    last_out[...] = last
    spread[0:NY, :] = jnp.zeros((NY, 3 * LANES), BF16)
    spread[NY + CELLS : 2 * NY + CELLS, :] = jnp.zeros((NY, 3 * LANES), BF16)
    spread[NY : NY + CELLS, 0:LANES] = from_above(grad).astype(BF16)
    spread[NY : NY + CELLS, LANES : 2 * LANES] = grad.astype(BF16)
    spread[NY : NY + CELLS, 2 * LANES :] = from_below(grad).astype(BF16)
    half = LANES // 2
    low = low_lanes(half)
    twice = {}
    for b in range(3):
        product = dot(lanes[...], spread[NY * (2 - b) : NY * (2 - b) + CELLS, :])
        for c in range(3):
            for a in range(3):
                blocks = [BLOCK_OF_DEPTH[out + a - 1] * half for out in range(2)]
                columns = slice(c * LANES, (c + 1) * LANES)
                both = jnp.where(
                    low,
                    product[blocks[0] : blocks[0] + half, columns],
                    product[blocks[1] : blocks[1] + half, columns],
                )
                twice[a * 9 + b * 3 + c] = both + swap_halves(both)
    pairs = []
    for k in range(0, OFFSETS, 2):
        pairs.append(jnp.where(low, twice[k], twice.get(k + 1, 0.0)))
    pairs.append(jnp.zeros((TERM_ROWS - half * len(pairs), LANES), F32))
    terms = jnp.concatenate(pairs, axis=0)
    if terms_in_slab:
        slab_store(back_out, back, terms)
    else:
        back_out[...] = back.astype(BF16)
        terms_out[...] = terms.astype(BF16)


def slab_store(slab, modes, terms):
    owners = slab.shape[0]
    modes = modes.reshape(owners, 8, LANES)
    terms = terms.reshape(owners, -1, LANES)
    slab[...] = jnp.concatenate([modes, terms], axis=1).astype(BF16)


def slab_load(slab):
    whole = slab[...].astype(F32)
    return whole[:, 0:8, :].reshape(-1, LANES), whole[:, 8:, :]


def unmix_kernel(snaps, scale, received, terms, gather, weights, scatter, grad_out, mixed_out, sums_out):
    in_slab = terms is None
    if in_slab:
        modes, terms = slab_load(received)
    else:
        modes, terms = received[...].astype(F32), terms[...].astype(F32)
    mixed = to_depth(modes, gather[...], snaps)
    mixed_out[...] = mixed.astype(BF16)
    count = mixed.shape[0]
    rows = GROUP * snaps
    depth = GROUP * LANES // 4
    sums = jnp.sum(terms, axis=0) * scale
    own = own_block(rows)
    placed = jnp.where(own_half(count), mixed, 0.0).astype(BF16)
    pieces = []
    for g in range(count // rows):
        full = dot(
            placed[g * rows : (g + 1) * rows, :], weights[g * depth : (g + 1) * depth, :], (1, 1)
        )
        full = jnp.where(own, full, 0.0)
        pieces.append(sum(full[:, k : k + LANES] for k in range(0, depth, LANES)))
    coef = jnp.concatenate(pieces, axis=0)
    coef = coef + swap_halves(coef)
    grad = from_depth(coef, scatter[...], snaps)
    if in_slab:
        owners = received.shape[0]
        share = sums.shape[0]
        slab_store(
            grad_out, grad, jnp.broadcast_to(sums[None], (owners, share, LANES)).reshape(-1, LANES)
        )
    else:
        grad_out[...] = grad.astype(BF16)
        sums_out[...] = sums


def weight_kernel(snaps, diagonal, mixed, out):
    rows = GROUP * snaps
    depth = GROUP * LANES // 4
    half = LANES // 2
    first = mode_in_group(rows, depth) < GROUP // 2
    for g in range(diagonal.shape[0] // rows):
        span = slice(g * rows, (g + 1) * rows)
        blocks = diagonal[span, :].astype(F32)
        blocks = [jnp.where(first, blocks, 0.0), jnp.where(first, 0.0, blocks)]
        blocks = jnp.concatenate(blocks, axis=1).astype(BF16)
        out[2 * g * depth : 2 * (g + 1) * depth, :] = dot(blocks, mixed[span, 0:half], (0, 0))


def output_kernel(cells, out):
    out[...] = to_field(cells[...])


def local_grad_kernel(grad, before, after, weights, out, padded, table):
    banded_backward(weights, table)
    pad_cells(padded, grad[...], beside_layers(before[...], after[...]))

    def store(start, result):
        out[start : start + STEP, :] = result

    stencil(padded, table, True, store)


def finish_kernel(received, sums, synthesis, local, grad_out, stencil_out):
    in_slab = sums is None
    if in_slab:
        modes, terms = slab_load(received)
        terms = terms.reshape(TERM_ROWS, LANES)
    else:
        modes, terms = received[...], sums[...].astype(F32)
    half = LANES // 2
    blocks = []
    for k in range(OFFSETS):
        row = (k // 2) * half
        lane = (k % 2) * half
        blocks.append(terms[row : row + half, lane : lane + half])
    stencil_out[...] = jnp.stack(blocks, axis=0)
    cells = (dot(synthesis[...], modes.astype(BF16)) + local[...]).astype(BF16)
    grad_out[...] = to_field(cells)


def shape(dims, dtype):
    return jax.ShapeDtypeStruct(dims, dtype)


class Staged:
    def __init__(self, source, buffer, semaphore):
        self.copy = pltpu.make_async_copy(source, buffer, semaphore)
        self.buffer = buffer
        self.copy.start()
        self.ready = False

    def load(self):
        if not self.ready:
            self.copy.wait()
            self.ready = True

    def __getitem__(self, index):
        self.load()
        return self.buffer[index]


class Sent:
    def __init__(self, target, buffer, semaphore):
        self.copy = pltpu.make_async_copy(buffer, target, semaphore)
        self.buffer = buffer

    def __setitem__(self, index, value):
        self.buffer[index] = value
        self.copy.start()

    def __getitem__(self, index):
        return self.buffer[index]

    @property
    def shape(self):
        return self.buffer.shape


def row_count(rows):
    return rows.stop - rows.start if isinstance(rows, slice) else rows


def run(
    body, outs, *operands, staged=(), sent=(), moved=(), plain=(), scratch=(), flops=0, limit=VMEM_BYTES
):
    given = [k for k, operand in enumerate(operands) if operand is not None]
    made = [k for k, out in enumerate(outs) if out is not None]

    def rows_of(chosen, places, arrays):
        chosen = {k: chosen[k] if isinstance(chosen, dict) else None for k in places if k in chosen}
        return {k: rows or arrays[k].shape[0] for k, rows in chosen.items()}

    moved = dict(moved)
    staged = rows_of(staged, given, operands)
    sent = rows_of(sent, made, outs)

    def kernel(*refs):
        refs = list(refs)

        def take(count):
            taken = refs[:count]
            del refs[:count]
            return taken

        def part(ref, rows):
            if isinstance(rows, slice):
                return ref.at[rows]
            return ref if ref.shape[0] == rows else ref.at[0:rows]

        filled = dict(zip(given, take(len(given))))
        kept = dict(zip(made, take(len(made))))
        own = take(len(scratch))
        copies = []
        for place, (k, out) in enumerate(moved.items()):
            source, target = filled.pop(k), kept.pop(out)
            rows = min(source.shape[0], target.shape[0])
            semaphore = refs[-1].at[len(staged) + len(sent) + place]
            copies.append(
                pltpu.make_async_copy(part(source, rows), part(target, rows), semaphore)
            )
        for place, (k, buffer) in enumerate(zip(staged, take(len(staged)))):
            filled[k] = Staged(part(filled[k], staged[k]), buffer, refs[-1].at[place])
        for place, (k, buffer) in enumerate(zip(sent, take(len(sent)))):
            kept[k] = Sent(part(kept[k], sent[k]), buffer, refs[-1].at[len(staged) + place])
        for copy in copies:
            copy.start()
        body(
            *[filled.get(k) for k in range(len(operands)) if k not in moved],
            *[kept.get(k) for k in range(len(outs)) if k not in moved.values()],
            *own,
        )
        for k in staged:
            filled[k].load()
        for k in sent:
            kept[k].copy.wait()
        for copy in copies:
            copy.wait()

    arrays = [operands[k] for k in given]
    results = [outs[k] for k in made]
    size = sum(x.size * x.dtype.itemsize for x in (*arrays, *results))
    in_vmem = pl.BlockSpec(memory_space=pltpu.VMEM)
    in_hbm = pl.BlockSpec(memory_space=pltpu.HBM)
    buffers = [(operands[k], rows) for k, rows in staged.items()]
    buffers += [(outs[k], rows) for k, rows in sent.items()]
    buffers = [pltpu.VMEM((row_count(rows), *x.shape[1:]), x.dtype) for x, rows in buffers]
    if len(buffers) + len(moved) > 0:
        buffers.append(pltpu.SemaphoreType.DMA((len(buffers) + len(moved),)))
    results = pl.pallas_call(
        kernel,
        out_shape=results,
        in_specs=[in_hbm if k in staged or k in moved else in_vmem for k in given],
        out_specs=[in_hbm if k in sent or k in plain else in_vmem for k in made],
        scratch_shapes=[*scratch, *buffers],
        compiler_params=pltpu.CompilerParams(vmem_limit_bytes=limit),
        cost_estimate=pl.CostEstimate(flops=flops, bytes_accessed=size, transcendentals=0),
        name=body.__name__ if hasattr(body, "__name__") else body.func.__name__,
    )(*arrays)
    results = dict(zip(made, results))
    return [results.get(k) for k in range(len(outs))]


def exchange(values):
    return lax.all_to_all(values, ("batch", "space"), split_axis=0, concat_axis=0, tiled=True)


def neighbours(first, last):
    ends = lax.axis_size("space") - 1
    before = lax.ppermute(last, "space", [(i, i + 1) for i in range(ends)])
    after = lax.ppermute(first, "space", [(i + 1, i) for i in range(ends)])
    return before, after


def shards(snapshots, cotangent, mode_weight, conv_weight):
    batches = lax.axis_size("batch")
    slabs = lax.axis_size("space")
    devices = batches * slabs
    _, channels, layers, plane = snapshots.shape
    modes = mode_weight.shape[0] * mode_weight.shape[1]
    half = LANES // 2
    assert channels == half and layers == 2 and plane == CELLS
    plane_rows = devices * modes
    count = modes * 2 * KZ * batches
    in_slab = modes == 8 and devices * 32 == TERM_ROWS

    analysis, synthesis = plane_tables(batches, slabs)
    gather, scatter, gather_back, scatter_back = depth_tables(slabs, layers, modes)
    weights = mode_weight.reshape(modes * 2 * KZ * channels, channels)
    taps = conv_weight.reshape(OFFSETS, channels, channels)
    field = shape((channels, layers, plane), BF16)
    wide = shape((CELLS, LANES), BF16)
    edge = shape((CELLS // 2, LANES), BF16)
    plane_modes = shape((plane_rows, LANES), BF16)
    padded = pltpu.VMEM((CELLS + 2 * NY, 2 * LANES), BF16)

    def send(values):
        return exchange(values.reshape(devices, modes, LANES)).reshape(plane_rows, LANES)

    packed = shape((weights.shape[0] // 2, LANES), BF16)
    share = weights.shape[0] // CHUNKS
    cells, coef, first, last, kept_weights = run(
        analyse_kernel,
        [wide, plane_modes, edge, edge, shape((HBM_BYTES // (2 * LANES), LANES), BF16)],
        snapshots.reshape(field.shape),
        analysis,
        *[weights] * CHUNKS,
        staged={0: None, 1: None} | {2 + k: slice(k * share, (k + 1) * share) for k in range(CHUNKS)},
        sent=(0, 1, 2, 3),
        plain=(4,),
        scratch=[pltpu.VMEM(packed.shape, BF16), pltpu.SemaphoreType.DMA((CHUNKS,))],
        limit=WHOLE_VMEM,
        flops=10**8,
    )
    coef = send(coef)
    (packed_weights,) = run(fetch_kernel, [packed], kept_weights, moved={0: 0})
    before, after = neighbours(first, last)
    local, lanes, outer_cells = run(
        local_kernel,
        [shape((CELLS, LANES), F32), shape((HBM_BYTES // (2 * CELLS), CELLS), BF16), wide],
        cells,
        before,
        after,
        cotangent.reshape(field.shape),
        taps,
        sent={1: 2 * LANES},
        scratch=[padded, pltpu.VMEM((3, 2 * LANES, 3 * LANES), BF16)],
        flops=7 * 10**8,
    )
    back, diagonal = run(
        functools.partial(mix_kernel, batches),
        [
            shape((devices, modes, LANES), BF16) if modes % 8 == 0 else plane_modes,
            shape((count, GROUP * half // 2), BF16),
        ],
        coef,
        gather,
        packed_weights,
        scatter,
        sent=(0, 1),
        flops=4 * 10**8,
    )
    back = send(back)
    slab = shape((devices, 8 + TERM_ROWS // devices, LANES), BF16)
    activated, grad, first, last, back, terms = run(
        functools.partial(activate_kernel, in_slab),
        [
            wide,
            shape((HBM_BYTES // (2 * LANES), LANES), BF16),
            edge,
            edge,
            slab if in_slab else plane_modes,
            None if in_slab else shape((TERM_ROWS, LANES), BF16),
        ],
        back,
        np.ascontiguousarray(synthesis.T),
        synthesis,
        local,
        outer_cells,
        lanes,
        staged={5: 2 * LANES},
        sent={1: CELLS, 2: None, 3: None, 4: None},
        scratch=[pltpu.VMEM((CELLS + 2 * NY, 3 * LANES), BF16)],
        flops=10**9,
    )
    if in_slab:
        back = exchange(back)
    else:
        back = send(back)
        terms = exchange(terms.reshape(devices, TERM_ROWS // devices, LANES))
    before, after = neighbours(first, last)
    activated, packed_weights = run(
        output_kernel,
        [field, packed],
        activated,
        kept_weights,
        moved={1: 1},
        flops=10**8,
    )
    back, before, after, activated, packed_weights = lax.optimization_barrier(
        (back, before, after, activated, packed_weights)
    )
    scale = 1.0 / math.sqrt(batches * slabs * layers * plane)
    grad_modes, mixed_grad, sums = run(
        functools.partial(unmix_kernel, batches, scale),
        [
            slab if in_slab else plane_modes,
            shape((count, LANES), BF16),
            None if in_slab else shape((TERM_ROWS // devices, LANES), F32),
        ],
        back,
        None if in_slab else terms,
        gather_back,
        packed_weights,
        scatter_back,
        sent=(0,),
        flops=4 * 10**8,
    )
    if in_slab:
        grad_modes = exchange(grad_modes)
    else:
        grad_modes = send(grad_modes)
        sums = lax.all_gather(sums, ("batch", "space"), axis=0, tiled=True)
    (local,) = run(
        local_grad_kernel,
        [shape((CELLS, LANES), F32)],
        grad,
        before,
        after,
        taps,
        staged={0: CELLS},
        scratch=[padded, pltpu.VMEM((3, 3 * LANES, 2 * LANES), BF16)],
        flops=7 * 10**8,
    )
    (mode_gradient,) = run(
        functools.partial(weight_kernel, batches),
        [shape((modes * 2 * KZ * channels, channels), F32)],
        diagonal,
        mixed_grad,
        flops=4 * 10**8,
    )
    input_gradient, conv_gradient = run(
        finish_kernel,
        [field, shape((OFFSETS, channels, channels), F32)],
        grad_modes,
        sums,
        np.ascontiguousarray(analysis.T),
        local,
        sent=(1,),
        flops=10**8,
    )
    return (
        activated.reshape(snapshots.shape),
        input_gradient.reshape(snapshots.shape),
        mode_gradient.reshape(mode_weight.shape),
        conv_gradient.reshape(conv_weight.shape),
    )


def solution(mesh):
    in_specs = (
        P("batch", None, "space", None),
        P("batch", None, "space", None),
        P("batch", "space", None, None, None),
        P(),
    )
    out_specs = (
        P("batch", None, "space", None),
        P("batch", None, "space", None),
        P("batch", "space", None, None, None),
        P(),
    )
    return jax.shard_map(shards, mesh=mesh, in_specs=in_specs, out_specs=out_specs, check_vma=False)
```

```python
import functools
import math

import jax
import jax.numpy as jnp
import ml_dtypes
import numpy as np
from jax import lax
from jax.experimental import pallas as pl
from jax.experimental.pallas import tpu as pltpu
from jax.sharding import PartitionSpec as P

KX = 8
KY = 8
KZ = 12
NX = 32
NY = 32
CELLS = NX * NY
LANES = 128
GROUP = 8
OFFSETS = 27
TERM_ROWS = 1024
CHUNKS = 3
VMEM_BYTES = 40 * 1024 * 1024
WHOLE_VMEM = 65000 * 1024
HBM_BYTES = 100 * 1024 * 256

F32 = jnp.float32
BF16 = jnp.bfloat16
inv_root_two = 1.0 / math.sqrt(2.0)
inv_root_two_pi = 1.0 / math.sqrt(2.0 * math.pi)


def basis_rows(half_count, length):
    row = np.arange(2 * half_count)[:, None]
    cell = np.arange(length)[None, :]
    frequency = np.where(row < half_count, row, row - half_count + 1)
    phases = (frequency * cell % length).astype(np.float32) * np.float32(2.0 * math.pi / length)
    return np.where(row < half_count, np.cos(phases), np.sin(phases)).astype(np.float32)


def plane_tables(batches, slabs):
    outer = (basis_rows(KX, NX)[:, None, :, None] * basis_rows(KY, NY)[None, :, None, :]).reshape(
        2 * KX, 2 * KY, CELLS
    )
    outer = outer.reshape(batches, 2 * KX // batches, slabs, 2 * KY // slabs, CELLS)
    outer = outer.transpose(2, 0, 1, 3, 4).reshape(4 * KX * KY, CELLS)
    analysis = (outer * np.float32(2.0 / math.sqrt(CELLS))).astype(ml_dtypes.bfloat16)
    synthesis = (outer * np.float32(2.0 / math.sqrt(4 * KX * KY))).astype(ml_dtypes.bfloat16)
    return analysis, synthesis


def depth_tables(slabs, layers, modes):
    rows = basis_rows(KZ, slabs * layers)
    analysis = (rows * np.float32(math.sqrt(2.0 / (slabs * layers)))).astype(ml_dtypes.bfloat16)
    synthesis = (rows * np.float32(math.sqrt(2.0 / (2 * KZ)))).astype(ml_dtypes.bfloat16)

    def spread(table, order):
        table = table.astype(np.float32).reshape(2 * KZ, slabs, layers)
        full = np.einsum("psz,mn->" + order, table, np.eye(modes, dtype=np.float32))
        return full.astype(ml_dtypes.bfloat16)

    def gathered(table):
        return spread(table, "mpzsn").reshape(modes * 2 * KZ, layers * slabs * modes)

    def scattered(table):
        return spread(table, "snzmp").reshape(slabs * modes, layers * modes * 2 * KZ)

    return gathered(analysis), scattered(synthesis), gathered(synthesis), scattered(analysis)


def dot(left, right, contract=(1, 0)):
    return lax.dot_general(
        left, right, (((contract[0],), (contract[1],)), ((), ())), preferred_element_type=F32
    )


def turn_table():
    row = lax.broadcasted_iota(jnp.int32, (LANES, LANES), 0)
    column = lax.broadcasted_iota(jnp.int32, (LANES, LANES), 1)
    return jnp.where(column == row % 2 * (LANES // 2) + row // 2, 1.0, 0.0).astype(BF16)


def to_cells(field):
    return dot(field.reshape(LANES, CELLS), turn_table(), (0, 0))


def to_field(cells):
    return dot(turn_table(), cells, (1, 1)).astype(BF16).reshape(LANES // 2, 2, CELLS)


def low_lanes(rows):
    return lax.broadcasted_iota(jnp.int32, (rows, LANES), 1) < LANES // 2


def swap_halves(values):
    return pltpu.roll(values, LANES // 2, 1)


def doubled(values):
    low = low_lanes(values.shape[0])
    swapped = swap_halves(values)
    return jnp.concatenate(
        [jnp.where(low, values, swapped), jnp.where(low, swapped, values)], axis=0
    )


def halved(values):
    low = low_lanes(values.shape[0])
    return jnp.concatenate([jnp.where(low, values, 0.0), jnp.where(low, 0.0, values)], axis=0)


def edge_layers(cells_first):
    top = cells_first[: CELLS // 2]
    bottom = cells_first[CELLS // 2 :]
    low = low_lanes(CELLS // 2)
    first = jnp.where(low, top, swap_halves(bottom))
    last = jnp.where(low, swap_halves(top), bottom)
    return first.astype(BF16), last.astype(BF16)


def beside_layers(before, after):
    before = before.astype(F32)
    after = after.astype(F32)
    low = low_lanes(CELLS // 2)
    top = jnp.where(low, before, swap_halves(after))
    bottom = jnp.where(low, swap_halves(before), after)
    return jnp.concatenate([top, bottom], axis=0).astype(BF16)


def y_cells(rows):
    return lax.broadcasted_iota(jnp.int32, (rows, LANES), 0) % NY


def from_below(values):
    return jnp.where(y_cells(values.shape[0]) == 0, 0.0, pltpu.roll(values, 1, 0))


def from_above(values):
    rows = values.shape[0]
    return jnp.where(y_cells(rows) == NY - 1, 0.0, pltpu.roll(values, rows - 1, 0))


def pad_cells(padded, own, beside):
    width = own.shape[1] + beside.shape[1]
    padded[0:NY, :] = jnp.zeros((NY, width), BF16)
    padded[NY + CELLS : 2 * NY + CELLS, :] = jnp.zeros((NY, width), BF16)
    padded[NY : NY + CELLS, 0 : own.shape[1]] = own
    padded[NY : NY + CELLS, own.shape[1] :] = beside


BLOCK_OF_DEPTH = {-1: 2, 0: 0, 1: 1, 2: 3}
STEP = 256


def stencil(padded, table, transposed, store):
    for start in range(0, CELLS, STEP):
        total = None
        for b in range(3):
            cells = padded[start + NY * b : start + NY * b + STEP, :]
            term = dot(cells, table[b], (1, 1) if transposed else (1, 0))
            total = term if total is None else total + term
        result = (
            from_below(total[:, 0:LANES])
            + total[:, LANES : 2 * LANES]
            + from_above(total[:, 2 * LANES :])
        )
        store(start, result)


def banded_forward(weights, table):
    half = LANES // 2
    for b in range(3):
        for c in range(3):
            for depth, block in BLOCK_OF_DEPTH.items():
                parts = []
                for out in range(2):
                    a = depth - out + 1
                    if 0 <= a < 3:
                        parts.append(weights[a * 9 + b * 3 + c])
                    else:
                        parts.append(jnp.zeros((half, half), BF16))
                table[b, block * half : (block + 1) * half, c * LANES : (c + 1) * LANES] = (
                    jnp.concatenate(parts, axis=1)
                )


def banded_backward(weights, table):
    half = LANES // 2
    for b in range(3):
        for c in range(3):
            for out in range(2):
                for pair in ((0, 1), (-1, 2)):
                    parts = []
                    for depth in pair:
                        a = depth - out + 1
                        if 0 <= a < 3:
                            parts.append(weights[(2 - a) * 9 + (2 - b) * 3 + 2 - c])
                        else:
                            parts.append(jnp.zeros((half, half), BF16))
                    row = c * LANES + out * half
                    column = BLOCK_OF_DEPTH[pair[0]] * half
                    table[b, row : row + half, column : column + LANES] = jnp.concatenate(
                        parts, axis=1
                    )


def analyse_kernel(field, analysis, *refs):
    weights = refs[:CHUNKS]
    cells_out, coef_out, first_out, last_out, packed_out, buffer, semaphores = refs[CHUNKS:]
    cells = to_cells(field[...])
    rounded = cells.astype(BF16)
    coef_out[...] = dot(analysis[...], rounded).astype(BF16)
    cells_out[...] = rounded
    first, last = edge_layers(cells)
    first_out[...] = first
    last_out[...] = last
    rows = GROUP * LANES // 4
    share = buffer.shape[0] // CHUNKS
    copies = []
    for place, part in enumerate(weights):
        for g in range(share // rows):
            pair = [part[k * rows : (k + 1) * rows, :] for k in (2 * g, 2 * g + 1)]
            row = place * share + g * rows
            buffer[row : row + rows, :] = jnp.concatenate(pair, axis=1)
        span = slice(place * share, (place + 1) * share)
        copies.append(
            pltpu.make_async_copy(buffer.at[span], packed_out.at[span], semaphores.at[place])
        )
        copies[-1].start()
    for copy in copies:
        copy.wait()


def local_kernel(
    cells, before, after, cotangent, weights, local_out, lanes_out, cotangent_out, padded, table
):
    banded_forward(weights, table)
    beside = beside_layers(before[...], after[...])
    pad_cells(padded, cells[...], beside)

    def store(start, result):
        local_out[start : start + STEP, :] = result

    stencil(padded, table, False, store)
    whole = jnp.concatenate([cells[...].astype(F32), beside.astype(F32)], axis=1)
    lanes_out[...] = whole.T.astype(BF16)
    cotangent_out[...] = to_cells(cotangent[...]).astype(BF16)


def fetch_kernel():
    pass


def mode_in_group(rows, lanes):
    return lax.broadcasted_iota(jnp.int32, (rows, lanes), 0) % GROUP


def own_block(rows):
    width = GROUP * LANES // 4
    lane = lax.broadcasted_iota(jnp.int32, (rows, width), 1)
    return mode_in_group(rows, width) % (GROUP // 2) == lane // (LANES // 2)


def own_half(rows):
    return (mode_in_group(rows, LANES) < GROUP // 2) == low_lanes(rows)


def to_depth(modes, table, snaps, slabs):
    modes = modes.reshape(slabs, snaps, -1, LANES)
    both = [doubled(modes[:, b].reshape(-1, LANES)) for b in range(snaps)]
    result = dot(table, jnp.concatenate(both, axis=1).astype(BF16))
    return jnp.concatenate(
        [
            result[g : g + GROUP, b * LANES : (b + 1) * LANES]
            for g in range(0, result.shape[0], GROUP)
            for b in range(snaps)
        ],
        axis=0,
    )


def from_depth(modes, table, snaps, slabs):
    count = modes.shape[0] // GROUP
    both = []
    for b in range(snaps):
        own = [modes[g * GROUP : (g + 1) * GROUP] for g in range(b, count, snaps)]
        both.append(halved(jnp.concatenate(own, axis=0)))
    result = dot(table, jnp.concatenate(both, axis=1).astype(BF16))
    own = [
        result[:, b * LANES : (b + 1) * LANES].reshape(slabs, -1, LANES) for b in range(snaps)
    ]
    return jnp.stack(own, axis=1).reshape(-1, LANES)


def mix_kernel(snaps, slabs, received, gather, weights, scatter, back_out, diagonal_out):
    coef = to_depth(received[...].astype(F32), gather[...], snaps, slabs)
    count = coef.shape[0]
    wide = jnp.concatenate([coef] * (GROUP // 4), axis=1)
    diagonal = jnp.where(own_block(count), wide, 0.0).astype(BF16)
    diagonal_out[...] = diagonal
    rows = GROUP * snaps
    depth = GROUP * LANES // 4
    mixed = jnp.concatenate(
        [
            dot(diagonal[g * rows : (g + 1) * rows, :], weights[g * depth : (g + 1) * depth, :])
            for g in range(count // rows)
        ],
        axis=0,
    )
    mixed = jnp.where(own_half(count), mixed, swap_halves(mixed))
    back = from_depth(mixed, scatter[...], snaps, slabs).astype(BF16)
    back_out[...] = back.reshape(back_out.shape)


def activate_kernel(
    terms_in_slab,
    received,
    synthesis,
    synthesis_rows,
    local,
    cotangent,
    lanes,
    activated_out,
    grad_out,
    first_out,
    last_out,
    back_out,
    terms_out,
    spread,
):
    pre = dot(synthesis[...], received[...]) + local[...]
    cdf = 0.5 * (1.0 + lax.erf(pre * inv_root_two))
    density = jnp.exp(-0.5 * pre * pre) * inv_root_two_pi
    activated_out[...] = (pre * cdf).astype(BF16)
    grad = (cotangent[...].astype(F32) * (cdf + pre * density)).astype(BF16)
    grad_out[...] = grad
    back = dot(synthesis_rows[...], grad)
    grad = grad.astype(F32)
    first, last = edge_layers(grad)
    first_out[...] = first
    last_out[...] = last
    spread[0:NY, :] = jnp.zeros((NY, 3 * LANES), BF16)
    spread[NY + CELLS : 2 * NY + CELLS, :] = jnp.zeros((NY, 3 * LANES), BF16)
    spread[NY : NY + CELLS, 0:LANES] = from_above(grad).astype(BF16)
    spread[NY : NY + CELLS, LANES : 2 * LANES] = grad.astype(BF16)
    spread[NY : NY + CELLS, 2 * LANES :] = from_below(grad).astype(BF16)
    half = LANES // 2
    low = low_lanes(half)
    twice = {}
    for b in range(3):
        product = dot(lanes[...], spread[NY * (2 - b) : NY * (2 - b) + CELLS, :])
        for c in range(3):
            for a in range(3):
                blocks = [BLOCK_OF_DEPTH[out + a - 1] * half for out in range(2)]
                columns = slice(c * LANES, (c + 1) * LANES)
                both = jnp.where(
                    low,
                    product[blocks[0] : blocks[0] + half, columns],
                    product[blocks[1] : blocks[1] + half, columns],
                )
                twice[a * 9 + b * 3 + c] = both + swap_halves(both)
    pairs = []
    for k in range(0, OFFSETS, 2):
        pairs.append(jnp.where(low, twice[k], twice.get(k + 1, 0.0)))
    pairs.append(jnp.zeros((TERM_ROWS - half * len(pairs), LANES), F32))
    terms = jnp.concatenate(pairs, axis=0)
    if terms_in_slab:
        slab_store(back_out, back, terms)
    else:
        back_out[...] = back.astype(BF16)
        terms_out[...] = terms.astype(BF16)


def slab_store(slab, modes, terms):
    owners = slab.shape[0]
    modes = modes.reshape(owners, 8, LANES)
    terms = terms.reshape(owners, -1, LANES)
    slab[...] = jnp.concatenate([modes, terms], axis=1).astype(BF16)


def slab_load(slab):
    whole = slab[...].astype(F32)
    return whole[:, 0:8, :].reshape(-1, LANES), whole[:, 8:, :]


def unmix_kernel(snaps, slabs, scale, received, terms, gather, weights, scatter, grad_out, mixed_out, sums_out):
    in_slab = terms is None
    if in_slab:
        modes, terms = slab_load(received)
    else:
        modes, terms = received[...].astype(F32), terms[...].astype(F32)
    mixed = to_depth(modes, gather[...], snaps, slabs)
    mixed_out[...] = mixed.astype(BF16)
    count = mixed.shape[0]
    rows = GROUP * snaps
    depth = GROUP * LANES // 4
    sums = jnp.sum(terms, axis=0) * scale
    own = own_block(rows)
    placed = jnp.where(own_half(count), mixed, 0.0).astype(BF16)
    pieces = []
    for g in range(count // rows):
        full = dot(
            placed[g * rows : (g + 1) * rows, :], weights[g * depth : (g + 1) * depth, :], (1, 1)
        )
        full = jnp.where(own, full, 0.0)
        pieces.append(sum(full[:, k : k + LANES] for k in range(0, depth, LANES)))
    coef = jnp.concatenate(pieces, axis=0)
    coef = coef + swap_halves(coef)
    grad = from_depth(coef, scatter[...], snaps, slabs)
    if in_slab:
        owners = received.shape[0]
        share = sums.shape[0]
        slab_store(
            grad_out, grad, jnp.broadcast_to(sums[None], (owners, share, LANES)).reshape(-1, LANES)
        )
    else:
        grad_out[...] = grad.astype(BF16)
        sums_out[...] = sums


def weight_kernel(snaps, diagonal, mixed, out):
    rows = GROUP * snaps
    depth = GROUP * LANES // 4
    half = LANES // 2
    first = mode_in_group(rows, depth) < GROUP // 2
    for g in range(diagonal.shape[0] // rows):
        span = slice(g * rows, (g + 1) * rows)
        blocks = diagonal[span, :].astype(F32)
        blocks = [jnp.where(first, blocks, 0.0), jnp.where(first, 0.0, blocks)]
        blocks = jnp.concatenate(blocks, axis=1).astype(BF16)
        out[2 * g * depth : 2 * (g + 1) * depth, :] = dot(blocks, mixed[span, 0:half], (0, 0))


def output_kernel(cells, out):
    out[...] = to_field(cells[...])


def local_grad_kernel(grad, before, after, weights, out, padded, table):
    banded_backward(weights, table)
    pad_cells(padded, grad[...], beside_layers(before[...], after[...]))

    def store(start, result):
        out[start : start + STEP, :] = result

    stencil(padded, table, True, store)


def finish_kernel(received, sums, synthesis, local, grad_out, stencil_out):
    in_slab = sums is None
    if in_slab:
        modes, terms = slab_load(received)
        terms = terms.reshape(TERM_ROWS, LANES)
    else:
        modes, terms = received[...], sums[...].astype(F32)
    cells = (dot(synthesis[...], modes.astype(BF16)) + local[...]).astype(BF16)
    grad_out[...] = to_field(cells)
    half = LANES // 2
    for k in range(OFFSETS):
        row = (k // 2) * half
        lane = (k % 2) * half
        stencil_out[k] = terms[row : row + half, lane : lane + half]


def shape(dims, dtype):
    return jax.ShapeDtypeStruct(dims, dtype)


class Staged:
    def __init__(self, source, buffer, semaphore):
        self.copy = pltpu.make_async_copy(source, buffer, semaphore)
        self.buffer = buffer
        self.copy.start()
        self.ready = False

    def load(self):
        if not self.ready:
            self.copy.wait()
            self.ready = True

    def __getitem__(self, index):
        self.load()
        return self.buffer[index]


class Sent:
    def __init__(self, target, buffer, semaphore):
        self.copy = pltpu.make_async_copy(buffer, target, semaphore)
        self.buffer = buffer

    def __setitem__(self, index, value):
        self.buffer[index] = value
        self.copy.start()

    def __getitem__(self, index):
        return self.buffer[index]

    @property
    def shape(self):
        return self.buffer.shape


def row_count(rows):
    return rows.stop - rows.start if isinstance(rows, slice) else rows


def run(
    body, outs, *operands, staged=(), sent=(), moved=(), plain=(), scratch=(), flops=0, limit=VMEM_BYTES
):
    given = [k for k, operand in enumerate(operands) if operand is not None]
    made = [k for k, out in enumerate(outs) if out is not None]

    def rows_of(chosen, places, arrays):
        chosen = {k: chosen[k] if isinstance(chosen, dict) else None for k in places if k in chosen}
        return {k: rows or arrays[k].shape[0] for k, rows in chosen.items()}

    moved = dict(moved)
    staged = rows_of(staged, given, operands)
    sent = rows_of(sent, made, outs)

    def kernel(*refs):
        refs = list(refs)

        def take(count):
            taken = refs[:count]
            del refs[:count]
            return taken

        def part(ref, rows):
            if isinstance(rows, slice):
                return ref.at[rows]
            return ref if ref.shape[0] == rows else ref.at[0:rows]

        filled = dict(zip(given, take(len(given))))
        kept = dict(zip(made, take(len(made))))
        own = take(len(scratch))
        copies = []
        for place, (k, out) in enumerate(moved.items()):
            source, target = filled.pop(k), kept.pop(out)
            rows = min(source.shape[0], target.shape[0])
            semaphore = refs[-1].at[len(staged) + len(sent) + place]
            copies.append(
                pltpu.make_async_copy(part(source, rows), part(target, rows), semaphore)
            )
        for place, (k, buffer) in enumerate(zip(staged, take(len(staged)))):
            filled[k] = Staged(part(filled[k], staged[k]), buffer, refs[-1].at[place])
        for place, (k, buffer) in enumerate(zip(sent, take(len(sent)))):
            kept[k] = Sent(part(kept[k], sent[k]), buffer, refs[-1].at[len(staged) + place])
        for copy in copies:
            copy.start()
        body(
            *[filled.get(k) for k in range(len(operands)) if k not in moved],
            *[kept.get(k) for k in range(len(outs)) if k not in moved.values()],
            *own,
        )
        for k in staged:
            filled[k].load()
        for k in sent:
            kept[k].copy.wait()
        for copy in copies:
            copy.wait()

    arrays = [operands[k] for k in given]
    results = [outs[k] for k in made]
    size = sum(x.size * x.dtype.itemsize for x in (*arrays, *results))
    in_vmem = pl.BlockSpec(memory_space=pltpu.VMEM)
    in_hbm = pl.BlockSpec(memory_space=pltpu.HBM)
    buffers = [(operands[k], rows) for k, rows in staged.items()]
    buffers += [(outs[k], rows) for k, rows in sent.items()]
    buffers = [pltpu.VMEM((row_count(rows), *x.shape[1:]), x.dtype) for x, rows in buffers]
    if len(buffers) + len(moved) > 0:
        buffers.append(pltpu.SemaphoreType.DMA((len(buffers) + len(moved),)))
    results = pl.pallas_call(
        kernel,
        out_shape=results,
        in_specs=[in_hbm if k in staged or k in moved else in_vmem for k in given],
        out_specs=[in_hbm if k in sent or k in plain else in_vmem for k in made],
        scratch_shapes=[*scratch, *buffers],
        compiler_params=pltpu.CompilerParams(vmem_limit_bytes=limit),
        cost_estimate=pl.CostEstimate(flops=flops, bytes_accessed=size, transcendentals=0),
        name=body.__name__ if hasattr(body, "__name__") else body.func.__name__,
    )(*arrays)
    results = dict(zip(made, results))
    return [results.get(k) for k in range(len(outs))]


def exchange(values):
    return lax.all_to_all(values, ("space", "batch"), split_axis=0, concat_axis=0, tiled=True)


def neighbours(first, last):
    ends = lax.axis_size("space") - 1
    before = lax.ppermute(last, "space", [(i, i + 1) for i in range(ends)])
    after = lax.ppermute(first, "space", [(i + 1, i) for i in range(ends)])
    return before, after


def shards(snapshots, cotangent, mode_weight, conv_weight):
    batches = lax.axis_size("batch")
    slabs = lax.axis_size("space")
    devices = batches * slabs
    _, channels, layers, plane = snapshots.shape
    modes = mode_weight.shape[0] * mode_weight.shape[1]
    half = LANES // 2
    assert channels == half and layers == 2 and plane == CELLS
    plane_rows = devices * modes
    count = modes * 2 * KZ * batches
    in_slab = modes == 8 and devices * 32 == TERM_ROWS

    analysis, synthesis = plane_tables(batches, slabs)
    gather, scatter, gather_back, scatter_back = depth_tables(slabs, layers, modes)
    weights = mode_weight.reshape(modes * 2 * KZ * channels, channels)
    taps = conv_weight.reshape(OFFSETS, channels, channels)
    field = shape((channels, layers, plane), BF16)
    wide = shape((CELLS, LANES), BF16)
    edge = shape((CELLS // 2, LANES), BF16)
    plane_modes = shape((plane_rows, LANES), BF16)
    padded = pltpu.VMEM((CELLS + 2 * NY, 2 * LANES), BF16)

    def send(values):
        return exchange(values.reshape(devices, modes, LANES)).reshape(plane_rows, LANES)

    packed = shape((weights.shape[0] // 2, LANES), BF16)
    share = weights.shape[0] // CHUNKS
    cells, coef, first, last, kept_weights = run(
        analyse_kernel,
        [wide, plane_modes, edge, edge, shape((HBM_BYTES // (2 * LANES), LANES), BF16)],
        snapshots.reshape(field.shape),
        analysis,
        *[weights] * CHUNKS,
        staged={0: None, 1: None} | {2 + k: slice(k * share, (k + 1) * share) for k in range(CHUNKS)},
        sent=(0, 1, 2, 3),
        plain=(4,),
        scratch=[pltpu.VMEM(packed.shape, BF16), pltpu.SemaphoreType.DMA((CHUNKS,))],
        limit=WHOLE_VMEM,
        flops=10**8,
    )
    coef = send(coef)
    (packed_weights,) = run(fetch_kernel, [packed], kept_weights, moved={0: 0})
    before, after = neighbours(first, last)
    local, lanes, outer_cells = run(
        local_kernel,
        [shape((CELLS, LANES), F32), shape((HBM_BYTES // (2 * CELLS), CELLS), BF16), wide],
        cells,
        before,
        after,
        cotangent.reshape(field.shape),
        taps,
        sent={1: 2 * LANES},
        scratch=[padded, pltpu.VMEM((3, 2 * LANES, 3 * LANES), BF16)],
        flops=7 * 10**8,
    )
    back, diagonal = run(
        functools.partial(mix_kernel, batches, slabs),
        [
            shape((devices, modes, LANES), BF16) if modes % 8 == 0 else plane_modes,
            shape((count, GROUP * half // 2), BF16),
        ],
        coef,
        gather,
        packed_weights,
        scatter,
        sent=(0, 1),
        flops=4 * 10**8,
    )
    back = send(back)
    slab = shape((devices, 8 + TERM_ROWS // devices, LANES), BF16)
    activated, grad, first, last, back, terms = run(
        functools.partial(activate_kernel, in_slab),
        [
            wide,
            shape((HBM_BYTES // (2 * LANES), LANES), BF16),
            edge,
            edge,
            slab if in_slab else plane_modes,
            None if in_slab else shape((TERM_ROWS, LANES), BF16),
        ],
        back,
        np.ascontiguousarray(synthesis.T),
        synthesis,
        local,
        outer_cells,
        lanes,
        staged={5: 2 * LANES},
        sent={1: CELLS, 2: None, 3: None, 4: None},
        scratch=[pltpu.VMEM((CELLS + 2 * NY, 3 * LANES), BF16)],
        flops=10**9,
    )
    if in_slab:
        back = exchange(back)
    else:
        back = send(back)
        terms = exchange(terms.reshape(devices, TERM_ROWS // devices, LANES))
    before, after = neighbours(first, last)
    activated, packed_weights = run(
        output_kernel,
        [field, packed],
        activated,
        kept_weights,
        moved={1: 1},
        flops=10**8,
    )
    back, before, after, activated, packed_weights = lax.optimization_barrier(
        (back, before, after, activated, packed_weights)
    )
    scale = 1.0 / math.sqrt(batches * slabs * layers * plane)
    grad_modes, mixed_grad, sums = run(
        functools.partial(unmix_kernel, batches, slabs, scale),
        [
            slab if in_slab else plane_modes,
            shape((count, LANES), BF16),
            None if in_slab else shape((TERM_ROWS // devices, LANES), F32),
        ],
        back,
        None if in_slab else terms,
        gather_back,
        packed_weights,
        scatter_back,
        sent=(0,),
        flops=4 * 10**8,
    )
    if in_slab:
        grad_modes = exchange(grad_modes)
    else:
        grad_modes = send(grad_modes)
        sums = lax.all_gather(sums, ("space", "batch"), axis=0, tiled=True)
    (local,) = run(
        local_grad_kernel,
        [shape((CELLS, LANES), F32)],
        grad,
        before,
        after,
        taps,
        staged={0: CELLS},
        scratch=[padded, pltpu.VMEM((3, 3 * LANES, 2 * LANES), BF16)],
        flops=7 * 10**8,
    )
    (mode_gradient,) = run(
        functools.partial(weight_kernel, batches),
        [shape((modes * 2 * KZ * channels, channels), F32)],
        diagonal,
        mixed_grad,
        flops=4 * 10**8,
    )
    input_gradient, conv_gradient = run(
        finish_kernel,
        [field, shape((OFFSETS, channels, channels), F32)],
        grad_modes,
        sums,
        np.ascontiguousarray(analysis.T),
        local,
        flops=10**8,
    )
    return (
        activated.reshape(snapshots.shape),
        input_gradient.reshape(snapshots.shape),
        mode_gradient.reshape(mode_weight.shape),
        conv_gradient.reshape(conv_weight.shape),
    )


def solution(mesh):
    in_specs = (
        P("batch", None, "space", None),
        P("batch", None, "space", None),
        P("batch", "space", None, None, None),
        P(),
    )
    out_specs = (
        P("batch", None, "space", None),
        P("batch", None, "space", None),
        P("batch", "space", None, None, None),
        P(),
    )
    return jax.shard_map(shards, mesh=mesh, in_specs=in_specs, out_specs=out_specs, check_vma=False)
```

```python
import functools
import math

import jax
import jax.numpy as jnp
import ml_dtypes
import numpy as np
from jax import lax
from jax.experimental import pallas as pl
from jax.experimental.pallas import tpu as pltpu
from jax.sharding import PartitionSpec as P

KX = 8
KY = 8
KZ = 12
NX = 32
NY = 32
CELLS = NX * NY
LANES = 128
GROUP = 8
OFFSETS = 27
TERM_ROWS = 1024
CHUNKS = 3
VMEM_BYTES = 40 * 1024 * 1024
WHOLE_VMEM = 65000 * 1024
HBM_BYTES = 100 * 1024 * 256

F32 = jnp.float32
BF16 = jnp.bfloat16
inv_root_two = 1.0 / math.sqrt(2.0)
inv_root_two_pi = 1.0 / math.sqrt(2.0 * math.pi)


def basis_rows(half_count, length):
    row = np.arange(2 * half_count)[:, None]
    cell = np.arange(length)[None, :]
    frequency = np.where(row < half_count, row, row - half_count + 1)
    phases = (frequency * cell % length).astype(np.float32) * np.float32(2.0 * math.pi / length)
    return np.where(row < half_count, np.cos(phases), np.sin(phases)).astype(np.float32)


def plane_tables(batches, slabs):
    outer = (basis_rows(KX, NX)[:, None, :, None] * basis_rows(KY, NY)[None, :, None, :]).reshape(
        2 * KX, 2 * KY, CELLS
    )
    outer = outer.reshape(batches, 2 * KX // batches, slabs, 2 * KY // slabs, CELLS)
    outer = outer.transpose(2, 0, 1, 3, 4).reshape(4 * KX * KY, CELLS)
    analysis = (outer * np.float32(2.0 / math.sqrt(CELLS))).astype(ml_dtypes.bfloat16)
    synthesis = (outer * np.float32(2.0 / math.sqrt(4 * KX * KY))).astype(ml_dtypes.bfloat16)
    return analysis, synthesis


def depth_tables(slabs, layers, modes):
    rows = basis_rows(KZ, slabs * layers)
    analysis = (rows * np.float32(math.sqrt(2.0 / (slabs * layers)))).astype(ml_dtypes.bfloat16)
    synthesis = (rows * np.float32(math.sqrt(2.0 / (2 * KZ)))).astype(ml_dtypes.bfloat16)

    def spread(table, order):
        table = table.astype(np.float32).reshape(2 * KZ, slabs, layers)
        full = np.einsum("psz,mn->" + order, table, np.eye(modes, dtype=np.float32))
        return full.astype(ml_dtypes.bfloat16)

    def gathered(table):
        return spread(table, "mpzsn").reshape(modes * 2 * KZ, layers * slabs * modes)

    def scattered(table):
        return spread(table, "snzmp").reshape(slabs * modes, layers * modes * 2 * KZ)

    return gathered(analysis), scattered(synthesis), gathered(synthesis), scattered(analysis)


def dot(left, right, contract=(1, 0)):
    return lax.dot_general(
        left, right, (((contract[0],), (contract[1],)), ((), ())), preferred_element_type=F32
    )


def turn_table():
    row = lax.broadcasted_iota(jnp.int32, (LANES, LANES), 0)
    column = lax.broadcasted_iota(jnp.int32, (LANES, LANES), 1)
    return jnp.where(column == row % 2 * (LANES // 2) + row // 2, 1.0, 0.0).astype(BF16)


def to_cells(field):
    return dot(field.reshape(LANES, CELLS), turn_table(), (0, 0))


def to_field(cells):
    return dot(turn_table(), cells, (1, 1)).astype(BF16).reshape(LANES // 2, 2, CELLS)


def low_lanes(rows):
    return lax.broadcasted_iota(jnp.int32, (rows, LANES), 1) < LANES // 2


def swap_halves(values):
    return pltpu.roll(values, LANES // 2, 1)


def doubled(values):
    low = low_lanes(values.shape[0])
    swapped = swap_halves(values)
    return jnp.concatenate(
        [jnp.where(low, values, swapped), jnp.where(low, swapped, values)], axis=0
    )


def halved(values):
    low = low_lanes(values.shape[0])
    return jnp.concatenate([jnp.where(low, values, 0.0), jnp.where(low, 0.0, values)], axis=0)


def edge_layers(cells_first):
    top = cells_first[: CELLS // 2]
    bottom = cells_first[CELLS // 2 :]
    low = low_lanes(CELLS // 2)
    first = jnp.where(low, top, swap_halves(bottom))
    last = jnp.where(low, swap_halves(top), bottom)
    return first.astype(BF16), last.astype(BF16)


def beside_layers(before, after):
    before = before.astype(F32)
    after = after.astype(F32)
    low = low_lanes(CELLS // 2)
    top = jnp.where(low, before, swap_halves(after))
    bottom = jnp.where(low, swap_halves(before), after)
    return jnp.concatenate([top, bottom], axis=0).astype(BF16)


def y_cells(rows):
    return lax.broadcasted_iota(jnp.int32, (rows, LANES), 0) % NY


def from_below(values):
    return jnp.where(y_cells(values.shape[0]) == 0, 0.0, pltpu.roll(values, 1, 0))


def from_above(values):
    rows = values.shape[0]
    return jnp.where(y_cells(rows) == NY - 1, 0.0, pltpu.roll(values, rows - 1, 0))


def pad_cells(padded, own, beside):
    width = own.shape[1] + beside.shape[1]
    padded[0:NY, :] = jnp.zeros((NY, width), BF16)
    padded[NY + CELLS : 2 * NY + CELLS, :] = jnp.zeros((NY, width), BF16)
    padded[NY : NY + CELLS, 0 : own.shape[1]] = own
    padded[NY : NY + CELLS, own.shape[1] :] = beside


BLOCK_OF_DEPTH = {-1: 2, 0: 0, 1: 1, 2: 3}
STEP = 256


def stencil(padded, table, transposed, store):
    for start in range(0, CELLS, STEP):
        total = None
        for b in range(3):
            cells = padded[start + NY * b : start + NY * b + STEP, :]
            term = dot(cells, table[b], (1, 1) if transposed else (1, 0))
            total = term if total is None else total + term
        result = (
            from_below(total[:, 0:LANES])
            + total[:, LANES : 2 * LANES]
            + from_above(total[:, 2 * LANES :])
        )
        store(start, result)


def banded_forward(weights, table):
    half = LANES // 2
    for b in range(3):
        for c in range(3):
            for depth, block in BLOCK_OF_DEPTH.items():
                parts = []
                for out in range(2):
                    a = depth - out + 1
                    if 0 <= a < 3:
                        parts.append(weights[a * 9 + b * 3 + c])
                    else:
                        parts.append(jnp.zeros((half, half), BF16))
                table[b, block * half : (block + 1) * half, c * LANES : (c + 1) * LANES] = (
                    jnp.concatenate(parts, axis=1)
                )


def banded_backward(weights, table):
    half = LANES // 2
    for b in range(3):
        for c in range(3):
            for out in range(2):
                for pair in ((0, 1), (-1, 2)):
                    parts = []
                    for depth in pair:
                        a = depth - out + 1
                        if 0 <= a < 3:
                            parts.append(weights[(2 - a) * 9 + (2 - b) * 3 + 2 - c])
                        else:
                            parts.append(jnp.zeros((half, half), BF16))
                    row = c * LANES + out * half
                    column = BLOCK_OF_DEPTH[pair[0]] * half
                    table[b, row : row + half, column : column + LANES] = jnp.concatenate(
                        parts, axis=1
                    )


def analyse_kernel(field, analysis, *refs):
    weights = refs[:CHUNKS]
    cells_out, coef_out, first_out, last_out, packed_out, _, buffer, semaphores = refs[CHUNKS:]
    cells = to_cells(field[...])
    rounded = cells.astype(BF16)
    coef_out[...] = dot(analysis[...], rounded).astype(BF16)
    cells_out[...] = rounded
    first, last = edge_layers(cells)
    first_out[...] = first
    last_out[...] = last
    rows = GROUP * LANES // 4
    share = buffer.shape[0] // CHUNKS
    copies = []
    for place, part in enumerate(weights):
        for g in range(share // rows):
            pair = [part[k * rows : (k + 1) * rows, :] for k in (2 * g, 2 * g + 1)]
            row = place * share + g * rows
            buffer[row : row + rows, :] = jnp.concatenate(pair, axis=1)
        span = slice(place * share, (place + 1) * share)
        copies.append(
            pltpu.make_async_copy(buffer.at[span], packed_out.at[span], semaphores.at[place])
        )
        copies[-1].start()
    for copy in copies:
        copy.wait()


def local_kernel(
    cells, before, after, cotangent, weights, local_out, lanes_out, cotangent_out, padded, table
):
    banded_forward(weights, table)
    beside = beside_layers(before[...], after[...])
    pad_cells(padded, cells[...], beside)

    def store(start, result):
        local_out[start : start + STEP, :] = result

    stencil(padded, table, False, store)
    whole = jnp.concatenate([cells[...].astype(F32), beside.astype(F32)], axis=1)
    lanes_out[...] = whole.T.astype(BF16)
    cotangent_out[...] = to_cells(cotangent[...]).astype(BF16)


def fetch_kernel():
    pass


def mode_in_group(rows, lanes):
    return lax.broadcasted_iota(jnp.int32, (rows, lanes), 0) % GROUP


def own_block(rows):
    width = GROUP * LANES // 4
    lane = lax.broadcasted_iota(jnp.int32, (rows, width), 1)
    return mode_in_group(rows, width) % (GROUP // 2) == lane // (LANES // 2)


def own_half(rows):
    return (mode_in_group(rows, LANES) < GROUP // 2) == low_lanes(rows)


def to_depth(modes, table, snaps, slabs):
    modes = modes.reshape(slabs, snaps, -1, LANES)
    both = [doubled(modes[:, b].reshape(-1, LANES)) for b in range(snaps)]
    result = dot(table, jnp.concatenate(both, axis=1).astype(BF16))
    return jnp.concatenate(
        [
            result[g : g + GROUP, b * LANES : (b + 1) * LANES]
            for g in range(0, result.shape[0], GROUP)
            for b in range(snaps)
        ],
        axis=0,
    )


def from_depth(modes, table, snaps, slabs):
    count = modes.shape[0] // GROUP
    both = []
    for b in range(snaps):
        own = [modes[g * GROUP : (g + 1) * GROUP] for g in range(b, count, snaps)]
        both.append(halved(jnp.concatenate(own, axis=0)))
    result = dot(table, jnp.concatenate(both, axis=1).astype(BF16))
    own = [
        result[:, b * LANES : (b + 1) * LANES].reshape(slabs, -1, LANES) for b in range(snaps)
    ]
    return jnp.stack(own, axis=1).reshape(-1, LANES)


def mix_kernel(snaps, slabs, received, gather, weights, scatter, back_out, diagonal_out):
    coef = to_depth(received[...].astype(F32), gather[...], snaps, slabs)
    count = coef.shape[0]
    wide = jnp.concatenate([coef] * (GROUP // 4), axis=1)
    diagonal = jnp.where(own_block(count), wide, 0.0).astype(BF16)
    diagonal_out[...] = diagonal
    rows = GROUP * snaps
    depth = GROUP * LANES // 4
    mixed = jnp.concatenate(
        [
            dot(diagonal[g * rows : (g + 1) * rows, :], weights[g * depth : (g + 1) * depth, :])
            for g in range(count // rows)
        ],
        axis=0,
    )
    mixed = jnp.where(own_half(count), mixed, swap_halves(mixed))
    back = from_depth(mixed, scatter[...], snaps, slabs).astype(BF16)
    back_out[...] = back.reshape(back_out.shape)


def activate_kernel(
    terms_in_slab,
    received,
    synthesis,
    synthesis_rows,
    local,
    cotangent,
    lanes,
    activated_out,
    grad_out,
    first_out,
    last_out,
    back_out,
    terms_out,
    spread,
):
    pre = dot(synthesis[...], received[...]) + local[...]
    cdf = 0.5 * (1.0 + lax.erf(pre * inv_root_two))
    density = jnp.exp(-0.5 * pre * pre) * inv_root_two_pi
    activated_out[...] = (pre * cdf).astype(BF16)
    grad = (cotangent[...].astype(F32) * (cdf + pre * density)).astype(BF16)
    back = dot(synthesis_rows[...], grad)
    rounded = grad
    grad = grad.astype(F32)
    first, last = edge_layers(grad)
    spread[0:NY, :] = jnp.zeros((NY, 3 * LANES), BF16)
    spread[NY + CELLS : 2 * NY + CELLS, :] = jnp.zeros((NY, 3 * LANES), BF16)
    spread[NY : NY + CELLS, 0:LANES] = from_above(grad).astype(BF16)
    spread[NY : NY + CELLS, LANES : 2 * LANES] = grad.astype(BF16)
    spread[NY : NY + CELLS, 2 * LANES :] = from_below(grad).astype(BF16)
    half = LANES // 2
    low = low_lanes(half)
    twice = {}
    for b in range(3):
        product = dot(lanes[...], spread[NY * (2 - b) : NY * (2 - b) + CELLS, :])
        for c in range(3):
            for a in range(3):
                blocks = [BLOCK_OF_DEPTH[out + a - 1] * half for out in range(2)]
                columns = slice(c * LANES, (c + 1) * LANES)
                both = jnp.where(
                    low,
                    product[blocks[0] : blocks[0] + half, columns],
                    product[blocks[1] : blocks[1] + half, columns],
                )
                twice[a * 9 + b * 3 + c] = both + swap_halves(both)
    pairs = []
    for k in range(0, OFFSETS, 2):
        pairs.append(jnp.where(low, twice[k], twice.get(k + 1, 0.0)))
    pairs.append(jnp.zeros((TERM_ROWS - half * len(pairs), LANES), F32))
    terms = jnp.concatenate(pairs, axis=0)
    if terms_in_slab:
        slab_store(back_out, back, terms)
    else:
        back_out[...] = back.astype(BF16)
        terms_out[...] = terms.astype(BF16)
    grad_out[...] = rounded
    first_out[...] = first
    last_out[...] = last


def slab_store(slab, modes, terms):
    owners = slab.shape[0]
    modes = modes.reshape(owners, 8, LANES)
    terms = terms.reshape(owners, -1, LANES)
    slab[...] = jnp.concatenate([modes, terms], axis=1).astype(BF16)


def slab_load(slab):
    whole = slab[...].astype(F32)
    return whole[:, 0:8, :].reshape(-1, LANES), whole[:, 8:, :]


def unmix_kernel(snaps, slabs, scale, received, terms, gather, weights, scatter, grad_out, mixed_out, sums_out):
    in_slab = terms is None
    if in_slab:
        modes, terms = slab_load(received)
    else:
        modes, terms = received[...].astype(F32), terms[...].astype(F32)
    mixed = to_depth(modes, gather[...], snaps, slabs)
    mixed_out[...] = mixed.astype(BF16)
    count = mixed.shape[0]
    rows = GROUP * snaps
    depth = GROUP * LANES // 4
    sums = jnp.sum(terms, axis=0) * scale
    own = own_block(rows)
    placed = jnp.where(own_half(count), mixed, 0.0).astype(BF16)
    pieces = []
    for g in range(count // rows):
        full = dot(
            placed[g * rows : (g + 1) * rows, :], weights[g * depth : (g + 1) * depth, :], (1, 1)
        )
        full = jnp.where(own, full, 0.0)
        pieces.append(sum(full[:, k : k + LANES] for k in range(0, depth, LANES)))
    coef = jnp.concatenate(pieces, axis=0)
    coef = coef + swap_halves(coef)
    grad = from_depth(coef, scatter[...], snaps, slabs)
    if in_slab:
        owners = received.shape[0]
        share = sums.shape[0]
        slab_store(
            grad_out, grad, jnp.broadcast_to(sums[None], (owners, share, LANES)).reshape(-1, LANES)
        )
    else:
        grad_out[...] = grad.astype(BF16)
        sums_out[...] = sums


def weight_kernel(snaps, diagonal, mixed, out):
    rows = GROUP * snaps
    depth = GROUP * LANES // 4
    half = LANES // 2
    first = mode_in_group(rows, depth) < GROUP // 2
    for g in range(diagonal.shape[0] // rows):
        span = slice(g * rows, (g + 1) * rows)
        blocks = diagonal[span, :].astype(F32)
        blocks = [jnp.where(first, blocks, 0.0), jnp.where(first, 0.0, blocks)]
        blocks = jnp.concatenate(blocks, axis=1).astype(BF16)
        out[2 * g * depth : 2 * (g + 1) * depth, :] = dot(blocks, mixed[span, 0:half], (0, 0))


def output_kernel(cells, out):
    out[...] = to_field(cells[...])


def local_grad_kernel(grad, before, after, weights, out, padded, table):
    banded_backward(weights, table)
    pad_cells(padded, grad[...], beside_layers(before[...], after[...]))

    def store(start, result):
        out[start : start + STEP, :] = result

    stencil(padded, table, True, store)


def finish_kernel(received, sums, synthesis, local, grad_out, stencil_out):
    in_slab = sums is None
    if in_slab:
        modes, terms = slab_load(received)
        terms = terms.reshape(TERM_ROWS, LANES)
    else:
        modes, terms = received[...], sums[...].astype(F32)
    cells = (dot(synthesis[...], modes.astype(BF16)) + local[...]).astype(BF16)
    grad_out[...] = to_field(cells)
    half = LANES // 2
    for k in range(OFFSETS):
        row = (k // 2) * half
        lane = (k % 2) * half
        stencil_out[k] = terms[row : row + half, lane : lane + half]


def shape(dims, dtype):
    return jax.ShapeDtypeStruct(dims, dtype)


class Staged:
    def __init__(self, source, buffer, semaphore):
        self.copy = pltpu.make_async_copy(source, buffer, semaphore)
        self.buffer = buffer
        self.copy.start()
        self.ready = False

    def load(self):
        if not self.ready:
            self.copy.wait()
            self.ready = True

    def __getitem__(self, index):
        self.load()
        return self.buffer[index]


class Sent:
    def __init__(self, target, buffer, semaphore):
        self.copy = pltpu.make_async_copy(buffer, target, semaphore)
        self.buffer = buffer

    def __setitem__(self, index, value):
        self.buffer[index] = value
        self.copy.start()

    def __getitem__(self, index):
        return self.buffer[index]

    @property
    def shape(self):
        return self.buffer.shape


def row_count(rows):
    return rows.stop - rows.start if isinstance(rows, slice) else rows


def run(
    body, outs, *operands, staged=(), sent=(), moved=(), plain=(), slots=(), scratch=(), flops=0, limit=VMEM_BYTES
):
    given = [k for k, operand in enumerate(operands) if operand is not None]
    made = [k for k, out in enumerate(outs) if out is not None]

    def rows_of(chosen, places, arrays):
        chosen = {k: chosen[k] if isinstance(chosen, dict) else None for k in places if k in chosen}
        return {k: rows or arrays[k].shape[0] for k, rows in chosen.items()}

    moved = dict(moved)
    slots = dict(slots)
    staged = rows_of(staged, given, operands)
    sent = rows_of(sent, made, outs)

    def kernel(*refs):
        refs = list(refs)

        def take(count):
            taken = refs[:count]
            del refs[:count]
            return taken

        def part(ref, rows):
            if isinstance(rows, slice):
                return ref.at[rows]
            return ref if ref.shape[0] == rows else ref.at[0:rows]

        filled = dict(zip(given, take(len(given))))
        take(len(slots))
        kept = dict(zip(made, take(len(made))))
        own = take(len(scratch))
        copies = []
        for place, (k, out) in enumerate(moved.items()):
            source, target = filled.pop(k), kept.pop(out)
            rows = min(source.shape[0], target.shape[0])
            semaphore = refs[-1].at[len(staged) + len(sent) + place]
            copies.append(
                pltpu.make_async_copy(part(source, rows), part(target, rows), semaphore)
            )
        for place, (k, buffer) in enumerate(zip(staged, take(len(staged)))):
            filled[k] = Staged(part(filled[k], staged[k]), buffer, refs[-1].at[place])
        for place, (k, buffer) in enumerate(zip(sent, take(len(sent)))):
            kept[k] = Sent(part(kept[k], sent[k]), buffer, refs[-1].at[len(staged) + place])
        for copy in copies:
            copy.start()
        body(
            *[filled.get(k) for k in range(len(operands)) if k not in moved],
            *[kept.get(k) for k in range(len(outs)) if k not in moved.values()],
            *own,
        )
        for k in staged:
            filled[k].load()
        for k in sent:
            kept[k].copy.wait()
        for copy in copies:
            copy.wait()

    arrays = [operands[k] for k in given]
    results = [outs[k] for k in made]
    size = sum(x.size * x.dtype.itemsize for x in (*arrays, *results))
    in_vmem = pl.BlockSpec(memory_space=pltpu.VMEM)
    in_hbm = pl.BlockSpec(memory_space=pltpu.HBM)
    buffers = [(operands[k], rows) for k, rows in staged.items()]
    buffers += [(outs[k], rows) for k, rows in sent.items()]
    buffers = [pltpu.VMEM((row_count(rows), *x.shape[1:]), x.dtype) for x, rows in buffers]
    if len(buffers) + len(moved) > 0:
        buffers.append(pltpu.SemaphoreType.DMA((len(buffers) + len(moved),)))
    results = pl.pallas_call(
        kernel,
        out_shape=results,
        in_specs=[in_hbm if k in staged or k in moved else in_vmem for k in given]
        + [in_hbm] * len(slots),
        out_specs=[in_hbm if k in sent or k in plain else in_vmem for k in made],
        input_output_aliases={len(given) + at: made.index(k) for at, k in enumerate(slots)},
        scratch_shapes=[*scratch, *buffers],
        compiler_params=pltpu.CompilerParams(vmem_limit_bytes=limit),
        cost_estimate=pl.CostEstimate(flops=flops, bytes_accessed=size, transcendentals=0),
        name=body.__name__ if hasattr(body, "__name__") else body.func.__name__,
    )(*arrays, *slots.values())
    results = dict(zip(made, results))
    return [results.get(k) for k in range(len(outs))]


def exchange(values):
    return lax.all_to_all(values, ("space", "batch"), split_axis=0, concat_axis=0, tiled=True)


def neighbours(first, last):
    ends = lax.axis_size("space") - 1
    before = lax.ppermute(last, "space", [(i, i + 1) for i in range(ends)])
    after = lax.ppermute(first, "space", [(i + 1, i) for i in range(ends)])
    return before, after


def shards(snapshots, cotangent, mode_weight, conv_weight):
    batches = lax.axis_size("batch")
    slabs = lax.axis_size("space")
    devices = batches * slabs
    _, channels, layers, plane = snapshots.shape
    modes = mode_weight.shape[0] * mode_weight.shape[1]
    half = LANES // 2
    assert channels == half and layers == 2 and plane == CELLS
    plane_rows = devices * modes
    count = modes * 2 * KZ * batches
    in_slab = modes == 8 and devices * 32 == TERM_ROWS

    analysis, synthesis = plane_tables(batches, slabs)
    gather, scatter, gather_back, scatter_back = depth_tables(slabs, layers, modes)
    weights = mode_weight.reshape(modes * 2 * KZ * channels, channels)
    taps = conv_weight.reshape(OFFSETS, channels, channels)
    field = shape((channels, layers, plane), BF16)
    wide = shape((CELLS, LANES), BF16)
    edge = shape((CELLS // 2, LANES), BF16)
    plane_modes = shape((plane_rows, LANES), BF16)
    padded = pltpu.VMEM((CELLS + 2 * NY, 2 * LANES), BF16)

    def send(values):
        return exchange(values.reshape(devices, modes, LANES)).reshape(plane_rows, LANES)

    packed = shape((weights.shape[0] // 2, LANES), BF16)
    share = weights.shape[0] // CHUNKS
    to_send = shape((devices, modes, LANES), BF16) if modes % 8 == 0 else plane_modes
    cells, coef, first, last, kept_weights, slot = run(
        analyse_kernel,
        [
            wide,
            plane_modes,
            edge,
            edge,
            shape((HBM_BYTES // (2 * LANES), LANES), BF16),
            to_send,
        ],
        snapshots.reshape(field.shape),
        analysis,
        *[weights] * CHUNKS,
        staged={0: None, 1: None} | {2 + k: slice(k * share, (k + 1) * share) for k in range(CHUNKS)},
        sent=(0, 1, 2, 3),
        plain=(4, 5),
        scratch=[pltpu.VMEM(packed.shape, BF16), pltpu.SemaphoreType.DMA((CHUNKS,))],
        limit=WHOLE_VMEM,
        flops=10**8,
    )
    coef = send(coef)
    (packed_weights,) = run(fetch_kernel, [packed], kept_weights, moved={0: 0})
    before, after = neighbours(first, last)
    local, lanes, outer_cells = run(
        local_kernel,
        [shape((CELLS, LANES), F32), shape((HBM_BYTES // (2 * CELLS), CELLS), BF16), wide],
        cells,
        before,
        after,
        cotangent.reshape(field.shape),
        taps,
        sent={1: 2 * LANES},
        scratch=[padded, pltpu.VMEM((3, 2 * LANES, 3 * LANES), BF16)],
        flops=7 * 10**8,
    )
    back, diagonal = run(
        functools.partial(mix_kernel, batches, slabs),
        [to_send, shape((count, GROUP * half // 2), BF16)],
        coef,
        gather,
        packed_weights,
        scatter,
        sent=(0, 1),
        slots={0: slot},
        flops=4 * 10**8,
    )
    back = send(back)
    slab = shape((devices, 8 + TERM_ROWS // devices, LANES), BF16)
    activated, grad, first, last, back, terms = run(
        functools.partial(activate_kernel, in_slab),
        [
            wide,
            shape((HBM_BYTES // (2 * LANES), LANES), BF16),
            edge,
            edge,
            slab if in_slab else plane_modes,
            None if in_slab else shape((TERM_ROWS, LANES), BF16),
        ],
        back,
        np.ascontiguousarray(synthesis.T),
        synthesis,
        local,
        outer_cells,
        lanes,
        staged={5: 2 * LANES},
        sent={1: CELLS, 2: None, 3: None, 4: None},
        scratch=[pltpu.VMEM((CELLS + 2 * NY, 3 * LANES), BF16)],
        flops=10**9,
    )
    if in_slab:
        back = exchange(back)
    else:
        back = send(back)
        terms = exchange(terms.reshape(devices, TERM_ROWS // devices, LANES))
    before, after = neighbours(first, last)
    activated, packed_weights = run(
        output_kernel,
        [field, packed],
        activated,
        kept_weights,
        moved={1: 1},
        flops=10**8,
    )
    back, before, after, activated, packed_weights = lax.optimization_barrier(
        (back, before, after, activated, packed_weights)
    )
    scale = 1.0 / math.sqrt(batches * slabs * layers * plane)
    grad_modes, mixed_grad, sums = run(
        functools.partial(unmix_kernel, batches, slabs, scale),
        [
            slab if in_slab else plane_modes,
            shape((count, LANES), BF16),
            None if in_slab else shape((TERM_ROWS // devices, LANES), F32),
        ],
        back,
        None if in_slab else terms,
        gather_back,
        packed_weights,
        scatter_back,
        sent=(0,),
        flops=4 * 10**8,
    )
    if in_slab:
        grad_modes = exchange(grad_modes)
    else:
        grad_modes = send(grad_modes)
        sums = lax.all_gather(sums, ("space", "batch"), axis=0, tiled=True)
    (local,) = run(
        local_grad_kernel,
        [shape((CELLS, LANES), F32)],
        grad,
        before,
        after,
        taps,
        staged={0: CELLS},
        scratch=[padded, pltpu.VMEM((3, 3 * LANES, 2 * LANES), BF16)],
        flops=7 * 10**8,
    )
    (mode_gradient,) = run(
        functools.partial(weight_kernel, batches),
        [shape((modes * 2 * KZ * channels, channels), F32)],
        diagonal,
        mixed_grad,
        flops=4 * 10**8,
    )
    input_gradient, conv_gradient = run(
        finish_kernel,
        [field, shape((OFFSETS, channels, channels), F32)],
        grad_modes,
        sums,
        np.ascontiguousarray(analysis.T),
        local,
        flops=10**8,
    )
    return (
        activated.reshape(snapshots.shape),
        input_gradient.reshape(snapshots.shape),
        mode_gradient.reshape(mode_weight.shape),
        conv_gradient.reshape(conv_weight.shape),
    )


def solution(mesh):
    in_specs = (
        P("batch", None, "space", None),
        P("batch", None, "space", None),
        P("batch", "space", None, None, None),
        P(),
    )
    out_specs = (
        P("batch", None, "space", None),
        P("batch", None, "space", None),
        P("batch", "space", None, None, None),
        P(),
    )
    return jax.shard_map(shards, mesh=mesh, in_specs=in_specs, out_specs=out_specs, check_vma=False)
```

```python
import functools
import math

import jax
import jax.numpy as jnp
import ml_dtypes
import numpy as np
from jax import lax
from jax.experimental import pallas as pl
from jax.experimental.pallas import tpu as pltpu
from jax.sharding import PartitionSpec as P

KX = 8
KY = 8
KZ = 12
NX = 32
NY = 32
CELLS = NX * NY
LANES = 128
GROUP = 8
OFFSETS = 27
TERM_ROWS = 1024
CHUNKS = 3
VMEM_BYTES = 40 * 1024 * 1024
WHOLE_VMEM = 65000 * 1024
HBM_BYTES = 100 * 1024 * 256

F32 = jnp.float32
BF16 = jnp.bfloat16
inv_root_two = 1.0 / math.sqrt(2.0)
inv_root_two_pi = 1.0 / math.sqrt(2.0 * math.pi)


def basis_rows(half_count, length):
    row = np.arange(2 * half_count)[:, None]
    cell = np.arange(length)[None, :]
    frequency = np.where(row < half_count, row, row - half_count + 1)
    phases = (frequency * cell % length).astype(np.float32) * np.float32(2.0 * math.pi / length)
    return np.where(row < half_count, np.cos(phases), np.sin(phases)).astype(np.float32)


def plane_tables(batches, slabs):
    outer = (basis_rows(KX, NX)[:, None, :, None] * basis_rows(KY, NY)[None, :, None, :]).reshape(
        2 * KX, 2 * KY, CELLS
    )
    outer = outer.reshape(batches, 2 * KX // batches, slabs, 2 * KY // slabs, CELLS)
    outer = outer.transpose(2, 0, 1, 3, 4).reshape(4 * KX * KY, CELLS)
    analysis = (outer * np.float32(2.0 / math.sqrt(CELLS))).astype(ml_dtypes.bfloat16)
    synthesis = (outer * np.float32(2.0 / math.sqrt(4 * KX * KY))).astype(ml_dtypes.bfloat16)
    return analysis, synthesis


def depth_tables(slabs, layers, modes):
    rows = basis_rows(KZ, slabs * layers)
    analysis = (rows * np.float32(math.sqrt(2.0 / (slabs * layers)))).astype(ml_dtypes.bfloat16)
    synthesis = (rows * np.float32(math.sqrt(2.0 / (2 * KZ)))).astype(ml_dtypes.bfloat16)

    def spread(table, order):
        table = table.astype(np.float32).reshape(2 * KZ, slabs, layers)
        full = np.einsum("psz,mn->" + order, table, np.eye(modes, dtype=np.float32))
        return full.astype(ml_dtypes.bfloat16)

    def gathered(table):
        return spread(table, "mpzsn").reshape(modes * 2 * KZ, layers * slabs * modes)

    def scattered(table):
        return spread(table, "snzmp").reshape(slabs * modes, layers * modes * 2 * KZ)

    return gathered(analysis), scattered(synthesis), gathered(synthesis), scattered(analysis)


def dot(left, right, contract=(1, 0)):
    return lax.dot_general(
        left, right, (((contract[0],), (contract[1],)), ((), ())), preferred_element_type=F32
    )


def turn_table():
    row = lax.broadcasted_iota(jnp.int32, (LANES, LANES), 0)
    column = lax.broadcasted_iota(jnp.int32, (LANES, LANES), 1)
    return jnp.where(column == row % 2 * (LANES // 2) + row // 2, 1.0, 0.0).astype(BF16)


def to_cells(field):
    return dot(field.reshape(LANES, CELLS), turn_table(), (0, 0))


def to_field(cells):
    return dot(turn_table(), cells, (1, 1)).astype(BF16).reshape(LANES // 2, 2, CELLS)


def low_lanes(rows):
    return lax.broadcasted_iota(jnp.int32, (rows, LANES), 1) < LANES // 2


def swap_halves(values):
    return pltpu.roll(values, LANES // 2, 1)


def doubled(values):
    low = low_lanes(values.shape[0])
    swapped = swap_halves(values)
    return jnp.concatenate(
        [jnp.where(low, values, swapped), jnp.where(low, swapped, values)], axis=0
    )


def halved(values):
    low = low_lanes(values.shape[0])
    return jnp.concatenate([jnp.where(low, values, 0.0), jnp.where(low, 0.0, values)], axis=0)


def edge_layers(cells_first):
    top = cells_first[: CELLS // 2]
    bottom = cells_first[CELLS // 2 :]
    low = low_lanes(CELLS // 2)
    first = jnp.where(low, top, swap_halves(bottom))
    last = jnp.where(low, swap_halves(top), bottom)
    return first.astype(BF16), last.astype(BF16)


def beside_layers(before, after):
    before = before.astype(F32)
    after = after.astype(F32)
    low = low_lanes(CELLS // 2)
    top = jnp.where(low, before, swap_halves(after))
    bottom = jnp.where(low, swap_halves(before), after)
    return jnp.concatenate([top, bottom], axis=0).astype(BF16)


def y_cells(rows):
    return lax.broadcasted_iota(jnp.int32, (rows, LANES), 0) % NY


def from_below(values):
    return jnp.where(y_cells(values.shape[0]) == 0, 0.0, pltpu.roll(values, 1, 0))


def from_above(values):
    rows = values.shape[0]
    return jnp.where(y_cells(rows) == NY - 1, 0.0, pltpu.roll(values, rows - 1, 0))


def pad_cells(padded, own, beside):
    width = own.shape[1] + beside.shape[1]
    padded[0:NY, :] = jnp.zeros((NY, width), BF16)
    padded[NY + CELLS : 2 * NY + CELLS, :] = jnp.zeros((NY, width), BF16)
    padded[NY : NY + CELLS, 0 : own.shape[1]] = own
    padded[NY : NY + CELLS, own.shape[1] :] = beside


BLOCK_OF_DEPTH = {-1: 2, 0: 0, 1: 1, 2: 3}
STEP = 256


def stencil(padded, table, transposed, store):
    for start in range(0, CELLS, STEP):
        total = None
        for b in range(3):
            cells = padded[start + NY * b : start + NY * b + STEP, :]
            term = dot(cells, table[b], (1, 1) if transposed else (1, 0))
            total = term if total is None else total + term
        result = (
            from_below(total[:, 0:LANES])
            + total[:, LANES : 2 * LANES]
            + from_above(total[:, 2 * LANES :])
        )
        store(start, result)


def banded_forward(weights, table):
    half = LANES // 2
    for b in range(3):
        for c in range(3):
            for depth, block in BLOCK_OF_DEPTH.items():
                parts = []
                for out in range(2):
                    a = depth - out + 1
                    if 0 <= a < 3:
                        parts.append(weights[a * 9 + b * 3 + c])
                    else:
                        parts.append(jnp.zeros((half, half), BF16))
                table[b, block * half : (block + 1) * half, c * LANES : (c + 1) * LANES] = (
                    jnp.concatenate(parts, axis=1)
                )


def banded_backward(weights, table):
    half = LANES // 2
    for b in range(3):
        for c in range(3):
            for out in range(2):
                for pair in ((0, 1), (-1, 2)):
                    parts = []
                    for depth in pair:
                        a = depth - out + 1
                        if 0 <= a < 3:
                            parts.append(weights[(2 - a) * 9 + (2 - b) * 3 + 2 - c])
                        else:
                            parts.append(jnp.zeros((half, half), BF16))
                    row = c * LANES + out * half
                    column = BLOCK_OF_DEPTH[pair[0]] * half
                    table[b, row : row + half, column : column + LANES] = jnp.concatenate(
                        parts, axis=1
                    )


def analyse_kernel(field, analysis, *refs):
    weights = refs[:CHUNKS]
    coef_out, first_out, last_out, packed_out, _, buffer, semaphores = refs[CHUNKS:]
    cells = to_cells(field[...])
    rounded = cells.astype(BF16)
    coef_out[...] = dot(analysis[...], rounded).astype(BF16)
    first, last = edge_layers(cells)
    first_out[...] = first
    last_out[...] = last
    rows = GROUP * LANES // 4
    share = buffer.shape[0] // CHUNKS
    copies = []
    for place, part in enumerate(weights):
        for g in range(share // rows):
            pair = [part[k * rows : (k + 1) * rows, :] for k in (2 * g, 2 * g + 1)]
            row = place * share + g * rows
            buffer[row : row + rows, :] = jnp.concatenate(pair, axis=1)
        span = slice(place * share, (place + 1) * share)
        copies.append(
            pltpu.make_async_copy(buffer.at[span], packed_out.at[span], semaphores.at[place])
        )
        copies[-1].start()
    for copy in copies:
        copy.wait()


def local_kernel(
    first, last, before, after, cotangent, weights, local_out, lanes_out, cotangent_out, padded, table
):
    banded_forward(weights, table)
    beside = beside_layers(before[...], after[...])
    own = beside_layers(first[...], last[...])
    pad_cells(padded, own, beside)

    def store(start, result):
        local_out[start : start + STEP, :] = result

    stencil(padded, table, False, store)
    whole = jnp.concatenate([own.astype(F32), beside.astype(F32)], axis=1)
    lanes_out[...] = whole.T.astype(BF16)
    cotangent_out[...] = to_cells(cotangent[...]).astype(BF16)


def fetch_kernel():
    pass


def mode_in_group(rows, lanes):
    return lax.broadcasted_iota(jnp.int32, (rows, lanes), 0) % GROUP


def own_block(rows):
    width = GROUP * LANES // 4
    lane = lax.broadcasted_iota(jnp.int32, (rows, width), 1)
    return mode_in_group(rows, width) % (GROUP // 2) == lane // (LANES // 2)


def own_half(rows):
    return (mode_in_group(rows, LANES) < GROUP // 2) == low_lanes(rows)


def to_depth(modes, table, snaps, slabs):
    modes = modes.reshape(slabs, snaps, -1, LANES)
    both = [doubled(modes[:, b].reshape(-1, LANES)) for b in range(snaps)]
    result = dot(table, jnp.concatenate(both, axis=1).astype(BF16))
    return jnp.concatenate(
        [
            result[g : g + GROUP, b * LANES : (b + 1) * LANES]
            for g in range(0, result.shape[0], GROUP)
            for b in range(snaps)
        ],
        axis=0,
    )


def from_depth(modes, table, snaps, slabs):
    count = modes.shape[0] // GROUP
    both = []
    for b in range(snaps):
        own = [modes[g * GROUP : (g + 1) * GROUP] for g in range(b, count, snaps)]
        both.append(halved(jnp.concatenate(own, axis=0)))
    result = dot(table, jnp.concatenate(both, axis=1).astype(BF16))
    own = [
        result[:, b * LANES : (b + 1) * LANES].reshape(slabs, -1, LANES) for b in range(snaps)
    ]
    return jnp.stack(own, axis=1).reshape(-1, LANES)


def mix_kernel(snaps, slabs, received, gather, weights, scatter, back_out, diagonal_out):
    coef = to_depth(received[...].astype(F32), gather[...], snaps, slabs)
    count = coef.shape[0]
    wide = jnp.concatenate([coef] * (GROUP // 4), axis=1)
    diagonal = jnp.where(own_block(count), wide, 0.0).astype(BF16)
    diagonal_out[...] = diagonal
    rows = GROUP * snaps
    depth = GROUP * LANES // 4
    mixed = jnp.concatenate(
        [
            dot(diagonal[g * rows : (g + 1) * rows, :], weights[g * depth : (g + 1) * depth, :])
            for g in range(count // rows)
        ],
        axis=0,
    )
    mixed = jnp.where(own_half(count), mixed, swap_halves(mixed))
    back = from_depth(mixed, scatter[...], snaps, slabs).astype(BF16)
    back_out[...] = back.reshape(back_out.shape)


def activate_kernel(
    terms_in_slab,
    received,
    synthesis,
    synthesis_rows,
    local,
    cotangent,
    lanes,
    activated_out,
    first_out,
    last_out,
    back_out,
    terms_out,
    spread,
):
    pre = dot(synthesis[...], received[...]) + local[...]
    cdf = 0.5 * (1.0 + lax.erf(pre * inv_root_two))
    density = jnp.exp(-0.5 * pre * pre) * inv_root_two_pi
    activated_out[...] = (pre * cdf).astype(BF16)
    grad = (cotangent[...].astype(F32) * (cdf + pre * density)).astype(BF16)
    back = dot(synthesis_rows[...], grad)
    grad = grad.astype(F32)
    first, last = edge_layers(grad)
    spread[0:NY, :] = jnp.zeros((NY, 3 * LANES), BF16)
    spread[NY + CELLS : 2 * NY + CELLS, :] = jnp.zeros((NY, 3 * LANES), BF16)
    spread[NY : NY + CELLS, 0:LANES] = from_above(grad).astype(BF16)
    spread[NY : NY + CELLS, LANES : 2 * LANES] = grad.astype(BF16)
    spread[NY : NY + CELLS, 2 * LANES :] = from_below(grad).astype(BF16)
    half = LANES // 2
    low = low_lanes(half)
    twice = {}
    for b in range(3):
        product = dot(lanes[...], spread[NY * (2 - b) : NY * (2 - b) + CELLS, :])
        for c in range(3):
            for a in range(3):
                blocks = [BLOCK_OF_DEPTH[out + a - 1] * half for out in range(2)]
                columns = slice(c * LANES, (c + 1) * LANES)
                both = jnp.where(
                    low,
                    product[blocks[0] : blocks[0] + half, columns],
                    product[blocks[1] : blocks[1] + half, columns],
                )
                twice[a * 9 + b * 3 + c] = both + swap_halves(both)
    pairs = []
    for k in range(0, OFFSETS, 2):
        pairs.append(jnp.where(low, twice[k], twice.get(k + 1, 0.0)))
    pairs.append(jnp.zeros((TERM_ROWS - half * len(pairs), LANES), F32))
    terms = jnp.concatenate(pairs, axis=0)
    if terms_in_slab:
        slab_store(back_out, back, terms)
    else:
        back_out[...] = back.astype(BF16)
        terms_out[...] = terms.astype(BF16)
    first_out[...] = first
    last_out[...] = last


def slab_store(slab, modes, terms):
    owners = slab.shape[0]
    modes = modes.reshape(owners, 8, LANES)
    terms = terms.reshape(owners, -1, LANES)
    slab[...] = jnp.concatenate([modes, terms], axis=1).astype(BF16)


def slab_load(slab):
    whole = slab[...].astype(F32)
    return whole[:, 0:8, :].reshape(-1, LANES), whole[:, 8:, :]


def unmix_kernel(snaps, slabs, scale, received, terms, gather, weights, scatter, grad_out, mixed_out, sums_out):
    in_slab = terms is None
    if in_slab:
        modes, terms = slab_load(received)
    else:
        modes, terms = received[...].astype(F32), terms[...].astype(F32)
    mixed = to_depth(modes, gather[...], snaps, slabs)
    mixed_out[...] = mixed.astype(BF16)
    count = mixed.shape[0]
    rows = GROUP * snaps
    depth = GROUP * LANES // 4
    sums = jnp.sum(terms, axis=0) * scale
    own = own_block(rows)
    placed = jnp.where(own_half(count), mixed, 0.0).astype(BF16)
    pieces = []
    for g in range(count // rows):
        full = dot(
            placed[g * rows : (g + 1) * rows, :], weights[g * depth : (g + 1) * depth, :], (1, 1)
        )
        full = jnp.where(own, full, 0.0)
        pieces.append(sum(full[:, k : k + LANES] for k in range(0, depth, LANES)))
    coef = jnp.concatenate(pieces, axis=0)
    coef = coef + swap_halves(coef)
    grad = from_depth(coef, scatter[...], snaps, slabs)
    if in_slab:
        owners = received.shape[0]
        share = sums.shape[0]
        slab_store(
            grad_out, grad, jnp.broadcast_to(sums[None], (owners, share, LANES)).reshape(-1, LANES)
        )
    else:
        grad_out[...] = grad.astype(BF16)
        sums_out[...] = sums


def weight_kernel(snaps, diagonal, mixed, out):
    rows = GROUP * snaps
    depth = GROUP * LANES // 4
    half = LANES // 2
    first = mode_in_group(rows, depth) < GROUP // 2
    for g in range(diagonal.shape[0] // rows):
        span = slice(g * rows, (g + 1) * rows)
        blocks = diagonal[span, :].astype(F32)
        blocks = [jnp.where(first, blocks, 0.0), jnp.where(first, 0.0, blocks)]
        blocks = jnp.concatenate(blocks, axis=1).astype(BF16)
        out[2 * g * depth : 2 * (g + 1) * depth, :] = dot(blocks, mixed[span, 0:half], (0, 0))


def output_kernel(cells, out):
    out[...] = to_field(cells[...])


def local_grad_kernel(first, last, before, after, weights, out, padded, table):
    banded_backward(weights, table)
    own = beside_layers(first[...], last[...])
    pad_cells(padded, own, beside_layers(before[...], after[...]))

    def store(start, result):
        out[start : start + STEP, :] = result

    stencil(padded, table, True, store)


def finish_kernel(received, sums, synthesis, local, grad_out, stencil_out):
    in_slab = sums is None
    if in_slab:
        modes, terms = slab_load(received)
        terms = terms.reshape(TERM_ROWS, LANES)
    else:
        modes, terms = received[...], sums[...].astype(F32)
    cells = (dot(synthesis[...], modes.astype(BF16)) + local[...]).astype(BF16)
    grad_out[...] = to_field(cells)
    half = LANES // 2
    for k in range(OFFSETS):
        row = (k // 2) * half
        lane = (k % 2) * half
        stencil_out[k] = terms[row : row + half, lane : lane + half]


def shape(dims, dtype):
    return jax.ShapeDtypeStruct(dims, dtype)


class Staged:
    def __init__(self, source, buffer, semaphore):
        self.copy = pltpu.make_async_copy(source, buffer, semaphore)
        self.buffer = buffer
        self.copy.start()
        self.ready = False

    def load(self):
        if not self.ready:
            self.copy.wait()
            self.ready = True

    def __getitem__(self, index):
        self.load()
        return self.buffer[index]


class Sent:
    def __init__(self, target, buffer, semaphore):
        self.copy = pltpu.make_async_copy(buffer, target, semaphore)
        self.buffer = buffer

    def __setitem__(self, index, value):
        self.buffer[index] = value
        self.copy.start()

    def __getitem__(self, index):
        return self.buffer[index]

    @property
    def shape(self):
        return self.buffer.shape


def row_count(rows):
    return rows.stop - rows.start if isinstance(rows, slice) else rows


def run(
    body, outs, *operands, staged=(), sent=(), moved=(), plain=(), slots=(), scratch=(), flops=0, limit=VMEM_BYTES
):
    given = [k for k, operand in enumerate(operands) if operand is not None]
    made = [k for k, out in enumerate(outs) if out is not None]

    def rows_of(chosen, places, arrays):
        chosen = {k: chosen[k] if isinstance(chosen, dict) else None for k in places if k in chosen}
        return {k: rows or arrays[k].shape[0] for k, rows in chosen.items()}

    moved = dict(moved)
    slots = dict(slots)
    staged = rows_of(staged, given, operands)
    sent = rows_of(sent, made, outs)

    def kernel(*refs):
        refs = list(refs)

        def take(count):
            taken = refs[:count]
            del refs[:count]
            return taken

        def part(ref, rows):
            if isinstance(rows, slice):
                return ref.at[rows]
            return ref if ref.shape[0] == rows else ref.at[0:rows]

        filled = dict(zip(given, take(len(given))))
        take(len(slots))
        kept = dict(zip(made, take(len(made))))
        own = take(len(scratch))
        copies = []
        for place, (k, out) in enumerate(moved.items()):
            source, target = filled.pop(k), kept.pop(out)
            rows = min(source.shape[0], target.shape[0])
            semaphore = refs[-1].at[len(staged) + len(sent) + place]
            copies.append(
                pltpu.make_async_copy(part(source, rows), part(target, rows), semaphore)
            )
        for place, (k, buffer) in enumerate(zip(staged, take(len(staged)))):
            filled[k] = Staged(part(filled[k], staged[k]), buffer, refs[-1].at[place])
        for place, (k, buffer) in enumerate(zip(sent, take(len(sent)))):
            kept[k] = Sent(part(kept[k], sent[k]), buffer, refs[-1].at[len(staged) + place])
        for copy in copies:
            copy.start()
        body(
            *[filled.get(k) for k in range(len(operands)) if k not in moved],
            *[kept.get(k) for k in range(len(outs)) if k not in moved.values()],
            *own,
        )
        for k in staged:
            filled[k].load()
        for k in sent:
            kept[k].copy.wait()
        for copy in copies:
            copy.wait()

    arrays = [operands[k] for k in given]
    results = [outs[k] for k in made]
    size = sum(x.size * x.dtype.itemsize for x in (*arrays, *results))
    in_vmem = pl.BlockSpec(memory_space=pltpu.VMEM)
    in_hbm = pl.BlockSpec(memory_space=pltpu.HBM)
    buffers = [(operands[k], rows) for k, rows in staged.items()]
    buffers += [(outs[k], rows) for k, rows in sent.items()]
    buffers = [pltpu.VMEM((row_count(rows), *x.shape[1:]), x.dtype) for x, rows in buffers]
    if len(buffers) + len(moved) > 0:
        buffers.append(pltpu.SemaphoreType.DMA((len(buffers) + len(moved),)))
    results = pl.pallas_call(
        kernel,
        out_shape=results,
        in_specs=[in_hbm if k in staged or k in moved else in_vmem for k in given]
        + [in_hbm] * len(slots),
        out_specs=[in_hbm if k in sent or k in plain else in_vmem for k in made],
        input_output_aliases={len(given) + at: made.index(k) for at, k in enumerate(slots)},
        scratch_shapes=[*scratch, *buffers],
        compiler_params=pltpu.CompilerParams(vmem_limit_bytes=limit),
        cost_estimate=pl.CostEstimate(flops=flops, bytes_accessed=size, transcendentals=0),
        name=body.__name__ if hasattr(body, "__name__") else body.func.__name__,
    )(*arrays, *slots.values())
    results = dict(zip(made, results))
    return [results.get(k) for k in range(len(outs))]


def exchange(values):
    return lax.all_to_all(values, ("space", "batch"), split_axis=0, concat_axis=0, tiled=True)


def neighbours(first, last):
    ends = lax.axis_size("space") - 1
    before = lax.ppermute(last, "space", [(i, i + 1) for i in range(ends)])
    after = lax.ppermute(first, "space", [(i + 1, i) for i in range(ends)])
    return before, after


def shards(snapshots, cotangent, mode_weight, conv_weight):
    batches = lax.axis_size("batch")
    slabs = lax.axis_size("space")
    devices = batches * slabs
    _, channels, layers, plane = snapshots.shape
    modes = mode_weight.shape[0] * mode_weight.shape[1]
    half = LANES // 2
    assert channels == half and layers == 2 and plane == CELLS
    plane_rows = devices * modes
    count = modes * 2 * KZ * batches
    in_slab = modes == 8 and devices * 32 == TERM_ROWS

    analysis, synthesis = plane_tables(batches, slabs)
    gather, scatter, gather_back, scatter_back = depth_tables(slabs, layers, modes)
    weights = mode_weight.reshape(modes * 2 * KZ * channels, channels)
    taps = conv_weight.reshape(OFFSETS, channels, channels)
    field = shape((channels, layers, plane), BF16)
    wide = shape((CELLS, LANES), BF16)
    edge = shape((CELLS // 2, LANES), BF16)
    plane_modes = shape((plane_rows, LANES), BF16)
    padded = pltpu.VMEM((CELLS + 2 * NY, 2 * LANES), BF16)

    def send(values):
        return exchange(values.reshape(devices, modes, LANES)).reshape(plane_rows, LANES)

    packed = shape((weights.shape[0] // 2, LANES), BF16)
    share = weights.shape[0] // CHUNKS
    to_send = shape((devices, modes, LANES), BF16) if modes % 8 == 0 else plane_modes
    coef, first, last, kept_weights, slot = run(
        analyse_kernel,
        [
            plane_modes,
            edge,
            edge,
            shape((HBM_BYTES // (2 * LANES), LANES), BF16),
            to_send,
        ],
        snapshots.reshape(field.shape),
        analysis,
        *[weights] * CHUNKS,
        staged={0: None, 1: None} | {2 + k: slice(k * share, (k + 1) * share) for k in range(CHUNKS)},
        sent=(0, 1, 2),
        plain=(3, 4),
        scratch=[pltpu.VMEM(packed.shape, BF16), pltpu.SemaphoreType.DMA((CHUNKS,))],
        limit=WHOLE_VMEM,
        flops=10**8,
    )
    coef = send(coef)
    (packed_weights,) = run(fetch_kernel, [packed], kept_weights, moved={0: 0})
    before, after = neighbours(first, last)
    local, lanes, outer_cells = run(
        local_kernel,
        [shape((CELLS, LANES), F32), shape((HBM_BYTES // (2 * CELLS), CELLS), BF16), wide],
        first,
        last,
        before,
        after,
        cotangent.reshape(field.shape),
        taps,
        sent={1: 2 * LANES},
        scratch=[padded, pltpu.VMEM((3, 2 * LANES, 3 * LANES), BF16)],
        flops=7 * 10**8,
    )
    back, diagonal = run(
        functools.partial(mix_kernel, batches, slabs),
        [to_send, shape((count, GROUP * half // 2), BF16)],
        coef,
        gather,
        packed_weights,
        scatter,
        sent=(0, 1),
        slots={0: slot},
        flops=4 * 10**8,
    )
    back = send(back)
    slab = shape((devices, 8 + TERM_ROWS // devices, LANES), BF16)
    activated, first, last, back, terms = run(
        functools.partial(activate_kernel, in_slab),
        [
            wide,
            edge,
            edge,
            slab if in_slab else plane_modes,
            None if in_slab else shape((TERM_ROWS, LANES), BF16),
        ],
        back,
        np.ascontiguousarray(synthesis.T),
        synthesis,
        local,
        outer_cells,
        lanes,
        staged={5: 2 * LANES},
        sent=(1, 2, 3),
        scratch=[pltpu.VMEM((CELLS + 2 * NY, 3 * LANES), BF16)],
        flops=10**9,
    )
    if in_slab:
        back = exchange(back)
    else:
        back = send(back)
        terms = exchange(terms.reshape(devices, TERM_ROWS // devices, LANES))
    before, after = neighbours(first, last)
    activated, packed_weights = run(
        output_kernel,
        [field, packed],
        activated,
        kept_weights,
        moved={1: 1},
        flops=10**8,
    )
    back, before, after, activated, packed_weights = lax.optimization_barrier(
        (back, before, after, activated, packed_weights)
    )
    scale = 1.0 / math.sqrt(batches * slabs * layers * plane)
    grad_modes, mixed_grad, sums = run(
        functools.partial(unmix_kernel, batches, slabs, scale),
        [
            slab if in_slab else plane_modes,
            shape((count, LANES), BF16),
            None if in_slab else shape((TERM_ROWS // devices, LANES), F32),
        ],
        back,
        None if in_slab else terms,
        gather_back,
        packed_weights,
        scatter_back,
        sent=(0,),
        flops=4 * 10**8,
    )
    if in_slab:
        grad_modes = exchange(grad_modes)
    else:
        grad_modes = send(grad_modes)
        sums = lax.all_gather(sums, ("space", "batch"), axis=0, tiled=True)
    (local,) = run(
        local_grad_kernel,
        [shape((CELLS, LANES), F32)],
        first,
        last,
        before,
        after,
        taps,
        scratch=[padded, pltpu.VMEM((3, 3 * LANES, 2 * LANES), BF16)],
        flops=7 * 10**8,
    )
    (mode_gradient,) = run(
        functools.partial(weight_kernel, batches),
        [shape((modes * 2 * KZ * channels, channels), F32)],
        diagonal,
        mixed_grad,
        flops=4 * 10**8,
    )
    input_gradient, conv_gradient = run(
        finish_kernel,
        [field, shape((OFFSETS, channels, channels), F32)],
        grad_modes,
        sums,
        np.ascontiguousarray(analysis.T),
        local,
        flops=10**8,
    )
    return (
        activated.reshape(snapshots.shape),
        input_gradient.reshape(snapshots.shape),
        mode_gradient.reshape(mode_weight.shape),
        conv_gradient.reshape(conv_weight.shape),
    )


def solution(mesh):
    in_specs = (
        P("batch", None, "space", None),
        P("batch", None, "space", None),
        P("batch", "space", None, None, None),
        P(),
    )
    out_specs = (
        P("batch", None, "space", None),
        P("batch", None, "space", None),
        P("batch", "space", None, None, None),
        P(),
    )
    return jax.shard_map(shards, mesh=mesh, in_specs=in_specs, out_specs=out_specs, check_vma=False)
```

```python
import functools
import math

import jax
import jax.numpy as jnp
import ml_dtypes
import numpy as np
from jax import lax
from jax.experimental import pallas as pl
from jax.experimental.pallas import tpu as pltpu
from jax.sharding import PartitionSpec as P

KX = 8
KY = 8
KZ = 12
NX = 32
NY = 32
CELLS = NX * NY
LANES = 128
GROUP = 8
OFFSETS = 27
TERM_ROWS = 1024
CHUNKS = 3
VMEM_BYTES = 40 * 1024 * 1024
WHOLE_VMEM = 65000 * 1024
HBM_BYTES = 100 * 1024 * 256

F32 = jnp.float32
BF16 = jnp.bfloat16
inv_root_two = 1.0 / math.sqrt(2.0)
inv_root_two_pi = 1.0 / math.sqrt(2.0 * math.pi)


def basis_rows(half_count, length):
    row = np.arange(2 * half_count)[:, None]
    cell = np.arange(length)[None, :]
    frequency = np.where(row < half_count, row, row - half_count + 1)
    phases = (frequency * cell % length).astype(np.float32) * np.float32(2.0 * math.pi / length)
    return np.where(row < half_count, np.cos(phases), np.sin(phases)).astype(np.float32)


def plane_tables(batches, slabs):
    outer = (basis_rows(KX, NX)[:, None, :, None] * basis_rows(KY, NY)[None, :, None, :]).reshape(
        2 * KX, 2 * KY, CELLS
    )
    outer = outer.reshape(batches, 2 * KX // batches, slabs, 2 * KY // slabs, CELLS)
    outer = outer.transpose(2, 0, 1, 3, 4).reshape(4 * KX * KY, CELLS)
    analysis = (outer * np.float32(2.0 / math.sqrt(CELLS))).astype(ml_dtypes.bfloat16)
    synthesis = (outer * np.float32(2.0 / math.sqrt(4 * KX * KY))).astype(ml_dtypes.bfloat16)
    return analysis, synthesis


def depth_tables(slabs, layers, modes):
    rows = basis_rows(KZ, slabs * layers)
    analysis = (rows * np.float32(math.sqrt(2.0 / (slabs * layers)))).astype(ml_dtypes.bfloat16)
    synthesis = (rows * np.float32(math.sqrt(2.0 / (2 * KZ)))).astype(ml_dtypes.bfloat16)

    def spread(table, order):
        table = table.astype(np.float32).reshape(2 * KZ, slabs, layers)
        full = np.einsum("psz,mn->" + order, table, np.eye(modes, dtype=np.float32))
        return full.astype(ml_dtypes.bfloat16)

    def gathered(table):
        return spread(table, "mpzsn").reshape(modes * 2 * KZ, layers * slabs * modes)

    def scattered(table):
        return spread(table, "snzmp").reshape(slabs * modes, layers * modes * 2 * KZ)

    return gathered(analysis), scattered(synthesis), gathered(synthesis), scattered(analysis)


def dot(left, right, contract=(1, 0)):
    return lax.dot_general(
        left, right, (((contract[0],), (contract[1],)), ((), ())), preferred_element_type=F32
    )


def turn_table():
    row = lax.broadcasted_iota(jnp.int32, (LANES, LANES), 0)
    column = lax.broadcasted_iota(jnp.int32, (LANES, LANES), 1)
    return jnp.where(column == row % 2 * (LANES // 2) + row // 2, 1.0, 0.0).astype(BF16)


def to_cells(field):
    return dot(field.reshape(LANES, CELLS), turn_table(), (0, 0))


def to_field(cells):
    return dot(turn_table(), cells, (1, 1)).astype(BF16).reshape(LANES // 2, 2, CELLS)


def low_lanes(rows):
    return lax.broadcasted_iota(jnp.int32, (rows, LANES), 1) < LANES // 2


def swap_halves(values):
    return pltpu.roll(values, LANES // 2, 1)


def doubled(values):
    low = low_lanes(values.shape[0])
    swapped = swap_halves(values)
    return jnp.concatenate(
        [jnp.where(low, values, swapped), jnp.where(low, swapped, values)], axis=0
    )


def halved(values):
    low = low_lanes(values.shape[0])
    return jnp.concatenate([jnp.where(low, values, 0.0), jnp.where(low, 0.0, values)], axis=0)


def edge_layers(cells_first):
    top = cells_first[: CELLS // 2]
    bottom = cells_first[CELLS // 2 :]
    low = low_lanes(CELLS // 2)
    first = jnp.where(low, top, swap_halves(bottom))
    last = jnp.where(low, swap_halves(top), bottom)
    return first.astype(BF16), last.astype(BF16)


def beside_layers(before, after):
    before = before.astype(F32)
    after = after.astype(F32)
    low = low_lanes(CELLS // 2)
    top = jnp.where(low, before, swap_halves(after))
    bottom = jnp.where(low, swap_halves(before), after)
    return jnp.concatenate([top, bottom], axis=0).astype(BF16)


def y_cells(rows):
    return lax.broadcasted_iota(jnp.int32, (rows, LANES), 0) % NY


def from_below(values):
    return jnp.where(y_cells(values.shape[0]) == 0, 0.0, pltpu.roll(values, 1, 0))


def from_above(values):
    rows = values.shape[0]
    return jnp.where(y_cells(rows) == NY - 1, 0.0, pltpu.roll(values, rows - 1, 0))


def pad_cells(padded, own, beside):
    width = own.shape[1] + beside.shape[1]
    padded[0:NY, :] = jnp.zeros((NY, width), BF16)
    padded[NY + CELLS : 2 * NY + CELLS, :] = jnp.zeros((NY, width), BF16)
    padded[NY : NY + CELLS, 0 : own.shape[1]] = own
    padded[NY : NY + CELLS, own.shape[1] :] = beside


BLOCK_OF_DEPTH = {-1: 2, 0: 0, 1: 1, 2: 3}
STEP = 256


def stencil(padded, table, transposed, store):
    for start in range(0, CELLS, STEP):
        total = None
        for b in range(3):
            cells = padded[start + NY * b : start + NY * b + STEP, :]
            term = dot(cells, table[b], (1, 1) if transposed else (1, 0))
            total = term if total is None else total + term
        result = (
            from_below(total[:, 0:LANES])
            + total[:, LANES : 2 * LANES]
            + from_above(total[:, 2 * LANES :])
        )
        store(start, result)


def banded_forward(weights, table):
    half = LANES // 2
    for b in range(3):
        for c in range(3):
            for depth, block in BLOCK_OF_DEPTH.items():
                parts = []
                for out in range(2):
                    a = depth - out + 1
                    if 0 <= a < 3:
                        parts.append(weights[a * 9 + b * 3 + c])
                    else:
                        parts.append(jnp.zeros((half, half), BF16))
                table[b, block * half : (block + 1) * half, c * LANES : (c + 1) * LANES] = (
                    jnp.concatenate(parts, axis=1)
                )


def banded_backward(weights, table):
    half = LANES // 2
    for b in range(3):
        for c in range(3):
            for out in range(2):
                for pair in ((0, 1), (-1, 2)):
                    parts = []
                    for depth in pair:
                        a = depth - out + 1
                        if 0 <= a < 3:
                            parts.append(weights[(2 - a) * 9 + (2 - b) * 3 + 2 - c])
                        else:
                            parts.append(jnp.zeros((half, half), BF16))
                    row = c * LANES + out * half
                    column = BLOCK_OF_DEPTH[pair[0]] * half
                    table[b, row : row + half, column : column + LANES] = jnp.concatenate(
                        parts, axis=1
                    )


def analyse_kernel(field, analysis, *refs):
    weights = refs[:CHUNKS]
    cells_out, coef_out, first_out, last_out, packed_out, _, buffer, semaphores = refs[CHUNKS:]
    cells = to_cells(field[...])
    rounded = cells.astype(BF16)
    coef_out[...] = dot(analysis[...], rounded).astype(BF16)
    cells_out[...] = rounded
    first, last = edge_layers(cells)
    first_out[...] = first
    last_out[...] = last
    rows = GROUP * LANES // 4
    share = buffer.shape[0] // CHUNKS
    copies = []
    for place, part in enumerate(weights):
        for g in range(share // rows):
            pair = [part[k * rows : (k + 1) * rows, :] for k in (2 * g, 2 * g + 1)]
            row = place * share + g * rows
            buffer[row : row + rows, :] = jnp.concatenate(pair, axis=1)
        span = slice(place * share, (place + 1) * share)
        copies.append(
            pltpu.make_async_copy(buffer.at[span], packed_out.at[span], semaphores.at[place])
        )
        copies[-1].start()
    for copy in copies:
        copy.wait()


def local_kernel(
    cells, before, after, cotangent, weights, local_out, lanes_out, cotangent_out, padded, table
):
    banded_forward(weights, table)
    beside = beside_layers(before[...], after[...])
    pad_cells(padded, cells[...], beside)

    def store(start, result):
        local_out[start : start + STEP, :] = result

    stencil(padded, table, False, store)
    whole = jnp.concatenate([cells[...].astype(F32), beside.astype(F32)], axis=1)
    lanes_out[...] = whole.T.astype(BF16)
    cotangent_out[...] = to_cells(cotangent[...]).astype(BF16)


def fetch_kernel():
    pass


def mode_in_group(rows, lanes):
    return lax.broadcasted_iota(jnp.int32, (rows, lanes), 0) % GROUP


def own_block(rows):
    width = GROUP * LANES // 4
    lane = lax.broadcasted_iota(jnp.int32, (rows, width), 1)
    return mode_in_group(rows, width) % (GROUP // 2) == lane // (LANES // 2)


def own_half(rows):
    return (mode_in_group(rows, LANES) < GROUP // 2) == low_lanes(rows)


def to_depth(modes, table, snaps, slabs):
    modes = modes.reshape(slabs, snaps, -1, LANES)
    both = [doubled(modes[:, b].reshape(-1, LANES)) for b in range(snaps)]
    result = dot(table, jnp.concatenate(both, axis=1).astype(BF16))
    return jnp.concatenate(
        [
            result[g : g + GROUP, b * LANES : (b + 1) * LANES]
            for g in range(0, result.shape[0], GROUP)
            for b in range(snaps)
        ],
        axis=0,
    )


def from_depth(modes, table, snaps, slabs):
    count = modes.shape[0] // GROUP
    both = []
    for b in range(snaps):
        own = [modes[g * GROUP : (g + 1) * GROUP] for g in range(b, count, snaps)]
        both.append(halved(jnp.concatenate(own, axis=0)))
    result = dot(table, jnp.concatenate(both, axis=1).astype(BF16))
    own = [
        result[:, b * LANES : (b + 1) * LANES].reshape(slabs, -1, LANES) for b in range(snaps)
    ]
    return jnp.stack(own, axis=1).reshape(-1, LANES)


def mix_kernel(snaps, slabs, received, gather, weights, scatter, back_out, diagonal_out):
    coef = to_depth(received[...].astype(F32), gather[...], snaps, slabs)
    count = coef.shape[0]
    wide = jnp.concatenate([coef] * (GROUP // 4), axis=1)
    diagonal = jnp.where(own_block(count), wide, 0.0).astype(BF16)
    diagonal_out[...] = diagonal
    rows = GROUP * snaps
    depth = GROUP * LANES // 4
    mixed = jnp.concatenate(
        [
            dot(diagonal[g * rows : (g + 1) * rows, :], weights[g * depth : (g + 1) * depth, :])
            for g in range(count // rows)
        ],
        axis=0,
    )
    mixed = jnp.where(own_half(count), mixed, swap_halves(mixed))
    back = from_depth(mixed, scatter[...], snaps, slabs).astype(BF16)
    back_out[...] = back.reshape(back_out.shape)


def activate_kernel(
    terms_in_slab,
    received,
    synthesis,
    local,
    cotangent,
    lanes,
    activated_out,
    grad_out,
    first_out,
    last_out,
    back_out,
    terms_out,
    spread,
):
    pre = dot(synthesis[...], received[...]) + local[...]
    cdf = 0.5 * (1.0 + lax.erf(pre * inv_root_two))
    density = jnp.exp(-0.5 * pre * pre) * inv_root_two_pi
    activated_out[...] = (pre * cdf).astype(BF16)
    grad = (cotangent[...].astype(F32) * (cdf + pre * density)).astype(BF16)
    back = dot(synthesis[...], grad, (0, 0))
    rounded = grad
    grad = grad.astype(F32)
    first, last = edge_layers(grad)
    spread[0:NY, :] = jnp.zeros((NY, 3 * LANES), BF16)
    spread[NY + CELLS : 2 * NY + CELLS, :] = jnp.zeros((NY, 3 * LANES), BF16)
    spread[NY : NY + CELLS, 0:LANES] = from_above(grad).astype(BF16)
    spread[NY : NY + CELLS, LANES : 2 * LANES] = grad.astype(BF16)
    spread[NY : NY + CELLS, 2 * LANES :] = from_below(grad).astype(BF16)
    half = LANES // 2
    low = low_lanes(half)
    twice = {}
    for b in range(3):
        product = dot(lanes[...], spread[NY * (2 - b) : NY * (2 - b) + CELLS, :])
        for c in range(3):
            for a in range(3):
                blocks = [BLOCK_OF_DEPTH[out + a - 1] * half for out in range(2)]
                columns = slice(c * LANES, (c + 1) * LANES)
                both = jnp.where(
                    low,
                    product[blocks[0] : blocks[0] + half, columns],
                    product[blocks[1] : blocks[1] + half, columns],
                )
                twice[a * 9 + b * 3 + c] = both + swap_halves(both)
    pairs = []
    for k in range(0, OFFSETS, 2):
        pairs.append(jnp.where(low, twice[k], twice.get(k + 1, 0.0)))
    pairs.append(jnp.zeros((TERM_ROWS - half * len(pairs), LANES), F32))
    terms = jnp.concatenate(pairs, axis=0)
    if terms_in_slab:
        slab_store(back_out, back, terms)
    else:
        back_out[...] = back.astype(BF16)
        terms_out[...] = terms.astype(BF16)
    grad_out[...] = rounded
    first_out[...] = first
    last_out[...] = last


def slab_store(slab, modes, terms):
    owners = slab.shape[0]
    modes = modes.reshape(owners, 8, LANES)
    terms = terms.reshape(owners, -1, LANES)
    slab[...] = jnp.concatenate([modes, terms], axis=1).astype(BF16)


def slab_load(slab):
    whole = slab[...].astype(F32)
    return whole[:, 0:8, :].reshape(-1, LANES), whole[:, 8:, :]


def unmix_kernel(snaps, slabs, scale, received, terms, gather, weights, scatter, grad_out, mixed_out, sums_out):
    in_slab = terms is None
    if in_slab:
        modes, terms = slab_load(received)
    else:
        modes, terms = received[...].astype(F32), terms[...].astype(F32)
    mixed = to_depth(modes, gather[...], snaps, slabs)
    mixed_out[...] = mixed.astype(BF16)
    count = mixed.shape[0]
    rows = GROUP * snaps
    depth = GROUP * LANES // 4
    sums = jnp.sum(terms, axis=0) * scale
    own = own_block(rows)
    placed = jnp.where(own_half(count), mixed, 0.0).astype(BF16)
    pieces = []
    for g in range(count // rows):
        full = dot(
            placed[g * rows : (g + 1) * rows, :], weights[g * depth : (g + 1) * depth, :], (1, 1)
        )
        full = jnp.where(own, full, 0.0)
        pieces.append(sum(full[:, k : k + LANES] for k in range(0, depth, LANES)))
    coef = jnp.concatenate(pieces, axis=0)
    coef = coef + swap_halves(coef)
    grad = from_depth(coef, scatter[...], snaps, slabs)
    if in_slab:
        owners = received.shape[0]
        share = sums.shape[0]
        slab_store(
            grad_out, grad, jnp.broadcast_to(sums[None], (owners, share, LANES)).reshape(-1, LANES)
        )
    else:
        grad_out[...] = grad.astype(BF16)
        sums_out[...] = sums


def weight_kernel(snaps, diagonal, mixed, out):
    rows = GROUP * snaps
    depth = GROUP * LANES // 4
    half = LANES // 2
    first = mode_in_group(rows, depth) < GROUP // 2
    for g in range(diagonal.shape[0] // rows):
        span = slice(g * rows, (g + 1) * rows)
        blocks = diagonal[span, :].astype(F32)
        blocks = [jnp.where(first, blocks, 0.0), jnp.where(first, 0.0, blocks)]
        blocks = jnp.concatenate(blocks, axis=1).astype(BF16)
        out[2 * g * depth : 2 * (g + 1) * depth, :] = dot(blocks, mixed[span, 0:half], (0, 0))


def output_kernel(cells, out):
    out[...] = to_field(cells[...])


def local_grad_kernel(grad, before, after, weights, out, padded, table):
    banded_backward(weights, table)
    pad_cells(padded, grad[...], beside_layers(before[...], after[...]))

    def store(start, result):
        out[start : start + STEP, :] = result

    stencil(padded, table, True, store)


def finish_kernel(received, sums, synthesis, local, grad_out, stencil_out):
    in_slab = sums is None
    if in_slab:
        modes, terms = slab_load(received)
        terms = terms.reshape(TERM_ROWS, LANES)
    else:
        modes, terms = received[...], sums[...].astype(F32)
    cells = (dot(synthesis[...], modes.astype(BF16)) + local[...]).astype(BF16)
    grad_out[...] = to_field(cells)
    half = LANES // 2
    for k in range(OFFSETS):
        row = (k // 2) * half
        lane = (k % 2) * half
        stencil_out[k] = terms[row : row + half, lane : lane + half]


def shape(dims, dtype):
    return jax.ShapeDtypeStruct(dims, dtype)


class Staged:
    def __init__(self, source, buffer, semaphore):
        self.copy = pltpu.make_async_copy(source, buffer, semaphore)
        self.buffer = buffer
        self.copy.start()
        self.ready = False

    def load(self):
        if not self.ready:
            self.copy.wait()
            self.ready = True

    def __getitem__(self, index):
        self.load()
        return self.buffer[index]


class Sent:
    def __init__(self, target, buffer, semaphore):
        self.copy = pltpu.make_async_copy(buffer, target, semaphore)
        self.buffer = buffer

    def __setitem__(self, index, value):
        self.buffer[index] = value
        self.copy.start()

    def __getitem__(self, index):
        return self.buffer[index]

    @property
    def shape(self):
        return self.buffer.shape


def row_count(rows):
    return rows.stop - rows.start if isinstance(rows, slice) else rows


def run(
    body, outs, *operands, staged=(), sent=(), moved=(), plain=(), slots=(), scratch=(), flops=0, limit=VMEM_BYTES
):
    given = [k for k, operand in enumerate(operands) if operand is not None]
    made = [k for k, out in enumerate(outs) if out is not None]

    def rows_of(chosen, places, arrays):
        chosen = {k: chosen[k] if isinstance(chosen, dict) else None for k in places if k in chosen}
        return {k: rows or arrays[k].shape[0] for k, rows in chosen.items()}

    moved = dict(moved)
    slots = dict(slots)
    staged = rows_of(staged, given, operands)
    sent = rows_of(sent, made, outs)

    def kernel(*refs):
        refs = list(refs)

        def take(count):
            taken = refs[:count]
            del refs[:count]
            return taken

        def part(ref, rows):
            if isinstance(rows, slice):
                return ref.at[rows]
            return ref if ref.shape[0] == rows else ref.at[0:rows]

        filled = dict(zip(given, take(len(given))))
        take(len(slots))
        kept = dict(zip(made, take(len(made))))
        own = take(len(scratch))
        copies = []
        for place, (k, out) in enumerate(moved.items()):
            source, target = filled.pop(k), kept.pop(out)
            rows = min(source.shape[0], target.shape[0])
            semaphore = refs[-1].at[len(staged) + len(sent) + place]
            copies.append(
                pltpu.make_async_copy(part(source, rows), part(target, rows), semaphore)
            )
        for place, (k, buffer) in enumerate(zip(staged, take(len(staged)))):
            filled[k] = Staged(part(filled[k], staged[k]), buffer, refs[-1].at[place])
        for place, (k, buffer) in enumerate(zip(sent, take(len(sent)))):
            kept[k] = Sent(part(kept[k], sent[k]), buffer, refs[-1].at[len(staged) + place])
        for copy in copies:
            copy.start()
        body(
            *[filled.get(k) for k in range(len(operands)) if k not in moved],
            *[kept.get(k) for k in range(len(outs)) if k not in moved.values()],
            *own,
        )
        for k in staged:
            filled[k].load()
        for k in sent:
            kept[k].copy.wait()
        for copy in copies:
            copy.wait()

    arrays = [operands[k] for k in given]
    results = [outs[k] for k in made]
    size = sum(x.size * x.dtype.itemsize for x in (*arrays, *results))
    in_vmem = pl.BlockSpec(memory_space=pltpu.VMEM)
    in_hbm = pl.BlockSpec(memory_space=pltpu.HBM)
    buffers = [(operands[k], rows) for k, rows in staged.items()]
    buffers += [(outs[k], rows) for k, rows in sent.items()]
    buffers = [pltpu.VMEM((row_count(rows), *x.shape[1:]), x.dtype) for x, rows in buffers]
    if len(buffers) + len(moved) > 0:
        buffers.append(pltpu.SemaphoreType.DMA((len(buffers) + len(moved),)))
    results = pl.pallas_call(
        kernel,
        out_shape=results,
        in_specs=[in_hbm if k in staged or k in moved else in_vmem for k in given]
        + [in_hbm] * len(slots),
        out_specs=[in_hbm if k in sent or k in plain else in_vmem for k in made],
        input_output_aliases={len(given) + at: made.index(k) for at, k in enumerate(slots)},
        scratch_shapes=[*scratch, *buffers],
        compiler_params=pltpu.CompilerParams(vmem_limit_bytes=limit),
        cost_estimate=pl.CostEstimate(flops=flops, bytes_accessed=size, transcendentals=0),
        name=body.__name__ if hasattr(body, "__name__") else body.func.__name__,
    )(*arrays, *slots.values())
    results = dict(zip(made, results))
    return [results.get(k) for k in range(len(outs))]


def exchange(values):
    return lax.all_to_all(values, ("space", "batch"), split_axis=0, concat_axis=0, tiled=True)


def neighbours(first, last):
    ends = lax.axis_size("space") - 1
    before = lax.ppermute(last, "space", [(i, i + 1) for i in range(ends)])
    after = lax.ppermute(first, "space", [(i + 1, i) for i in range(ends)])
    return before, after


def shards(snapshots, cotangent, mode_weight, conv_weight):
    batches = lax.axis_size("batch")
    slabs = lax.axis_size("space")
    devices = batches * slabs
    _, channels, layers, plane = snapshots.shape
    modes = mode_weight.shape[0] * mode_weight.shape[1]
    half = LANES // 2
    assert channels == half and layers == 2 and plane == CELLS
    plane_rows = devices * modes
    count = modes * 2 * KZ * batches
    in_slab = modes == 8 and devices * 32 == TERM_ROWS

    analysis, synthesis = plane_tables(batches, slabs)
    gather, scatter, gather_back, scatter_back = depth_tables(slabs, layers, modes)
    weights = mode_weight.reshape(modes * 2 * KZ * channels, channels)
    taps = conv_weight.reshape(OFFSETS, channels, channels)
    field = shape((channels, layers, plane), BF16)
    wide = shape((CELLS, LANES), BF16)
    edge = shape((CELLS // 2, LANES), BF16)
    plane_modes = shape((plane_rows, LANES), BF16)
    padded = pltpu.VMEM((CELLS + 2 * NY, 2 * LANES), BF16)

    def send(values):
        return exchange(values.reshape(devices, modes, LANES)).reshape(plane_rows, LANES)

    packed = shape((weights.shape[0] // 2, LANES), BF16)
    share = weights.shape[0] // CHUNKS
    to_send = shape((devices, modes, LANES), BF16) if modes % 8 == 0 else plane_modes
    cells, coef, first, last, kept_weights, slot = run(
        analyse_kernel,
        [
            wide,
            plane_modes,
            edge,
            edge,
            shape((HBM_BYTES // (2 * LANES), LANES), BF16),
            to_send,
        ],
        snapshots.reshape(field.shape),
        analysis,
        *[weights] * CHUNKS,
        staged={0: None, 1: None} | {2 + k: slice(k * share, (k + 1) * share) for k in range(CHUNKS)},
        sent=(0, 1, 2, 3),
        plain=(4, 5),
        scratch=[pltpu.VMEM(packed.shape, BF16), pltpu.SemaphoreType.DMA((CHUNKS,))],
        limit=WHOLE_VMEM,
        flops=10**8,
    )
    coef = send(coef)
    (packed_weights,) = run(fetch_kernel, [packed], kept_weights, moved={0: 0})
    before, after = neighbours(first, last)
    local, lanes, outer_cells = run(
        local_kernel,
        [shape((CELLS, LANES), F32), shape((2 * LANES, CELLS), BF16), wide],
        cells,
        before,
        after,
        cotangent.reshape(field.shape),
        taps,
        scratch=[padded, pltpu.VMEM((3, 2 * LANES, 3 * LANES), BF16)],
        flops=7 * 10**8,
    )
    back, diagonal = run(
        functools.partial(mix_kernel, batches, slabs),
        [to_send, shape((count, GROUP * half // 2), BF16)],
        coef,
        gather,
        packed_weights,
        scatter,
        sent=(0, 1),
        slots={0: slot},
        flops=4 * 10**8,
    )
    back = send(back)
    slab = shape((devices, 8 + TERM_ROWS // devices, LANES), BF16)
    activated, grad, first, last, back, terms = run(
        functools.partial(activate_kernel, in_slab),
        [
            wide,
            shape((HBM_BYTES // (2 * LANES), LANES), BF16),
            edge,
            edge,
            slab if in_slab else plane_modes,
            None if in_slab else shape((TERM_ROWS, LANES), BF16),
        ],
        back,
        np.ascontiguousarray(synthesis.T),
        local,
        outer_cells,
        lanes,
        sent={1: CELLS, 2: None, 3: None, 4: None},
        scratch=[pltpu.VMEM((CELLS + 2 * NY, 3 * LANES), BF16)],
        flops=10**9,
    )
    if in_slab:
        back = exchange(back)
    else:
        back = send(back)
        terms = exchange(terms.reshape(devices, TERM_ROWS // devices, LANES))
    before, after = neighbours(first, last)
    activated, packed_weights = run(
        output_kernel,
        [field, packed],
        activated,
        kept_weights,
        moved={1: 1},
        flops=10**8,
    )
    back, before, after, activated, packed_weights = lax.optimization_barrier(
        (back, before, after, activated, packed_weights)
    )
    scale = 1.0 / math.sqrt(batches * slabs * layers * plane)
    grad_modes, mixed_grad, sums = run(
        functools.partial(unmix_kernel, batches, slabs, scale),
        [
            slab if in_slab else plane_modes,
            shape((count, LANES), BF16),
            None if in_slab else shape((TERM_ROWS // devices, LANES), F32),
        ],
        back,
        None if in_slab else terms,
        gather_back,
        packed_weights,
        scatter_back,
        sent=(0,),
        flops=4 * 10**8,
    )
    if in_slab:
        grad_modes = exchange(grad_modes)
    else:
        grad_modes = send(grad_modes)
        sums = lax.all_gather(sums, ("space", "batch"), axis=0, tiled=True)
    (local,) = run(
        local_grad_kernel,
        [shape((CELLS, LANES), F32)],
        grad,
        before,
        after,
        taps,
        staged={0: CELLS},
        scratch=[padded, pltpu.VMEM((3, 3 * LANES, 2 * LANES), BF16)],
        flops=7 * 10**8,
    )
    (mode_gradient,) = run(
        functools.partial(weight_kernel, batches),
        [shape((modes * 2 * KZ * channels, channels), F32)],
        diagonal,
        mixed_grad,
        flops=4 * 10**8,
    )
    input_gradient, conv_gradient = run(
        finish_kernel,
        [field, shape((OFFSETS, channels, channels), F32)],
        grad_modes,
        sums,
        np.ascontiguousarray(analysis.T),
        local,
        flops=10**8,
    )
    return (
        activated.reshape(snapshots.shape),
        input_gradient.reshape(snapshots.shape),
        mode_gradient.reshape(mode_weight.shape),
        conv_gradient.reshape(conv_weight.shape),
    )


def solution(mesh):
    in_specs = (
        P("batch", None, "space", None),
        P("batch", None, "space", None),
        P("batch", "space", None, None, None),
        P(),
    )
    out_specs = (
        P("batch", None, "space", None),
        P("batch", None, "space", None),
        P("batch", "space", None, None, None),
        P(),
    )
    return jax.shard_map(shards, mesh=mesh, in_specs=in_specs, out_specs=out_specs, check_vma=False)
```

```python
import functools
import math

import jax
import jax.numpy as jnp
import ml_dtypes
import numpy as np
from jax import lax
from jax.experimental import pallas as pl
from jax.experimental.pallas import tpu as pltpu
from jax.sharding import PartitionSpec as P

KX = 8
KY = 8
KZ = 12
NX = 32
NY = 32
CELLS = NX * NY
LANES = 128
GROUP = 8
OFFSETS = 27
TERM_ROWS = 1024
CHUNKS = 3
VMEM_BYTES = 40 * 1024 * 1024
WHOLE_VMEM = 65000 * 1024
HBM_BYTES = 100 * 1024 * 256

F32 = jnp.float32
BF16 = jnp.bfloat16
inv_root_two = 1.0 / math.sqrt(2.0)
inv_root_two_pi = 1.0 / math.sqrt(2.0 * math.pi)


def basis_rows(half_count, length):
    row = np.arange(2 * half_count)[:, None]
    cell = np.arange(length)[None, :]
    frequency = np.where(row < half_count, row, row - half_count + 1)
    phases = (frequency * cell % length).astype(np.float32) * np.float32(2.0 * math.pi / length)
    return np.where(row < half_count, np.cos(phases), np.sin(phases)).astype(np.float32)


def plane_tables(batches, slabs):
    outer = (basis_rows(KX, NX)[:, None, :, None] * basis_rows(KY, NY)[None, :, None, :]).reshape(
        2 * KX, 2 * KY, CELLS
    )
    outer = outer.reshape(batches, 2 * KX // batches, slabs, 2 * KY // slabs, CELLS)
    outer = outer.transpose(2, 0, 1, 3, 4).reshape(4 * KX * KY, CELLS)
    analysis = (outer * np.float32(2.0 / math.sqrt(CELLS))).astype(ml_dtypes.bfloat16)
    synthesis = (outer * np.float32(2.0 / math.sqrt(4 * KX * KY))).astype(ml_dtypes.bfloat16)
    return analysis, synthesis


def depth_tables(slabs, layers, modes):
    rows = basis_rows(KZ, slabs * layers)
    analysis = (rows * np.float32(math.sqrt(2.0 / (slabs * layers)))).astype(ml_dtypes.bfloat16)
    synthesis = (rows * np.float32(math.sqrt(2.0 / (2 * KZ)))).astype(ml_dtypes.bfloat16)

    def spread(table, order):
        table = table.astype(np.float32).reshape(2 * KZ, slabs, layers)
        full = np.einsum("psz,mn->" + order, table, np.eye(modes, dtype=np.float32))
        return full.astype(ml_dtypes.bfloat16)

    def gathered(table):
        return spread(table, "mpzsn").reshape(modes * 2 * KZ, layers * slabs * modes)

    def scattered(table):
        return spread(table, "snzmp").reshape(slabs * modes, layers * modes * 2 * KZ)

    return gathered(analysis), scattered(synthesis), gathered(synthesis), scattered(analysis)


def dot(left, right, contract=(1, 0)):
    return lax.dot_general(
        left, right, (((contract[0],), (contract[1],)), ((), ())), preferred_element_type=F32
    )


def turn_table():
    row = lax.broadcasted_iota(jnp.int32, (LANES, LANES), 0)
    column = lax.broadcasted_iota(jnp.int32, (LANES, LANES), 1)
    return jnp.where(column == row % 2 * (LANES // 2) + row // 2, 1.0, 0.0).astype(BF16)


def to_cells(field):
    return dot(field.reshape(LANES, CELLS), turn_table(), (0, 0))


def to_field(cells):
    return dot(turn_table(), cells, (1, 1)).astype(BF16).reshape(LANES // 2, 2, CELLS)


def low_lanes(rows):
    return lax.broadcasted_iota(jnp.int32, (rows, LANES), 1) < LANES // 2


def swap_halves(values):
    return pltpu.roll(values, LANES // 2, 1)


def doubled(values):
    low = low_lanes(values.shape[0])
    swapped = swap_halves(values)
    return jnp.concatenate(
        [jnp.where(low, values, swapped), jnp.where(low, swapped, values)], axis=0
    )


def halved(values):
    low = low_lanes(values.shape[0])
    return jnp.concatenate([jnp.where(low, values, 0.0), jnp.where(low, 0.0, values)], axis=0)


def edge_layers(cells_first):
    top = cells_first[: CELLS // 2]
    bottom = cells_first[CELLS // 2 :]
    low = low_lanes(CELLS // 2)
    first = jnp.where(low, top, swap_halves(bottom))
    last = jnp.where(low, swap_halves(top), bottom)
    return first.astype(BF16), last.astype(BF16)


def beside_layers(before, after):
    before = before.astype(F32)
    after = after.astype(F32)
    low = low_lanes(CELLS // 2)
    top = jnp.where(low, before, swap_halves(after))
    bottom = jnp.where(low, swap_halves(before), after)
    return jnp.concatenate([top, bottom], axis=0).astype(BF16)


def y_cells(rows):
    return lax.broadcasted_iota(jnp.int32, (rows, LANES), 0) % NY


def from_below(values):
    return jnp.where(y_cells(values.shape[0]) == 0, 0.0, pltpu.roll(values, 1, 0))


def from_above(values):
    rows = values.shape[0]
    return jnp.where(y_cells(rows) == NY - 1, 0.0, pltpu.roll(values, rows - 1, 0))


def pad_cells(padded, own, beside):
    width = own.shape[1] + beside.shape[1]
    padded[0:NY, :] = jnp.zeros((NY, width), BF16)
    padded[NY + CELLS : 2 * NY + CELLS, :] = jnp.zeros((NY, width), BF16)
    padded[NY : NY + CELLS, 0 : own.shape[1]] = own
    padded[NY : NY + CELLS, own.shape[1] :] = beside


BLOCK_OF_DEPTH = {-1: 2, 0: 0, 1: 1, 2: 3}
STEP = 256


def stencil(padded, table, transposed, store):
    for start in range(0, CELLS, STEP):
        total = None
        for b in range(3):
            cells = padded[start + NY * b : start + NY * b + STEP, :]
            term = dot(cells, table[b], (1, 1) if transposed else (1, 0))
            total = term if total is None else total + term
        result = (
            from_below(total[:, 0:LANES])
            + total[:, LANES : 2 * LANES]
            + from_above(total[:, 2 * LANES :])
        )
        store(start, result)


def banded_forward(weights, table):
    half = LANES // 2
    for b in range(3):
        for c in range(3):
            for depth, block in BLOCK_OF_DEPTH.items():
                parts = []
                for out in range(2):
                    a = depth - out + 1
                    if 0 <= a < 3:
                        parts.append(weights[a * 9 + b * 3 + c])
                    else:
                        parts.append(jnp.zeros((half, half), BF16))
                table[b, block * half : (block + 1) * half, c * LANES : (c + 1) * LANES] = (
                    jnp.concatenate(parts, axis=1)
                )


def banded_backward(weights, table):
    half = LANES // 2
    for b in range(3):
        for c in range(3):
            for out in range(2):
                for pair in ((0, 1), (-1, 2)):
                    parts = []
                    for depth in pair:
                        a = depth - out + 1
                        if 0 <= a < 3:
                            parts.append(weights[(2 - a) * 9 + (2 - b) * 3 + 2 - c])
                        else:
                            parts.append(jnp.zeros((half, half), BF16))
                    row = c * LANES + out * half
                    column = BLOCK_OF_DEPTH[pair[0]] * half
                    table[b, row : row + half, column : column + LANES] = jnp.concatenate(
                        parts, axis=1
                    )


def analyse_kernel(field, analysis, *refs):
    weights = refs[:CHUNKS]
    cells_out, coef_out, first_out, last_out, packed_out, _, buffer, semaphores = refs[CHUNKS:]
    cells = to_cells(field[...])
    rounded = cells.astype(BF16)
    coef_out[...] = dot(analysis[...], rounded).astype(BF16)
    cells_out[...] = rounded
    first, last = edge_layers(cells)
    first_out[...] = first
    last_out[...] = last
    rows = GROUP * LANES // 4
    share = buffer.shape[0] // CHUNKS
    copies = []
    for place, part in enumerate(weights):
        for g in range(share // rows):
            pair = [part[k * rows : (k + 1) * rows, :] for k in (2 * g, 2 * g + 1)]
            row = place * share + g * rows
            buffer[row : row + rows, :] = jnp.concatenate(pair, axis=1)
        span = slice(place * share, (place + 1) * share)
        copies.append(
            pltpu.make_async_copy(buffer.at[span], packed_out.at[span], semaphores.at[place])
        )
        copies[-1].start()
    for copy in copies:
        copy.wait()


def local_kernel(
    cells, before, after, cotangent, weights, local_out, lanes_out, cotangent_out, padded, table
):
    banded_forward(weights, table)
    beside = beside_layers(before[...], after[...])
    pad_cells(padded, cells[...], beside)

    def store(start, result):
        local_out[start : start + STEP, :] = result

    stencil(padded, table, False, store)
    whole = jnp.concatenate([cells[...].astype(F32), beside.astype(F32)], axis=1)
    lanes_out[...] = whole.T.astype(BF16)
    cotangent_out[...] = to_cells(cotangent[...]).astype(BF16)


def fetch_kernel():
    pass


def mode_in_group(rows, lanes):
    return lax.broadcasted_iota(jnp.int32, (rows, lanes), 0) % GROUP


def own_block(rows):
    width = GROUP * LANES // 4
    lane = lax.broadcasted_iota(jnp.int32, (rows, width), 1)
    return mode_in_group(rows, width) % (GROUP // 2) == lane // (LANES // 2)


def own_half(rows):
    return (mode_in_group(rows, LANES) < GROUP // 2) == low_lanes(rows)


def to_depth(modes, table, snaps, slabs):
    modes = modes.reshape(slabs, snaps, -1, LANES)
    both = [doubled(modes[:, b].reshape(-1, LANES)) for b in range(snaps)]
    result = dot(table, jnp.concatenate(both, axis=1).astype(BF16))
    return jnp.concatenate(
        [
            result[g : g + GROUP, b * LANES : (b + 1) * LANES]
            for g in range(0, result.shape[0], GROUP)
            for b in range(snaps)
        ],
        axis=0,
    )


def from_depth(modes, table, snaps, slabs):
    count = modes.shape[0] // GROUP
    both = []
    for b in range(snaps):
        own = [modes[g * GROUP : (g + 1) * GROUP] for g in range(b, count, snaps)]
        both.append(halved(jnp.concatenate(own, axis=0)))
    result = dot(table, jnp.concatenate(both, axis=1).astype(BF16))
    own = [
        result[:, b * LANES : (b + 1) * LANES].reshape(slabs, -1, LANES) for b in range(snaps)
    ]
    return jnp.stack(own, axis=1).reshape(-1, LANES)


def mix_kernel(snaps, slabs, received, gather, weights, scatter, back_out, diagonal_out):
    coef = to_depth(received[...].astype(F32), gather[...], snaps, slabs)
    count = coef.shape[0]
    wide = jnp.concatenate([coef] * (GROUP // 4), axis=1)
    diagonal = jnp.where(own_block(count), wide, 0.0).astype(BF16)
    diagonal_out[...] = diagonal
    rows = GROUP * snaps
    depth = GROUP * LANES // 4
    mixed = jnp.concatenate(
        [
            dot(diagonal[g * rows : (g + 1) * rows, :], weights[g * depth : (g + 1) * depth, :])
            for g in range(count // rows)
        ],
        axis=0,
    )
    mixed = jnp.where(own_half(count), mixed, swap_halves(mixed))
    back = from_depth(mixed, scatter[...], snaps, slabs).astype(BF16)
    back_out[...] = back.reshape(back_out.shape)


def activate_kernel(
    terms_in_slab,
    received,
    synthesis,
    local,
    cotangent,
    lanes,
    activated_out,
    grad_out,
    first_out,
    last_out,
    back_out,
    terms_out,
    spread,
):
    pre = dot(synthesis[...], received[...]) + local[...]
    cdf = 0.5 * (1.0 + lax.erf(pre * inv_root_two))
    density = jnp.exp(-0.5 * pre * pre) * inv_root_two_pi
    activated_out[...] = (pre * cdf).astype(BF16)
    grad = (cotangent[...].astype(F32) * (cdf + pre * density)).astype(BF16)
    back = dot(synthesis[...], grad, (0, 0))
    rounded = grad
    grad = grad.astype(F32)
    first, last = edge_layers(grad)
    spread[0:NY, :] = jnp.zeros((NY, 3 * LANES), BF16)
    spread[NY + CELLS : 2 * NY + CELLS, :] = jnp.zeros((NY, 3 * LANES), BF16)
    spread[NY : NY + CELLS, 0:LANES] = from_above(grad).astype(BF16)
    spread[NY : NY + CELLS, LANES : 2 * LANES] = grad.astype(BF16)
    spread[NY : NY + CELLS, 2 * LANES :] = from_below(grad).astype(BF16)
    half = LANES // 2
    low = low_lanes(half)
    twice = {}
    for b in range(3):
        product = dot(lanes[...], spread[NY * (2 - b) : NY * (2 - b) + CELLS, :])
        for c in range(3):
            for a in range(3):
                blocks = [BLOCK_OF_DEPTH[out + a - 1] * half for out in range(2)]
                columns = slice(c * LANES, (c + 1) * LANES)
                both = jnp.where(
                    low,
                    product[blocks[0] : blocks[0] + half, columns],
                    product[blocks[1] : blocks[1] + half, columns],
                )
                twice[a * 9 + b * 3 + c] = both + swap_halves(both)
    pairs = []
    for k in range(0, OFFSETS, 2):
        pairs.append(jnp.where(low, twice[k], twice.get(k + 1, 0.0)))
    pairs.append(jnp.zeros((TERM_ROWS - half * len(pairs), LANES), F32))
    terms = jnp.concatenate(pairs, axis=0)
    if terms_in_slab:
        slab_store(back_out, back, terms)
    else:
        back_out[...] = back.astype(BF16)
        terms_out[...] = terms.astype(BF16)
    grad_out[...] = rounded
    first_out[...] = first
    last_out[...] = last


def slab_store(slab, modes, terms):
    owners = slab.shape[0]
    modes = modes.reshape(owners, 8, LANES)
    terms = terms.reshape(owners, -1, LANES)
    slab[...] = jnp.concatenate([modes, terms], axis=1).astype(BF16)


def slab_load(slab):
    whole = slab[...].astype(F32)
    return whole[:, 0:8, :].reshape(-1, LANES), whole[:, 8:, :]


def unmix_kernel(snaps, slabs, scale, received, terms, gather, weights, scatter, grad_out, mixed_out, sums_out):
    in_slab = terms is None
    if in_slab:
        modes, terms = slab_load(received)
    else:
        modes, terms = received[...].astype(F32), terms[...].astype(F32)
    mixed = to_depth(modes, gather[...], snaps, slabs)
    mixed_out[...] = mixed.astype(BF16)
    count = mixed.shape[0]
    rows = GROUP * snaps
    depth = GROUP * LANES // 4
    sums = jnp.sum(terms, axis=0) * scale
    own = own_block(rows)
    placed = jnp.where(own_half(count), mixed, 0.0).astype(BF16)
    pieces = []
    for g in range(count // rows):
        full = dot(
            placed[g * rows : (g + 1) * rows, :], weights[g * depth : (g + 1) * depth, :], (1, 1)
        )
        full = jnp.where(own, full, 0.0)
        pieces.append(sum(full[:, k : k + LANES] for k in range(0, depth, LANES)))
    coef = jnp.concatenate(pieces, axis=0)
    coef = coef + swap_halves(coef)
    grad = from_depth(coef, scatter[...], snaps, slabs)
    if in_slab:
        owners = received.shape[0]
        share = sums.shape[0]
        slab_store(
            grad_out, grad, jnp.broadcast_to(sums[None], (owners, share, LANES)).reshape(-1, LANES)
        )
    else:
        grad_out[...] = grad.astype(BF16)
        sums_out[...] = sums


def weight_kernel(snaps, diagonal, mixed, out):
    rows = GROUP * snaps
    depth = GROUP * LANES // 4
    half = LANES // 2
    first = mode_in_group(rows, depth) < GROUP // 2
    for g in range(diagonal.shape[0] // rows):
        span = slice(g * rows, (g + 1) * rows)
        blocks = diagonal[span, :].astype(F32)
        blocks = [jnp.where(first, blocks, 0.0), jnp.where(first, 0.0, blocks)]
        blocks = jnp.concatenate(blocks, axis=1).astype(BF16)
        out[2 * g * depth : 2 * (g + 1) * depth, :] = dot(blocks, mixed[span, 0:half], (0, 0))


def output_kernel(cells, out):
    out[...] = to_field(cells[...])


def local_grad_kernel(grad, before, after, weights, out, padded, table):
    banded_backward(weights, table)
    pad_cells(padded, grad[...], beside_layers(before[...], after[...]))

    def store(start, result):
        out[start : start + STEP, :] = result

    stencil(padded, table, True, store)


def finish_kernel(received, sums, synthesis, local, grad_out, stencil_out):
    in_slab = sums is None
    if in_slab:
        modes, terms = slab_load(received)
        terms = terms.reshape(TERM_ROWS, LANES)
    else:
        modes, terms = received[...], sums[...].astype(F32)
    cells = (dot(synthesis[...], modes.astype(BF16)) + local[...]).astype(BF16)
    grad_out[...] = to_field(cells)
    half = LANES // 2
    for k in range(OFFSETS):
        row = (k // 2) * half
        lane = (k % 2) * half
        stencil_out[k] = terms[row : row + half, lane : lane + half]


def shape(dims, dtype):
    return jax.ShapeDtypeStruct(dims, dtype)


class Staged:
    def __init__(self, source, buffer, semaphore):
        self.copy = pltpu.make_async_copy(source, buffer, semaphore)
        self.buffer = buffer
        self.copy.start()
        self.ready = False

    def load(self):
        if not self.ready:
            self.copy.wait()
            self.ready = True

    def __getitem__(self, index):
        self.load()
        return self.buffer[index]


class Sent:
    def __init__(self, target, buffer, semaphore):
        self.copy = pltpu.make_async_copy(buffer, target, semaphore)
        self.buffer = buffer

    def __setitem__(self, index, value):
        self.buffer[index] = value
        self.copy.start()

    def __getitem__(self, index):
        return self.buffer[index]

    @property
    def shape(self):
        return self.buffer.shape


def row_count(rows):
    return rows.stop - rows.start if isinstance(rows, slice) else rows


def run(
    body, outs, *operands, staged=(), sent=(), moved=(), plain=(), slots=(), scratch=(), flops=0, limit=VMEM_BYTES
):
    given = [k for k, operand in enumerate(operands) if operand is not None]
    made = [k for k, out in enumerate(outs) if out is not None]

    def rows_of(chosen, places, arrays):
        chosen = {k: chosen[k] if isinstance(chosen, dict) else None for k in places if k in chosen}
        return {k: rows or arrays[k].shape[0] for k, rows in chosen.items()}

    moved = dict(moved)
    slots = dict(slots)
    staged = rows_of(staged, given, operands)
    sent = rows_of(sent, made, outs)

    def kernel(*refs):
        refs = list(refs)

        def take(count):
            taken = refs[:count]
            del refs[:count]
            return taken

        def part(ref, rows):
            if isinstance(rows, slice):
                return ref.at[rows]
            return ref if ref.shape[0] == rows else ref.at[0:rows]

        filled = dict(zip(given, take(len(given))))
        take(len(slots))
        kept = dict(zip(made, take(len(made))))
        own = take(len(scratch))
        copies = []
        for place, (k, out) in enumerate(moved.items()):
            source, target = filled.pop(k), kept.pop(out)
            rows = min(source.shape[0], target.shape[0])
            semaphore = refs[-1].at[len(staged) + len(sent) + place]
            copies.append(
                pltpu.make_async_copy(part(source, rows), part(target, rows), semaphore)
            )
        for place, (k, buffer) in enumerate(zip(staged, take(len(staged)))):
            filled[k] = Staged(part(filled[k], staged[k]), buffer, refs[-1].at[place])
        for place, (k, buffer) in enumerate(zip(sent, take(len(sent)))):
            kept[k] = Sent(part(kept[k], sent[k]), buffer, refs[-1].at[len(staged) + place])
        for copy in copies:
            copy.start()
        body(
            *[filled.get(k) for k in range(len(operands)) if k not in moved],
            *[kept.get(k) for k in range(len(outs)) if k not in moved.values()],
            *own,
        )
        for k in staged:
            filled[k].load()
        for k in sent:
            kept[k].copy.wait()
        for copy in copies:
            copy.wait()

    arrays = [operands[k] for k in given]
    results = [outs[k] for k in made]
    size = sum(x.size * x.dtype.itemsize for x in (*arrays, *results))
    in_vmem = pl.BlockSpec(memory_space=pltpu.VMEM)
    in_hbm = pl.BlockSpec(memory_space=pltpu.HBM)
    buffers = [(operands[k], rows) for k, rows in staged.items()]
    buffers += [(outs[k], rows) for k, rows in sent.items()]
    buffers = [pltpu.VMEM((row_count(rows), *x.shape[1:]), x.dtype) for x, rows in buffers]
    if len(buffers) + len(moved) > 0:
        buffers.append(pltpu.SemaphoreType.DMA((len(buffers) + len(moved),)))
    results = pl.pallas_call(
        kernel,
        out_shape=results,
        in_specs=[in_hbm if k in staged or k in moved else in_vmem for k in given]
        + [in_hbm] * len(slots),
        out_specs=[in_hbm if k in sent or k in plain else in_vmem for k in made],
        input_output_aliases={len(given) + at: made.index(k) for at, k in enumerate(slots)},
        scratch_shapes=[*scratch, *buffers],
        compiler_params=pltpu.CompilerParams(vmem_limit_bytes=limit),
        cost_estimate=pl.CostEstimate(flops=flops, bytes_accessed=size, transcendentals=0),
        name=body.__name__ if hasattr(body, "__name__") else body.func.__name__,
    )(*arrays, *slots.values())
    results = dict(zip(made, results))
    return [results.get(k) for k in range(len(outs))]


def exchange(values):
    return lax.all_to_all(values, ("space", "batch"), split_axis=0, concat_axis=0, tiled=True)


def neighbours(first, last):
    ends = lax.axis_size("space") - 1
    before = lax.ppermute(last, "space", [(i, i + 1) for i in range(ends)])
    after = lax.ppermute(first, "space", [(i + 1, i) for i in range(ends)])
    return before, after


def shards(snapshots, cotangent, mode_weight, conv_weight):
    batches = lax.axis_size("batch")
    slabs = lax.axis_size("space")
    devices = batches * slabs
    _, channels, layers, plane = snapshots.shape
    modes = mode_weight.shape[0] * mode_weight.shape[1]
    half = LANES // 2
    assert channels == half and layers == 2 and plane == CELLS
    plane_rows = devices * modes
    count = modes * 2 * KZ * batches
    in_slab = modes == 8 and devices * 32 == TERM_ROWS

    analysis, synthesis = plane_tables(batches, slabs)
    gather, scatter, gather_back, scatter_back = depth_tables(slabs, layers, modes)
    weights = mode_weight.reshape(modes * 2 * KZ * channels, channels)
    taps = conv_weight.reshape(OFFSETS, channels, channels)
    field = shape((channels, layers, plane), BF16)
    wide = shape((CELLS, LANES), BF16)
    edge = shape((CELLS // 2, LANES), BF16)
    plane_modes = shape((plane_rows, LANES), BF16)
    padded = pltpu.VMEM((CELLS + 2 * NY, 2 * LANES), BF16)

    def send(values):
        return exchange(values.reshape(devices, modes, LANES)).reshape(plane_rows, LANES)

    packed = shape((weights.shape[0] // 2, LANES), BF16)
    share = weights.shape[0] // CHUNKS
    to_send = shape((devices, modes, LANES), BF16) if modes % 8 == 0 else plane_modes
    cells, coef, first, last, kept_weights, slot = run(
        analyse_kernel,
        [
            wide,
            plane_modes,
            edge,
            edge,
            shape((HBM_BYTES // (2 * LANES), LANES), BF16),
            to_send,
        ],
        snapshots.reshape(field.shape),
        analysis,
        *[weights] * CHUNKS,
        staged={0: None, 1: None} | {2 + k: slice(k * share, (k + 1) * share) for k in range(CHUNKS)},
        sent=(0, 1, 2, 3),
        plain=(4, 5),
        scratch=[pltpu.VMEM(packed.shape, BF16), pltpu.SemaphoreType.DMA((CHUNKS,))],
        limit=WHOLE_VMEM,
        flops=10**8,
    )
    coef = send(coef)
    (packed_weights,) = run(fetch_kernel, [packed], kept_weights, moved={0: 0})
    before, after = neighbours(first, last)
    local, lanes, outer_cells = run(
        local_kernel,
        [shape((CELLS, LANES), F32), shape((2 * LANES, CELLS), BF16), wide],
        cells,
        before,
        after,
        cotangent.reshape(field.shape),
        taps,
        scratch=[padded, pltpu.VMEM((3, 2 * LANES, 3 * LANES), BF16)],
        flops=8 * 10**9,
    )
    back, diagonal = run(
        functools.partial(mix_kernel, batches, slabs),
        [to_send, shape((count, GROUP * half // 2), BF16)],
        coef,
        gather,
        packed_weights,
        scatter,
        sent=(0, 1),
        slots={0: slot},
        flops=4 * 10**8,
    )
    back = send(back)
    slab = shape((devices, 8 + TERM_ROWS // devices, LANES), BF16)
    activated, grad, first, last, back, terms = run(
        functools.partial(activate_kernel, in_slab),
        [
            wide,
            shape((HBM_BYTES // (2 * LANES), LANES), BF16),
            edge,
            edge,
            slab if in_slab else plane_modes,
            None if in_slab else shape((TERM_ROWS, LANES), BF16),
        ],
        back,
        np.ascontiguousarray(synthesis.T),
        local,
        outer_cells,
        lanes,
        sent={1: CELLS, 2: None, 3: None, 4: None},
        scratch=[pltpu.VMEM((CELLS + 2 * NY, 3 * LANES), BF16)],
        flops=10**9,
    )
    if in_slab:
        back = exchange(back)
    else:
        back = send(back)
        terms = exchange(terms.reshape(devices, TERM_ROWS // devices, LANES))
    before, after = neighbours(first, last)
    activated, packed_weights = run(
        output_kernel,
        [field, packed],
        activated,
        kept_weights,
        moved={1: 1},
        flops=10**8,
    )
    back, before, after, activated, packed_weights = lax.optimization_barrier(
        (back, before, after, activated, packed_weights)
    )
    scale = 1.0 / math.sqrt(batches * slabs * layers * plane)
    grad_modes, mixed_grad, sums = run(
        functools.partial(unmix_kernel, batches, slabs, scale),
        [
            slab if in_slab else plane_modes,
            shape((count, LANES), BF16),
            None if in_slab else shape((TERM_ROWS // devices, LANES), F32),
        ],
        back,
        None if in_slab else terms,
        gather_back,
        packed_weights,
        scatter_back,
        sent=(0,),
        flops=4 * 10**8,
    )
    if in_slab:
        grad_modes = exchange(grad_modes)
    else:
        grad_modes = send(grad_modes)
        sums = lax.all_gather(sums, ("space", "batch"), axis=0, tiled=True)
    (local,) = run(
        local_grad_kernel,
        [shape((CELLS, LANES), F32)],
        grad,
        before,
        after,
        taps,
        staged={0: CELLS},
        scratch=[padded, pltpu.VMEM((3, 3 * LANES, 2 * LANES), BF16)],
        flops=7 * 10**8,
    )
    (mode_gradient,) = run(
        functools.partial(weight_kernel, batches),
        [shape((modes * 2 * KZ * channels, channels), F32)],
        diagonal,
        mixed_grad,
        flops=4 * 10**8,
    )
    input_gradient, conv_gradient = run(
        finish_kernel,
        [field, shape((OFFSETS, channels, channels), F32)],
        grad_modes,
        sums,
        np.ascontiguousarray(analysis.T),
        local,
        flops=10**8,
    )
    return (
        activated.reshape(snapshots.shape),
        input_gradient.reshape(snapshots.shape),
        mode_gradient.reshape(mode_weight.shape),
        conv_gradient.reshape(conv_weight.shape),
    )


def solution(mesh):
    in_specs = (
        P("batch", None, "space", None),
        P("batch", None, "space", None),
        P("batch", "space", None, None, None),
        P(),
    )
    out_specs = (
        P("batch", None, "space", None),
        P("batch", None, "space", None),
        P("batch", "space", None, None, None),
        P(),
    )
    return jax.shard_map(shards, mesh=mesh, in_specs=in_specs, out_specs=out_specs, check_vma=False)
```

```python
import functools
import math

import jax
import jax.numpy as jnp
import ml_dtypes
import numpy as np
from jax import lax
from jax.experimental import pallas as pl
from jax.experimental.pallas import tpu as pltpu
from jax.sharding import PartitionSpec as P

KX = 8
KY = 8
KZ = 12
NX = 32
NY = 32
CELLS = NX * NY
LANES = 128
GROUP = 8
OFFSETS = 27
TERM_ROWS = 1024
CHUNKS = 3
VMEM_BYTES = 40 * 1024 * 1024
LARGE_VMEM = 60 * 1024 * 1024
WHOLE_VMEM = 65000 * 1024
HBM_BYTES = 100 * 1024 * 256

F32 = jnp.float32
BF16 = jnp.bfloat16
inv_root_two = 1.0 / math.sqrt(2.0)
inv_root_two_pi = 1.0 / math.sqrt(2.0 * math.pi)


def basis_rows(half_count, length):
    row = np.arange(2 * half_count)[:, None]
    cell = np.arange(length)[None, :]
    frequency = np.where(row < half_count, row, row - half_count + 1)
    phases = (frequency * cell % length).astype(np.float32) * np.float32(2.0 * math.pi / length)
    return np.where(row < half_count, np.cos(phases), np.sin(phases)).astype(np.float32)


def plane_tables(batches, slabs):
    outer = (basis_rows(KX, NX)[:, None, :, None] * basis_rows(KY, NY)[None, :, None, :]).reshape(
        2 * KX, 2 * KY, CELLS
    )
    outer = outer.reshape(batches, 2 * KX // batches, slabs, 2 * KY // slabs, CELLS)
    outer = outer.transpose(2, 0, 1, 3, 4).reshape(4 * KX * KY, CELLS)
    analysis = (outer * np.float32(2.0 / math.sqrt(CELLS))).astype(ml_dtypes.bfloat16)
    synthesis = (outer * np.float32(2.0 / math.sqrt(4 * KX * KY))).astype(ml_dtypes.bfloat16)
    return analysis, synthesis


def depth_tables(slabs, layers, modes):
    rows = basis_rows(KZ, slabs * layers)
    analysis = (rows * np.float32(math.sqrt(2.0 / (slabs * layers)))).astype(ml_dtypes.bfloat16)
    synthesis = (rows * np.float32(math.sqrt(2.0 / (2 * KZ)))).astype(ml_dtypes.bfloat16)

    def spread(table, order):
        table = table.astype(np.float32).reshape(2 * KZ, slabs, layers)
        full = np.einsum("psz,mn->" + order, table, np.eye(modes, dtype=np.float32))
        return full.astype(ml_dtypes.bfloat16)

    def gathered(table):
        return spread(table, "mpzsn").reshape(modes * 2 * KZ, layers * slabs * modes)

    def scattered(table):
        return spread(table, "snzmp").reshape(slabs * modes, layers * modes * 2 * KZ)

    return gathered(analysis), scattered(synthesis), gathered(synthesis), scattered(analysis)


def dot(left, right, contract=(1, 0)):
    return lax.dot_general(
        left, right, (((contract[0],), (contract[1],)), ((), ())), preferred_element_type=F32
    )


def turn_table():
    row = lax.broadcasted_iota(jnp.int32, (LANES, LANES), 0)
    column = lax.broadcasted_iota(jnp.int32, (LANES, LANES), 1)
    return jnp.where(column == row % 2 * (LANES // 2) + row // 2, 1.0, 0.0).astype(BF16)


def to_cells(field):
    return dot(field.reshape(LANES, CELLS), turn_table(), (0, 0))


def to_field(cells):
    return dot(turn_table(), cells, (1, 1)).astype(BF16).reshape(LANES // 2, 2, CELLS)


def low_lanes(rows):
    return lax.broadcasted_iota(jnp.int32, (rows, LANES), 1) < LANES // 2


def swap_halves(values):
    return pltpu.roll(values, LANES // 2, 1)


def doubled(values):
    low = low_lanes(values.shape[0])
    swapped = swap_halves(values)
    return jnp.concatenate(
        [jnp.where(low, values, swapped), jnp.where(low, swapped, values)], axis=0
    )


def halved(values):
    low = low_lanes(values.shape[0])
    return jnp.concatenate([jnp.where(low, values, 0.0), jnp.where(low, 0.0, values)], axis=0)


def edge_layers(cells_first):
    top = cells_first[: CELLS // 2]
    bottom = cells_first[CELLS // 2 :]
    low = low_lanes(CELLS // 2)
    first = jnp.where(low, top, swap_halves(bottom))
    last = jnp.where(low, swap_halves(top), bottom)
    return first.astype(BF16), last.astype(BF16)


def beside_layers(before, after):
    before = before.astype(F32)
    after = after.astype(F32)
    low = low_lanes(CELLS // 2)
    top = jnp.where(low, before, swap_halves(after))
    bottom = jnp.where(low, swap_halves(before), after)
    return jnp.concatenate([top, bottom], axis=0).astype(BF16)


def y_cells(rows):
    return lax.broadcasted_iota(jnp.int32, (rows, LANES), 0) % NY


def from_below(values):
    return jnp.where(y_cells(values.shape[0]) == 0, 0.0, pltpu.roll(values, 1, 0))


def from_above(values):
    rows = values.shape[0]
    return jnp.where(y_cells(rows) == NY - 1, 0.0, pltpu.roll(values, rows - 1, 0))


def pad_cells(padded, own, beside):
    width = own.shape[1] + beside.shape[1]
    padded[0:NY, :] = jnp.zeros((NY, width), BF16)
    padded[NY + CELLS : 2 * NY + CELLS, :] = jnp.zeros((NY, width), BF16)
    padded[NY : NY + CELLS, 0 : own.shape[1]] = own
    padded[NY : NY + CELLS, own.shape[1] :] = beside


BLOCK_OF_DEPTH = {-1: 2, 0: 0, 1: 1, 2: 3}
STEP = 256


def stencil(padded, table, transposed, store):
    for start in range(0, CELLS, STEP):
        total = None
        for b in range(3):
            cells = padded[start + NY * b : start + NY * b + STEP, :]
            term = dot(cells, table[b], (1, 1) if transposed else (1, 0))
            total = term if total is None else total + term
        result = (
            from_below(total[:, 0:LANES])
            + total[:, LANES : 2 * LANES]
            + from_above(total[:, 2 * LANES :])
        )
        store(start, result)


def banded_forward(weights, table):
    half = LANES // 2
    for b in range(3):
        for c in range(3):
            for depth, block in BLOCK_OF_DEPTH.items():
                parts = []
                for out in range(2):
                    a = depth - out + 1
                    if 0 <= a < 3:
                        parts.append(weights[a * 9 + b * 3 + c])
                    else:
                        parts.append(jnp.zeros((half, half), BF16))
                table[b, block * half : (block + 1) * half, c * LANES : (c + 1) * LANES] = (
                    jnp.concatenate(parts, axis=1)
                )


def banded_backward(weights, table):
    half = LANES // 2
    for b in range(3):
        for c in range(3):
            for out in range(2):
                for pair in ((0, 1), (-1, 2)):
                    parts = []
                    for depth in pair:
                        a = depth - out + 1
                        if 0 <= a < 3:
                            parts.append(weights[(2 - a) * 9 + (2 - b) * 3 + 2 - c])
                        else:
                            parts.append(jnp.zeros((half, half), BF16))
                    row = c * LANES + out * half
                    column = BLOCK_OF_DEPTH[pair[0]] * half
                    table[b, row : row + half, column : column + LANES] = jnp.concatenate(
                        parts, axis=1
                    )


def analyse_kernel(field, analysis, cells_out, coef_out, first_out, last_out, _):
    cells = to_cells(field[...])
    rounded = cells.astype(BF16)
    coef_out[...] = dot(analysis[...], rounded).astype(BF16)
    cells_out[...] = rounded
    first, last = edge_layers(cells)
    first_out[...] = first
    last_out[...] = last


def pack_kernel(*refs):
    weights = refs[:CHUNKS]
    packed_out, buffer, semaphores = refs[CHUNKS:]
    rows = GROUP * LANES // 4
    share = buffer.shape[0] // CHUNKS
    copies = []
    for place, part in enumerate(weights):
        for g in range(share // rows):
            pair = [part[k * rows : (k + 1) * rows, :] for k in (2 * g, 2 * g + 1)]
            row = place * share + g * rows
            buffer[row : row + rows, :] = jnp.concatenate(pair, axis=1)
        span = slice(place * share, (place + 1) * share)
        copies.append(
            pltpu.make_async_copy(buffer.at[span], packed_out.at[span], semaphores.at[place])
        )
        copies[-1].start()
    for copy in copies:
        copy.wait()


def local_kernel(
    cells, before, after, cotangent, weights, local_out, lanes_out, cotangent_out, padded, table
):
    banded_forward(weights, table)
    beside = beside_layers(before[...], after[...])
    pad_cells(padded, cells[...], beside)

    def store(start, result):
        local_out[start : start + STEP, :] = result

    stencil(padded, table, False, store)
    whole = jnp.concatenate([cells[...].astype(F32), beside.astype(F32)], axis=1)
    lanes_out[...] = whole.T.astype(BF16)
    cotangent_out[...] = to_cells(cotangent[...]).astype(BF16)


def fetch_kernel():
    pass


def mode_in_group(rows, lanes):
    return lax.broadcasted_iota(jnp.int32, (rows, lanes), 0) % GROUP


def own_block(rows):
    width = GROUP * LANES // 4
    lane = lax.broadcasted_iota(jnp.int32, (rows, width), 1)
    return mode_in_group(rows, width) % (GROUP // 2) == lane // (LANES // 2)


def own_half(rows):
    return (mode_in_group(rows, LANES) < GROUP // 2) == low_lanes(rows)


def to_depth(modes, table, snaps, slabs):
    modes = modes.reshape(slabs, snaps, -1, LANES)
    both = [doubled(modes[:, b].reshape(-1, LANES)) for b in range(snaps)]
    result = dot(table, jnp.concatenate(both, axis=1).astype(BF16))
    return jnp.concatenate(
        [
            result[g : g + GROUP, b * LANES : (b + 1) * LANES]
            for g in range(0, result.shape[0], GROUP)
            for b in range(snaps)
        ],
        axis=0,
    )


def from_depth(modes, table, snaps, slabs):
    count = modes.shape[0] // GROUP
    both = []
    for b in range(snaps):
        own = [modes[g * GROUP : (g + 1) * GROUP] for g in range(b, count, snaps)]
        both.append(halved(jnp.concatenate(own, axis=0)))
    result = dot(table, jnp.concatenate(both, axis=1).astype(BF16))
    own = [
        result[:, b * LANES : (b + 1) * LANES].reshape(slabs, -1, LANES) for b in range(snaps)
    ]
    return jnp.stack(own, axis=1).reshape(-1, LANES)


def mix_kernel(snaps, slabs, received, gather, weights, scatter, back_out, diagonal_out):
    coef = to_depth(received[...].astype(F32), gather[...], snaps, slabs)
    count = coef.shape[0]
    wide = jnp.concatenate([coef] * (GROUP // 4), axis=1)
    diagonal = jnp.where(own_block(count), wide, 0.0).astype(BF16)
    diagonal_out[...] = diagonal
    rows = GROUP * snaps
    depth = GROUP * LANES // 4
    mixed = jnp.concatenate(
        [
            dot(diagonal[g * rows : (g + 1) * rows, :], weights[g * depth : (g + 1) * depth, :])
            for g in range(count // rows)
        ],
        axis=0,
    )
    mixed = jnp.where(own_half(count), mixed, swap_halves(mixed))
    back = from_depth(mixed, scatter[...], snaps, slabs).astype(BF16)
    back_out[...] = back.reshape(back_out.shape)


def activate_kernel(
    terms_in_slab,
    received,
    synthesis,
    local,
    cotangent,
    lanes,
    activated_out,
    grad_out,
    first_out,
    last_out,
    back_out,
    terms_out,
    spread,
):
    pre = dot(synthesis[...], received[...]) + local[...]
    cdf = 0.5 * (1.0 + lax.erf(pre * inv_root_two))
    density = jnp.exp(-0.5 * pre * pre) * inv_root_two_pi
    activated_out[...] = (pre * cdf).astype(BF16)
    grad = (cotangent[...].astype(F32) * (cdf + pre * density)).astype(BF16)
    back = dot(synthesis[...], grad, (0, 0))
    rounded = grad
    grad = grad.astype(F32)
    first, last = edge_layers(grad)
    spread[0:NY, :] = jnp.zeros((NY, 3 * LANES), BF16)
    spread[NY + CELLS : 2 * NY + CELLS, :] = jnp.zeros((NY, 3 * LANES), BF16)
    spread[NY : NY + CELLS, 0:LANES] = from_above(grad).astype(BF16)
    spread[NY : NY + CELLS, LANES : 2 * LANES] = grad.astype(BF16)
    spread[NY : NY + CELLS, 2 * LANES :] = from_below(grad).astype(BF16)
    half = LANES // 2
    low = low_lanes(half)
    twice = {}
    for b in range(3):
        product = dot(lanes[...], spread[NY * (2 - b) : NY * (2 - b) + CELLS, :])
        for c in range(3):
            for a in range(3):
                blocks = [BLOCK_OF_DEPTH[out + a - 1] * half for out in range(2)]
                columns = slice(c * LANES, (c + 1) * LANES)
                both = jnp.where(
                    low,
                    product[blocks[0] : blocks[0] + half, columns],
                    product[blocks[1] : blocks[1] + half, columns],
                )
                twice[a * 9 + b * 3 + c] = both + swap_halves(both)
    pairs = []
    for k in range(0, OFFSETS, 2):
        pairs.append(jnp.where(low, twice[k], twice.get(k + 1, 0.0)))
    pairs.append(jnp.zeros((TERM_ROWS - half * len(pairs), LANES), F32))
    terms = jnp.concatenate(pairs, axis=0)
    if terms_in_slab:
        slab_store(back_out, back, terms)
    else:
        back_out[...] = back.astype(BF16)
        terms_out[...] = terms.astype(BF16)
    grad_out[...] = rounded
    first_out[...] = first
    last_out[...] = last


def slab_store(slab, modes, terms):
    owners = slab.shape[0]
    modes = modes.reshape(owners, 8, LANES)
    terms = terms.reshape(owners, -1, LANES)
    slab[...] = jnp.concatenate([modes, terms], axis=1).astype(BF16)


def slab_load(slab):
    whole = slab[...].astype(F32)
    return whole[:, 0:8, :].reshape(-1, LANES), whole[:, 8:, :]


def unmix_kernel(snaps, slabs, scale, received, terms, gather, weights, scatter, grad_out, mixed_out, sums_out):
    in_slab = terms is None
    if in_slab:
        modes, terms = slab_load(received)
    else:
        modes, terms = received[...].astype(F32), terms[...].astype(F32)
    mixed = to_depth(modes, gather[...], snaps, slabs)
    mixed_out[...] = mixed.astype(BF16)
    count = mixed.shape[0]
    rows = GROUP * snaps
    depth = GROUP * LANES // 4
    sums = jnp.sum(terms, axis=0) * scale
    own = own_block(rows)
    placed = jnp.where(own_half(count), mixed, 0.0).astype(BF16)
    pieces = []
    for g in range(count // rows):
        full = dot(
            placed[g * rows : (g + 1) * rows, :], weights[g * depth : (g + 1) * depth, :], (1, 1)
        )
        full = jnp.where(own, full, 0.0)
        pieces.append(sum(full[:, k : k + LANES] for k in range(0, depth, LANES)))
    coef = jnp.concatenate(pieces, axis=0)
    coef = coef + swap_halves(coef)
    grad = from_depth(coef, scatter[...], snaps, slabs)
    if in_slab:
        owners = received.shape[0]
        share = sums.shape[0]
        slab_store(
            grad_out, grad, jnp.broadcast_to(sums[None], (owners, share, LANES)).reshape(-1, LANES)
        )
    else:
        grad_out[...] = grad.astype(BF16)
        sums_out[...] = sums


def weight_kernel(snaps, diagonal, mixed, out):
    rows = GROUP * snaps
    depth = GROUP * LANES // 4
    half = LANES // 2
    first = mode_in_group(rows, depth) < GROUP // 2
    for g in range(diagonal.shape[0] // rows):
        span = slice(g * rows, (g + 1) * rows)
        blocks = diagonal[span, :].astype(F32)
        blocks = [jnp.where(first, blocks, 0.0), jnp.where(first, 0.0, blocks)]
        blocks = jnp.concatenate(blocks, axis=1).astype(BF16)
        out[2 * g * depth : 2 * (g + 1) * depth, :] = dot(blocks, mixed[span, 0:half], (0, 0))


def output_kernel(cells, out):
    out[...] = to_field(cells[...])


def local_grad_kernel(grad, before, after, weights, out, padded, table):
    banded_backward(weights, table)
    pad_cells(padded, grad[...], beside_layers(before[...], after[...]))

    def store(start, result):
        out[start : start + STEP, :] = result

    stencil(padded, table, True, store)


def finish_kernel(received, sums, synthesis, local, grad_out, stencil_out):
    in_slab = sums is None
    if in_slab:
        modes, terms = slab_load(received)
        terms = terms.reshape(TERM_ROWS, LANES)
    else:
        modes, terms = received[...], sums[...].astype(F32)
    half = LANES // 2
    for k in range(OFFSETS):
        row = (k // 2) * half
        lane = (k % 2) * half
        stencil_out.buffer[k] = terms[row : row + half, lane : lane + half]
    stencil_out.copy.start()
    cells = (dot(synthesis[...], modes.astype(BF16)) + local[...]).astype(BF16)
    grad_out[...] = to_field(cells)


def shape(dims, dtype):
    return jax.ShapeDtypeStruct(dims, dtype)


class Staged:
    def __init__(self, source, buffer, semaphore):
        self.copy = pltpu.make_async_copy(source, buffer, semaphore)
        self.buffer = buffer
        self.copy.start()
        self.ready = False

    def load(self):
        if not self.ready:
            self.copy.wait()
            self.ready = True

    def __getitem__(self, index):
        self.load()
        return self.buffer[index]


class Sent:
    def __init__(self, target, buffer, semaphore):
        self.copy = pltpu.make_async_copy(buffer, target, semaphore)
        self.buffer = buffer

    def __setitem__(self, index, value):
        self.buffer[index] = value
        self.copy.start()

    def __getitem__(self, index):
        return self.buffer[index]

    @property
    def shape(self):
        return self.buffer.shape


def row_count(rows):
    return rows.stop - rows.start if isinstance(rows, slice) else rows


def run(
    body, outs, *operands, staged=(), sent=(), moved=(), plain=(), slots=(), scratch=(), flops=0, limit=VMEM_BYTES
):
    given = [k for k, operand in enumerate(operands) if operand is not None]
    made = [k for k, out in enumerate(outs) if out is not None]

    def rows_of(chosen, places, arrays):
        chosen = {k: chosen[k] if isinstance(chosen, dict) else None for k in places if k in chosen}
        return {k: rows or arrays[k].shape[0] for k, rows in chosen.items()}

    moved = dict(moved)
    slots = dict(slots)
    staged = rows_of(staged, given, operands)
    sent = rows_of(sent, made, outs)

    def kernel(*refs):
        refs = list(refs)

        def take(count):
            taken = refs[:count]
            del refs[:count]
            return taken

        def part(ref, rows):
            if isinstance(rows, slice):
                return ref.at[rows]
            return ref if ref.shape[0] == rows else ref.at[0:rows]

        filled = dict(zip(given, take(len(given))))
        take(len(slots))
        kept = dict(zip(made, take(len(made))))
        own = take(len(scratch))
        copies = []
        for place, (k, out) in enumerate(moved.items()):
            source, target = filled.pop(k), kept.pop(out)
            rows = min(source.shape[0], target.shape[0])
            semaphore = refs[-1].at[len(staged) + len(sent) + place]
            copies.append(
                pltpu.make_async_copy(part(source, rows), part(target, rows), semaphore)
            )
        for place, (k, buffer) in enumerate(zip(staged, take(len(staged)))):
            filled[k] = Staged(part(filled[k], staged[k]), buffer, refs[-1].at[place])
        for place, (k, buffer) in enumerate(zip(sent, take(len(sent)))):
            kept[k] = Sent(part(kept[k], sent[k]), buffer, refs[-1].at[len(staged) + place])
        for copy in copies:
            copy.start()
        body(
            *[filled.get(k) for k in range(len(operands)) if k not in moved],
            *[kept.get(k) for k in range(len(outs)) if k not in moved.values()],
            *own,
        )
        for k in staged:
            filled[k].load()
        for k in sent:
            kept[k].copy.wait()
        for copy in copies:
            copy.wait()

    arrays = [operands[k] for k in given]
    results = [outs[k] for k in made]
    size = sum(x.size * x.dtype.itemsize for x in (*arrays, *results))
    in_vmem = pl.BlockSpec(memory_space=pltpu.VMEM)
    in_hbm = pl.BlockSpec(memory_space=pltpu.HBM)
    buffers = [(operands[k], rows) for k, rows in staged.items()]
    buffers += [(outs[k], rows) for k, rows in sent.items()]
    buffers = [pltpu.VMEM((row_count(rows), *x.shape[1:]), x.dtype) for x, rows in buffers]
    if len(buffers) + len(moved) > 0:
        buffers.append(pltpu.SemaphoreType.DMA((len(buffers) + len(moved),)))
    results = pl.pallas_call(
        kernel,
        out_shape=results,
        in_specs=[in_hbm if k in staged or k in moved else in_vmem for k in given]
        + [in_hbm] * len(slots),
        out_specs=[in_hbm if k in sent or k in plain else in_vmem for k in made],
        input_output_aliases={len(given) + at: made.index(k) for at, k in enumerate(slots)},
        scratch_shapes=[*scratch, *buffers],
        compiler_params=pltpu.CompilerParams(vmem_limit_bytes=limit),
        cost_estimate=pl.CostEstimate(flops=flops, bytes_accessed=size, transcendentals=0),
        name=body.__name__ if hasattr(body, "__name__") else body.func.__name__,
    )(*arrays, *slots.values())
    results = dict(zip(made, results))
    return [results.get(k) for k in range(len(outs))]


def exchange(values):
    return lax.all_to_all(values, ("space", "batch"), split_axis=0, concat_axis=0, tiled=True)


def neighbours(first, last):
    ends = lax.axis_size("space") - 1
    before = lax.ppermute(last, "space", [(i, i + 1) for i in range(ends)])
    after = lax.ppermute(first, "space", [(i + 1, i) for i in range(ends)])
    return before, after


def shards(snapshots, cotangent, mode_weight, conv_weight):
    batches = lax.axis_size("batch")
    slabs = lax.axis_size("space")
    devices = batches * slabs
    _, channels, layers, plane = snapshots.shape
    modes = mode_weight.shape[0] * mode_weight.shape[1]
    half = LANES // 2
    assert channels == half and layers == 2 and plane == CELLS
    plane_rows = devices * modes
    count = modes * 2 * KZ * batches
    in_slab = modes == 8 and devices * 32 == TERM_ROWS

    analysis, synthesis = plane_tables(batches, slabs)
    gather, scatter, gather_back, scatter_back = depth_tables(slabs, layers, modes)
    weights = mode_weight.reshape(modes * 2 * KZ * channels, channels)
    taps = conv_weight.reshape(OFFSETS, channels, channels)
    field = shape((channels, layers, plane), BF16)
    wide = shape((CELLS, LANES), BF16)
    edge = shape((CELLS // 2, LANES), BF16)
    plane_modes = shape((plane_rows, LANES), BF16)
    padded = pltpu.VMEM((CELLS + 2 * NY, 2 * LANES), BF16)

    def send(values):
        return exchange(values.reshape(devices, modes, LANES)).reshape(plane_rows, LANES)

    packed = shape((weights.shape[0] // 2, LANES), BF16)
    to_send = shape((devices, modes, LANES), BF16) if modes % 8 == 0 else plane_modes
    cells, coef, first, last, slot = run(
        analyse_kernel,
        [wide, plane_modes, edge, edge, to_send],
        snapshots.reshape(field.shape),
        analysis,
        staged=(0, 1),
        sent=(0, 1, 2, 3),
        plain=(4,),
        limit=WHOLE_VMEM,
        flops=10**8,
    )
    weights, coef = lax.optimization_barrier((weights, coef))
    coef = send(coef)
    share = weights.shape[0] // CHUNKS
    (kept_weights,) = run(
        pack_kernel,
        [shape((HBM_BYTES // (2 * LANES), LANES), BF16)],
        *[weights] * CHUNKS,
        staged={k: slice(k * share, (k + 1) * share) for k in range(CHUNKS)},
        plain=(0,),
        scratch=[pltpu.VMEM(packed.shape, BF16), pltpu.SemaphoreType.DMA((CHUNKS,))],
        limit=LARGE_VMEM,
    )
    (packed_weights,) = run(fetch_kernel, [packed], kept_weights, moved={0: 0})
    before, after = neighbours(first, last)
    local, lanes, outer_cells = run(
        local_kernel,
        [shape((CELLS, LANES), F32), shape((2 * LANES, CELLS), BF16), wide],
        cells,
        before,
        after,
        cotangent.reshape(field.shape),
        taps,
        scratch=[padded, pltpu.VMEM((3, 2 * LANES, 3 * LANES), BF16)],
        flops=8 * 10**9,
    )
    back, diagonal = run(
        functools.partial(mix_kernel, batches, slabs),
        [to_send, shape((count, GROUP * half // 2), BF16)],
        coef,
        gather,
        packed_weights,
        scatter,
        sent=(0, 1),
        slots={0: slot},
        flops=4 * 10**8,
    )
    back = send(back)
    slab = shape((devices, 8 + TERM_ROWS // devices, LANES), BF16)
    activated, grad, first, last, back, terms = run(
        functools.partial(activate_kernel, in_slab),
        [
            wide,
            shape((HBM_BYTES // (2 * LANES), LANES), BF16),
            edge,
            edge,
            slab if in_slab else plane_modes,
            None if in_slab else shape((TERM_ROWS, LANES), BF16),
        ],
        back,
        np.ascontiguousarray(synthesis.T),
        local,
        outer_cells,
        lanes,
        sent={1: CELLS, 2: None, 3: None, 4: None},
        scratch=[pltpu.VMEM((CELLS + 2 * NY, 3 * LANES), BF16)],
        flops=10**9,
    )
    if in_slab:
        back = exchange(back)
    else:
        back = send(back)
        terms = exchange(terms.reshape(devices, TERM_ROWS // devices, LANES))
    before, after = neighbours(first, last)
    activated, packed_weights = run(
        output_kernel,
        [field, packed],
        activated,
        kept_weights,
        moved={1: 1},
        flops=10**8,
    )
    back, before, after, activated, packed_weights = lax.optimization_barrier(
        (back, before, after, activated, packed_weights)
    )
    scale = 1.0 / math.sqrt(batches * slabs * layers * plane)
    grad_modes, mixed_grad, sums = run(
        functools.partial(unmix_kernel, batches, slabs, scale),
        [
            slab if in_slab else plane_modes,
            shape((count, LANES), BF16),
            None if in_slab else shape((TERM_ROWS // devices, LANES), F32),
        ],
        back,
        None if in_slab else terms,
        gather_back,
        packed_weights,
        scatter_back,
        sent=(0,),
        flops=4 * 10**8,
    )
    if in_slab:
        grad_modes = exchange(grad_modes)
    else:
        grad_modes = send(grad_modes)
        sums = lax.all_gather(sums, ("space", "batch"), axis=0, tiled=True)
    (local,) = run(
        local_grad_kernel,
        [shape((CELLS, LANES), F32)],
        grad,
        before,
        after,
        taps,
        staged={0: CELLS},
        scratch=[padded, pltpu.VMEM((3, 3 * LANES, 2 * LANES), BF16)],
        flops=7 * 10**8,
    )
    (mode_gradient,) = run(
        functools.partial(weight_kernel, batches),
        [shape((modes * 2 * KZ * channels, channels), F32)],
        diagonal,
        mixed_grad,
        flops=4 * 10**8,
    )
    input_gradient, conv_gradient = run(
        finish_kernel,
        [field, shape((OFFSETS, channels, channels), F32)],
        grad_modes,
        sums,
        np.ascontiguousarray(analysis.T),
        local,
        sent=(1,),
        flops=10**8,
    )
    return (
        activated.reshape(snapshots.shape),
        input_gradient.reshape(snapshots.shape),
        mode_gradient.reshape(mode_weight.shape),
        conv_gradient.reshape(conv_weight.shape),
    )


def solution(mesh):
    in_specs = (
        P("batch", None, "space", None),
        P("batch", None, "space", None),
        P("batch", "space", None, None, None),
        P(),
    )
    out_specs = (
        P("batch", None, "space", None),
        P("batch", None, "space", None),
        P("batch", "space", None, None, None),
        P(),
    )
    return jax.shard_map(shards, mesh=mesh, in_specs=in_specs, out_specs=out_specs, check_vma=False)
```

```python
import functools
import math

import jax
import jax.numpy as jnp
import ml_dtypes
import numpy as np
from jax import lax
from jax.experimental import pallas as pl
from jax.experimental.pallas import tpu as pltpu
from jax.sharding import PartitionSpec as P

KX = 8
KY = 8
KZ = 12
NX = 32
NY = 32
CELLS = NX * NY
LANES = 128
GROUP = 8
OFFSETS = 27
TERM_ROWS = 1024
CHUNKS = 3
VMEM_BYTES = 40 * 1024 * 1024
LARGE_VMEM = 60 * 1024 * 1024
WHOLE_VMEM = 65000 * 1024
HBM_BYTES = 100 * 1024 * 256

F32 = jnp.float32
BF16 = jnp.bfloat16
inv_root_two = 1.0 / math.sqrt(2.0)
inv_root_two_pi = 1.0 / math.sqrt(2.0 * math.pi)


def basis_rows(half_count, length):
    row = np.arange(2 * half_count)[:, None]
    cell = np.arange(length)[None, :]
    frequency = np.where(row < half_count, row, row - half_count + 1)
    phases = (frequency * cell % length).astype(np.float32) * np.float32(2.0 * math.pi / length)
    return np.where(row < half_count, np.cos(phases), np.sin(phases)).astype(np.float32)


def plane_tables(batches, slabs):
    outer = (basis_rows(KX, NX)[:, None, :, None] * basis_rows(KY, NY)[None, :, None, :]).reshape(
        2 * KX, 2 * KY, CELLS
    )
    outer = outer.reshape(batches, 2 * KX // batches, slabs, 2 * KY // slabs, CELLS)
    outer = outer.transpose(2, 0, 1, 3, 4).reshape(4 * KX * KY, CELLS)
    analysis = (outer * np.float32(2.0 / math.sqrt(CELLS))).astype(ml_dtypes.bfloat16)
    synthesis = (outer * np.float32(2.0 / math.sqrt(4 * KX * KY))).astype(ml_dtypes.bfloat16)
    return analysis, synthesis


def depth_tables(slabs, layers, modes):
    rows = basis_rows(KZ, slabs * layers)
    analysis = (rows * np.float32(math.sqrt(2.0 / (slabs * layers)))).astype(ml_dtypes.bfloat16)
    synthesis = (rows * np.float32(math.sqrt(2.0 / (2 * KZ)))).astype(ml_dtypes.bfloat16)

    def spread(table, order):
        table = table.astype(np.float32).reshape(2 * KZ, slabs, layers)
        full = np.einsum("psz,mn->" + order, table, np.eye(modes, dtype=np.float32))
        return full.astype(ml_dtypes.bfloat16)

    def gathered(table):
        return spread(table, "mpzsn").reshape(modes * 2 * KZ, layers * slabs * modes)

    def scattered(table):
        return spread(table, "snzmp").reshape(slabs * modes, layers * modes * 2 * KZ)

    return gathered(analysis), scattered(synthesis), gathered(synthesis), scattered(analysis)


def dot(left, right, contract=(1, 0)):
    return lax.dot_general(
        left, right, (((contract[0],), (contract[1],)), ((), ())), preferred_element_type=F32
    )


def turn_table():
    row = lax.broadcasted_iota(jnp.int32, (LANES, LANES), 0)
    column = lax.broadcasted_iota(jnp.int32, (LANES, LANES), 1)
    return jnp.where(column == row % 2 * (LANES // 2) + row // 2, 1.0, 0.0).astype(BF16)


def to_cells(field):
    return dot(field.reshape(LANES, CELLS), turn_table(), (0, 0))


def to_field(cells):
    return dot(turn_table(), cells, (1, 1)).astype(BF16).reshape(LANES // 2, 2, CELLS)


def low_lanes(rows):
    return lax.broadcasted_iota(jnp.int32, (rows, LANES), 1) < LANES // 2


def swap_halves(values):
    return pltpu.roll(values, LANES // 2, 1)


def doubled(values):
    low = low_lanes(values.shape[0])
    swapped = swap_halves(values)
    return jnp.concatenate(
        [jnp.where(low, values, swapped), jnp.where(low, swapped, values)], axis=0
    )


def halved(values):
    low = low_lanes(values.shape[0])
    return jnp.concatenate([jnp.where(low, values, 0.0), jnp.where(low, 0.0, values)], axis=0)


def edge_layers(cells_first):
    top = cells_first[: CELLS // 2]
    bottom = cells_first[CELLS // 2 :]
    low = low_lanes(CELLS // 2)
    first = jnp.where(low, top, swap_halves(bottom))
    last = jnp.where(low, swap_halves(top), bottom)
    return first.astype(BF16), last.astype(BF16)


def beside_layers(before, after):
    before = before.astype(F32)
    after = after.astype(F32)
    low = low_lanes(CELLS // 2)
    top = jnp.where(low, before, swap_halves(after))
    bottom = jnp.where(low, swap_halves(before), after)
    return jnp.concatenate([top, bottom], axis=0).astype(BF16)


def y_cells(rows):
    return lax.broadcasted_iota(jnp.int32, (rows, LANES), 0) % NY


def from_below(values):
    return jnp.where(y_cells(values.shape[0]) == 0, 0.0, pltpu.roll(values, 1, 0))


def from_above(values):
    rows = values.shape[0]
    return jnp.where(y_cells(rows) == NY - 1, 0.0, pltpu.roll(values, rows - 1, 0))


def pad_cells(padded, own, beside):
    width = own.shape[1] + beside.shape[1]
    padded[0:NY, :] = jnp.zeros((NY, width), BF16)
    padded[NY + CELLS : 2 * NY + CELLS, :] = jnp.zeros((NY, width), BF16)
    padded[NY : NY + CELLS, 0 : own.shape[1]] = own
    padded[NY : NY + CELLS, own.shape[1] :] = beside


BLOCK_OF_DEPTH = {-1: 2, 0: 0, 1: 1, 2: 3}
STEP = 256


def stencil(padded, table, transposed, store):
    for start in range(0, CELLS, STEP):
        total = None
        for b in range(3):
            cells = padded[start + NY * b : start + NY * b + STEP, :]
            term = dot(cells, table[b], (1, 1) if transposed else (1, 0))
            total = term if total is None else total + term
        result = (
            from_below(total[:, 0:LANES])
            + total[:, LANES : 2 * LANES]
            + from_above(total[:, 2 * LANES :])
        )
        store(start, result)


def banded_forward(weights, table):
    half = LANES // 2
    for b in range(3):
        for c in range(3):
            for depth, block in BLOCK_OF_DEPTH.items():
                parts = []
                for out in range(2):
                    a = depth - out + 1
                    if 0 <= a < 3:
                        parts.append(weights[a * 9 + b * 3 + c])
                    else:
                        parts.append(jnp.zeros((half, half), BF16))
                table[b, block * half : (block + 1) * half, c * LANES : (c + 1) * LANES] = (
                    jnp.concatenate(parts, axis=1)
                )


def banded_backward(weights, table):
    half = LANES // 2
    for b in range(3):
        for c in range(3):
            for out in range(2):
                for pair in ((0, 1), (-1, 2)):
                    parts = []
                    for depth in pair:
                        a = depth - out + 1
                        if 0 <= a < 3:
                            parts.append(weights[(2 - a) * 9 + (2 - b) * 3 + 2 - c])
                        else:
                            parts.append(jnp.zeros((half, half), BF16))
                    row = c * LANES + out * half
                    column = BLOCK_OF_DEPTH[pair[0]] * half
                    table[b, row : row + half, column : column + LANES] = jnp.concatenate(
                        parts, axis=1
                    )


def analyse_kernel(field, analysis, cells_out, coef_out, first_out, last_out, _):
    cells = to_cells(field[...])
    rounded = cells.astype(BF16)
    coef_out[...] = dot(analysis[...], rounded).astype(BF16)
    cells_out[...] = rounded
    first, last = edge_layers(cells)
    first_out[...] = first
    last_out[...] = last


def pack_kernel(*refs):
    weights = refs[:CHUNKS]
    packed_out, buffer, semaphores = refs[CHUNKS:]
    rows = GROUP * LANES // 4
    share = buffer.shape[0] // CHUNKS
    copies = []
    for place, part in enumerate(weights):
        for g in range(share // rows):
            pair = [part[k * rows : (k + 1) * rows, :] for k in (2 * g, 2 * g + 1)]
            row = place * share + g * rows
            buffer[row : row + rows, :] = jnp.concatenate(pair, axis=1)
        span = slice(place * share, (place + 1) * share)
        copies.append(
            pltpu.make_async_copy(buffer.at[span], packed_out.at[span], semaphores.at[place])
        )
        copies[-1].start()
    for copy in copies:
        copy.wait()


def local_kernel(
    cells, before, after, cotangent, weights, local_out, lanes_out, cotangent_out, padded, table
):
    banded_forward(weights, table)
    beside = beside_layers(before[...], after[...])
    pad_cells(padded, cells[...], beside)

    def store(start, result):
        local_out[start : start + STEP, :] = result

    stencil(padded, table, False, store)
    whole = jnp.concatenate([cells[...].astype(F32), beside.astype(F32)], axis=1)
    lanes_out[...] = whole.T.astype(BF16)
    cotangent_out[...] = to_cells(cotangent[...]).astype(BF16)


def fetch_kernel():
    pass


def mode_in_group(rows, lanes):
    return lax.broadcasted_iota(jnp.int32, (rows, lanes), 0) % GROUP


def own_block(rows):
    width = GROUP * LANES // 4
    lane = lax.broadcasted_iota(jnp.int32, (rows, width), 1)
    return mode_in_group(rows, width) % (GROUP // 2) == lane // (LANES // 2)


def own_half(rows):
    return (mode_in_group(rows, LANES) < GROUP // 2) == low_lanes(rows)


def to_depth(modes, table, snaps, slabs):
    modes = modes.reshape(slabs, snaps, -1, LANES)
    both = [doubled(modes[:, b].reshape(-1, LANES)) for b in range(snaps)]
    result = dot(table, jnp.concatenate(both, axis=1).astype(BF16))
    return jnp.concatenate(
        [
            result[g : g + GROUP, b * LANES : (b + 1) * LANES]
            for g in range(0, result.shape[0], GROUP)
            for b in range(snaps)
        ],
        axis=0,
    )


def from_depth(modes, table, snaps, slabs):
    count = modes.shape[0] // GROUP
    both = []
    for b in range(snaps):
        own = [modes[g * GROUP : (g + 1) * GROUP] for g in range(b, count, snaps)]
        both.append(halved(jnp.concatenate(own, axis=0)))
    result = dot(table, jnp.concatenate(both, axis=1).astype(BF16))
    own = [
        result[:, b * LANES : (b + 1) * LANES].reshape(slabs, -1, LANES) for b in range(snaps)
    ]
    return jnp.stack(own, axis=1).reshape(-1, LANES)


def mix_kernel(snaps, slabs, received, gather, weights, scatter, back_out, diagonal_out):
    coef = to_depth(received[...].astype(F32), gather[...], snaps, slabs)
    count = coef.shape[0]
    wide = jnp.concatenate([coef] * (GROUP // 4), axis=1)
    diagonal = jnp.where(own_block(count), wide, 0.0).astype(BF16)
    diagonal_out[...] = diagonal
    rows = GROUP * snaps
    depth = GROUP * LANES // 4
    mixed = jnp.concatenate(
        [
            dot(diagonal[g * rows : (g + 1) * rows, :], weights[g * depth : (g + 1) * depth, :])
            for g in range(count // rows)
        ],
        axis=0,
    )
    mixed = jnp.where(own_half(count), mixed, swap_halves(mixed))
    back = from_depth(mixed, scatter[...], snaps, slabs).astype(BF16)
    back_out[...] = back.reshape(back_out.shape)


def activate_kernel(
    terms_in_slab,
    received,
    synthesis,
    local,
    cotangent,
    lanes,
    activated_out,
    grad_out,
    first_out,
    last_out,
    back_out,
    terms_out,
    spread,
):
    pre = dot(synthesis[...], received[...]) + local[...]
    cdf = 0.5 * (1.0 + lax.erf(pre * inv_root_two))
    density = jnp.exp(-0.5 * pre * pre) * inv_root_two_pi
    activated_out[...] = (pre * cdf).astype(BF16)
    grad = (cotangent[...].astype(F32) * (cdf + pre * density)).astype(BF16)
    back = dot(synthesis[...], grad, (0, 0))
    rounded = grad
    grad = grad.astype(F32)
    first, last = edge_layers(grad)
    spread[0:NY, :] = jnp.zeros((NY, 3 * LANES), BF16)
    spread[NY + CELLS : 2 * NY + CELLS, :] = jnp.zeros((NY, 3 * LANES), BF16)
    spread[NY : NY + CELLS, 0:LANES] = from_above(grad).astype(BF16)
    spread[NY : NY + CELLS, LANES : 2 * LANES] = grad.astype(BF16)
    spread[NY : NY + CELLS, 2 * LANES :] = from_below(grad).astype(BF16)
    half = LANES // 2
    low = low_lanes(half)
    twice = {}
    for b in range(3):
        product = dot(lanes[...], spread[NY * (2 - b) : NY * (2 - b) + CELLS, :])
        for c in range(3):
            for a in range(3):
                blocks = [BLOCK_OF_DEPTH[out + a - 1] * half for out in range(2)]
                columns = slice(c * LANES, (c + 1) * LANES)
                both = jnp.where(
                    low,
                    product[blocks[0] : blocks[0] + half, columns],
                    product[blocks[1] : blocks[1] + half, columns],
                )
                twice[a * 9 + b * 3 + c] = both + swap_halves(both)
    pairs = []
    for k in range(0, OFFSETS, 2):
        pairs.append(jnp.where(low, twice[k], twice.get(k + 1, 0.0)))
    pairs.append(jnp.zeros((TERM_ROWS - half * len(pairs), LANES), F32))
    terms = jnp.concatenate(pairs, axis=0)
    if terms_in_slab:
        slab_store(back_out, back, terms)
    else:
        back_out[...] = back.astype(BF16)
        terms_out[...] = terms.astype(BF16)
    grad_out[...] = rounded
    first_out[...] = first
    last_out[...] = last


def slab_store(slab, modes, terms):
    owners = slab.shape[0]
    modes = modes.reshape(owners, 8, LANES)
    terms = terms.reshape(owners, -1, LANES)
    slab[...] = jnp.concatenate([modes, terms], axis=1).astype(BF16)


def slab_load(slab):
    whole = slab[...].astype(F32)
    return whole[:, 0:8, :].reshape(-1, LANES), whole[:, 8:, :]


def unmix_kernel(snaps, slabs, scale, received, terms, gather, weights, scatter, grad_out, mixed_out, sums_out):
    in_slab = terms is None
    if in_slab:
        modes, terms = slab_load(received)
    else:
        modes, terms = received[...].astype(F32), terms[...].astype(F32)
    mixed = to_depth(modes, gather[...], snaps, slabs)
    mixed_out[...] = mixed.astype(BF16)
    count = mixed.shape[0]
    rows = GROUP * snaps
    depth = GROUP * LANES // 4
    sums = jnp.sum(terms, axis=0) * scale
    own = own_block(rows)
    placed = jnp.where(own_half(count), mixed, 0.0).astype(BF16)
    pieces = []
    for g in range(count // rows):
        full = dot(
            placed[g * rows : (g + 1) * rows, :], weights[g * depth : (g + 1) * depth, :], (1, 1)
        )
        full = jnp.where(own, full, 0.0)
        pieces.append(sum(full[:, k : k + LANES] for k in range(0, depth, LANES)))
    coef = jnp.concatenate(pieces, axis=0)
    coef = coef + swap_halves(coef)
    grad = from_depth(coef, scatter[...], snaps, slabs)
    if in_slab:
        owners = received.shape[0]
        share = sums.shape[0]
        slab_store(
            grad_out, grad, jnp.broadcast_to(sums[None], (owners, share, LANES)).reshape(-1, LANES)
        )
    else:
        grad_out[...] = grad.astype(BF16)
        sums_out[...] = sums


def weight_kernel(snaps, diagonal, mixed, out):
    rows = GROUP * snaps
    depth = GROUP * LANES // 4
    half = LANES // 2
    first = mode_in_group(rows, depth) < GROUP // 2
    for g in range(diagonal.shape[0] // rows):
        span = slice(g * rows, (g + 1) * rows)
        blocks = diagonal[span, :].astype(F32)
        blocks = [jnp.where(first, blocks, 0.0), jnp.where(first, 0.0, blocks)]
        blocks = jnp.concatenate(blocks, axis=1).astype(BF16)
        out[2 * g * depth : 2 * (g + 1) * depth, :] = dot(blocks, mixed[span, 0:half], (0, 0))


def output_kernel(cells, out):
    out[...] = to_field(cells[...])


def local_grad_kernel(grad, before, after, weights, out, padded, table):
    banded_backward(weights, table)
    pad_cells(padded, grad[...], beside_layers(before[...], after[...]))

    def store(start, result):
        out[start : start + STEP, :] = result

    stencil(padded, table, True, store)


def finish_kernel(received, sums, synthesis, local, grad_out, stencil_out):
    in_slab = sums is None
    if in_slab:
        modes, terms = slab_load(received)
        terms = terms.reshape(TERM_ROWS, LANES)
    else:
        modes, terms = received[...], sums[...].astype(F32)
    cells = (dot(synthesis[...], modes.astype(BF16)) + local[...]).astype(BF16)
    grad_out[...] = to_field(cells)
    half = LANES // 2
    for k in range(OFFSETS):
        row = (k // 2) * half
        lane = (k % 2) * half
        stencil_out[k] = terms[row : row + half, lane : lane + half]


def shape(dims, dtype):
    return jax.ShapeDtypeStruct(dims, dtype)


class Staged:
    def __init__(self, source, buffer, semaphore):
        self.copy = pltpu.make_async_copy(source, buffer, semaphore)
        self.buffer = buffer
        self.copy.start()
        self.ready = False

    def load(self):
        if not self.ready:
            self.copy.wait()
            self.ready = True

    def __getitem__(self, index):
        self.load()
        return self.buffer[index]


class Sent:
    def __init__(self, target, buffer, semaphore):
        self.copy = pltpu.make_async_copy(buffer, target, semaphore)
        self.buffer = buffer

    def __setitem__(self, index, value):
        self.buffer[index] = value
        self.copy.start()

    def __getitem__(self, index):
        return self.buffer[index]

    @property
    def shape(self):
        return self.buffer.shape


def row_count(rows):
    return rows.stop - rows.start if isinstance(rows, slice) else rows


def run(
    body, outs, *operands, staged=(), sent=(), moved=(), plain=(), slots=(), scratch=(), flops=0, limit=VMEM_BYTES
):
    given = [k for k, operand in enumerate(operands) if operand is not None]
    made = [k for k, out in enumerate(outs) if out is not None]

    def rows_of(chosen, places, arrays):
        chosen = {k: chosen[k] if isinstance(chosen, dict) else None for k in places if k in chosen}
        return {k: rows or arrays[k].shape[0] for k, rows in chosen.items()}

    moved = dict(moved)
    slots = dict(slots)
    staged = rows_of(staged, given, operands)
    sent = rows_of(sent, made, outs)

    def kernel(*refs):
        refs = list(refs)

        def take(count):
            taken = refs[:count]
            del refs[:count]
            return taken

        def part(ref, rows):
            if isinstance(rows, slice):
                return ref.at[rows]
            return ref if ref.shape[0] == rows else ref.at[0:rows]

        filled = dict(zip(given, take(len(given))))
        take(len(slots))
        kept = dict(zip(made, take(len(made))))
        own = take(len(scratch))
        copies = []
        for place, (k, out) in enumerate(moved.items()):
            source, target = filled.pop(k), kept.pop(out)
            rows = min(source.shape[0], target.shape[0])
            semaphore = refs[-1].at[len(staged) + len(sent) + place]
            copies.append(
                pltpu.make_async_copy(part(source, rows), part(target, rows), semaphore)
            )
        for place, (k, buffer) in enumerate(zip(staged, take(len(staged)))):
            filled[k] = Staged(part(filled[k], staged[k]), buffer, refs[-1].at[place])
        for place, (k, buffer) in enumerate(zip(sent, take(len(sent)))):
            kept[k] = Sent(part(kept[k], sent[k]), buffer, refs[-1].at[len(staged) + place])
        for copy in copies:
            copy.start()
        body(
            *[filled.get(k) for k in range(len(operands)) if k not in moved],
            *[kept.get(k) for k in range(len(outs)) if k not in moved.values()],
            *own,
        )
        for k in staged:
            filled[k].load()
        for k in sent:
            kept[k].copy.wait()
        for copy in copies:
            copy.wait()

    arrays = [operands[k] for k in given]
    results = [outs[k] for k in made]
    size = sum(x.size * x.dtype.itemsize for x in (*arrays, *results))
    in_vmem = pl.BlockSpec(memory_space=pltpu.VMEM)
    in_hbm = pl.BlockSpec(memory_space=pltpu.HBM)
    buffers = [(operands[k], rows) for k, rows in staged.items()]
    buffers += [(outs[k], rows) for k, rows in sent.items()]
    buffers = [pltpu.VMEM((row_count(rows), *x.shape[1:]), x.dtype) for x, rows in buffers]
    if len(buffers) + len(moved) > 0:
        buffers.append(pltpu.SemaphoreType.DMA((len(buffers) + len(moved),)))
    results = pl.pallas_call(
        kernel,
        out_shape=results,
        in_specs=[in_hbm if k in staged or k in moved else in_vmem for k in given]
        + [in_hbm] * len(slots),
        out_specs=[in_hbm if k in sent or k in plain else in_vmem for k in made],
        input_output_aliases={len(given) + at: made.index(k) for at, k in enumerate(slots)},
        scratch_shapes=[*scratch, *buffers],
        compiler_params=pltpu.CompilerParams(vmem_limit_bytes=limit),
        cost_estimate=pl.CostEstimate(flops=flops, bytes_accessed=size, transcendentals=0),
        name=body.__name__ if hasattr(body, "__name__") else body.func.__name__,
    )(*arrays, *slots.values())
    results = dict(zip(made, results))
    return [results.get(k) for k in range(len(outs))]


def exchange(values):
    return lax.all_to_all(values, ("space", "batch"), split_axis=0, concat_axis=0, tiled=True)


def neighbours(first, last):
    ends = lax.axis_size("space") - 1
    before = lax.ppermute(last, "space", [(i, i + 1) for i in range(ends)])
    after = lax.ppermute(first, "space", [(i + 1, i) for i in range(ends)])
    return before, after


def shards(snapshots, cotangent, mode_weight, conv_weight):
    batches = lax.axis_size("batch")
    slabs = lax.axis_size("space")
    devices = batches * slabs
    _, channels, layers, plane = snapshots.shape
    modes = mode_weight.shape[0] * mode_weight.shape[1]
    half = LANES // 2
    assert channels == half and layers == 2 and plane == CELLS
    plane_rows = devices * modes
    count = modes * 2 * KZ * batches
    in_slab = modes == 8 and devices * 32 == TERM_ROWS

    analysis, synthesis = plane_tables(batches, slabs)
    gather, scatter, gather_back, scatter_back = depth_tables(slabs, layers, modes)
    weights = mode_weight.reshape(modes * 2 * KZ * channels, channels)
    taps = conv_weight.reshape(OFFSETS, channels, channels)
    field = shape((channels, layers, plane), BF16)
    wide = shape((CELLS, LANES), BF16)
    edge = shape((CELLS // 2, LANES), BF16)
    plane_modes = shape((plane_rows, LANES), BF16)
    padded = pltpu.VMEM((CELLS + 2 * NY, 2 * LANES), BF16)

    def send(values):
        return exchange(values.reshape(devices, modes, LANES)).reshape(plane_rows, LANES)

    packed = shape((weights.shape[0] // 2, LANES), BF16)
    to_send = shape((devices, modes, LANES), BF16) if modes % 8 == 0 else plane_modes
    cells, coef, first, last, slot = run(
        analyse_kernel,
        [wide, plane_modes, edge, edge, to_send],
        snapshots.reshape(field.shape),
        analysis,
        staged=(0, 1),
        sent=(0, 1, 2, 3),
        plain=(4,),
        limit=WHOLE_VMEM,
        flops=10**8,
    )
    weights, coef = lax.optimization_barrier((weights, coef))
    coef = send(coef)
    share = weights.shape[0] // CHUNKS
    (kept_weights,) = run(
        pack_kernel,
        [shape((HBM_BYTES // (2 * LANES), LANES), BF16)],
        *[weights] * CHUNKS,
        staged={k: slice(k * share, (k + 1) * share) for k in range(CHUNKS)},
        plain=(0,),
        scratch=[pltpu.VMEM(packed.shape, BF16), pltpu.SemaphoreType.DMA((CHUNKS,))],
        limit=LARGE_VMEM,
    )
    (packed_weights,) = run(fetch_kernel, [packed], kept_weights, moved={0: 0})
    back, diagonal = run(
        functools.partial(mix_kernel, batches, slabs),
        [to_send, shape((count, GROUP * half // 2), BF16)],
        coef,
        gather,
        packed_weights,
        scatter,
        sent=(0, 1),
        slots={0: slot},
        flops=4 * 10**8,
    )
    back, first, last = lax.optimization_barrier((back, first, last))
    back = send(back)
    before, after = neighbours(first, last)
    local, lanes, outer_cells = run(
        local_kernel,
        [shape((CELLS, LANES), F32), shape((2 * LANES, CELLS), BF16), wide],
        cells,
        before,
        after,
        cotangent.reshape(field.shape),
        taps,
        scratch=[padded, pltpu.VMEM((3, 2 * LANES, 3 * LANES), BF16)],
        flops=8 * 10**9,
    )
    slab = shape((devices, 8 + TERM_ROWS // devices, LANES), BF16)
    activated, grad, first, last, back, terms = run(
        functools.partial(activate_kernel, in_slab),
        [
            wide,
            shape((HBM_BYTES // (2 * LANES), LANES), BF16),
            edge,
            edge,
            slab if in_slab else plane_modes,
            None if in_slab else shape((TERM_ROWS, LANES), BF16),
        ],
        back,
        np.ascontiguousarray(synthesis.T),
        local,
        outer_cells,
        lanes,
        sent={1: CELLS, 2: None, 3: None, 4: None},
        scratch=[pltpu.VMEM((CELLS + 2 * NY, 3 * LANES), BF16)],
        flops=10**9,
    )
    if in_slab:
        back = exchange(back)
    else:
        back = send(back)
        terms = exchange(terms.reshape(devices, TERM_ROWS // devices, LANES))
    before, after = neighbours(first, last)
    activated, packed_weights = run(
        output_kernel,
        [field, packed],
        activated,
        kept_weights,
        moved={1: 1},
        flops=10**8,
    )
    back, before, after, activated, packed_weights = lax.optimization_barrier(
        (back, before, after, activated, packed_weights)
    )
    scale = 1.0 / math.sqrt(batches * slabs * layers * plane)
    grad_modes, mixed_grad, sums = run(
        functools.partial(unmix_kernel, batches, slabs, scale),
        [
            slab if in_slab else plane_modes,
            shape((count, LANES), BF16),
            None if in_slab else shape((TERM_ROWS // devices, LANES), F32),
        ],
        back,
        None if in_slab else terms,
        gather_back,
        packed_weights,
        scatter_back,
        sent=(0,),
        flops=4 * 10**8,
    )
    if in_slab:
        grad_modes = exchange(grad_modes)
    else:
        grad_modes = send(grad_modes)
        sums = lax.all_gather(sums, ("space", "batch"), axis=0, tiled=True)
    (local,) = run(
        local_grad_kernel,
        [shape((CELLS, LANES), F32)],
        grad,
        before,
        after,
        taps,
        staged={0: CELLS},
        scratch=[padded, pltpu.VMEM((3, 3 * LANES, 2 * LANES), BF16)],
        flops=7 * 10**8,
    )
    (mode_gradient,) = run(
        functools.partial(weight_kernel, batches),
        [shape((modes * 2 * KZ * channels, channels), F32)],
        diagonal,
        mixed_grad,
        flops=4 * 10**8,
    )
    input_gradient, conv_gradient = run(
        finish_kernel,
        [field, shape((OFFSETS, channels, channels), F32)],
        grad_modes,
        sums,
        np.ascontiguousarray(analysis.T),
        local,
        flops=10**8,
    )
    return (
        activated.reshape(snapshots.shape),
        input_gradient.reshape(snapshots.shape),
        mode_gradient.reshape(mode_weight.shape),
        conv_gradient.reshape(conv_weight.shape),
    )


def solution(mesh):
    in_specs = (
        P("batch", None, "space", None),
        P("batch", None, "space", None),
        P("batch", "space", None, None, None),
        P(),
    )
    out_specs = (
        P("batch", None, "space", None),
        P("batch", None, "space", None),
        P("batch", "space", None, None, None),
        P(),
    )
    return jax.shard_map(shards, mesh=mesh, in_specs=in_specs, out_specs=out_specs, check_vma=False)
```

```python
import functools
import math

import jax
import jax.numpy as jnp
import ml_dtypes
import numpy as np
from jax import lax
from jax.experimental import pallas as pl
from jax.experimental.pallas import tpu as pltpu
from jax.sharding import PartitionSpec as P

KX = 8
KY = 8
KZ = 12
NX = 32
NY = 32
CELLS = NX * NY
LANES = 128
GROUP = 8
OFFSETS = 27
TERM_ROWS = 1024
CHUNKS = 3
VMEM_BYTES = 40 * 1024 * 1024
LARGE_VMEM = 60 * 1024 * 1024
WHOLE_VMEM = 65000 * 1024
HBM_BYTES = 100 * 1024 * 256

F32 = jnp.float32
BF16 = jnp.bfloat16
inv_root_two = 1.0 / math.sqrt(2.0)
inv_root_two_pi = 1.0 / math.sqrt(2.0 * math.pi)


def basis_rows(half_count, length):
    row = np.arange(2 * half_count)[:, None]
    cell = np.arange(length)[None, :]
    frequency = np.where(row < half_count, row, row - half_count + 1)
    phases = (frequency * cell % length).astype(np.float32) * np.float32(2.0 * math.pi / length)
    return np.where(row < half_count, np.cos(phases), np.sin(phases)).astype(np.float32)


def plane_factors(batches, slabs):
    modes_x, modes_y = 2 * KX, 2 * KY

    def columns(values, cells):
        values = np.broadcast_to(values, (modes_x, modes_y, cells))
        values = values.reshape(batches, modes_x // batches, slabs, modes_y // slabs, cells)
        values = values.transpose(2, 0, 1, 3, 4).reshape(modes_x * modes_y, cells)
        return np.ascontiguousarray(values.T)

    across = columns(basis_rows(KX, NX)[:, None, :], NX)
    along_y = columns(basis_rows(KY, NY)[None, :, :], NY)
    return across, along_y


def plane_analysis(across, along_y):
    outer = (across[:, None, :] * along_y[None, :, :]).reshape(CELLS, -1).T
    return (outer * np.float32(2.0 / math.sqrt(CELLS))).astype(ml_dtypes.bfloat16)


def depth_tables(slabs, layers, modes):
    rows = basis_rows(KZ, slabs * layers)
    analysis = (rows * np.float32(math.sqrt(2.0 / (slabs * layers)))).astype(ml_dtypes.bfloat16)
    synthesis = (rows * np.float32(math.sqrt(2.0 / (2 * KZ)))).astype(ml_dtypes.bfloat16)

    def spread(table, order):
        table = table.astype(np.float32).reshape(2 * KZ, slabs, layers)
        full = np.einsum("psz,mn->" + order, table, np.eye(modes, dtype=np.float32))
        return full.astype(ml_dtypes.bfloat16)

    def gathered(table):
        return spread(table, "mpzsn").reshape(modes * 2 * KZ, layers * slabs * modes)

    def scattered(table):
        return spread(table, "snzmp").reshape(slabs * modes, layers * modes * 2 * KZ)

    return gathered(analysis), scattered(synthesis), gathered(synthesis), scattered(analysis)


def dot(left, right, contract=(1, 0)):
    return lax.dot_general(
        left, right, (((contract[0],), (contract[1],)), ((), ())), preferred_element_type=F32
    )


def turn_table():
    row = lax.broadcasted_iota(jnp.int32, (LANES, LANES), 0)
    column = lax.broadcasted_iota(jnp.int32, (LANES, LANES), 1)
    return jnp.where(column == row % 2 * (LANES // 2) + row // 2, 1.0, 0.0).astype(BF16)


def to_cells(field):
    return dot(field.reshape(LANES, CELLS), turn_table(), (0, 0))


def to_field(cells):
    return dot(turn_table(), cells, (1, 1)).astype(BF16).reshape(LANES // 2, 2, CELLS)


def low_lanes(rows):
    return lax.broadcasted_iota(jnp.int32, (rows, LANES), 1) < LANES // 2


def swap_halves(values):
    return pltpu.roll(values, LANES // 2, 1)


def doubled(values):
    low = low_lanes(values.shape[0])
    swapped = swap_halves(values)
    return jnp.concatenate(
        [jnp.where(low, values, swapped), jnp.where(low, swapped, values)], axis=0
    )


def halved(values):
    low = low_lanes(values.shape[0])
    return jnp.concatenate([jnp.where(low, values, 0.0), jnp.where(low, 0.0, values)], axis=0)


def edge_layers(cells_first):
    top = cells_first[: CELLS // 2]
    bottom = cells_first[CELLS // 2 :]
    low = low_lanes(CELLS // 2)
    first = jnp.where(low, top, swap_halves(bottom))
    last = jnp.where(low, swap_halves(top), bottom)
    return first.astype(BF16), last.astype(BF16)


def beside_layers(before, after):
    before = before.astype(F32)
    after = after.astype(F32)
    low = low_lanes(CELLS // 2)
    top = jnp.where(low, before, swap_halves(after))
    bottom = jnp.where(low, swap_halves(before), after)
    return jnp.concatenate([top, bottom], axis=0).astype(BF16)


def y_cells(rows):
    return lax.broadcasted_iota(jnp.int32, (rows, LANES), 0) % NY


def from_below(values):
    return jnp.where(y_cells(values.shape[0]) == 0, 0.0, pltpu.roll(values, 1, 0))


def from_above(values):
    rows = values.shape[0]
    return jnp.where(y_cells(rows) == NY - 1, 0.0, pltpu.roll(values, rows - 1, 0))


def pad_cells(padded, own, beside):
    width = own.shape[1] + beside.shape[1]
    padded[0:NY, :] = jnp.zeros((NY, width), BF16)
    padded[NY + CELLS : 2 * NY + CELLS, :] = jnp.zeros((NY, width), BF16)
    padded[NY : NY + CELLS, 0 : own.shape[1]] = own
    padded[NY : NY + CELLS, own.shape[1] :] = beside


BLOCK_OF_DEPTH = {-1: 2, 0: 0, 1: 1, 2: 3}
STEP = 256


def stencil(padded, table, transposed, store):
    for start in range(0, CELLS, STEP):
        total = None
        for b in range(3):
            cells = padded[start + NY * b : start + NY * b + STEP, :]
            term = dot(cells, table[b], (1, 1) if transposed else (1, 0))
            total = term if total is None else total + term
        result = (
            from_below(total[:, 0:LANES])
            + total[:, LANES : 2 * LANES]
            + from_above(total[:, 2 * LANES :])
        )
        store(start, result)


def banded_forward(weights, table):
    half = LANES // 2
    for b in range(3):
        for c in range(3):
            for depth, block in BLOCK_OF_DEPTH.items():
                parts = []
                for out in range(2):
                    a = depth - out + 1
                    if 0 <= a < 3:
                        parts.append(weights[a * 9 + b * 3 + c])
                    else:
                        parts.append(jnp.zeros((half, half), BF16))
                table[b, block * half : (block + 1) * half, c * LANES : (c + 1) * LANES] = (
                    jnp.concatenate(parts, axis=1)
                )


def banded_backward(weights, table):
    half = LANES // 2
    for b in range(3):
        for c in range(3):
            for out in range(2):
                for pair in ((0, 1), (-1, 2)):
                    parts = []
                    for depth in pair:
                        a = depth - out + 1
                        if 0 <= a < 3:
                            parts.append(weights[(2 - a) * 9 + (2 - b) * 3 + 2 - c])
                        else:
                            parts.append(jnp.zeros((half, half), BF16))
                    row = c * LANES + out * half
                    column = BLOCK_OF_DEPTH[pair[0]] * half
                    table[b, row : row + half, column : column + LANES] = jnp.concatenate(
                        parts, axis=1
                    )


def analyse_kernel(field, analysis, cells_out, coef_out, first_out, last_out, _):
    cells = to_cells(field[...])
    rounded = cells.astype(BF16)
    coef_out[...] = dot(analysis[...], rounded).astype(BF16)
    cells_out[...] = rounded
    first, last = edge_layers(cells)
    first_out[...] = first
    last_out[...] = last


def pack_kernel(*refs):
    weights = refs[:CHUNKS]
    packed_out, buffer, semaphores = refs[CHUNKS:]
    rows = GROUP * LANES // 4
    share = buffer.shape[0] // CHUNKS
    copies = []
    for place, part in enumerate(weights):
        for g in range(share // rows):
            pair = [part[k * rows : (k + 1) * rows, :] for k in (2 * g, 2 * g + 1)]
            row = place * share + g * rows
            buffer[row : row + rows, :] = jnp.concatenate(pair, axis=1)
        span = slice(place * share, (place + 1) * share)
        copies.append(
            pltpu.make_async_copy(buffer.at[span], packed_out.at[span], semaphores.at[place])
        )
        copies[-1].start()
    for copy in copies:
        copy.wait()


def local_kernel(
    cells,
    before,
    after,
    cotangent,
    weights,
    across,
    along_y,
    local_out,
    lanes_out,
    cotangent_out,
    synthesis_out,
    padded,
    table,
):
    scale = 2.0 / math.sqrt(4 * KX * KY)
    for x in range(NX):
        rows = across[x : x + 1, :] * along_y[...] * scale
        synthesis_out[x * NY : (x + 1) * NY, :] = rows.astype(BF16)
    banded_forward(weights, table)
    beside = beside_layers(before[...], after[...])
    pad_cells(padded, cells[...], beside)

    def store(start, result):
        local_out[start : start + STEP, :] = result

    stencil(padded, table, False, store)
    whole = jnp.concatenate([cells[...].astype(F32), beside.astype(F32)], axis=1)
    lanes_out[...] = whole.T.astype(BF16)
    cotangent_out[...] = to_cells(cotangent[...]).astype(BF16)


def fetch_kernel():
    pass


def mode_in_group(rows, lanes):
    return lax.broadcasted_iota(jnp.int32, (rows, lanes), 0) % GROUP


def own_block(rows):
    width = GROUP * LANES // 4
    lane = lax.broadcasted_iota(jnp.int32, (rows, width), 1)
    return mode_in_group(rows, width) % (GROUP // 2) == lane // (LANES // 2)


def own_half(rows):
    return (mode_in_group(rows, LANES) < GROUP // 2) == low_lanes(rows)


def to_depth(modes, table, snaps, slabs):
    modes = modes.reshape(slabs, snaps, -1, LANES)
    both = [doubled(modes[:, b].reshape(-1, LANES)) for b in range(snaps)]
    result = dot(table, jnp.concatenate(both, axis=1).astype(BF16))
    return jnp.concatenate(
        [
            result[g : g + GROUP, b * LANES : (b + 1) * LANES]
            for g in range(0, result.shape[0], GROUP)
            for b in range(snaps)
        ],
        axis=0,
    )


def from_depth(modes, table, snaps, slabs):
    count = modes.shape[0] // GROUP
    both = []
    for b in range(snaps):
        own = [modes[g * GROUP : (g + 1) * GROUP] for g in range(b, count, snaps)]
        both.append(halved(jnp.concatenate(own, axis=0)))
    result = dot(table, jnp.concatenate(both, axis=1).astype(BF16))
    own = [
        result[:, b * LANES : (b + 1) * LANES].reshape(slabs, -1, LANES) for b in range(snaps)
    ]
    return jnp.stack(own, axis=1).reshape(-1, LANES)


def mix_kernel(snaps, slabs, received, gather, weights, scatter, back_out, diagonal_out):
    coef = to_depth(received[...].astype(F32), gather[...], snaps, slabs)
    count = coef.shape[0]
    wide = jnp.concatenate([coef] * (GROUP // 4), axis=1)
    diagonal = jnp.where(own_block(count), wide, 0.0).astype(BF16)
    diagonal_out[...] = diagonal
    rows = GROUP * snaps
    depth = GROUP * LANES // 4
    mixed = jnp.concatenate(
        [
            dot(diagonal[g * rows : (g + 1) * rows, :], weights[g * depth : (g + 1) * depth, :])
            for g in range(count // rows)
        ],
        axis=0,
    )
    mixed = jnp.where(own_half(count), mixed, swap_halves(mixed))
    back = from_depth(mixed, scatter[...], snaps, slabs).astype(BF16)
    back_out[...] = back.reshape(back_out.shape)


def activate_kernel(
    terms_in_slab,
    received,
    synthesis,
    local,
    cotangent,
    lanes,
    activated_out,
    grad_out,
    first_out,
    last_out,
    back_out,
    terms_out,
    spread,
):
    pre = dot(synthesis[...], received[...]) + local[...]
    cdf = 0.5 * (1.0 + lax.erf(pre * inv_root_two))
    density = jnp.exp(-0.5 * pre * pre) * inv_root_two_pi
    activated_out[...] = (pre * cdf).astype(BF16)
    grad = (cotangent[...].astype(F32) * (cdf + pre * density)).astype(BF16)
    back = dot(synthesis[...], grad, (0, 0))
    rounded = grad
    grad = grad.astype(F32)
    first, last = edge_layers(grad)
    spread[0:NY, :] = jnp.zeros((NY, 3 * LANES), BF16)
    spread[NY + CELLS : 2 * NY + CELLS, :] = jnp.zeros((NY, 3 * LANES), BF16)
    spread[NY : NY + CELLS, 0:LANES] = from_above(grad).astype(BF16)
    spread[NY : NY + CELLS, LANES : 2 * LANES] = grad.astype(BF16)
    spread[NY : NY + CELLS, 2 * LANES :] = from_below(grad).astype(BF16)
    half = LANES // 2
    low = low_lanes(half)
    twice = {}
    for b in range(3):
        product = dot(lanes[...], spread[NY * (2 - b) : NY * (2 - b) + CELLS, :])
        for c in range(3):
            for a in range(3):
                blocks = [BLOCK_OF_DEPTH[out + a - 1] * half for out in range(2)]
                columns = slice(c * LANES, (c + 1) * LANES)
                both = jnp.where(
                    low,
                    product[blocks[0] : blocks[0] + half, columns],
                    product[blocks[1] : blocks[1] + half, columns],
                )
                twice[a * 9 + b * 3 + c] = both + swap_halves(both)
    pairs = []
    for k in range(0, OFFSETS, 2):
        pairs.append(jnp.where(low, twice[k], twice.get(k + 1, 0.0)))
    pairs.append(jnp.zeros((TERM_ROWS - half * len(pairs), LANES), F32))
    terms = jnp.concatenate(pairs, axis=0)
    if terms_in_slab:
        slab_store(back_out, back, terms)
    else:
        back_out[...] = back.astype(BF16)
        terms_out[...] = terms.astype(BF16)
    grad_out[...] = rounded
    first_out[...] = first
    last_out[...] = last


def slab_store(slab, modes, terms):
    owners = slab.shape[0]
    modes = modes.reshape(owners, 8, LANES)
    terms = terms.reshape(owners, -1, LANES)
    slab[...] = jnp.concatenate([modes, terms], axis=1).astype(BF16)


def slab_load(slab):
    whole = slab[...].astype(F32)
    return whole[:, 0:8, :].reshape(-1, LANES), whole[:, 8:, :]


def unmix_kernel(snaps, slabs, scale, received, terms, gather, weights, scatter, grad_out, mixed_out, sums_out):
    in_slab = terms is None
    if in_slab:
        modes, terms = slab_load(received)
    else:
        modes, terms = received[...].astype(F32), terms[...].astype(F32)
    mixed = to_depth(modes, gather[...], snaps, slabs)
    mixed_out[...] = mixed.astype(BF16)
    count = mixed.shape[0]
    rows = GROUP * snaps
    depth = GROUP * LANES // 4
    sums = jnp.sum(terms, axis=0) * scale
    own = own_block(rows)
    placed = jnp.where(own_half(count), mixed, 0.0).astype(BF16)
    pieces = []
    for g in range(count // rows):
        full = dot(
            placed[g * rows : (g + 1) * rows, :], weights[g * depth : (g + 1) * depth, :], (1, 1)
        )
        full = jnp.where(own, full, 0.0)
        pieces.append(sum(full[:, k : k + LANES] for k in range(0, depth, LANES)))
    coef = jnp.concatenate(pieces, axis=0)
    coef = coef + swap_halves(coef)
    grad = from_depth(coef, scatter[...], snaps, slabs)
    if in_slab:
        owners = received.shape[0]
        share = sums.shape[0]
        slab_store(
            grad_out, grad, jnp.broadcast_to(sums[None], (owners, share, LANES)).reshape(-1, LANES)
        )
    else:
        grad_out[...] = grad.astype(BF16)
        sums_out[...] = sums


def weight_kernel(snaps, diagonal, mixed, out):
    rows = GROUP * snaps
    depth = GROUP * LANES // 4
    half = LANES // 2
    first = mode_in_group(rows, depth) < GROUP // 2
    for g in range(diagonal.shape[0] // rows):
        span = slice(g * rows, (g + 1) * rows)
        blocks = diagonal[span, :].astype(F32)
        blocks = [jnp.where(first, blocks, 0.0), jnp.where(first, 0.0, blocks)]
        blocks = jnp.concatenate(blocks, axis=1).astype(BF16)
        out[2 * g * depth : 2 * (g + 1) * depth, :] = dot(blocks, mixed[span, 0:half], (0, 0))


def output_kernel(cells, out):
    out[...] = to_field(cells[...])


def local_grad_kernel(grad, before, after, weights, out, padded, table):
    banded_backward(weights, table)
    pad_cells(padded, grad[...], beside_layers(before[...], after[...]))

    def store(start, result):
        out[start : start + STEP, :] = result

    stencil(padded, table, True, store)


def finish_kernel(received, sums, synthesis, local, grad_out, stencil_out):
    in_slab = sums is None
    if in_slab:
        modes, terms = slab_load(received)
        terms = terms.reshape(TERM_ROWS, LANES)
    else:
        modes, terms = received[...], sums[...].astype(F32)
    cells = (dot(synthesis[...], modes.astype(BF16)) + local[...]).astype(BF16)
    grad_out[...] = to_field(cells)
    half = LANES // 2
    for k in range(OFFSETS):
        row = (k // 2) * half
        lane = (k % 2) * half
        stencil_out[k] = terms[row : row + half, lane : lane + half]


def shape(dims, dtype):
    return jax.ShapeDtypeStruct(dims, dtype)


class Staged:
    def __init__(self, source, buffer, semaphore):
        self.copy = pltpu.make_async_copy(source, buffer, semaphore)
        self.buffer = buffer
        self.copy.start()
        self.ready = False

    def load(self):
        if not self.ready:
            self.copy.wait()
            self.ready = True

    def __getitem__(self, index):
        self.load()
        return self.buffer[index]


class Sent:
    def __init__(self, target, buffer, semaphore):
        self.copy = pltpu.make_async_copy(buffer, target, semaphore)
        self.buffer = buffer

    def __setitem__(self, index, value):
        self.buffer[index] = value
        self.copy.start()

    def __getitem__(self, index):
        return self.buffer[index]

    @property
    def shape(self):
        return self.buffer.shape


def row_count(rows):
    return rows.stop - rows.start if isinstance(rows, slice) else rows


def run(
    body, outs, *operands, staged=(), sent=(), moved=(), plain=(), slots=(), scratch=(), flops=0, limit=VMEM_BYTES
):
    given = [k for k, operand in enumerate(operands) if operand is not None]
    made = [k for k, out in enumerate(outs) if out is not None]

    def rows_of(chosen, places, arrays):
        chosen = {k: chosen[k] if isinstance(chosen, dict) else None for k in places if k in chosen}
        return {k: rows or arrays[k].shape[0] for k, rows in chosen.items()}

    moved = dict(moved)
    slots = dict(slots)
    staged = rows_of(staged, given, operands)
    sent = rows_of(sent, made, outs)

    def kernel(*refs):
        refs = list(refs)

        def take(count):
            taken = refs[:count]
            del refs[:count]
            return taken

        def part(ref, rows):
            if isinstance(rows, slice):
                return ref.at[rows]
            return ref if ref.shape[0] == rows else ref.at[0:rows]

        filled = dict(zip(given, take(len(given))))
        take(len(slots))
        kept = dict(zip(made, take(len(made))))
        own = take(len(scratch))
        copies = []
        for place, (k, out) in enumerate(moved.items()):
            source, target = filled.pop(k), kept.pop(out)
            rows = min(source.shape[0], target.shape[0])
            semaphore = refs[-1].at[len(staged) + len(sent) + place]
            copies.append(
                pltpu.make_async_copy(part(source, rows), part(target, rows), semaphore)
            )
        for place, (k, buffer) in enumerate(zip(staged, take(len(staged)))):
            filled[k] = Staged(part(filled[k], staged[k]), buffer, refs[-1].at[place])
        for place, (k, buffer) in enumerate(zip(sent, take(len(sent)))):
            kept[k] = Sent(part(kept[k], sent[k]), buffer, refs[-1].at[len(staged) + place])
        for copy in copies:
            copy.start()
        body(
            *[filled.get(k) for k in range(len(operands)) if k not in moved],
            *[kept.get(k) for k in range(len(outs)) if k not in moved.values()],
            *own,
        )
        for k in staged:
            filled[k].load()
        for k in sent:
            kept[k].copy.wait()
        for copy in copies:
            copy.wait()

    arrays = [operands[k] for k in given]
    results = [outs[k] for k in made]
    size = sum(x.size * x.dtype.itemsize for x in (*arrays, *results))
    in_vmem = pl.BlockSpec(memory_space=pltpu.VMEM)
    in_hbm = pl.BlockSpec(memory_space=pltpu.HBM)
    buffers = [(operands[k], rows) for k, rows in staged.items()]
    buffers += [(outs[k], rows) for k, rows in sent.items()]
    buffers = [pltpu.VMEM((row_count(rows), *x.shape[1:]), x.dtype) for x, rows in buffers]
    if len(buffers) + len(moved) > 0:
        buffers.append(pltpu.SemaphoreType.DMA((len(buffers) + len(moved),)))
    results = pl.pallas_call(
        kernel,
        out_shape=results,
        in_specs=[in_hbm if k in staged or k in moved else in_vmem for k in given]
        + [in_hbm] * len(slots),
        out_specs=[in_hbm if k in sent or k in plain else in_vmem for k in made],
        input_output_aliases={len(given) + at: made.index(k) for at, k in enumerate(slots)},
        scratch_shapes=[*scratch, *buffers],
        compiler_params=pltpu.CompilerParams(vmem_limit_bytes=limit),
        cost_estimate=pl.CostEstimate(flops=flops, bytes_accessed=size, transcendentals=0),
        name=body.__name__ if hasattr(body, "__name__") else body.func.__name__,
    )(*arrays, *slots.values())
    results = dict(zip(made, results))
    return [results.get(k) for k in range(len(outs))]


def exchange(values):
    return lax.all_to_all(values, ("space", "batch"), split_axis=0, concat_axis=0, tiled=True)


def neighbours(first, last):
    ends = lax.axis_size("space") - 1
    before = lax.ppermute(last, "space", [(i, i + 1) for i in range(ends)])
    after = lax.ppermute(first, "space", [(i + 1, i) for i in range(ends)])
    return before, after


def shards(snapshots, cotangent, mode_weight, conv_weight):
    batches = lax.axis_size("batch")
    slabs = lax.axis_size("space")
    devices = batches * slabs
    _, channels, layers, plane = snapshots.shape
    modes = mode_weight.shape[0] * mode_weight.shape[1]
    half = LANES // 2
    assert channels == half and layers == 2 and plane == CELLS
    plane_rows = devices * modes
    count = modes * 2 * KZ * batches
    in_slab = modes == 8 and devices * 32 == TERM_ROWS

    across, along_y = plane_factors(batches, slabs)
    analysis = np.ascontiguousarray(plane_analysis(across, along_y))
    gather, scatter, gather_back, scatter_back = depth_tables(slabs, layers, modes)
    weights = mode_weight.reshape(modes * 2 * KZ * channels, channels)
    taps = conv_weight.reshape(OFFSETS, channels, channels)
    field = shape((channels, layers, plane), BF16)
    wide = shape((CELLS, LANES), BF16)
    edge = shape((CELLS // 2, LANES), BF16)
    plane_modes = shape((plane_rows, LANES), BF16)
    padded = pltpu.VMEM((CELLS + 2 * NY, 2 * LANES), BF16)

    def send(values):
        return exchange(values.reshape(devices, modes, LANES)).reshape(plane_rows, LANES)

    packed = shape((weights.shape[0] // 2, LANES), BF16)
    to_send = shape((devices, modes, LANES), BF16) if modes % 8 == 0 else plane_modes
    cells, coef, first, last, slot = run(
        analyse_kernel,
        [wide, plane_modes, edge, edge, to_send],
        snapshots.reshape(field.shape),
        analysis,
        staged=(0, 1),
        sent=(0, 1, 2, 3),
        plain=(4,),
        limit=WHOLE_VMEM,
        flops=10**8,
    )
    weights, coef = lax.optimization_barrier((weights, coef))
    coef = send(coef)
    share = weights.shape[0] // CHUNKS
    (kept_weights,) = run(
        pack_kernel,
        [shape((HBM_BYTES // (2 * LANES), LANES), BF16)],
        *[weights] * CHUNKS,
        staged={k: slice(k * share, (k + 1) * share) for k in range(CHUNKS)},
        plain=(0,),
        scratch=[pltpu.VMEM(packed.shape, BF16), pltpu.SemaphoreType.DMA((CHUNKS,))],
        limit=LARGE_VMEM,
    )
    (packed_weights,) = run(fetch_kernel, [packed], kept_weights, moved={0: 0})
    back, diagonal = run(
        functools.partial(mix_kernel, batches, slabs),
        [to_send, shape((count, GROUP * half // 2), BF16)],
        coef,
        gather,
        packed_weights,
        scatter,
        sent=(0, 1),
        slots={0: slot},
        flops=4 * 10**8,
    )
    back, first, last = lax.optimization_barrier((back, first, last))
    back = send(back)
    before, after = neighbours(first, last)
    local, lanes, outer_cells, synthesis = run(
        local_kernel,
        [
            shape((CELLS, LANES), F32),
            shape((2 * LANES, CELLS), BF16),
            wide,
            shape((CELLS, plane_rows), BF16),
        ],
        cells,
        before,
        after,
        cotangent.reshape(field.shape),
        taps,
        across,
        along_y,
        scratch=[padded, pltpu.VMEM((3, 2 * LANES, 3 * LANES), BF16)],
        flops=7 * 10**8,
    )
    slab = shape((devices, 8 + TERM_ROWS // devices, LANES), BF16)
    activated, grad, first, last, back, terms = run(
        functools.partial(activate_kernel, in_slab),
        [
            wide,
            shape((HBM_BYTES // (2 * LANES), LANES), BF16),
            edge,
            edge,
            slab if in_slab else plane_modes,
            None if in_slab else shape((TERM_ROWS, LANES), BF16),
        ],
        back,
        synthesis,
        local,
        outer_cells,
        lanes,
        sent={1: CELLS, 2: None, 3: None, 4: None},
        scratch=[pltpu.VMEM((CELLS + 2 * NY, 3 * LANES), BF16)],
        flops=10**9,
    )
    if in_slab:
        back = exchange(back)
    else:
        back = send(back)
        terms = exchange(terms.reshape(devices, TERM_ROWS // devices, LANES))
    before, after = neighbours(first, last)
    activated, packed_weights = run(
        output_kernel,
        [field, packed],
        activated,
        kept_weights,
        moved={1: 1},
        flops=10**8,
    )
    back, before, after, activated, packed_weights = lax.optimization_barrier(
        (back, before, after, activated, packed_weights)
    )
    scale = 1.0 / math.sqrt(batches * slabs * layers * plane)
    grad_modes, mixed_grad, sums = run(
        functools.partial(unmix_kernel, batches, slabs, scale),
        [
            slab if in_slab else plane_modes,
            shape((count, LANES), BF16),
            None if in_slab else shape((TERM_ROWS // devices, LANES), F32),
        ],
        back,
        None if in_slab else terms,
        gather_back,
        packed_weights,
        scatter_back,
        sent=(0,),
        flops=4 * 10**8,
    )
    if in_slab:
        grad_modes = exchange(grad_modes)
    else:
        grad_modes = send(grad_modes)
        sums = lax.all_gather(sums, ("space", "batch"), axis=0, tiled=True)
    (local,) = run(
        local_grad_kernel,
        [shape((CELLS, LANES), F32)],
        grad,
        before,
        after,
        taps,
        staged={0: CELLS},
        scratch=[padded, pltpu.VMEM((3, 3 * LANES, 2 * LANES), BF16)],
        flops=7 * 10**8,
    )
    (mode_gradient,) = run(
        functools.partial(weight_kernel, batches),
        [shape((modes * 2 * KZ * channels, channels), F32)],
        diagonal,
        mixed_grad,
        flops=4 * 10**8,
    )
    input_gradient, conv_gradient = run(
        finish_kernel,
        [field, shape((OFFSETS, channels, channels), F32)],
        grad_modes,
        sums,
        np.ascontiguousarray(analysis.T),
        local,
        flops=10**8,
    )
    return (
        activated.reshape(snapshots.shape),
        input_gradient.reshape(snapshots.shape),
        mode_gradient.reshape(mode_weight.shape),
        conv_gradient.reshape(conv_weight.shape),
    )


def solution(mesh):
    in_specs = (
        P("batch", None, "space", None),
        P("batch", None, "space", None),
        P("batch", "space", None, None, None),
        P(),
    )
    out_specs = (
        P("batch", None, "space", None),
        P("batch", None, "space", None),
        P("batch", "space", None, None, None),
        P(),
    )
    return jax.shard_map(shards, mesh=mesh, in_specs=in_specs, out_specs=out_specs, check_vma=False)
```

```python
import functools
import math

import jax
import jax.numpy as jnp
import ml_dtypes
import numpy as np
from jax import lax
from jax.experimental import pallas as pl
from jax.experimental.pallas import tpu as pltpu
from jax.sharding import PartitionSpec as P

KX = 8
KY = 8
KZ = 12
NX = 32
NY = 32
CELLS = NX * NY
LANES = 128
GROUP = 8
OFFSETS = 27
TERM_ROWS = 1024
CHUNKS = 3
VMEM_BYTES = 40 * 1024 * 1024
LARGE_VMEM = 60 * 1024 * 1024
WHOLE_VMEM = 65000 * 1024
HBM_BYTES = 100 * 1024 * 256

F32 = jnp.float32
BF16 = jnp.bfloat16
inv_root_two = 1.0 / math.sqrt(2.0)
inv_root_two_pi = 1.0 / math.sqrt(2.0 * math.pi)


def basis_rows(half_count, length):
    row = np.arange(2 * half_count)[:, None]
    cell = np.arange(length)[None, :]
    frequency = np.where(row < half_count, row, row - half_count + 1)
    phases = (frequency * cell % length).astype(np.float32) * np.float32(2.0 * math.pi / length)
    return np.where(row < half_count, np.cos(phases), np.sin(phases)).astype(np.float32)


def plane_tables(batches, slabs):
    outer = (basis_rows(KX, NX)[:, None, :, None] * basis_rows(KY, NY)[None, :, None, :]).reshape(
        2 * KX, 2 * KY, CELLS
    )
    outer = outer.reshape(batches, 2 * KX // batches, slabs, 2 * KY // slabs, CELLS)
    outer = outer.transpose(2, 0, 1, 3, 4).reshape(4 * KX * KY, CELLS)
    analysis = (outer * np.float32(2.0 / math.sqrt(CELLS))).astype(ml_dtypes.bfloat16)
    synthesis = (outer * np.float32(2.0 / math.sqrt(4 * KX * KY))).astype(ml_dtypes.bfloat16)
    return analysis, synthesis


def depth_tables(slabs, layers, modes):
    rows = basis_rows(KZ, slabs * layers)
    analysis = (rows * np.float32(math.sqrt(2.0 / (slabs * layers)))).astype(ml_dtypes.bfloat16)
    synthesis = (rows * np.float32(math.sqrt(2.0 / (2 * KZ)))).astype(ml_dtypes.bfloat16)

    def spread(table, order):
        table = table.astype(np.float32).reshape(2 * KZ, slabs, layers)
        full = np.einsum("psz,mn->" + order, table, np.eye(modes, dtype=np.float32))
        return full.astype(ml_dtypes.bfloat16)

    def gathered(table):
        return spread(table, "mpzsn").reshape(modes * 2 * KZ, layers * slabs * modes)

    def scattered(table):
        return spread(table, "snzmp").reshape(slabs * modes, layers * modes * 2 * KZ)

    return gathered(analysis), scattered(synthesis), gathered(synthesis), scattered(analysis)


def dot(left, right, contract=(1, 0)):
    return lax.dot_general(
        left, right, (((contract[0],), (contract[1],)), ((), ())), preferred_element_type=F32
    )


def turn_table():
    row = lax.broadcasted_iota(jnp.int32, (LANES, LANES), 0)
    column = lax.broadcasted_iota(jnp.int32, (LANES, LANES), 1)
    return jnp.where(column == row % 2 * (LANES // 2) + row // 2, 1.0, 0.0).astype(BF16)


def to_cells(field):
    return dot(field.reshape(LANES, CELLS), turn_table(), (0, 0))


def to_field(cells):
    return dot(turn_table(), cells, (1, 1)).astype(BF16).reshape(LANES // 2, 2, CELLS)


def low_lanes(rows):
    return lax.broadcasted_iota(jnp.int32, (rows, LANES), 1) < LANES // 2


def swap_halves(values):
    return pltpu.roll(values, LANES // 2, 1)


def doubled(values):
    low = low_lanes(values.shape[0])
    swapped = swap_halves(values)
    return jnp.concatenate(
        [jnp.where(low, values, swapped), jnp.where(low, swapped, values)], axis=0
    )


def halved(values):
    low = low_lanes(values.shape[0])
    return jnp.concatenate([jnp.where(low, values, 0.0), jnp.where(low, 0.0, values)], axis=0)


def edge_layers(cells_first):
    top = cells_first[: CELLS // 2]
    bottom = cells_first[CELLS // 2 :]
    low = low_lanes(CELLS // 2)
    first = jnp.where(low, top, swap_halves(bottom))
    last = jnp.where(low, swap_halves(top), bottom)
    return first.astype(BF16), last.astype(BF16)


def beside_layers(before, after):
    before = before.astype(F32)
    after = after.astype(F32)
    low = low_lanes(CELLS // 2)
    top = jnp.where(low, before, swap_halves(after))
    bottom = jnp.where(low, swap_halves(before), after)
    return jnp.concatenate([top, bottom], axis=0).astype(BF16)


def y_cells(rows):
    return lax.broadcasted_iota(jnp.int32, (rows, LANES), 0) % NY


def from_below(values):
    return jnp.where(y_cells(values.shape[0]) == 0, 0.0, pltpu.roll(values, 1, 0))


def from_above(values):
    rows = values.shape[0]
    return jnp.where(y_cells(rows) == NY - 1, 0.0, pltpu.roll(values, rows - 1, 0))


def pad_cells(padded, own, beside):
    width = own.shape[1] + beside.shape[1]
    padded[0:NY, :] = jnp.zeros((NY, width), BF16)
    padded[NY + CELLS : 2 * NY + CELLS, :] = jnp.zeros((NY, width), BF16)
    padded[NY : NY + CELLS, 0 : own.shape[1]] = own
    padded[NY : NY + CELLS, own.shape[1] :] = beside


BLOCK_OF_DEPTH = {-1: 2, 0: 0, 1: 1, 2: 3}
STEP = 256


def stencil(padded, table, transposed, store):
    for start in range(0, CELLS, STEP):
        total = None
        for b in range(3):
            cells = padded[start + NY * b : start + NY * b + STEP, :]
            term = dot(cells, table[b], (1, 1) if transposed else (1, 0))
            total = term if total is None else total + term
        result = (
            from_below(total[:, 0:LANES])
            + total[:, LANES : 2 * LANES]
            + from_above(total[:, 2 * LANES :])
        )
        store(start, result)


def banded_forward(weights, table):
    half = LANES // 2
    for b in range(3):
        for c in range(3):
            for depth, block in BLOCK_OF_DEPTH.items():
                parts = []
                for out in range(2):
                    a = depth - out + 1
                    if 0 <= a < 3:
                        parts.append(weights[a * 9 + b * 3 + c])
                    else:
                        parts.append(jnp.zeros((half, half), BF16))
                table[b, block * half : (block + 1) * half, c * LANES : (c + 1) * LANES] = (
                    jnp.concatenate(parts, axis=1)
                )


def banded_backward(weights, table):
    half = LANES // 2
    for b in range(3):
        for c in range(3):
            for out in range(2):
                for pair in ((0, 1), (-1, 2)):
                    parts = []
                    for depth in pair:
                        a = depth - out + 1
                        if 0 <= a < 3:
                            parts.append(weights[(2 - a) * 9 + (2 - b) * 3 + 2 - c])
                        else:
                            parts.append(jnp.zeros((half, half), BF16))
                    row = c * LANES + out * half
                    column = BLOCK_OF_DEPTH[pair[0]] * half
                    table[b, row : row + half, column : column + LANES] = jnp.concatenate(
                        parts, axis=1
                    )


def analyse_kernel(field, analysis, cells_out, coef_out, first_out, last_out, _):
    cells = to_cells(field[...])
    rounded = cells.astype(BF16)
    coef_out[...] = dot(analysis[...], rounded).astype(BF16)
    cells_out[...] = rounded
    first, last = edge_layers(cells)
    first_out[...] = first
    last_out[...] = last


def pack_kernel(*refs):
    weights = refs[:CHUNKS]
    packed_out, buffer, semaphores = refs[CHUNKS:]
    rows = GROUP * LANES // 4
    share = buffer.shape[0] // CHUNKS
    copies = []
    for place, part in enumerate(weights):
        for g in range(share // rows):
            pair = [part[k * rows : (k + 1) * rows, :] for k in (2 * g, 2 * g + 1)]
            row = place * share + g * rows
            buffer[row : row + rows, :] = jnp.concatenate(pair, axis=1)
        span = slice(place * share, (place + 1) * share)
        copies.append(
            pltpu.make_async_copy(buffer.at[span], packed_out.at[span], semaphores.at[place])
        )
        copies[-1].start()
    for copy in copies:
        copy.wait()


def local_kernel(
    cells, before, after, cotangent, weights, local_out, lanes_out, cotangent_out, padded, table
):
    banded_forward(weights, table)
    beside = beside_layers(before[...], after[...])
    pad_cells(padded, cells[...], beside)

    def store(start, result):
        local_out[start : start + STEP, :] = result

    stencil(padded, table, False, store)
    whole = jnp.concatenate([cells[...].astype(F32), beside.astype(F32)], axis=1)
    lanes_out[...] = whole.T.astype(BF16)
    cotangent_out[...] = to_cells(cotangent[...]).astype(BF16)


def tables_kernel(gather, scatter, _, gather_out, scatter_out):
    gather_out[...] = gather[...]
    scatter_out[...] = scatter[...]


def mode_in_group(rows, lanes):
    return lax.broadcasted_iota(jnp.int32, (rows, lanes), 0) % GROUP


def own_block(rows):
    width = GROUP * LANES // 4
    lane = lax.broadcasted_iota(jnp.int32, (rows, width), 1)
    return mode_in_group(rows, width) % (GROUP // 2) == lane // (LANES // 2)


def own_half(rows):
    return (mode_in_group(rows, LANES) < GROUP // 2) == low_lanes(rows)


def to_depth(modes, table, snaps, slabs):
    modes = modes.reshape(slabs, snaps, -1, LANES)
    both = [doubled(modes[:, b].reshape(-1, LANES)) for b in range(snaps)]
    result = dot(table, jnp.concatenate(both, axis=1).astype(BF16))
    return jnp.concatenate(
        [
            result[g : g + GROUP, b * LANES : (b + 1) * LANES]
            for g in range(0, result.shape[0], GROUP)
            for b in range(snaps)
        ],
        axis=0,
    )


def from_depth(modes, table, snaps, slabs):
    count = modes.shape[0] // GROUP
    both = []
    for b in range(snaps):
        own = [modes[g * GROUP : (g + 1) * GROUP] for g in range(b, count, snaps)]
        both.append(halved(jnp.concatenate(own, axis=0)))
    result = dot(table, jnp.concatenate(both, axis=1).astype(BF16))
    own = [
        result[:, b * LANES : (b + 1) * LANES].reshape(slabs, -1, LANES) for b in range(snaps)
    ]
    return jnp.stack(own, axis=1).reshape(-1, LANES)


def wide_blocks(diagonal, snaps):
    first = mode_in_group(*diagonal.shape) < GROUP // 2
    blocks = diagonal.astype(F32)
    blocks = [jnp.where(first, blocks, 0.0), jnp.where(first, 0.0, blocks)]
    return jnp.concatenate(blocks, axis=1).astype(BF16)


def mix_kernel(snaps, slabs, received, gather, weights, scatter, back_out, diagonal_out):
    coef = to_depth(received[...].astype(F32), gather[...], snaps, slabs)
    count = coef.shape[0]
    wide = jnp.concatenate([coef] * (GROUP // 4), axis=1)
    diagonal = jnp.where(own_block(count), wide, 0.0).astype(BF16)
    diagonal_out[...] = diagonal
    rows = GROUP * snaps
    depth = GROUP * LANES // 2
    wide = wide_blocks(diagonal, snaps)
    mixed = jnp.concatenate(
        [
            dot(wide[g * rows : (g + 1) * rows, :], weights[g * depth : (g + 1) * depth, :])
            for g in range(count // rows)
        ],
        axis=0,
    )
    mixed = jnp.concatenate([mixed, mixed], axis=1)
    back = from_depth(mixed, scatter[...], snaps, slabs).astype(BF16)
    back_out[...] = back.reshape(back_out.shape)


def activate_kernel(
    terms_in_slab,
    received,
    synthesis,
    local,
    cotangent,
    lanes,
    activated_out,
    grad_out,
    first_out,
    last_out,
    back_out,
    terms_out,
    spread,
):
    pre = dot(synthesis[...], received[...]) + local[...]
    cdf = 0.5 * (1.0 + lax.erf(pre * inv_root_two))
    density = jnp.exp(-0.5 * pre * pre) * inv_root_two_pi
    activated_out[...] = (pre * cdf).astype(BF16)
    grad = (cotangent[...].astype(F32) * (cdf + pre * density)).astype(BF16)
    back = dot(synthesis[...], grad, (0, 0))
    rounded = grad
    grad = grad.astype(F32)
    first, last = edge_layers(grad)
    spread[0:NY, :] = jnp.zeros((NY, 3 * LANES), BF16)
    spread[NY + CELLS : 2 * NY + CELLS, :] = jnp.zeros((NY, 3 * LANES), BF16)
    spread[NY : NY + CELLS, 0:LANES] = from_above(grad).astype(BF16)
    spread[NY : NY + CELLS, LANES : 2 * LANES] = grad.astype(BF16)
    spread[NY : NY + CELLS, 2 * LANES :] = from_below(grad).astype(BF16)
    half = LANES // 2
    low = low_lanes(half)
    twice = {}
    for b in range(3):
        product = dot(lanes[...], spread[NY * (2 - b) : NY * (2 - b) + CELLS, :])
        for c in range(3):
            for a in range(3):
                blocks = [BLOCK_OF_DEPTH[out + a - 1] * half for out in range(2)]
                columns = slice(c * LANES, (c + 1) * LANES)
                both = jnp.where(
                    low,
                    product[blocks[0] : blocks[0] + half, columns],
                    product[blocks[1] : blocks[1] + half, columns],
                )
                twice[a * 9 + b * 3 + c] = both + swap_halves(both)
    pairs = []
    for k in range(0, OFFSETS, 2):
        pairs.append(jnp.where(low, twice[k], twice.get(k + 1, 0.0)))
    pairs.append(jnp.zeros((TERM_ROWS - half * len(pairs), LANES), F32))
    terms = jnp.concatenate(pairs, axis=0)
    if terms_in_slab:
        slab_store(back_out, back, terms)
    else:
        back_out[...] = back.astype(BF16)
        terms_out[...] = terms.astype(BF16)
    grad_out[...] = rounded
    first_out[...] = first
    last_out[...] = last


def slab_store(slab, modes, terms):
    owners = slab.shape[0]
    modes = modes.reshape(owners, 8, LANES)
    terms = terms.reshape(owners, -1, LANES)
    slab[...] = jnp.concatenate([modes, terms], axis=1).astype(BF16)


def slab_load(slab):
    whole = slab[...].astype(F32)
    return whole[:, 0:8, :].reshape(-1, LANES), whole[:, 8:, :]


def unmix_kernel(snaps, slabs, scale, received, terms, gather, weights, scatter, grad_out, mixed_out, sums_out):
    in_slab = terms is None
    if in_slab:
        modes, terms = slab_load(received)
    else:
        modes, terms = received[...].astype(F32), terms[...].astype(F32)
    mixed = to_depth(modes, gather[...], snaps, slabs)
    mixed_out[...] = mixed.astype(BF16)
    count = mixed.shape[0]
    rows = GROUP * snaps
    depth = GROUP * LANES // 4
    sums = jnp.sum(terms, axis=0) * scale
    own = own_block(rows)
    placed = jnp.where(own_half(count), mixed, 0.0).astype(BF16)
    pieces = []
    for g in range(count // rows):
        full = dot(
            placed[g * rows : (g + 1) * rows, :], weights[g * depth : (g + 1) * depth, :], (1, 1)
        )
        full = jnp.where(own, full, 0.0)
        pieces.append(sum(full[:, k : k + LANES] for k in range(0, depth, LANES)))
    coef = jnp.concatenate(pieces, axis=0)
    coef = coef + swap_halves(coef)
    grad = from_depth(coef, scatter[...], snaps, slabs)
    if in_slab:
        owners = received.shape[0]
        share = sums.shape[0]
        slab_store(
            grad_out, grad, jnp.broadcast_to(sums[None], (owners, share, LANES)).reshape(-1, LANES)
        )
    else:
        grad_out[...] = grad.astype(BF16)
        sums_out[...] = sums


def weight_kernel(snaps, diagonal, mixed, out):
    rows = GROUP * snaps
    depth = GROUP * LANES // 4
    half = LANES // 2
    first = mode_in_group(rows, depth) < GROUP // 2
    for g in range(diagonal.shape[0] // rows):
        span = slice(g * rows, (g + 1) * rows)
        blocks = diagonal[span, :].astype(F32)
        blocks = [jnp.where(first, blocks, 0.0), jnp.where(first, 0.0, blocks)]
        blocks = jnp.concatenate(blocks, axis=1).astype(BF16)
        out[2 * g * depth : 2 * (g + 1) * depth, :] = dot(blocks, mixed[span, 0:half], (0, 0))


def output_kernel(cells, out):
    out[...] = to_field(cells[...])


def local_grad_kernel(grad, before, after, weights, out, padded, table):
    banded_backward(weights, table)
    pad_cells(padded, grad[...], beside_layers(before[...], after[...]))

    def store(start, result):
        out[start : start + STEP, :] = result

    stencil(padded, table, True, store)


def finish_kernel(received, sums, synthesis, local, grad_out, stencil_out):
    in_slab = sums is None
    if in_slab:
        modes, terms = slab_load(received)
        terms = terms.reshape(TERM_ROWS, LANES)
    else:
        modes, terms = received[...], sums[...].astype(F32)
    cells = (dot(synthesis[...], modes.astype(BF16)) + local[...]).astype(BF16)
    grad_out[...] = to_field(cells)
    half = LANES // 2
    for k in range(OFFSETS):
        row = (k // 2) * half
        lane = (k % 2) * half
        stencil_out[k] = terms[row : row + half, lane : lane + half]


def shape(dims, dtype):
    return jax.ShapeDtypeStruct(dims, dtype)


class Staged:
    def __init__(self, source, buffer, semaphore):
        self.copy = pltpu.make_async_copy(source, buffer, semaphore)
        self.buffer = buffer
        self.copy.start()
        self.ready = False

    def load(self):
        if not self.ready:
            self.copy.wait()
            self.ready = True

    def __getitem__(self, index):
        self.load()
        return self.buffer[index]


class Sent:
    def __init__(self, target, buffer, semaphore):
        self.copy = pltpu.make_async_copy(buffer, target, semaphore)
        self.buffer = buffer

    def __setitem__(self, index, value):
        self.buffer[index] = value
        self.copy.start()

    def __getitem__(self, index):
        return self.buffer[index]

    @property
    def shape(self):
        return self.buffer.shape


def row_count(rows):
    return rows.stop - rows.start if isinstance(rows, slice) else rows


def run(
    body, outs, *operands, staged=(), sent=(), moved=(), plain=(), slots=(), scratch=(), flops=0, limit=VMEM_BYTES
):
    given = [k for k, operand in enumerate(operands) if operand is not None]
    made = [k for k, out in enumerate(outs) if out is not None]

    def rows_of(chosen, places, arrays):
        chosen = {k: chosen[k] if isinstance(chosen, dict) else None for k in places if k in chosen}
        return {k: rows or arrays[k].shape[0] for k, rows in chosen.items()}

    moved = dict(moved)
    slots = dict(slots)
    staged = rows_of(staged, given, operands)
    sent = rows_of(sent, made, outs)

    def kernel(*refs):
        refs = list(refs)

        def take(count):
            taken = refs[:count]
            del refs[:count]
            return taken

        def part(ref, rows):
            if isinstance(rows, slice):
                return ref.at[rows]
            return ref if ref.shape[0] == rows else ref.at[0:rows]

        filled = dict(zip(given, take(len(given))))
        take(len(slots))
        kept = dict(zip(made, take(len(made))))
        own = take(len(scratch))
        copies = []
        for place, (k, out) in enumerate(moved.items()):
            source, target = filled.pop(k), kept.pop(out)
            rows = min(source.shape[0], target.shape[0])
            semaphore = refs[-1].at[len(staged) + len(sent) + place]
            copies.append(
                pltpu.make_async_copy(part(source, rows), part(target, rows), semaphore)
            )
        for place, (k, buffer) in enumerate(zip(staged, take(len(staged)))):
            filled[k] = Staged(part(filled[k], staged[k]), buffer, refs[-1].at[place])
        for place, (k, buffer) in enumerate(zip(sent, take(len(sent)))):
            kept[k] = Sent(part(kept[k], sent[k]), buffer, refs[-1].at[len(staged) + place])
        for copy in copies:
            copy.start()
        body(
            *[filled.get(k) for k in range(len(operands)) if k not in moved],
            *[kept.get(k) for k in range(len(outs)) if k not in moved.values()],
            *own,
        )
        for k in staged:
            filled[k].load()
        for k in sent:
            kept[k].copy.wait()
        for copy in copies:
            copy.wait()

    arrays = [operands[k] for k in given]
    results = [outs[k] for k in made]
    size = sum(x.size * x.dtype.itemsize for x in (*arrays, *results))
    in_vmem = pl.BlockSpec(memory_space=pltpu.VMEM)
    in_hbm = pl.BlockSpec(memory_space=pltpu.HBM)
    buffers = [(operands[k], rows) for k, rows in staged.items()]
    buffers += [(outs[k], rows) for k, rows in sent.items()]
    buffers = [pltpu.VMEM((row_count(rows), *x.shape[1:]), x.dtype) for x, rows in buffers]
    if len(buffers) + len(moved) > 0:
        buffers.append(pltpu.SemaphoreType.DMA((len(buffers) + len(moved),)))
    results = pl.pallas_call(
        kernel,
        out_shape=results,
        in_specs=[in_hbm if k in staged or k in moved else in_vmem for k in given]
        + [in_hbm] * len(slots),
        out_specs=[in_hbm if k in sent or k in plain else in_vmem for k in made],
        input_output_aliases={len(given) + at: made.index(k) for at, k in enumerate(slots)},
        scratch_shapes=[*scratch, *buffers],
        compiler_params=pltpu.CompilerParams(vmem_limit_bytes=limit),
        cost_estimate=pl.CostEstimate(flops=flops, bytes_accessed=size, transcendentals=0),
        name=body.__name__ if hasattr(body, "__name__") else body.func.__name__,
    )(*arrays, *slots.values())
    results = dict(zip(made, results))
    return [results.get(k) for k in range(len(outs))]


def exchange(values):
    return lax.all_to_all(values, ("space", "batch"), split_axis=0, concat_axis=0, tiled=True)


def neighbours(first, last):
    ends = lax.axis_size("space") - 1
    before = lax.ppermute(last, "space", [(i, i + 1) for i in range(ends)])
    after = lax.ppermute(first, "space", [(i + 1, i) for i in range(ends)])
    return before, after


def shards(snapshots, cotangent, mode_weight, conv_weight):
    batches = lax.axis_size("batch")
    slabs = lax.axis_size("space")
    devices = batches * slabs
    _, channels, layers, plane = snapshots.shape
    modes = mode_weight.shape[0] * mode_weight.shape[1]
    half = LANES // 2
    assert channels == half and layers == 2 and plane == CELLS
    plane_rows = devices * modes
    count = modes * 2 * KZ * batches
    in_slab = modes == 8 and devices * 32 == TERM_ROWS

    analysis, synthesis = plane_tables(batches, slabs)
    gather, scatter, gather_back, scatter_back = depth_tables(slabs, layers, modes)
    weights = mode_weight.reshape(modes * 2 * KZ * channels, channels)
    taps = conv_weight.reshape(OFFSETS, channels, channels)
    field = shape((channels, layers, plane), BF16)
    wide = shape((CELLS, LANES), BF16)
    edge = shape((CELLS // 2, LANES), BF16)
    plane_modes = shape((plane_rows, LANES), BF16)
    padded = pltpu.VMEM((CELLS + 2 * NY, 2 * LANES), BF16)

    def send(values):
        return exchange(values.reshape(devices, modes, LANES)).reshape(plane_rows, LANES)

    packed = shape((weights.shape[0] // 2, LANES), BF16)
    to_send = shape((devices, modes, LANES), BF16) if modes % 8 == 0 else plane_modes
    cells, coef, first, last, slot = run(
        analyse_kernel,
        [wide, plane_modes, edge, edge, to_send],
        snapshots.reshape(field.shape),
        analysis,
        staged=(0, 1),
        sent=(0, 1, 2, 3),
        plain=(4,),
        limit=WHOLE_VMEM,
        flops=10**8,
    )
    ahead = first
    coef = send(coef)
    gather, scatter = run(
        tables_kernel,
        [shape(gather.shape, BF16), shape(scatter.shape, BF16)],
        gather,
        scatter,
        ahead,
    )
    before, after = neighbours(first, last)
    local, lanes, outer_cells = run(
        local_kernel,
        [shape((CELLS, LANES), F32), shape((2 * LANES, CELLS), BF16), wide],
        cells,
        before,
        after,
        cotangent.reshape(field.shape),
        taps,
        scratch=[padded, pltpu.VMEM((3, 2 * LANES, 3 * LANES), BF16)],
        flops=8 * 10**9,
    )
    back, diagonal = run(
        functools.partial(mix_kernel, batches, slabs),
        [to_send, shape((count, GROUP * half // 2), BF16)],
        coef,
        gather,
        weights,
        scatter,
        sent=(0, 1),
        slots={0: slot},
        flops=4 * 10**8,
    )
    weights, back = lax.optimization_barrier((weights, back))
    back = send(back)
    share = weights.shape[0] // CHUNKS
    (kept_weights,) = run(
        pack_kernel,
        [shape((HBM_BYTES // (2 * LANES), LANES), BF16)],
        *[weights] * CHUNKS,
        staged={k: slice(k * share, (k + 1) * share) for k in range(CHUNKS)},
        plain=(0,),
        scratch=[pltpu.VMEM(packed.shape, BF16), pltpu.SemaphoreType.DMA((CHUNKS,))],
        limit=LARGE_VMEM,
    )
    slab = shape((devices, 8 + TERM_ROWS // devices, LANES), BF16)
    activated, grad, first, last, back, terms = run(
        functools.partial(activate_kernel, in_slab),
        [
            wide,
            shape((HBM_BYTES // (2 * LANES), LANES), BF16),
            edge,
            edge,
            slab if in_slab else plane_modes,
            None if in_slab else shape((TERM_ROWS, LANES), BF16),
        ],
        back,
        np.ascontiguousarray(synthesis.T),
        local,
        outer_cells,
        lanes,
        sent={1: CELLS, 2: None, 3: None, 4: None},
        scratch=[pltpu.VMEM((CELLS + 2 * NY, 3 * LANES), BF16)],
        flops=10**9,
    )
    if in_slab:
        back = exchange(back)
    else:
        back = send(back)
        terms = exchange(terms.reshape(devices, TERM_ROWS // devices, LANES))
    before, after = neighbours(first, last)
    activated, packed_weights = run(
        output_kernel,
        [field, packed],
        activated,
        kept_weights,
        moved={1: 1},
        flops=10**8,
    )
    back, before, after, activated, packed_weights = lax.optimization_barrier(
        (back, before, after, activated, packed_weights)
    )
    scale = 1.0 / math.sqrt(batches * slabs * layers * plane)
    grad_modes, mixed_grad, sums = run(
        functools.partial(unmix_kernel, batches, slabs, scale),
        [
            slab if in_slab else plane_modes,
            shape((count, LANES), BF16),
            None if in_slab else shape((TERM_ROWS // devices, LANES), F32),
        ],
        back,
        None if in_slab else terms,
        gather_back,
        packed_weights,
        scatter_back,
        sent=(0,),
        flops=4 * 10**8,
    )
    if in_slab:
        grad_modes = exchange(grad_modes)
    else:
        grad_modes = send(grad_modes)
        sums = lax.all_gather(sums, ("space", "batch"), axis=0, tiled=True)
    (local,) = run(
        local_grad_kernel,
        [shape((CELLS, LANES), F32)],
        grad,
        before,
        after,
        taps,
        staged={0: CELLS},
        scratch=[padded, pltpu.VMEM((3, 3 * LANES, 2 * LANES), BF16)],
        flops=7 * 10**8,
    )
    (mode_gradient,) = run(
        functools.partial(weight_kernel, batches),
        [shape((modes * 2 * KZ * channels, channels), F32)],
        diagonal,
        mixed_grad,
        flops=4 * 10**8,
    )
    input_gradient, conv_gradient = run(
        finish_kernel,
        [field, shape((OFFSETS, channels, channels), F32)],
        grad_modes,
        sums,
        np.ascontiguousarray(analysis.T),
        local,
        flops=10**8,
    )
    return (
        activated.reshape(snapshots.shape),
        input_gradient.reshape(snapshots.shape),
        mode_gradient.reshape(mode_weight.shape),
        conv_gradient.reshape(conv_weight.shape),
    )


def solution(mesh):
    in_specs = (
        P("batch", None, "space", None),
        P("batch", None, "space", None),
        P("batch", "space", None, None, None),
        P(),
    )
    out_specs = (
        P("batch", None, "space", None),
        P("batch", None, "space", None),
        P("batch", "space", None, None, None),
        P(),
    )
    return jax.shard_map(shards, mesh=mesh, in_specs=in_specs, out_specs=out_specs, check_vma=False)
```

```python
import functools
import math

import jax
import jax.numpy as jnp
import ml_dtypes
import numpy as np
from jax import lax
from jax.experimental import pallas as pl
from jax.experimental.pallas import tpu as pltpu
from jax.sharding import PartitionSpec as P

KX = 8
KY = 8
KZ = 12
NX = 32
NY = 32
CELLS = NX * NY
LANES = 128
GROUP = 8
OFFSETS = 27
TERM_ROWS = 1024
CHUNKS = 3
VMEM_BYTES = 40 * 1024 * 1024
WHOLE_VMEM = 65000 * 1024
HBM_BYTES = 100 * 1024 * 256

F32 = jnp.float32
BF16 = jnp.bfloat16
inv_root_two = 1.0 / math.sqrt(2.0)
inv_root_two_pi = 1.0 / math.sqrt(2.0 * math.pi)


def basis_rows(half_count, length):
    row = np.arange(2 * half_count)[:, None]
    cell = np.arange(length)[None, :]
    frequency = np.where(row < half_count, row, row - half_count + 1)
    phases = (frequency * cell % length).astype(np.float32) * np.float32(2.0 * math.pi / length)
    return np.where(row < half_count, np.cos(phases), np.sin(phases)).astype(np.float32)


def plane_tables(batches, slabs):
    outer = (basis_rows(KX, NX)[:, None, :, None] * basis_rows(KY, NY)[None, :, None, :]).reshape(
        2 * KX, 2 * KY, CELLS
    )
    outer = outer.reshape(batches, 2 * KX // batches, slabs, 2 * KY // slabs, CELLS)
    outer = outer.transpose(2, 0, 1, 3, 4).reshape(4 * KX * KY, CELLS)
    analysis = (outer * np.float32(2.0 / math.sqrt(CELLS))).astype(ml_dtypes.bfloat16)
    synthesis = (outer * np.float32(2.0 / math.sqrt(4 * KX * KY))).astype(ml_dtypes.bfloat16)
    return analysis, synthesis


def depth_tables(slabs, layers, modes):
    rows = basis_rows(KZ, slabs * layers)
    analysis = (rows * np.float32(math.sqrt(2.0 / (slabs * layers)))).astype(ml_dtypes.bfloat16)
    synthesis = (rows * np.float32(math.sqrt(2.0 / (2 * KZ)))).astype(ml_dtypes.bfloat16)

    def spread(table, order):
        table = table.astype(np.float32).reshape(2 * KZ, slabs, layers)
        full = np.einsum("psz,mn->" + order, table, np.eye(modes, dtype=np.float32))
        return full.astype(ml_dtypes.bfloat16)

    def gathered(table):
        return spread(table, "mpzsn").reshape(modes * 2 * KZ, layers * slabs * modes)

    def scattered(table):
        return spread(table, "snzmp").reshape(slabs * modes, layers * modes * 2 * KZ)

    return gathered(analysis), scattered(synthesis), gathered(synthesis), scattered(analysis)


def dot(left, right, contract=(1, 0)):
    return lax.dot_general(
        left, right, (((contract[0],), (contract[1],)), ((), ())), preferred_element_type=F32
    )


def turn_table():
    row = lax.broadcasted_iota(jnp.int32, (LANES, LANES), 0)
    column = lax.broadcasted_iota(jnp.int32, (LANES, LANES), 1)
    return jnp.where(column == row % 2 * (LANES // 2) + row // 2, 1.0, 0.0).astype(BF16)


def to_cells(field):
    return dot(field.reshape(LANES, CELLS), turn_table(), (0, 0))


def to_field(cells):
    return dot(turn_table(), cells, (1, 1)).astype(BF16).reshape(LANES // 2, 2, CELLS)


def low_lanes(rows):
    return lax.broadcasted_iota(jnp.int32, (rows, LANES), 1) < LANES // 2


def swap_halves(values):
    return pltpu.roll(values, LANES // 2, 1)


def doubled(values):
    low = low_lanes(values.shape[0])
    swapped = swap_halves(values)
    return jnp.concatenate(
        [jnp.where(low, values, swapped), jnp.where(low, swapped, values)], axis=0
    )


def halved(values):
    low = low_lanes(values.shape[0])
    return jnp.concatenate([jnp.where(low, values, 0.0), jnp.where(low, 0.0, values)], axis=0)


def edge_layers(cells_first):
    top = cells_first[: CELLS // 2]
    bottom = cells_first[CELLS // 2 :]
    low = low_lanes(CELLS // 2)
    first = jnp.where(low, top, swap_halves(bottom))
    last = jnp.where(low, swap_halves(top), bottom)
    return first.astype(BF16), last.astype(BF16)


def beside_layers(before, after):
    before = before.astype(F32)
    after = after.astype(F32)
    low = low_lanes(CELLS // 2)
    top = jnp.where(low, before, swap_halves(after))
    bottom = jnp.where(low, swap_halves(before), after)
    return jnp.concatenate([top, bottom], axis=0).astype(BF16)


def y_cells(rows):
    return lax.broadcasted_iota(jnp.int32, (rows, LANES), 0) % NY


def from_below(values):
    return jnp.where(y_cells(values.shape[0]) == 0, 0.0, pltpu.roll(values, 1, 0))


def from_above(values):
    rows = values.shape[0]
    return jnp.where(y_cells(rows) == NY - 1, 0.0, pltpu.roll(values, rows - 1, 0))


def pad_cells(padded, own, beside):
    width = own.shape[1] + beside.shape[1]
    padded[0:NY, :] = jnp.zeros((NY, width), BF16)
    padded[NY + CELLS : 2 * NY + CELLS, :] = jnp.zeros((NY, width), BF16)
    padded[NY : NY + CELLS, 0 : own.shape[1]] = own
    padded[NY : NY + CELLS, own.shape[1] :] = beside


BLOCK_OF_DEPTH = {-1: 2, 0: 0, 1: 1, 2: 3}
STEP = 256


def stencil(padded, table, transposed, store):
    for start in range(0, CELLS, STEP):
        total = None
        for b in range(3):
            cells = padded[start + NY * b : start + NY * b + STEP, :]
            term = dot(cells, table[b], (1, 1) if transposed else (1, 0))
            total = term if total is None else total + term
        result = (
            from_below(total[:, 0:LANES])
            + total[:, LANES : 2 * LANES]
            + from_above(total[:, 2 * LANES :])
        )
        store(start, result)


def banded_forward(weights, table):
    half = LANES // 2
    for b in range(3):
        for c in range(3):
            for depth, block in BLOCK_OF_DEPTH.items():
                parts = []
                for out in range(2):
                    a = depth - out + 1
                    if 0 <= a < 3:
                        parts.append(weights[a * 9 + b * 3 + c])
                    else:
                        parts.append(jnp.zeros((half, half), BF16))
                table[b, block * half : (block + 1) * half, c * LANES : (c + 1) * LANES] = (
                    jnp.concatenate(parts, axis=1)
                )


def banded_backward(weights, table):
    half = LANES // 2
    for b in range(3):
        for c in range(3):
            for out in range(2):
                for pair in ((0, 1), (-1, 2)):
                    parts = []
                    for depth in pair:
                        a = depth - out + 1
                        if 0 <= a < 3:
                            parts.append(weights[(2 - a) * 9 + (2 - b) * 3 + 2 - c])
                        else:
                            parts.append(jnp.zeros((half, half), BF16))
                    row = c * LANES + out * half
                    column = BLOCK_OF_DEPTH[pair[0]] * half
                    table[b, row : row + half, column : column + LANES] = jnp.concatenate(
                        parts, axis=1
                    )


def analyse_kernel(field, analysis, *refs):
    weights = refs[:CHUNKS]
    cells_out, coef_out, first_out, last_out, packed_out, _, buffer, semaphores = refs[CHUNKS:]
    cells = to_cells(field[...])
    rounded = cells.astype(BF16)
    coef_out[...] = dot(analysis[...], rounded).astype(BF16)
    cells_out[...] = rounded
    first, last = edge_layers(cells)
    first_out[...] = first
    last_out[...] = last
    rows = GROUP * LANES // 4
    share = buffer.shape[0] // CHUNKS
    copies = []
    for place, part in enumerate(weights):
        for g in range(share // rows):
            pair = [part[k * rows : (k + 1) * rows, :] for k in (2 * g, 2 * g + 1)]
            row = place * share + g * rows
            buffer[row : row + rows, :] = jnp.concatenate(pair, axis=1)
        span = slice(place * share, (place + 1) * share)
        copies.append(
            pltpu.make_async_copy(buffer.at[span], packed_out.at[span], semaphores.at[place])
        )
        copies[-1].start()
    for copy in copies:
        copy.wait()


def local_kernel(
    cells, before, after, cotangent, weights, local_out, lanes_out, cotangent_out, padded, table
):
    banded_forward(weights, table)
    beside = beside_layers(before[...], after[...])
    pad_cells(padded, cells[...], beside)

    def store(start, result):
        local_out[start : start + STEP, :] = result

    stencil(padded, table, False, store)
    whole = jnp.concatenate([cells[...].astype(F32), beside.astype(F32)], axis=1)
    lanes_out[...] = whole.T.astype(BF16)
    cotangent_out[...] = to_cells(cotangent[...]).astype(BF16)


def fetch_kernel():
    pass


def mode_in_group(rows, lanes):
    return lax.broadcasted_iota(jnp.int32, (rows, lanes), 0) % GROUP


def own_block(rows):
    width = GROUP * LANES // 4
    lane = lax.broadcasted_iota(jnp.int32, (rows, width), 1)
    return mode_in_group(rows, width) % (GROUP // 2) == lane // (LANES // 2)


def own_half(rows):
    return (mode_in_group(rows, LANES) < GROUP // 2) == low_lanes(rows)


def to_depth(modes, table, snaps, slabs):
    modes = modes.reshape(slabs, snaps, -1, LANES)
    both = [doubled(modes[:, b].reshape(-1, LANES)) for b in range(snaps)]
    result = dot(table, jnp.concatenate(both, axis=1).astype(BF16))
    return jnp.concatenate(
        [
            result[g : g + GROUP, b * LANES : (b + 1) * LANES]
            for g in range(0, result.shape[0], GROUP)
            for b in range(snaps)
        ],
        axis=0,
    )


def from_depth(modes, table, snaps, slabs):
    count = modes.shape[0] // GROUP
    both = []
    for b in range(snaps):
        own = [modes[g * GROUP : (g + 1) * GROUP] for g in range(b, count, snaps)]
        both.append(halved(jnp.concatenate(own, axis=0)))
    result = dot(table, jnp.concatenate(both, axis=1).astype(BF16))
    own = [
        result[:, b * LANES : (b + 1) * LANES].reshape(slabs, -1, LANES) for b in range(snaps)
    ]
    return jnp.stack(own, axis=1).reshape(-1, LANES)


def mix_kernel(snaps, slabs, received, gather, weights, scatter, back_out, diagonal_out):
    coef = to_depth(received[...].astype(F32), gather[...], snaps, slabs)
    count = coef.shape[0]
    wide = jnp.concatenate([coef] * (GROUP // 4), axis=1)
    diagonal = jnp.where(own_block(count), wide, 0.0).astype(BF16)
    diagonal_out[...] = diagonal
    rows = GROUP * snaps
    depth = GROUP * LANES // 4
    mixed = jnp.concatenate(
        [
            dot(diagonal[g * rows : (g + 1) * rows, :], weights[g * depth : (g + 1) * depth, :])
            for g in range(count // rows)
        ],
        axis=0,
    )
    mixed = jnp.where(own_half(count), mixed, swap_halves(mixed))
    back = from_depth(mixed, scatter[...], snaps, slabs).astype(BF16)
    back_out[...] = back.reshape(back_out.shape)


def activate_kernel(
    terms_in_slab,
    received,
    synthesis,
    local,
    cotangent,
    lanes,
    activated_out,
    grad_out,
    first_out,
    last_out,
    back_out,
    terms_out,
    spread,
    before_grad,
):
    before_grad[...] = dot(synthesis[...], received[...]) + local[...]
    spread[0:NY, :] = jnp.zeros((NY, 3 * LANES), BF16)
    spread[NY + CELLS : 2 * NY + CELLS, :] = jnp.zeros((NY, 3 * LANES), BF16)

    def block(k, carry):
        rows = pl.ds(pl.multiple_of(k * STEP, STEP), STEP)
        pre = before_grad[rows, :]
        cdf = 0.5 * (1.0 + lax.erf(pre * inv_root_two))
        density = jnp.exp(-0.5 * pre * pre) * inv_root_two_pi
        activated_out[rows, :] = (pre * cdf).astype(BF16)
        rounded = (cotangent[rows, :].astype(F32) * (cdf + pre * density)).astype(BF16)
        grad_out.buffer[rows, :] = rounded
        grad = rounded.astype(F32)
        rows = pl.ds(pl.multiple_of(k * STEP + NY, NY), STEP)
        spread[rows, 0:LANES] = from_above(grad).astype(BF16)
        spread[rows, LANES : 2 * LANES] = rounded
        spread[rows, 2 * LANES : 3 * LANES] = from_below(grad).astype(BF16)
        return carry

    lax.fori_loop(0, CELLS // STEP, block, None)
    grad_out.copy.start()
    back = dot(synthesis[...], grad_out.buffer[...], (0, 0))
    first, last = edge_layers(grad_out.buffer[...].astype(F32))
    half = LANES // 2
    low = low_lanes(half)
    twice = {}
    for b in range(3):
        product = dot(lanes[...], spread[NY * (2 - b) : NY * (2 - b) + CELLS, :])
        for c in range(3):
            for a in range(3):
                blocks = [BLOCK_OF_DEPTH[out + a - 1] * half for out in range(2)]
                columns = slice(c * LANES, (c + 1) * LANES)
                both = jnp.where(
                    low,
                    product[blocks[0] : blocks[0] + half, columns],
                    product[blocks[1] : blocks[1] + half, columns],
                )
                twice[a * 9 + b * 3 + c] = both + swap_halves(both)
    pairs = []
    for k in range(0, OFFSETS, 2):
        pairs.append(jnp.where(low, twice[k], twice.get(k + 1, 0.0)))
    pairs.append(jnp.zeros((TERM_ROWS - half * len(pairs), LANES), F32))
    terms = jnp.concatenate(pairs, axis=0)
    if terms_in_slab:
        slab_store(back_out, back, terms)
    else:
        back_out[...] = back.astype(BF16)
        terms_out[...] = terms.astype(BF16)
    first_out[...] = first
    last_out[...] = last


def slab_store(slab, modes, terms):
    owners = slab.shape[0]
    modes = modes.reshape(owners, 8, LANES)
    terms = terms.reshape(owners, -1, LANES)
    slab[...] = jnp.concatenate([modes, terms], axis=1).astype(BF16)


def slab_load(slab):
    whole = slab[...].astype(F32)
    return whole[:, 0:8, :].reshape(-1, LANES), whole[:, 8:, :]


def unmix_kernel(snaps, slabs, scale, received, terms, gather, weights, scatter, grad_out, mixed_out, sums_out):
    in_slab = terms is None
    if in_slab:
        modes, terms = slab_load(received)
    else:
        modes, terms = received[...].astype(F32), terms[...].astype(F32)
    mixed = to_depth(modes, gather[...], snaps, slabs)
    mixed_out[...] = mixed.astype(BF16)
    count = mixed.shape[0]
    rows = GROUP * snaps
    depth = GROUP * LANES // 4
    sums = jnp.sum(terms, axis=0) * scale
    own = own_block(rows)
    placed = jnp.where(own_half(count), mixed, 0.0).astype(BF16)
    pieces = []
    for g in range(count // rows):
        full = dot(
            placed[g * rows : (g + 1) * rows, :], weights[g * depth : (g + 1) * depth, :], (1, 1)
        )
        full = jnp.where(own, full, 0.0)
        pieces.append(sum(full[:, k : k + LANES] for k in range(0, depth, LANES)))
    coef = jnp.concatenate(pieces, axis=0)
    coef = coef + swap_halves(coef)
    grad = from_depth(coef, scatter[...], snaps, slabs)
    if in_slab:
        owners = received.shape[0]
        share = sums.shape[0]
        slab_store(
            grad_out, grad, jnp.broadcast_to(sums[None], (owners, share, LANES)).reshape(-1, LANES)
        )
    else:
        grad_out[...] = grad.astype(BF16)
        sums_out[...] = sums


def weight_kernel(snaps, diagonal, mixed, out):
    rows = GROUP * snaps
    depth = GROUP * LANES // 4
    half = LANES // 2
    first = mode_in_group(rows, depth) < GROUP // 2
    for g in range(diagonal.shape[0] // rows):
        span = slice(g * rows, (g + 1) * rows)
        blocks = diagonal[span, :].astype(F32)
        blocks = [jnp.where(first, blocks, 0.0), jnp.where(first, 0.0, blocks)]
        blocks = jnp.concatenate(blocks, axis=1).astype(BF16)
        out[2 * g * depth : 2 * (g + 1) * depth, :] = dot(blocks, mixed[span, 0:half], (0, 0))


def output_kernel(cells, out):
    out[...] = to_field(cells[...])


def local_grad_kernel(grad, before, after, weights, out, padded, table):
    banded_backward(weights, table)
    pad_cells(padded, grad[...], beside_layers(before[...], after[...]))

    def store(start, result):
        out[start : start + STEP, :] = result

    stencil(padded, table, True, store)


def finish_kernel(received, sums, synthesis, local, grad_out, stencil_out):
    in_slab = sums is None
    if in_slab:
        modes, terms = slab_load(received)
        terms = terms.reshape(TERM_ROWS, LANES)
    else:
        modes, terms = received[...], sums[...].astype(F32)
    cells = (dot(synthesis[...], modes.astype(BF16)) + local[...]).astype(BF16)
    grad_out[...] = to_field(cells)
    half = LANES // 2
    for k in range(OFFSETS):
        row = (k // 2) * half
        lane = (k % 2) * half
        stencil_out[k] = terms[row : row + half, lane : lane + half]


def shape(dims, dtype):
    return jax.ShapeDtypeStruct(dims, dtype)


class Staged:
    def __init__(self, source, buffer, semaphore):
        self.copy = pltpu.make_async_copy(source, buffer, semaphore)
        self.buffer = buffer
        self.copy.start()
        self.ready = False

    def load(self):
        if not self.ready:
            self.copy.wait()
            self.ready = True

    def __getitem__(self, index):
        self.load()
        return self.buffer[index]


class Sent:
    def __init__(self, target, buffer, semaphore):
        self.copy = pltpu.make_async_copy(buffer, target, semaphore)
        self.buffer = buffer

    def __setitem__(self, index, value):
        self.buffer[index] = value
        self.copy.start()

    def __getitem__(self, index):
        return self.buffer[index]

    @property
    def shape(self):
        return self.buffer.shape


def row_count(rows):
    return rows.stop - rows.start if isinstance(rows, slice) else rows


def run(
    body, outs, *operands, staged=(), sent=(), moved=(), plain=(), slots=(), scratch=(), flops=0, limit=VMEM_BYTES
):
    given = [k for k, operand in enumerate(operands) if operand is not None]
    made = [k for k, out in enumerate(outs) if out is not None]

    def rows_of(chosen, places, arrays):
        chosen = {k: chosen[k] if isinstance(chosen, dict) else None for k in places if k in chosen}
        return {k: rows or arrays[k].shape[0] for k, rows in chosen.items()}

    moved = dict(moved)
    slots = dict(slots)
    staged = rows_of(staged, given, operands)
    sent = rows_of(sent, made, outs)

    def kernel(*refs):
        refs = list(refs)

        def take(count):
            taken = refs[:count]
            del refs[:count]
            return taken

        def part(ref, rows):
            if isinstance(rows, slice):
                return ref.at[rows]
            return ref if ref.shape[0] == rows else ref.at[0:rows]

        filled = dict(zip(given, take(len(given))))
        take(len(slots))
        kept = dict(zip(made, take(len(made))))
        own = take(len(scratch))
        copies = []
        for place, (k, out) in enumerate(moved.items()):
            source, target = filled.pop(k), kept.pop(out)
            rows = min(source.shape[0], target.shape[0])
            semaphore = refs[-1].at[len(staged) + len(sent) + place]
            copies.append(
                pltpu.make_async_copy(part(source, rows), part(target, rows), semaphore)
            )
        for place, (k, buffer) in enumerate(zip(staged, take(len(staged)))):
            filled[k] = Staged(part(filled[k], staged[k]), buffer, refs[-1].at[place])
        for place, (k, buffer) in enumerate(zip(sent, take(len(sent)))):
            kept[k] = Sent(part(kept[k], sent[k]), buffer, refs[-1].at[len(staged) + place])
        for copy in copies:
            copy.start()
        body(
            *[filled.get(k) for k in range(len(operands)) if k not in moved],
            *[kept.get(k) for k in range(len(outs)) if k not in moved.values()],
            *own,
        )
        for k in staged:
            filled[k].load()
        for k in sent:
            kept[k].copy.wait()
        for copy in copies:
            copy.wait()

    arrays = [operands[k] for k in given]
    results = [outs[k] for k in made]
    size = sum(x.size * x.dtype.itemsize for x in (*arrays, *results))
    in_vmem = pl.BlockSpec(memory_space=pltpu.VMEM)
    in_hbm = pl.BlockSpec(memory_space=pltpu.HBM)
    buffers = [(operands[k], rows) for k, rows in staged.items()]
    buffers += [(outs[k], rows) for k, rows in sent.items()]
    buffers = [pltpu.VMEM((row_count(rows), *x.shape[1:]), x.dtype) for x, rows in buffers]
    if len(buffers) + len(moved) > 0:
        buffers.append(pltpu.SemaphoreType.DMA((len(buffers) + len(moved),)))
    results = pl.pallas_call(
        kernel,
        out_shape=results,
        in_specs=[in_hbm if k in staged or k in moved else in_vmem for k in given]
        + [in_hbm] * len(slots),
        out_specs=[in_hbm if k in sent or k in plain else in_vmem for k in made],
        input_output_aliases={len(given) + at: made.index(k) for at, k in enumerate(slots)},
        scratch_shapes=[*scratch, *buffers],
        compiler_params=pltpu.CompilerParams(vmem_limit_bytes=limit),
        cost_estimate=pl.CostEstimate(flops=flops, bytes_accessed=size, transcendentals=0),
        name=body.__name__ if hasattr(body, "__name__") else body.func.__name__,
    )(*arrays, *slots.values())
    results = dict(zip(made, results))
    return [results.get(k) for k in range(len(outs))]


def exchange(values):
    return lax.all_to_all(values, ("space", "batch"), split_axis=0, concat_axis=0, tiled=True)


def neighbours(first, last):
    ends = lax.axis_size("space") - 1
    before = lax.ppermute(last, "space", [(i, i + 1) for i in range(ends)])
    after = lax.ppermute(first, "space", [(i + 1, i) for i in range(ends)])
    return before, after


def shards(snapshots, cotangent, mode_weight, conv_weight):
    batches = lax.axis_size("batch")
    slabs = lax.axis_size("space")
    devices = batches * slabs
    _, channels, layers, plane = snapshots.shape
    modes = mode_weight.shape[0] * mode_weight.shape[1]
    half = LANES // 2
    assert channels == half and layers == 2 and plane == CELLS
    plane_rows = devices * modes
    count = modes * 2 * KZ * batches
    in_slab = modes == 8 and devices * 32 == TERM_ROWS

    analysis, synthesis = plane_tables(batches, slabs)
    gather, scatter, gather_back, scatter_back = depth_tables(slabs, layers, modes)
    weights = mode_weight.reshape(modes * 2 * KZ * channels, channels)
    taps = conv_weight.reshape(OFFSETS, channels, channels)
    field = shape((channels, layers, plane), BF16)
    wide = shape((CELLS, LANES), BF16)
    edge = shape((CELLS // 2, LANES), BF16)
    plane_modes = shape((plane_rows, LANES), BF16)
    padded = pltpu.VMEM((CELLS + 2 * NY, 2 * LANES), BF16)

    def send(values):
        return exchange(values.reshape(devices, modes, LANES)).reshape(plane_rows, LANES)

    packed = shape((weights.shape[0] // 2, LANES), BF16)
    share = weights.shape[0] // CHUNKS
    to_send = shape((devices, modes, LANES), BF16) if modes % 8 == 0 else plane_modes
    cells, coef, first, last, kept_weights, slot = run(
        analyse_kernel,
        [
            wide,
            plane_modes,
            edge,
            edge,
            shape((HBM_BYTES // (2 * LANES), LANES), BF16),
            to_send,
        ],
        snapshots.reshape(field.shape),
        analysis,
        *[weights] * CHUNKS,
        staged={0: None, 1: None} | {2 + k: slice(k * share, (k + 1) * share) for k in range(CHUNKS)},
        sent=(0, 1, 2, 3),
        plain=(4, 5),
        scratch=[pltpu.VMEM(packed.shape, BF16), pltpu.SemaphoreType.DMA((CHUNKS,))],
        limit=WHOLE_VMEM,
        flops=10**8,
    )
    coef = send(coef)
    (packed_weights,) = run(fetch_kernel, [packed], kept_weights, moved={0: 0})
    before, after = neighbours(first, last)
    local, lanes, outer_cells = run(
        local_kernel,
        [shape((CELLS, LANES), F32), shape((2 * LANES, CELLS), BF16), wide],
        cells,
        before,
        after,
        cotangent.reshape(field.shape),
        taps,
        scratch=[padded, pltpu.VMEM((3, 2 * LANES, 3 * LANES), BF16)],
        flops=8 * 10**9,
    )
    back, diagonal = run(
        functools.partial(mix_kernel, batches, slabs),
        [to_send, shape((count, GROUP * half // 2), BF16)],
        coef,
        gather,
        packed_weights,
        scatter,
        sent=(0, 1),
        slots={0: slot},
        flops=4 * 10**8,
    )
    back = send(back)
    slab = shape((devices, 8 + TERM_ROWS // devices, LANES), BF16)
    activated, grad, first, last, back, terms = run(
        functools.partial(activate_kernel, in_slab),
        [
            wide,
            shape((HBM_BYTES // (2 * LANES), LANES), BF16),
            edge,
            edge,
            slab if in_slab else plane_modes,
            None if in_slab else shape((TERM_ROWS, LANES), BF16),
        ],
        back,
        np.ascontiguousarray(synthesis.T),
        local,
        outer_cells,
        lanes,
        sent={1: CELLS, 2: None, 3: None, 4: None},
        scratch=[pltpu.VMEM((CELLS + 2 * NY, 3 * LANES), BF16), pltpu.VMEM((CELLS, LANES), F32)],
        flops=10**9,
    )
    if in_slab:
        back = exchange(back)
    else:
        back = send(back)
        terms = exchange(terms.reshape(devices, TERM_ROWS // devices, LANES))
    before, after = neighbours(first, last)
    activated, packed_weights = run(
        output_kernel,
        [field, packed],
        activated,
        kept_weights,
        moved={1: 1},
        flops=10**8,
    )
    back, before, after, activated, packed_weights = lax.optimization_barrier(
        (back, before, after, activated, packed_weights)
    )
    scale = 1.0 / math.sqrt(batches * slabs * layers * plane)
    grad_modes, mixed_grad, sums = run(
        functools.partial(unmix_kernel, batches, slabs, scale),
        [
            slab if in_slab else plane_modes,
            shape((count, LANES), BF16),
            None if in_slab else shape((TERM_ROWS // devices, LANES), F32),
        ],
        back,
        None if in_slab else terms,
        gather_back,
        packed_weights,
        scatter_back,
        sent=(0,),
        flops=4 * 10**8,
    )
    if in_slab:
        grad_modes = exchange(grad_modes)
    else:
        grad_modes = send(grad_modes)
        sums = lax.all_gather(sums, ("space", "batch"), axis=0, tiled=True)
    (local,) = run(
        local_grad_kernel,
        [shape((CELLS, LANES), F32)],
        grad,
        before,
        after,
        taps,
        staged={0: CELLS},
        scratch=[padded, pltpu.VMEM((3, 3 * LANES, 2 * LANES), BF16)],
        flops=7 * 10**8,
    )
    (mode_gradient,) = run(
        functools.partial(weight_kernel, batches),
        [shape((modes * 2 * KZ * channels, channels), F32)],
        diagonal,
        mixed_grad,
        flops=4 * 10**8,
    )
    input_gradient, conv_gradient = run(
        finish_kernel,
        [field, shape((OFFSETS, channels, channels), F32)],
        grad_modes,
        sums,
        np.ascontiguousarray(analysis.T),
        local,
        flops=10**8,
    )
    return (
        activated.reshape(snapshots.shape),
        input_gradient.reshape(snapshots.shape),
        mode_gradient.reshape(mode_weight.shape),
        conv_gradient.reshape(conv_weight.shape),
    )


def solution(mesh):
    in_specs = (
        P("batch", None, "space", None),
        P("batch", None, "space", None),
        P("batch", "space", None, None, None),
        P(),
    )
    out_specs = (
        P("batch", None, "space", None),
        P("batch", None, "space", None),
        P("batch", "space", None, None, None),
        P(),
    )
    return jax.shard_map(shards, mesh=mesh, in_specs=in_specs, out_specs=out_specs, check_vma=False)
```

```python
import functools
import math

import jax
import jax.numpy as jnp
import ml_dtypes
import numpy as np
from jax import lax
from jax.experimental import pallas as pl
from jax.experimental.pallas import tpu as pltpu
from jax.sharding import PartitionSpec as P

KX = 8
KY = 8
KZ = 12
NX = 32
NY = 32
CELLS = NX * NY
LANES = 128
GROUP = 8
OFFSETS = 27
TERM_ROWS = 1024
CHUNKS = 3
VMEM_BYTES = 40 * 1024 * 1024
LARGE_VMEM = 60 * 1024 * 1024
WHOLE_VMEM = 65000 * 1024
HBM_BYTES = 100 * 1024 * 256

F32 = jnp.float32
BF16 = jnp.bfloat16
inv_root_two = 1.0 / math.sqrt(2.0)
inv_root_two_pi = 1.0 / math.sqrt(2.0 * math.pi)


def basis_rows(half_count, length):
    row = np.arange(2 * half_count)[:, None]
    cell = np.arange(length)[None, :]
    frequency = np.where(row < half_count, row, row - half_count + 1)
    phases = (frequency * cell % length).astype(np.float32) * np.float32(2.0 * math.pi / length)
    return np.where(row < half_count, np.cos(phases), np.sin(phases)).astype(np.float32)


def plane_tables(batches, slabs):
    outer = (basis_rows(KX, NX)[:, None, :, None] * basis_rows(KY, NY)[None, :, None, :]).reshape(
        2 * KX, 2 * KY, CELLS
    )
    outer = outer.reshape(batches, 2 * KX // batches, slabs, 2 * KY // slabs, CELLS)
    outer = outer.transpose(2, 0, 1, 3, 4).reshape(4 * KX * KY, CELLS)
    analysis = (outer * np.float32(2.0 / math.sqrt(CELLS))).astype(ml_dtypes.bfloat16)
    synthesis = (outer * np.float32(2.0 / math.sqrt(4 * KX * KY))).astype(ml_dtypes.bfloat16)
    return analysis, synthesis


def depth_tables(slabs, layers, modes):
    rows = basis_rows(KZ, slabs * layers)
    analysis = (rows * np.float32(math.sqrt(2.0 / (slabs * layers)))).astype(ml_dtypes.bfloat16)
    synthesis = (rows * np.float32(math.sqrt(2.0 / (2 * KZ)))).astype(ml_dtypes.bfloat16)

    def spread(table, order):
        table = table.astype(np.float32).reshape(2 * KZ, slabs, layers)
        full = np.einsum("psz,mn->" + order, table, np.eye(modes, dtype=np.float32))
        return full.astype(ml_dtypes.bfloat16)

    def gathered(table):
        return spread(table, "mpzsn").reshape(modes * 2 * KZ, layers * slabs * modes)

    def scattered(table):
        return spread(table, "snzmp").reshape(slabs * modes, layers * modes * 2 * KZ)

    return gathered(analysis), scattered(synthesis), gathered(synthesis), scattered(analysis)


def dot(left, right, contract=(1, 0)):
    return lax.dot_general(
        left, right, (((contract[0],), (contract[1],)), ((), ())), preferred_element_type=F32
    )


def turn_table():
    row = lax.broadcasted_iota(jnp.int32, (LANES, LANES), 0)
    column = lax.broadcasted_iota(jnp.int32, (LANES, LANES), 1)
    return jnp.where(column == row % 2 * (LANES // 2) + row // 2, 1.0, 0.0).astype(BF16)


def to_cells(field):
    return dot(field.reshape(LANES, CELLS), turn_table(), (0, 0))


def to_field(cells):
    return dot(turn_table(), cells, (1, 1)).astype(BF16).reshape(LANES // 2, 2, CELLS)


def low_lanes(rows):
    return lax.broadcasted_iota(jnp.int32, (rows, LANES), 1) < LANES // 2


def swap_halves(values):
    return pltpu.roll(values, LANES // 2, 1)


def doubled(values):
    low = low_lanes(values.shape[0])
    swapped = swap_halves(values)
    return jnp.concatenate(
        [jnp.where(low, values, swapped), jnp.where(low, swapped, values)], axis=0
    )


def halved(values):
    low = low_lanes(values.shape[0])
    return jnp.concatenate([jnp.where(low, values, 0.0), jnp.where(low, 0.0, values)], axis=0)


def edge_layers(cells_first):
    top = cells_first[: CELLS // 2]
    bottom = cells_first[CELLS // 2 :]
    low = low_lanes(CELLS // 2)
    first = jnp.where(low, top, swap_halves(bottom))
    last = jnp.where(low, swap_halves(top), bottom)
    return first.astype(BF16), last.astype(BF16)


def beside_layers(before, after):
    before = before.astype(F32)
    after = after.astype(F32)
    low = low_lanes(CELLS // 2)
    top = jnp.where(low, before, swap_halves(after))
    bottom = jnp.where(low, swap_halves(before), after)
    return jnp.concatenate([top, bottom], axis=0).astype(BF16)


def y_cells(rows):
    return lax.broadcasted_iota(jnp.int32, (rows, LANES), 0) % NY


def from_below(values):
    return jnp.where(y_cells(values.shape[0]) == 0, 0.0, pltpu.roll(values, 1, 0))


def from_above(values):
    rows = values.shape[0]
    return jnp.where(y_cells(rows) == NY - 1, 0.0, pltpu.roll(values, rows - 1, 0))


def pad_cells(padded, own, beside):
    width = own.shape[1] + beside.shape[1]
    padded[0:NY, :] = jnp.zeros((NY, width), BF16)
    padded[NY + CELLS : 2 * NY + CELLS, :] = jnp.zeros((NY, width), BF16)
    padded[NY : NY + CELLS, 0 : own.shape[1]] = own
    padded[NY : NY + CELLS, own.shape[1] :] = beside


BLOCK_OF_DEPTH = {-1: 2, 0: 0, 1: 1, 2: 3}
STEP = 256


def stencil(padded, table, transposed, store):
    for start in range(0, CELLS, STEP):
        total = None
        for b in range(3):
            cells = padded[start + NY * b : start + NY * b + STEP, :]
            term = dot(cells, table[b], (1, 1) if transposed else (1, 0))
            total = term if total is None else total + term
        result = (
            from_below(total[:, 0:LANES])
            + total[:, LANES : 2 * LANES]
            + from_above(total[:, 2 * LANES :])
        )
        store(start, result)


def banded_forward(weights, table):
    half = LANES // 2
    for b in range(3):
        for c in range(3):
            for depth, block in BLOCK_OF_DEPTH.items():
                parts = []
                for out in range(2):
                    a = depth - out + 1
                    if 0 <= a < 3:
                        parts.append(weights[a * 9 + b * 3 + c])
                    else:
                        parts.append(jnp.zeros((half, half), BF16))
                table[b, block * half : (block + 1) * half, c * LANES : (c + 1) * LANES] = (
                    jnp.concatenate(parts, axis=1)
                )


def banded_backward(weights, table):
    half = LANES // 2
    for b in range(3):
        for c in range(3):
            for out in range(2):
                for pair in ((0, 1), (-1, 2)):
                    parts = []
                    for depth in pair:
                        a = depth - out + 1
                        if 0 <= a < 3:
                            parts.append(weights[(2 - a) * 9 + (2 - b) * 3 + 2 - c])
                        else:
                            parts.append(jnp.zeros((half, half), BF16))
                    row = c * LANES + out * half
                    column = BLOCK_OF_DEPTH[pair[0]] * half
                    table[b, row : row + half, column : column + LANES] = jnp.concatenate(
                        parts, axis=1
                    )


def analyse_kernel(field, analysis, cells_out, coef_out, _):
    cells = to_cells(field[...])
    rounded = cells.astype(BF16)
    coef_out[...] = dot(analysis[...], rounded).astype(BF16)
    cells_out[...] = rounded


def edges_kernel(cells, first_out, last_out):
    first_out[...], last_out[...] = edge_layers(cells[...].astype(F32))


def pack_kernel(*refs):
    weights = refs[:CHUNKS]
    packed_out, buffer, semaphores = refs[CHUNKS:]
    rows = GROUP * LANES // 4
    share = buffer.shape[0] // CHUNKS
    copies = []
    for place, part in enumerate(weights):
        for g in range(share // rows):
            pair = [part[k * rows : (k + 1) * rows, :] for k in (2 * g, 2 * g + 1)]
            row = place * share + g * rows
            buffer[row : row + rows, :] = jnp.concatenate(pair, axis=1)
        span = slice(place * share, (place + 1) * share)
        copies.append(
            pltpu.make_async_copy(buffer.at[span], packed_out.at[span], semaphores.at[place])
        )
        copies[-1].start()
    for copy in copies:
        copy.wait()


def local_kernel(
    cells, before, after, cotangent, weights, local_out, lanes_out, cotangent_out, padded, table
):
    banded_forward(weights, table)
    beside = beside_layers(before[...], after[...])
    pad_cells(padded, cells[...], beside)

    def store(start, result):
        local_out[start : start + STEP, :] = result

    stencil(padded, table, False, store)
    whole = jnp.concatenate([cells[...].astype(F32), beside.astype(F32)], axis=1)
    lanes_out[...] = whole.T.astype(BF16)
    cotangent_out[...] = to_cells(cotangent[...]).astype(BF16)


def fetch_kernel():
    pass


def mode_in_group(rows, lanes):
    return lax.broadcasted_iota(jnp.int32, (rows, lanes), 0) % GROUP


def own_block(rows):
    width = GROUP * LANES // 4
    lane = lax.broadcasted_iota(jnp.int32, (rows, width), 1)
    return mode_in_group(rows, width) % (GROUP // 2) == lane // (LANES // 2)


def own_half(rows):
    return (mode_in_group(rows, LANES) < GROUP // 2) == low_lanes(rows)


def to_depth(modes, table, snaps, slabs):
    modes = modes.reshape(slabs, snaps, -1, LANES)
    both = [doubled(modes[:, b].reshape(-1, LANES)) for b in range(snaps)]
    result = dot(table, jnp.concatenate(both, axis=1).astype(BF16))
    return jnp.concatenate(
        [
            result[g : g + GROUP, b * LANES : (b + 1) * LANES]
            for g in range(0, result.shape[0], GROUP)
            for b in range(snaps)
        ],
        axis=0,
    )


def from_depth(modes, table, snaps, slabs):
    count = modes.shape[0] // GROUP
    both = []
    for b in range(snaps):
        own = [modes[g * GROUP : (g + 1) * GROUP] for g in range(b, count, snaps)]
        both.append(halved(jnp.concatenate(own, axis=0)))
    result = dot(table, jnp.concatenate(both, axis=1).astype(BF16))
    own = [
        result[:, b * LANES : (b + 1) * LANES].reshape(slabs, -1, LANES) for b in range(snaps)
    ]
    return jnp.stack(own, axis=1).reshape(-1, LANES)


def mix_kernel(snaps, slabs, received, gather, weights, scatter, back_out, diagonal_out):
    coef = to_depth(received[...].astype(F32), gather[...], snaps, slabs)
    count = coef.shape[0]
    wide = jnp.concatenate([coef] * (GROUP // 4), axis=1)
    diagonal = jnp.where(own_block(count), wide, 0.0).astype(BF16)
    diagonal_out[...] = diagonal
    rows = GROUP * snaps
    depth = GROUP * LANES // 4
    mixed = jnp.concatenate(
        [
            dot(diagonal[g * rows : (g + 1) * rows, :], weights[g * depth : (g + 1) * depth, :])
            for g in range(count // rows)
        ],
        axis=0,
    )
    mixed = jnp.where(own_half(count), mixed, swap_halves(mixed))
    back = from_depth(mixed, scatter[...], snaps, slabs).astype(BF16)
    back_out[...] = back.reshape(back_out.shape)


def activate_kernel(
    terms_in_slab,
    received,
    synthesis,
    local,
    cotangent,
    lanes,
    activated_out,
    grad_out,
    first_out,
    last_out,
    back_out,
    terms_out,
    spread,
):
    pre = dot(synthesis[...], received[...]) + local[...]
    cdf = 0.5 * (1.0 + lax.erf(pre * inv_root_two))
    density = jnp.exp(-0.5 * pre * pre) * inv_root_two_pi
    activated_out[...] = (pre * cdf).astype(BF16)
    grad = (cotangent[...].astype(F32) * (cdf + pre * density)).astype(BF16)
    back = dot(synthesis[...], grad, (0, 0))
    rounded = grad
    grad = grad.astype(F32)
    first, last = edge_layers(grad)
    spread[0:NY, :] = jnp.zeros((NY, 3 * LANES), BF16)
    spread[NY + CELLS : 2 * NY + CELLS, :] = jnp.zeros((NY, 3 * LANES), BF16)
    spread[NY : NY + CELLS, 0:LANES] = from_above(grad).astype(BF16)
    spread[NY : NY + CELLS, LANES : 2 * LANES] = grad.astype(BF16)
    spread[NY : NY + CELLS, 2 * LANES :] = from_below(grad).astype(BF16)
    half = LANES // 2
    low = low_lanes(half)
    twice = {}
    for b in range(3):
        product = dot(lanes[...], spread[NY * (2 - b) : NY * (2 - b) + CELLS, :])
        for c in range(3):
            for a in range(3):
                blocks = [BLOCK_OF_DEPTH[out + a - 1] * half for out in range(2)]
                columns = slice(c * LANES, (c + 1) * LANES)
                both = jnp.where(
                    low,
                    product[blocks[0] : blocks[0] + half, columns],
                    product[blocks[1] : blocks[1] + half, columns],
                )
                twice[a * 9 + b * 3 + c] = both + swap_halves(both)
    pairs = []
    for k in range(0, OFFSETS, 2):
        pairs.append(jnp.where(low, twice[k], twice.get(k + 1, 0.0)))
    pairs.append(jnp.zeros((TERM_ROWS - half * len(pairs), LANES), F32))
    terms = jnp.concatenate(pairs, axis=0)
    if terms_in_slab:
        slab_store(back_out, back, terms)
    else:
        back_out[...] = back.astype(BF16)
        terms_out[...] = terms.astype(BF16)
    grad_out[...] = rounded
    first_out[...] = first
    last_out[...] = last


def slab_store(slab, modes, terms):
    owners = slab.shape[0]
    modes = modes.reshape(owners, 8, LANES)
    terms = terms.reshape(owners, -1, LANES)
    slab[...] = jnp.concatenate([modes, terms], axis=1).astype(BF16)


def slab_load(slab):
    whole = slab[...].astype(F32)
    return whole[:, 0:8, :].reshape(-1, LANES), whole[:, 8:, :]


def unmix_kernel(snaps, slabs, scale, received, terms, gather, weights, scatter, grad_out, mixed_out, sums_out):
    in_slab = terms is None
    if in_slab:
        modes, terms = slab_load(received)
    else:
        modes, terms = received[...].astype(F32), terms[...].astype(F32)
    mixed = to_depth(modes, gather[...], snaps, slabs)
    mixed_out[...] = mixed.astype(BF16)
    count = mixed.shape[0]
    rows = GROUP * snaps
    depth = GROUP * LANES // 4
    sums = jnp.sum(terms, axis=0) * scale
    own = own_block(rows)
    placed = jnp.where(own_half(count), mixed, 0.0).astype(BF16)
    pieces = []
    for g in range(count // rows):
        full = dot(
            placed[g * rows : (g + 1) * rows, :], weights[g * depth : (g + 1) * depth, :], (1, 1)
        )
        full = jnp.where(own, full, 0.0)
        pieces.append(sum(full[:, k : k + LANES] for k in range(0, depth, LANES)))
    coef = jnp.concatenate(pieces, axis=0)
    coef = coef + swap_halves(coef)
    grad = from_depth(coef, scatter[...], snaps, slabs)
    if in_slab:
        owners = received.shape[0]
        share = sums.shape[0]
        slab_store(
            grad_out, grad, jnp.broadcast_to(sums[None], (owners, share, LANES)).reshape(-1, LANES)
        )
    else:
        grad_out[...] = grad.astype(BF16)
        sums_out[...] = sums


def weight_kernel(snaps, diagonal, mixed, out):
    rows = GROUP * snaps
    depth = GROUP * LANES // 4
    half = LANES // 2
    first = mode_in_group(rows, depth) < GROUP // 2
    for g in range(diagonal.shape[0] // rows):
        span = slice(g * rows, (g + 1) * rows)
        blocks = diagonal[span, :].astype(F32)
        blocks = [jnp.where(first, blocks, 0.0), jnp.where(first, 0.0, blocks)]
        blocks = jnp.concatenate(blocks, axis=1).astype(BF16)
        out[2 * g * depth : 2 * (g + 1) * depth, :] = dot(blocks, mixed[span, 0:half], (0, 0))


def output_kernel(cells, out):
    out[...] = to_field(cells[...])


def local_grad_kernel(grad, before, after, weights, out, padded, table):
    banded_backward(weights, table)
    pad_cells(padded, grad[...], beside_layers(before[...], after[...]))

    def store(start, result):
        out[start : start + STEP, :] = result

    stencil(padded, table, True, store)


def finish_kernel(received, sums, synthesis, local, grad_out, stencil_out):
    in_slab = sums is None
    if in_slab:
        modes, terms = slab_load(received)
        terms = terms.reshape(TERM_ROWS, LANES)
    else:
        modes, terms = received[...], sums[...].astype(F32)
    cells = (dot(synthesis[...], modes.astype(BF16)) + local[...]).astype(BF16)
    grad_out[...] = to_field(cells)
    half = LANES // 2
    for k in range(OFFSETS):
        row = (k // 2) * half
        lane = (k % 2) * half
        stencil_out[k] = terms[row : row + half, lane : lane + half]


def shape(dims, dtype):
    return jax.ShapeDtypeStruct(dims, dtype)


class Staged:
    def __init__(self, source, buffer, semaphore):
        self.copy = pltpu.make_async_copy(source, buffer, semaphore)
        self.buffer = buffer
        self.copy.start()
        self.ready = False

    def load(self):
        if not self.ready:
            self.copy.wait()
            self.ready = True

    def __getitem__(self, index):
        self.load()
        return self.buffer[index]


class Sent:
    def __init__(self, target, buffer, semaphore):
        self.copy = pltpu.make_async_copy(buffer, target, semaphore)
        self.buffer = buffer

    def __setitem__(self, index, value):
        self.buffer[index] = value
        self.copy.start()

    def __getitem__(self, index):
        return self.buffer[index]

    @property
    def shape(self):
        return self.buffer.shape


def row_count(rows):
    return rows.stop - rows.start if isinstance(rows, slice) else rows


def run(
    body, outs, *operands, staged=(), sent=(), moved=(), plain=(), slots=(), scratch=(), flops=0, limit=VMEM_BYTES
):
    given = [k for k, operand in enumerate(operands) if operand is not None]
    made = [k for k, out in enumerate(outs) if out is not None]

    def rows_of(chosen, places, arrays):
        chosen = {k: chosen[k] if isinstance(chosen, dict) else None for k in places if k in chosen}
        return {k: rows or arrays[k].shape[0] for k, rows in chosen.items()}

    moved = dict(moved)
    slots = dict(slots)
    staged = rows_of(staged, given, operands)
    sent = rows_of(sent, made, outs)

    def kernel(*refs):
        refs = list(refs)

        def take(count):
            taken = refs[:count]
            del refs[:count]
            return taken

        def part(ref, rows):
            if isinstance(rows, slice):
                return ref.at[rows]
            return ref if ref.shape[0] == rows else ref.at[0:rows]

        filled = dict(zip(given, take(len(given))))
        take(len(slots))
        kept = dict(zip(made, take(len(made))))
        own = take(len(scratch))
        copies = []
        for place, (k, out) in enumerate(moved.items()):
            source, target = filled.pop(k), kept.pop(out)
            rows = min(source.shape[0], target.shape[0])
            semaphore = refs[-1].at[len(staged) + len(sent) + place]
            copies.append(
                pltpu.make_async_copy(part(source, rows), part(target, rows), semaphore)
            )
        for place, (k, buffer) in enumerate(zip(staged, take(len(staged)))):
            filled[k] = Staged(part(filled[k], staged[k]), buffer, refs[-1].at[place])
        for place, (k, buffer) in enumerate(zip(sent, take(len(sent)))):
            kept[k] = Sent(part(kept[k], sent[k]), buffer, refs[-1].at[len(staged) + place])
        for copy in copies:
            copy.start()
        body(
            *[filled.get(k) for k in range(len(operands)) if k not in moved],
            *[kept.get(k) for k in range(len(outs)) if k not in moved.values()],
            *own,
        )
        for k in staged:
            filled[k].load()
        for k in sent:
            kept[k].copy.wait()
        for copy in copies:
            copy.wait()

    arrays = [operands[k] for k in given]
    results = [outs[k] for k in made]
    size = sum(x.size * x.dtype.itemsize for x in (*arrays, *results))
    in_vmem = pl.BlockSpec(memory_space=pltpu.VMEM)
    in_hbm = pl.BlockSpec(memory_space=pltpu.HBM)
    buffers = [(operands[k], rows) for k, rows in staged.items()]
    buffers += [(outs[k], rows) for k, rows in sent.items()]
    buffers = [pltpu.VMEM((row_count(rows), *x.shape[1:]), x.dtype) for x, rows in buffers]
    if len(buffers) + len(moved) > 0:
        buffers.append(pltpu.SemaphoreType.DMA((len(buffers) + len(moved),)))
    results = pl.pallas_call(
        kernel,
        out_shape=results,
        in_specs=[in_hbm if k in staged or k in moved else in_vmem for k in given]
        + [in_hbm] * len(slots),
        out_specs=[in_hbm if k in sent or k in plain else in_vmem for k in made],
        input_output_aliases={len(given) + at: made.index(k) for at, k in enumerate(slots)},
        scratch_shapes=[*scratch, *buffers],
        compiler_params=pltpu.CompilerParams(vmem_limit_bytes=limit),
        cost_estimate=pl.CostEstimate(flops=flops, bytes_accessed=size, transcendentals=0),
        name=body.__name__ if hasattr(body, "__name__") else body.func.__name__,
    )(*arrays, *slots.values())
    results = dict(zip(made, results))
    return [results.get(k) for k in range(len(outs))]


def exchange(values):
    return lax.all_to_all(values, ("space", "batch"), split_axis=0, concat_axis=0, tiled=True)


def neighbours(first, last):
    ends = lax.axis_size("space") - 1
    before = lax.ppermute(last, "space", [(i, i + 1) for i in range(ends)])
    after = lax.ppermute(first, "space", [(i + 1, i) for i in range(ends)])
    return before, after


def shards(snapshots, cotangent, mode_weight, conv_weight):
    batches = lax.axis_size("batch")
    slabs = lax.axis_size("space")
    devices = batches * slabs
    _, channels, layers, plane = snapshots.shape
    modes = mode_weight.shape[0] * mode_weight.shape[1]
    half = LANES // 2
    assert channels == half and layers == 2 and plane == CELLS
    plane_rows = devices * modes
    count = modes * 2 * KZ * batches
    in_slab = modes == 8 and devices * 32 == TERM_ROWS

    analysis, synthesis = plane_tables(batches, slabs)
    gather, scatter, gather_back, scatter_back = depth_tables(slabs, layers, modes)
    weights = mode_weight.reshape(modes * 2 * KZ * channels, channels)
    taps = conv_weight.reshape(OFFSETS, channels, channels)
    field = shape((channels, layers, plane), BF16)
    wide = shape((CELLS, LANES), BF16)
    edge = shape((CELLS // 2, LANES), BF16)
    plane_modes = shape((plane_rows, LANES), BF16)
    padded = pltpu.VMEM((CELLS + 2 * NY, 2 * LANES), BF16)

    def send(values):
        return exchange(values.reshape(devices, modes, LANES)).reshape(plane_rows, LANES)

    packed = shape((weights.shape[0] // 2, LANES), BF16)
    to_send = shape((devices, modes, LANES), BF16) if modes % 8 == 0 else plane_modes
    cells, coef, slot = run(
        analyse_kernel,
        [wide, plane_modes, to_send],
        snapshots.reshape(field.shape),
        analysis,
        staged=(0, 1),
        sent=(0, 1),
        plain=(2,),
        limit=WHOLE_VMEM,
        flops=10**8,
    )
    weights, coef = lax.optimization_barrier((weights, coef))
    coef = send(coef)
    share = weights.shape[0] // CHUNKS
    (kept_weights,) = run(
        pack_kernel,
        [shape((HBM_BYTES // (2 * LANES), LANES), BF16)],
        *[weights] * CHUNKS,
        staged={k: slice(k * share, (k + 1) * share) for k in range(CHUNKS)},
        plain=(0,),
        scratch=[pltpu.VMEM(packed.shape, BF16), pltpu.SemaphoreType.DMA((CHUNKS,))],
        limit=LARGE_VMEM,
    )
    (packed_weights,) = run(fetch_kernel, [packed], kept_weights, moved={0: 0})
    back, diagonal = run(
        functools.partial(mix_kernel, batches, slabs),
        [to_send, shape((count, GROUP * half // 2), BF16)],
        coef,
        gather,
        packed_weights,
        scatter,
        sent=(0, 1),
        slots={0: slot},
        flops=4 * 10**8,
    )
    back, cells = lax.optimization_barrier((back, cells))
    back = send(back)
    first, last = run(edges_kernel, [edge, edge], cells)
    before, after = neighbours(first, last)
    local, lanes, outer_cells = run(
        local_kernel,
        [shape((CELLS, LANES), F32), shape((2 * LANES, CELLS), BF16), wide],
        cells,
        before,
        after,
        cotangent.reshape(field.shape),
        taps,
        scratch=[padded, pltpu.VMEM((3, 2 * LANES, 3 * LANES), BF16)],
        flops=8 * 10**9,
    )
    slab = shape((devices, 8 + TERM_ROWS // devices, LANES), BF16)
    activated, grad, first, last, back, terms = run(
        functools.partial(activate_kernel, in_slab),
        [
            wide,
            shape((HBM_BYTES // (2 * LANES), LANES), BF16),
            edge,
            edge,
            slab if in_slab else plane_modes,
            None if in_slab else shape((TERM_ROWS, LANES), BF16),
        ],
        back,
        np.ascontiguousarray(synthesis.T),
        local,
        outer_cells,
        lanes,
        sent={1: CELLS, 2: None, 3: None, 4: None},
        scratch=[pltpu.VMEM((CELLS + 2 * NY, 3 * LANES), BF16)],
        flops=10**9,
    )
    if in_slab:
        back = exchange(back)
    else:
        back = send(back)
        terms = exchange(terms.reshape(devices, TERM_ROWS // devices, LANES))
    before, after = neighbours(first, last)
    activated, packed_weights = run(
        output_kernel,
        [field, packed],
        activated,
        kept_weights,
        moved={1: 1},
        flops=10**8,
    )
    back, before, after, activated, packed_weights = lax.optimization_barrier(
        (back, before, after, activated, packed_weights)
    )
    scale = 1.0 / math.sqrt(batches * slabs * layers * plane)
    grad_modes, mixed_grad, sums = run(
        functools.partial(unmix_kernel, batches, slabs, scale),
        [
            slab if in_slab else plane_modes,
            shape((count, LANES), BF16),
            None if in_slab else shape((TERM_ROWS // devices, LANES), F32),
        ],
        back,
        None if in_slab else terms,
        gather_back,
        packed_weights,
        scatter_back,
        sent=(0,),
        flops=4 * 10**8,
    )
    if in_slab:
        grad_modes = exchange(grad_modes)
    else:
        grad_modes = send(grad_modes)
        sums = lax.all_gather(sums, ("space", "batch"), axis=0, tiled=True)
    (local,) = run(
        local_grad_kernel,
        [shape((CELLS, LANES), F32)],
        grad,
        before,
        after,
        taps,
        staged={0: CELLS},
        scratch=[padded, pltpu.VMEM((3, 3 * LANES, 2 * LANES), BF16)],
        flops=7 * 10**8,
    )
    (mode_gradient,) = run(
        functools.partial(weight_kernel, batches),
        [shape((modes * 2 * KZ * channels, channels), F32)],
        diagonal,
        mixed_grad,
        flops=4 * 10**8,
    )
    input_gradient, conv_gradient = run(
        finish_kernel,
        [field, shape((OFFSETS, channels, channels), F32)],
        grad_modes,
        sums,
        np.ascontiguousarray(analysis.T),
        local,
        flops=10**8,
    )
    return (
        activated.reshape(snapshots.shape),
        input_gradient.reshape(snapshots.shape),
        mode_gradient.reshape(mode_weight.shape),
        conv_gradient.reshape(conv_weight.shape),
    )


def solution(mesh):
    in_specs = (
        P("batch", None, "space", None),
        P("batch", None, "space", None),
        P("batch", "space", None, None, None),
        P(),
    )
    out_specs = (
        P("batch", None, "space", None),
        P("batch", None, "space", None),
        P("batch", "space", None, None, None),
        P(),
    )
    return jax.shard_map(shards, mesh=mesh, in_specs=in_specs, out_specs=out_specs, check_vma=False)
```

```python
import functools
import math

import jax
import jax.numpy as jnp
import ml_dtypes
import numpy as np
from jax import lax
from jax.experimental import pallas as pl
from jax.experimental.pallas import tpu as pltpu
from jax.sharding import PartitionSpec as P

KX = 8
KY = 8
KZ = 12
NX = 32
NY = 32
CELLS = NX * NY
LANES = 128
GROUP = 8
OFFSETS = 27
TERM_ROWS = 1024
CHUNKS = 3
VMEM_BYTES = 40 * 1024 * 1024
WHOLE_VMEM = 65000 * 1024
HBM_BYTES = 100 * 1024 * 256

F32 = jnp.float32
BF16 = jnp.bfloat16
inv_root_two = 1.0 / math.sqrt(2.0)
inv_root_two_pi = 1.0 / math.sqrt(2.0 * math.pi)


def basis_rows(half_count, length):
    row = np.arange(2 * half_count)[:, None]
    cell = np.arange(length)[None, :]
    frequency = np.where(row < half_count, row, row - half_count + 1)
    phases = (frequency * cell % length).astype(np.float32) * np.float32(2.0 * math.pi / length)
    return np.where(row < half_count, np.cos(phases), np.sin(phases)).astype(np.float32)


def plane_tables(batches, slabs):
    outer = (basis_rows(KX, NX)[:, None, :, None] * basis_rows(KY, NY)[None, :, None, :]).reshape(
        2 * KX, 2 * KY, CELLS
    )
    outer = outer.reshape(batches, 2 * KX // batches, slabs, 2 * KY // slabs, CELLS)
    outer = outer.transpose(2, 0, 1, 3, 4).reshape(4 * KX * KY, CELLS)
    analysis = (outer * np.float32(2.0 / math.sqrt(CELLS))).astype(ml_dtypes.bfloat16)
    synthesis = (outer * np.float32(2.0 / math.sqrt(4 * KX * KY))).astype(ml_dtypes.bfloat16)
    return analysis, synthesis


def depth_tables(slabs, layers, modes):
    rows = basis_rows(KZ, slabs * layers)
    analysis = (rows * np.float32(math.sqrt(2.0 / (slabs * layers)))).astype(ml_dtypes.bfloat16)
    synthesis = (rows * np.float32(math.sqrt(2.0 / (2 * KZ)))).astype(ml_dtypes.bfloat16)

    def spread(table, order):
        table = table.astype(np.float32).reshape(2 * KZ, slabs, layers)
        full = np.einsum("psz,mn->" + order, table, np.eye(modes, dtype=np.float32))
        return full.astype(ml_dtypes.bfloat16)

    def gathered(table):
        return spread(table, "mpzsn").reshape(modes * 2 * KZ, layers * slabs * modes)

    def scattered(table):
        return spread(table, "snzmp").reshape(slabs * modes, layers * modes * 2 * KZ)

    return gathered(analysis), scattered(synthesis), gathered(synthesis), scattered(analysis)


def dot(left, right, contract=(1, 0)):
    return lax.dot_general(
        left, right, (((contract[0],), (contract[1],)), ((), ())), preferred_element_type=F32
    )


def turn_table():
    row = lax.broadcasted_iota(jnp.int32, (LANES, LANES), 0)
    column = lax.broadcasted_iota(jnp.int32, (LANES, LANES), 1)
    return jnp.where(column == row % 2 * (LANES // 2) + row // 2, 1.0, 0.0).astype(BF16)


def to_cells(field):
    return dot(field.reshape(LANES, CELLS), turn_table(), (0, 0))


def to_field(cells):
    return dot(turn_table(), cells, (1, 1)).astype(BF16).reshape(LANES // 2, 2, CELLS)


def low_lanes(rows):
    return lax.broadcasted_iota(jnp.int32, (rows, LANES), 1) < LANES // 2


def swap_halves(values):
    return pltpu.roll(values, LANES // 2, 1)


def doubled(values):
    low = low_lanes(values.shape[0])
    swapped = swap_halves(values)
    return jnp.concatenate(
        [jnp.where(low, values, swapped), jnp.where(low, swapped, values)], axis=0
    )


def halved(values):
    low = low_lanes(values.shape[0])
    return jnp.concatenate([jnp.where(low, values, 0.0), jnp.where(low, 0.0, values)], axis=0)


def edge_layers(cells_first):
    top = cells_first[: CELLS // 2]
    bottom = cells_first[CELLS // 2 :]
    low = low_lanes(CELLS // 2)
    first = jnp.where(low, top, swap_halves(bottom))
    last = jnp.where(low, swap_halves(top), bottom)
    return first.astype(BF16), last.astype(BF16)


def beside_layers(before, after):
    before = before.astype(F32)
    after = after.astype(F32)
    low = low_lanes(CELLS // 2)
    top = jnp.where(low, before, swap_halves(after))
    bottom = jnp.where(low, swap_halves(before), after)
    return jnp.concatenate([top, bottom], axis=0).astype(BF16)


def y_cells(rows):
    return lax.broadcasted_iota(jnp.int32, (rows, LANES), 0) % NY


def from_below(values):
    return jnp.where(y_cells(values.shape[0]) == 0, 0.0, pltpu.roll(values, 1, 0))


def from_above(values):
    rows = values.shape[0]
    return jnp.where(y_cells(rows) == NY - 1, 0.0, pltpu.roll(values, rows - 1, 0))


def pad_cells(padded, own, beside):
    width = own.shape[1] + beside.shape[1]
    padded[0:NY, :] = jnp.zeros((NY, width), BF16)
    padded[NY + CELLS : 2 * NY + CELLS, :] = jnp.zeros((NY, width), BF16)
    padded[NY : NY + CELLS, 0 : own.shape[1]] = own
    padded[NY : NY + CELLS, own.shape[1] :] = beside


BLOCK_OF_DEPTH = {-1: 2, 0: 0, 1: 1, 2: 3}
STEP = 256


def stencil(padded, table, transposed, store):
    for start in range(0, CELLS, STEP):
        total = None
        for b in range(3):
            cells = padded[start + NY * b : start + NY * b + STEP, :]
            term = dot(cells, table[b], (1, 1) if transposed else (1, 0))
            total = term if total is None else total + term
        result = (
            from_below(total[:, 0:LANES])
            + total[:, LANES : 2 * LANES]
            + from_above(total[:, 2 * LANES :])
        )
        store(start, result)


def banded_forward(weights, table):
    half = LANES // 2
    for b in range(3):
        for c in range(3):
            for depth, block in BLOCK_OF_DEPTH.items():
                parts = []
                for out in range(2):
                    a = depth - out + 1
                    if 0 <= a < 3:
                        parts.append(weights[a * 9 + b * 3 + c])
                    else:
                        parts.append(jnp.zeros((half, half), BF16))
                table[b, block * half : (block + 1) * half, c * LANES : (c + 1) * LANES] = (
                    jnp.concatenate(parts, axis=1)
                )


def banded_backward(weights, table):
    half = LANES // 2
    for b in range(3):
        for c in range(3):
            for out in range(2):
                for pair in ((0, 1), (-1, 2)):
                    parts = []
                    for depth in pair:
                        a = depth - out + 1
                        if 0 <= a < 3:
                            parts.append(weights[(2 - a) * 9 + (2 - b) * 3 + 2 - c])
                        else:
                            parts.append(jnp.zeros((half, half), BF16))
                    row = c * LANES + out * half
                    column = BLOCK_OF_DEPTH[pair[0]] * half
                    table[b, row : row + half, column : column + LANES] = jnp.concatenate(
                        parts, axis=1
                    )


def analyse_kernel(field, analysis, *refs):
    weights = refs[:CHUNKS]
    cells_out, coef_out, first_out, last_out, packed_out, _, buffer, semaphores = refs[CHUNKS:]
    cells = to_cells(field[...])
    rounded = cells.astype(BF16)
    coef_out[...] = dot(analysis[...], rounded).astype(BF16)
    cells_out[...] = rounded
    first, last = edge_layers(cells)
    first_out[...] = first
    last_out[...] = last
    rows = GROUP * LANES // 4
    share = buffer.shape[0] // CHUNKS
    copies = []
    for place, part in enumerate(weights):
        for g in range(share // rows):
            pair = [part[k * rows : (k + 1) * rows, :] for k in (2 * g, 2 * g + 1)]
            row = place * share + g * rows
            buffer[row : row + rows, :] = jnp.concatenate(pair, axis=1)
        span = slice(place * share, (place + 1) * share)
        copies.append(
            pltpu.make_async_copy(buffer.at[span], packed_out.at[span], semaphores.at[place])
        )
        copies[-1].start()
    for copy in copies:
        copy.wait()


def local_kernel(
    cells, before, after, cotangent, weights, local_out, lanes_out, cotangent_out, padded, table
):
    banded_forward(weights, table)
    beside = beside_layers(before[...], after[...])
    pad_cells(padded, cells[...], beside)

    def store(start, result):
        local_out[start : start + STEP, :] = result

    stencil(padded, table, False, store)
    whole = jnp.concatenate([cells[...].astype(F32), beside.astype(F32)], axis=1)
    lanes_out[...] = whole.T.astype(BF16)
    cotangent_out[...] = to_cells(cotangent[...]).astype(BF16)


def fetch_kernel():
    pass


def mode_in_group(rows, lanes):
    return lax.broadcasted_iota(jnp.int32, (rows, lanes), 0) % GROUP


def own_block(rows):
    width = GROUP * LANES // 4
    lane = lax.broadcasted_iota(jnp.int32, (rows, width), 1)
    return mode_in_group(rows, width) % (GROUP // 2) == lane // (LANES // 2)


def own_half(rows):
    return (mode_in_group(rows, LANES) < GROUP // 2) == low_lanes(rows)


def to_depth(modes, table, snaps, slabs):
    modes = modes.reshape(slabs, snaps, -1, LANES)
    both = [doubled(modes[:, b].reshape(-1, LANES)) for b in range(snaps)]
    result = dot(table, jnp.concatenate(both, axis=1).astype(BF16))
    return jnp.concatenate(
        [
            result[g : g + GROUP, b * LANES : (b + 1) * LANES]
            for g in range(0, result.shape[0], GROUP)
            for b in range(snaps)
        ],
        axis=0,
    )


def from_depth(modes, table, snaps, slabs):
    count = modes.shape[0] // GROUP
    both = []
    for b in range(snaps):
        own = [modes[g * GROUP : (g + 1) * GROUP] for g in range(b, count, snaps)]
        both.append(halved(jnp.concatenate(own, axis=0)))
    result = dot(table, jnp.concatenate(both, axis=1).astype(BF16))
    own = [
        result[:, b * LANES : (b + 1) * LANES].reshape(slabs, -1, LANES) for b in range(snaps)
    ]
    return jnp.stack(own, axis=1).reshape(-1, LANES)


def mix_kernel(snaps, slabs, received, gather, weights, scatter, back_out, diagonal_out):
    coef = to_depth(received[...].astype(F32), gather[...], snaps, slabs)
    count = coef.shape[0]
    wide = jnp.concatenate([coef] * (GROUP // 4), axis=1)
    diagonal = jnp.where(own_block(count), wide, 0.0).astype(BF16)
    diagonal_out[...] = diagonal
    rows = GROUP * snaps
    depth = GROUP * LANES // 4
    mixed = jnp.concatenate(
        [
            dot(diagonal[g * rows : (g + 1) * rows, :], weights[g * depth : (g + 1) * depth, :])
            for g in range(count // rows)
        ],
        axis=0,
    )
    mixed = jnp.where(own_half(count), mixed, swap_halves(mixed))
    back = from_depth(mixed, scatter[...], snaps, slabs).astype(BF16)
    back_out[...] = back.reshape(back_out.shape)


def activate_kernel(
    terms_in_slab,
    received,
    synthesis,
    local,
    cotangent,
    lanes,
    activated_out,
    grad_out,
    first_out,
    last_out,
    back_out,
    terms_out,
    spread,
):
    pre = dot(synthesis[...], received[...]) + local[...]
    cdf = 0.5 * (1.0 + lax.erf(pre * inv_root_two))
    density = jnp.exp(-0.5 * pre * pre) * inv_root_two_pi
    activated_out[...] = (pre * cdf).astype(BF16)
    grad = (cotangent[...].astype(F32) * (cdf + pre * density)).astype(BF16)
    back = dot(synthesis[...], grad, (0, 0))
    rounded = grad
    grad = grad.astype(F32)
    first, last = edge_layers(grad)
    spread[0:NY, :] = jnp.zeros((NY, 3 * LANES), BF16)
    spread[NY + CELLS : 2 * NY + CELLS, :] = jnp.zeros((NY, 3 * LANES), BF16)
    spread[NY : NY + CELLS, 0:LANES] = from_above(grad).astype(BF16)
    spread[NY : NY + CELLS, LANES : 2 * LANES] = grad.astype(BF16)
    spread[NY : NY + CELLS, 2 * LANES :] = from_below(grad).astype(BF16)
    half = LANES // 2
    low = low_lanes(half)
    twice = {}
    for b in range(3):
        product = dot(lanes[...], spread[NY * (2 - b) : NY * (2 - b) + CELLS, :])
        for c in range(3):
            for a in range(3):
                blocks = [BLOCK_OF_DEPTH[out + a - 1] * half for out in range(2)]
                columns = slice(c * LANES, (c + 1) * LANES)
                both = jnp.where(
                    low,
                    product[blocks[0] : blocks[0] + half, columns],
                    product[blocks[1] : blocks[1] + half, columns],
                )
                twice[a * 9 + b * 3 + c] = both + swap_halves(both)
    pairs = []
    for k in range(0, OFFSETS, 2):
        pairs.append(jnp.where(low, twice[k], twice.get(k + 1, 0.0)))
    pairs.append(jnp.zeros((TERM_ROWS - half * len(pairs), LANES), F32))
    terms = jnp.concatenate(pairs, axis=0)
    if terms_in_slab:
        slab_store(back_out, back, terms)
    else:
        back_out[...] = back.astype(BF16)
        terms_out[...] = terms.astype(BF16)
    grad_out[...] = rounded
    first_out[...] = first
    last_out[...] = last


def slab_owners(slab):
    return (slab.shape[0] - TERM_ROWS) // 8


def slab_store(slab, modes, terms):
    owners = slab_owners(slab)
    modes = modes.reshape(owners, 8, LANES)
    terms = terms.reshape(owners, -1, LANES)
    slab[...] = jnp.concatenate([modes, terms], axis=1).reshape(-1, LANES).astype(BF16)


def slab_load(slab):
    whole = slab[...].astype(F32).reshape(slab_owners(slab), -1, LANES)
    return whole[:, 0:8, :].reshape(-1, LANES), whole[:, 8:, :]


def unmix_kernel(snaps, slabs, scale, received, terms, gather, weights, scatter, grad_out, mixed_out, sums_out):
    in_slab = terms is None
    if in_slab:
        modes, terms = slab_load(received)
    else:
        modes, terms = received[...].astype(F32), terms[...].astype(F32)
    mixed = to_depth(modes, gather[...], snaps, slabs)
    mixed_out[...] = mixed.astype(BF16)
    count = mixed.shape[0]
    rows = GROUP * snaps
    depth = GROUP * LANES // 4
    sums = jnp.sum(terms, axis=0) * scale
    own = own_block(rows)
    placed = jnp.where(own_half(count), mixed, 0.0).astype(BF16)
    pieces = []
    for g in range(count // rows):
        full = dot(
            placed[g * rows : (g + 1) * rows, :], weights[g * depth : (g + 1) * depth, :], (1, 1)
        )
        full = jnp.where(own, full, 0.0)
        pieces.append(sum(full[:, k : k + LANES] for k in range(0, depth, LANES)))
    coef = jnp.concatenate(pieces, axis=0)
    coef = coef + swap_halves(coef)
    grad = from_depth(coef, scatter[...], snaps, slabs)
    if in_slab:
        owners = slab_owners(received)
        share = sums.shape[0]
        slab_store(
            grad_out, grad, jnp.broadcast_to(sums[None], (owners, share, LANES)).reshape(-1, LANES)
        )
    else:
        grad_out[...] = grad.astype(BF16)
        sums_out[...] = sums


def weight_kernel(snaps, diagonal, mixed, out):
    rows = GROUP * snaps
    depth = GROUP * LANES // 4
    half = LANES // 2
    first = mode_in_group(rows, depth) < GROUP // 2
    for g in range(diagonal.shape[0] // rows):
        span = slice(g * rows, (g + 1) * rows)
        blocks = diagonal[span, :].astype(F32)
        blocks = [jnp.where(first, blocks, 0.0), jnp.where(first, 0.0, blocks)]
        blocks = jnp.concatenate(blocks, axis=1).astype(BF16)
        out[2 * g * depth : 2 * (g + 1) * depth, :] = dot(blocks, mixed[span, 0:half], (0, 0))


def output_kernel(cells, out):
    out[...] = to_field(cells[...])


def local_grad_kernel(grad, before, after, weights, out, padded, table):
    banded_backward(weights, table)
    pad_cells(padded, grad[...], beside_layers(before[...], after[...]))

    def store(start, result):
        out[start : start + STEP, :] = result

    stencil(padded, table, True, store)


def finish_kernel(received, sums, synthesis, local, grad_out, stencil_out):
    in_slab = sums is None
    if in_slab:
        modes, terms = slab_load(received)
        terms = terms.reshape(TERM_ROWS, LANES)
    else:
        modes, terms = received[...], sums[...].astype(F32)
    cells = (dot(synthesis[...], modes.astype(BF16)) + local[...]).astype(BF16)
    grad_out[...] = to_field(cells)
    half = LANES // 2
    for k in range(OFFSETS):
        row = (k // 2) * half
        lane = (k % 2) * half
        stencil_out[k] = terms[row : row + half, lane : lane + half]


def shape(dims, dtype):
    return jax.ShapeDtypeStruct(dims, dtype)


class Staged:
    def __init__(self, source, buffer, semaphore):
        self.copy = pltpu.make_async_copy(source, buffer, semaphore)
        self.buffer = buffer
        self.copy.start()
        self.ready = False

    def load(self):
        if not self.ready:
            self.copy.wait()
            self.ready = True

    def __getitem__(self, index):
        self.load()
        return self.buffer[index]


class Sent:
    def __init__(self, target, buffer, semaphore):
        self.copy = pltpu.make_async_copy(buffer, target, semaphore)
        self.buffer = buffer

    def __setitem__(self, index, value):
        self.buffer[index] = value
        self.copy.start()

    def __getitem__(self, index):
        return self.buffer[index]

    @property
    def shape(self):
        return self.buffer.shape


def row_count(rows):
    return rows.stop - rows.start if isinstance(rows, slice) else rows


def run(
    body, outs, *operands, staged=(), sent=(), moved=(), plain=(), slots=(), scratch=(), flops=0, limit=VMEM_BYTES
):
    given = [k for k, operand in enumerate(operands) if operand is not None]
    made = [k for k, out in enumerate(outs) if out is not None]

    def rows_of(chosen, places, arrays):
        chosen = {k: chosen[k] if isinstance(chosen, dict) else None for k in places if k in chosen}
        return {k: rows or arrays[k].shape[0] for k, rows in chosen.items()}

    moved = dict(moved)
    slots = dict(slots)
    staged = rows_of(staged, given, operands)
    sent = rows_of(sent, made, outs)

    def kernel(*refs):
        refs = list(refs)

        def take(count):
            taken = refs[:count]
            del refs[:count]
            return taken

        def part(ref, rows):
            if isinstance(rows, slice):
                return ref.at[rows]
            return ref if ref.shape[0] == rows else ref.at[0:rows]

        filled = dict(zip(given, take(len(given))))
        take(len(slots))
        kept = dict(zip(made, take(len(made))))
        own = take(len(scratch))
        copies = []
        for place, (k, out) in enumerate(moved.items()):
            source, target = filled.pop(k), kept.pop(out)
            rows = min(source.shape[0], target.shape[0])
            semaphore = refs[-1].at[len(staged) + len(sent) + place]
            copies.append(
                pltpu.make_async_copy(part(source, rows), part(target, rows), semaphore)
            )
        for place, (k, buffer) in enumerate(zip(staged, take(len(staged)))):
            filled[k] = Staged(part(filled[k], staged[k]), buffer, refs[-1].at[place])
        for place, (k, buffer) in enumerate(zip(sent, take(len(sent)))):
            kept[k] = Sent(part(kept[k], sent[k]), buffer, refs[-1].at[len(staged) + place])
        for copy in copies:
            copy.start()
        body(
            *[filled.get(k) for k in range(len(operands)) if k not in moved],
            *[kept.get(k) for k in range(len(outs)) if k not in moved.values()],
            *own,
        )
        for k in staged:
            filled[k].load()
        for k in sent:
            kept[k].copy.wait()
        for copy in copies:
            copy.wait()

    arrays = [operands[k] for k in given]
    results = [outs[k] for k in made]
    size = sum(x.size * x.dtype.itemsize for x in (*arrays, *results))
    in_vmem = pl.BlockSpec(memory_space=pltpu.VMEM)
    in_hbm = pl.BlockSpec(memory_space=pltpu.HBM)
    buffers = [(operands[k], rows) for k, rows in staged.items()]
    buffers += [(outs[k], rows) for k, rows in sent.items()]
    buffers = [pltpu.VMEM((row_count(rows), *x.shape[1:]), x.dtype) for x, rows in buffers]
    if len(buffers) + len(moved) > 0:
        buffers.append(pltpu.SemaphoreType.DMA((len(buffers) + len(moved),)))
    results = pl.pallas_call(
        kernel,
        out_shape=results,
        in_specs=[in_hbm if k in staged or k in moved else in_vmem for k in given]
        + [in_hbm] * len(slots),
        out_specs=[in_hbm if k in sent or k in plain else in_vmem for k in made],
        input_output_aliases={len(given) + at: made.index(k) for at, k in enumerate(slots)},
        scratch_shapes=[*scratch, *buffers],
        compiler_params=pltpu.CompilerParams(vmem_limit_bytes=limit),
        cost_estimate=pl.CostEstimate(flops=flops, bytes_accessed=size, transcendentals=0),
        name=body.__name__ if hasattr(body, "__name__") else body.func.__name__,
    )(*arrays, *slots.values())
    results = dict(zip(made, results))
    return [results.get(k) for k in range(len(outs))]


def exchange(values):
    return lax.all_to_all(values, ("space", "batch"), split_axis=0, concat_axis=0, tiled=True)


def neighbours(first, last):
    ends = lax.axis_size("space") - 1
    before = lax.ppermute(last, "space", [(i, i + 1) for i in range(ends)])
    after = lax.ppermute(first, "space", [(i + 1, i) for i in range(ends)])
    return before, after


def shards(snapshots, cotangent, mode_weight, conv_weight):
    batches = lax.axis_size("batch")
    slabs = lax.axis_size("space")
    devices = batches * slabs
    _, channels, layers, plane = snapshots.shape
    modes = mode_weight.shape[0] * mode_weight.shape[1]
    half = LANES // 2
    assert channels == half and layers == 2 and plane == CELLS
    plane_rows = devices * modes
    count = modes * 2 * KZ * batches
    in_slab = modes == 8 and devices * 32 == TERM_ROWS

    analysis, synthesis = plane_tables(batches, slabs)
    gather, scatter, gather_back, scatter_back = depth_tables(slabs, layers, modes)
    weights = mode_weight.reshape(modes * 2 * KZ * channels, channels)
    taps = conv_weight.reshape(OFFSETS, channels, channels)
    field = shape((channels, layers, plane), BF16)
    wide = shape((CELLS, LANES), BF16)
    edge = shape((CELLS // 2, LANES), BF16)
    plane_modes = shape((plane_rows, LANES), BF16)
    padded = pltpu.VMEM((CELLS + 2 * NY, 2 * LANES), BF16)

    def send(values):
        return exchange(values.reshape(devices, modes, LANES)).reshape(plane_rows, LANES)

    packed = shape((weights.shape[0] // 2, LANES), BF16)
    share = weights.shape[0] // CHUNKS
    cells, coef, first, last, kept_weights, slot = run(
        analyse_kernel,
        [
            wide,
            plane_modes,
            edge,
            edge,
            shape((HBM_BYTES // (2 * LANES), LANES), BF16),
            plane_modes,
        ],
        snapshots.reshape(field.shape),
        analysis,
        *[weights] * CHUNKS,
        staged={0: None, 1: None} | {2 + k: slice(k * share, (k + 1) * share) for k in range(CHUNKS)},
        sent=(0, 1, 2, 3),
        plain=(4, 5),
        scratch=[pltpu.VMEM(packed.shape, BF16), pltpu.SemaphoreType.DMA((CHUNKS,))],
        limit=WHOLE_VMEM,
        flops=10**8,
    )
    coef = send(coef)
    (packed_weights,) = run(fetch_kernel, [packed], kept_weights, moved={0: 0})
    before, after = neighbours(first, last)
    local, lanes, outer_cells = run(
        local_kernel,
        [shape((CELLS, LANES), F32), shape((2 * LANES, CELLS), BF16), wide],
        cells,
        before,
        after,
        cotangent.reshape(field.shape),
        taps,
        scratch=[padded, pltpu.VMEM((3, 2 * LANES, 3 * LANES), BF16)],
        flops=8 * 10**9,
    )
    back, diagonal = run(
        functools.partial(mix_kernel, batches, slabs),
        [plane_modes, shape((count, GROUP * half // 2), BF16)],
        coef,
        gather,
        packed_weights,
        scatter,
        sent=(0, 1),
        slots={0: slot},
        flops=4 * 10**8,
    )
    back = send(back)
    slab = shape((devices * 8 + TERM_ROWS, LANES), BF16)
    activated, grad, first, last, back, terms = run(
        functools.partial(activate_kernel, in_slab),
        [
            wide,
            shape((HBM_BYTES // (2 * LANES), LANES), BF16),
            edge,
            edge,
            slab if in_slab else plane_modes,
            None if in_slab else shape((TERM_ROWS, LANES), BF16),
        ],
        back,
        np.ascontiguousarray(synthesis.T),
        local,
        outer_cells,
        lanes,
        sent={1: CELLS, 2: None, 3: None, 4: None},
        scratch=[pltpu.VMEM((CELLS + 2 * NY, 3 * LANES), BF16)],
        flops=10**9,
    )
    if in_slab:
        back = exchange(back.reshape(devices, -1, LANES)).reshape(-1, LANES)
    else:
        back = send(back)
        terms = exchange(terms.reshape(devices, TERM_ROWS // devices, LANES))
    before, after = neighbours(first, last)
    activated, packed_weights = run(
        output_kernel,
        [field, packed],
        activated,
        kept_weights,
        moved={1: 1},
        flops=10**8,
    )
    back, before, after, activated, packed_weights = lax.optimization_barrier(
        (back, before, after, activated, packed_weights)
    )
    scale = 1.0 / math.sqrt(batches * slabs * layers * plane)
    grad_modes, mixed_grad, sums = run(
        functools.partial(unmix_kernel, batches, slabs, scale),
        [
            slab if in_slab else plane_modes,
            shape((count, LANES), BF16),
            None if in_slab else shape((TERM_ROWS // devices, LANES), F32),
        ],
        back,
        None if in_slab else terms,
        gather_back,
        packed_weights,
        scatter_back,
        sent=(0,),
        flops=4 * 10**8,
    )
    if in_slab:
        grad_modes = exchange(grad_modes.reshape(devices, -1, LANES)).reshape(-1, LANES)
    else:
        grad_modes = send(grad_modes)
        sums = lax.all_gather(sums, ("space", "batch"), axis=0, tiled=True)
    (local,) = run(
        local_grad_kernel,
        [shape((CELLS, LANES), F32)],
        grad,
        before,
        after,
        taps,
        staged={0: CELLS},
        scratch=[padded, pltpu.VMEM((3, 3 * LANES, 2 * LANES), BF16)],
        flops=7 * 10**8,
    )
    (mode_gradient,) = run(
        functools.partial(weight_kernel, batches),
        [shape((modes * 2 * KZ * channels, channels), F32)],
        diagonal,
        mixed_grad,
        flops=4 * 10**8,
    )
    input_gradient, conv_gradient = run(
        finish_kernel,
        [field, shape((OFFSETS, channels, channels), F32)],
        grad_modes,
        sums,
        np.ascontiguousarray(analysis.T),
        local,
        flops=10**8,
    )
    return (
        activated.reshape(snapshots.shape),
        input_gradient.reshape(snapshots.shape),
        mode_gradient.reshape(mode_weight.shape),
        conv_gradient.reshape(conv_weight.shape),
    )


def solution(mesh):
    in_specs = (
        P("batch", None, "space", None),
        P("batch", None, "space", None),
        P("batch", "space", None, None, None),
        P(),
    )
    out_specs = (
        P("batch", None, "space", None),
        P("batch", None, "space", None),
        P("batch", "space", None, None, None),
        P(),
    )
    return jax.shard_map(shards, mesh=mesh, in_specs=in_specs, out_specs=out_specs, check_vma=False)
```

```python
import functools
import math

import jax
import jax.numpy as jnp
import ml_dtypes
import numpy as np
from jax import lax
from jax.experimental import pallas as pl
from jax.experimental.pallas import tpu as pltpu
from jax.sharding import PartitionSpec as P

KX = 8
KY = 8
KZ = 12
NX = 32
NY = 32
CELLS = NX * NY
LANES = 128
GROUP = 8
OFFSETS = 27
TERM_ROWS = 1024
CHUNKS = 6
VMEM_BYTES = 40 * 1024 * 1024
WHOLE_VMEM = 65000 * 1024
HBM_BYTES = 100 * 1024 * 256

F32 = jnp.float32
BF16 = jnp.bfloat16
inv_root_two = 1.0 / math.sqrt(2.0)
inv_root_two_pi = 1.0 / math.sqrt(2.0 * math.pi)


def basis_rows(half_count, length):
    row = np.arange(2 * half_count)[:, None]
    cell = np.arange(length)[None, :]
    frequency = np.where(row < half_count, row, row - half_count + 1)
    phases = (frequency * cell % length).astype(np.float32) * np.float32(2.0 * math.pi / length)
    return np.where(row < half_count, np.cos(phases), np.sin(phases)).astype(np.float32)


def plane_tables(batches, slabs):
    outer = (basis_rows(KX, NX)[:, None, :, None] * basis_rows(KY, NY)[None, :, None, :]).reshape(
        2 * KX, 2 * KY, CELLS
    )
    outer = outer.reshape(batches, 2 * KX // batches, slabs, 2 * KY // slabs, CELLS)
    outer = outer.transpose(2, 0, 1, 3, 4).reshape(4 * KX * KY, CELLS)
    analysis = (outer * np.float32(2.0 / math.sqrt(CELLS))).astype(ml_dtypes.bfloat16)
    synthesis = (outer * np.float32(2.0 / math.sqrt(4 * KX * KY))).astype(ml_dtypes.bfloat16)
    return analysis, synthesis


def depth_tables(slabs, layers, modes):
    rows = basis_rows(KZ, slabs * layers)
    analysis = (rows * np.float32(math.sqrt(2.0 / (slabs * layers)))).astype(ml_dtypes.bfloat16)
    synthesis = (rows * np.float32(math.sqrt(2.0 / (2 * KZ)))).astype(ml_dtypes.bfloat16)

    def spread(table, order):
        table = table.astype(np.float32).reshape(2 * KZ, slabs, layers)
        full = np.einsum("psz,mn->" + order, table, np.eye(modes, dtype=np.float32))
        return full.astype(ml_dtypes.bfloat16)

    def gathered(table):
        return spread(table, "mpzsn").reshape(modes * 2 * KZ, layers * slabs * modes)

    def scattered(table):
        return spread(table, "snzmp").reshape(slabs * modes, layers * modes * 2 * KZ)

    return gathered(analysis), scattered(synthesis), gathered(synthesis), scattered(analysis)


def dot(left, right, contract=(1, 0)):
    return lax.dot_general(
        left, right, (((contract[0],), (contract[1],)), ((), ())), preferred_element_type=F32
    )


def turn_table():
    row = lax.broadcasted_iota(jnp.int32, (LANES, LANES), 0)
    column = lax.broadcasted_iota(jnp.int32, (LANES, LANES), 1)
    return jnp.where(column == row % 2 * (LANES // 2) + row // 2, 1.0, 0.0).astype(BF16)


def to_cells(field):
    return dot(field.reshape(LANES, CELLS), turn_table(), (0, 0))


def to_field(cells):
    return dot(turn_table(), cells, (1, 1)).astype(BF16).reshape(LANES // 2, 2, CELLS)


def low_lanes(rows):
    return lax.broadcasted_iota(jnp.int32, (rows, LANES), 1) < LANES // 2


def swap_halves(values):
    return pltpu.roll(values, LANES // 2, 1)


def doubled(values):
    low = low_lanes(values.shape[0])
    swapped = swap_halves(values)
    return jnp.concatenate(
        [jnp.where(low, values, swapped), jnp.where(low, swapped, values)], axis=0
    )


def halved(values):
    low = low_lanes(values.shape[0])
    return jnp.concatenate([jnp.where(low, values, 0.0), jnp.where(low, 0.0, values)], axis=0)


def edge_layers(cells_first):
    top = cells_first[: CELLS // 2]
    bottom = cells_first[CELLS // 2 :]
    low = low_lanes(CELLS // 2)
    first = jnp.where(low, top, swap_halves(bottom))
    last = jnp.where(low, swap_halves(top), bottom)
    return first.astype(BF16), last.astype(BF16)


def beside_layers(before, after):
    before = before.astype(F32)
    after = after.astype(F32)
    low = low_lanes(CELLS // 2)
    top = jnp.where(low, before, swap_halves(after))
    bottom = jnp.where(low, swap_halves(before), after)
    return jnp.concatenate([top, bottom], axis=0).astype(BF16)


def y_cells(rows):
    return lax.broadcasted_iota(jnp.int32, (rows, LANES), 0) % NY


def from_below(values):
    return jnp.where(y_cells(values.shape[0]) == 0, 0.0, pltpu.roll(values, 1, 0))


def from_above(values):
    rows = values.shape[0]
    return jnp.where(y_cells(rows) == NY - 1, 0.0, pltpu.roll(values, rows - 1, 0))


def pad_cells(padded, own, beside):
    width = own.shape[1] + beside.shape[1]
    padded[0:NY, :] = jnp.zeros((NY, width), BF16)
    padded[NY + CELLS : 2 * NY + CELLS, :] = jnp.zeros((NY, width), BF16)
    padded[NY : NY + CELLS, 0 : own.shape[1]] = own
    padded[NY : NY + CELLS, own.shape[1] :] = beside


BLOCK_OF_DEPTH = {-1: 2, 0: 0, 1: 1, 2: 3}
STEP = 256


def stencil(padded, table, transposed, store):
    for start in range(0, CELLS, STEP):
        total = None
        for b in range(3):
            cells = padded[start + NY * b : start + NY * b + STEP, :]
            term = dot(cells, table[b], (1, 1) if transposed else (1, 0))
            total = term if total is None else total + term
        result = (
            from_below(total[:, 0:LANES])
            + total[:, LANES : 2 * LANES]
            + from_above(total[:, 2 * LANES :])
        )
        store(start, result)


def banded_forward(weights, table):
    half = LANES // 2
    for b in range(3):
        for c in range(3):
            for depth, block in BLOCK_OF_DEPTH.items():
                parts = []
                for out in range(2):
                    a = depth - out + 1
                    if 0 <= a < 3:
                        parts.append(weights[a * 9 + b * 3 + c])
                    else:
                        parts.append(jnp.zeros((half, half), BF16))
                table[b, block * half : (block + 1) * half, c * LANES : (c + 1) * LANES] = (
                    jnp.concatenate(parts, axis=1)
                )


def banded_backward(weights, table):
    half = LANES // 2
    for b in range(3):
        for c in range(3):
            for out in range(2):
                for pair in ((0, 1), (-1, 2)):
                    parts = []
                    for depth in pair:
                        a = depth - out + 1
                        if 0 <= a < 3:
                            parts.append(weights[(2 - a) * 9 + (2 - b) * 3 + 2 - c])
                        else:
                            parts.append(jnp.zeros((half, half), BF16))
                    row = c * LANES + out * half
                    column = BLOCK_OF_DEPTH[pair[0]] * half
                    table[b, row : row + half, column : column + LANES] = jnp.concatenate(
                        parts, axis=1
                    )


def analyse_kernel(chunks, field, analysis, *refs):
    weights = refs[:chunks]
    cells_out, coef_out, first_out, last_out, packed_out, _, buffer, semaphores = refs[chunks:]
    cells = to_cells(field[...])
    rounded = cells.astype(BF16)
    coef_out[...] = dot(analysis[...], rounded).astype(BF16)
    cells_out[...] = rounded
    first, last = edge_layers(cells)
    first_out[...] = first
    last_out[...] = last
    rows = GROUP * LANES // 4
    share = buffer.shape[0] // chunks
    copies = []
    for place, part in enumerate(weights):
        for g in range(share // rows):
            pair = [part[k * rows : (k + 1) * rows, :] for k in (2 * g, 2 * g + 1)]
            row = place * share + g * rows
            buffer[row : row + rows, :] = jnp.concatenate(pair, axis=1)
        span = slice(place * share, (place + 1) * share)
        copies.append(
            pltpu.make_async_copy(buffer.at[span], packed_out.at[span], semaphores.at[place])
        )
        copies[-1].start()
    for copy in copies:
        copy.wait()


def local_kernel(
    cells, before, after, cotangent, weights, local_out, lanes_out, cotangent_out, padded, table
):
    banded_forward(weights, table)
    beside = beside_layers(before[...], after[...])
    pad_cells(padded, cells[...], beside)

    def store(start, result):
        local_out[start : start + STEP, :] = result

    stencil(padded, table, False, store)
    whole = jnp.concatenate([cells[...].astype(F32), beside.astype(F32)], axis=1)
    lanes_out[...] = whole.T.astype(BF16)
    cotangent_out[...] = to_cells(cotangent[...]).astype(BF16)


def fetch_kernel():
    pass


def mode_in_group(rows, lanes):
    return lax.broadcasted_iota(jnp.int32, (rows, lanes), 0) % GROUP


def own_block(rows):
    width = GROUP * LANES // 4
    lane = lax.broadcasted_iota(jnp.int32, (rows, width), 1)
    return mode_in_group(rows, width) % (GROUP // 2) == lane // (LANES // 2)


def own_half(rows):
    return (mode_in_group(rows, LANES) < GROUP // 2) == low_lanes(rows)


def to_depth(modes, table, snaps, slabs):
    modes = modes.reshape(slabs, snaps, -1, LANES)
    both = [doubled(modes[:, b].reshape(-1, LANES)) for b in range(snaps)]
    result = dot(table, jnp.concatenate(both, axis=1).astype(BF16))
    return jnp.concatenate(
        [
            result[g : g + GROUP, b * LANES : (b + 1) * LANES]
            for g in range(0, result.shape[0], GROUP)
            for b in range(snaps)
        ],
        axis=0,
    )


def from_depth(modes, table, snaps, slabs):
    count = modes.shape[0] // GROUP
    both = []
    for b in range(snaps):
        own = [modes[g * GROUP : (g + 1) * GROUP] for g in range(b, count, snaps)]
        both.append(halved(jnp.concatenate(own, axis=0)))
    result = dot(table, jnp.concatenate(both, axis=1).astype(BF16))
    own = [
        result[:, b * LANES : (b + 1) * LANES].reshape(slabs, -1, LANES) for b in range(snaps)
    ]
    return jnp.stack(own, axis=1).reshape(-1, LANES)


def mix_kernel(snaps, slabs, received, gather, weights, scatter, back_out, diagonal_out):
    coef = to_depth(received[...].astype(F32), gather[...], snaps, slabs)
    count = coef.shape[0]
    wide = jnp.concatenate([coef] * (GROUP // 4), axis=1)
    diagonal = jnp.where(own_block(count), wide, 0.0).astype(BF16)
    diagonal_out[...] = diagonal
    rows = GROUP * snaps
    depth = GROUP * LANES // 4
    mixed = jnp.concatenate(
        [
            dot(diagonal[g * rows : (g + 1) * rows, :], weights[g * depth : (g + 1) * depth, :])
            for g in range(count // rows)
        ],
        axis=0,
    )
    mixed = jnp.where(own_half(count), mixed, swap_halves(mixed))
    back = from_depth(mixed, scatter[...], snaps, slabs).astype(BF16)
    back_out[...] = back.reshape(back_out.shape)


def activate_kernel(
    terms_in_slab,
    received,
    synthesis,
    local,
    cotangent,
    lanes,
    activated_out,
    grad_out,
    first_out,
    last_out,
    back_out,
    terms_out,
    spread,
):
    pre = dot(synthesis[...], received[...]) + local[...]
    cdf = 0.5 * (1.0 + lax.erf(pre * inv_root_two))
    density = jnp.exp(-0.5 * pre * pre) * inv_root_two_pi
    activated_out[...] = (pre * cdf).astype(BF16)
    grad = (cotangent[...].astype(F32) * (cdf + pre * density)).astype(BF16)
    back = dot(synthesis[...], grad, (0, 0))
    rounded = grad
    grad = grad.astype(F32)
    first, last = edge_layers(grad)
    spread[0:NY, :] = jnp.zeros((NY, 3 * LANES), BF16)
    spread[NY + CELLS : 2 * NY + CELLS, :] = jnp.zeros((NY, 3 * LANES), BF16)
    spread[NY : NY + CELLS, 0:LANES] = from_above(grad).astype(BF16)
    spread[NY : NY + CELLS, LANES : 2 * LANES] = grad.astype(BF16)
    spread[NY : NY + CELLS, 2 * LANES :] = from_below(grad).astype(BF16)
    half = LANES // 2
    low = low_lanes(half)
    twice = {}
    for b in range(3):
        product = dot(lanes[...], spread[NY * (2 - b) : NY * (2 - b) + CELLS, :])
        for c in range(3):
            for a in range(3):
                blocks = [BLOCK_OF_DEPTH[out + a - 1] * half for out in range(2)]
                columns = slice(c * LANES, (c + 1) * LANES)
                both = jnp.where(
                    low,
                    product[blocks[0] : blocks[0] + half, columns],
                    product[blocks[1] : blocks[1] + half, columns],
                )
                twice[a * 9 + b * 3 + c] = both + swap_halves(both)
    pairs = []
    for k in range(0, OFFSETS, 2):
        pairs.append(jnp.where(low, twice[k], twice.get(k + 1, 0.0)))
    pairs.append(jnp.zeros((TERM_ROWS - half * len(pairs), LANES), F32))
    terms = jnp.concatenate(pairs, axis=0)
    if terms_in_slab:
        slab_store(back_out, back, terms)
    else:
        back_out[...] = back.astype(BF16)
        terms_out[...] = terms.astype(BF16)
    grad_out[...] = rounded
    first_out[...] = first
    last_out[...] = last


def slab_owners(slab):
    return (slab.shape[0] - TERM_ROWS) // 8


def slab_store(slab, modes, terms):
    owners = slab_owners(slab)
    modes = modes.reshape(owners, 8, LANES)
    terms = terms.reshape(owners, -1, LANES)
    slab[...] = jnp.concatenate([modes, terms], axis=1).reshape(-1, LANES).astype(BF16)


def slab_load(slab):
    whole = slab[...].astype(F32).reshape(slab_owners(slab), -1, LANES)
    return whole[:, 0:8, :].reshape(-1, LANES), whole[:, 8:, :]


def unmix_kernel(snaps, slabs, scale, received, terms, gather, weights, scatter, grad_out, mixed_out, sums_out):
    in_slab = terms is None
    if in_slab:
        modes, terms = slab_load(received)
    else:
        modes, terms = received[...].astype(F32), terms[...].astype(F32)
    mixed = to_depth(modes, gather[...], snaps, slabs)
    mixed_out[...] = mixed.astype(BF16)
    count = mixed.shape[0]
    rows = GROUP * snaps
    depth = GROUP * LANES // 4
    sums = jnp.sum(terms, axis=0) * scale
    own = own_block(rows)
    placed = jnp.where(own_half(count), mixed, 0.0).astype(BF16)
    pieces = []
    for g in range(count // rows):
        full = dot(
            placed[g * rows : (g + 1) * rows, :], weights[g * depth : (g + 1) * depth, :], (1, 1)
        )
        full = jnp.where(own, full, 0.0)
        pieces.append(sum(full[:, k : k + LANES] for k in range(0, depth, LANES)))
    coef = jnp.concatenate(pieces, axis=0)
    coef = coef + swap_halves(coef)
    grad = from_depth(coef, scatter[...], snaps, slabs)
    if in_slab:
        owners = slab_owners(received)
        share = sums.shape[0]
        slab_store(
            grad_out, grad, jnp.broadcast_to(sums[None], (owners, share, LANES)).reshape(-1, LANES)
        )
    else:
        grad_out[...] = grad.astype(BF16)
        sums_out[...] = sums


def weight_kernel(snaps, diagonal, mixed, out):
    rows = GROUP * snaps
    depth = GROUP * LANES // 4
    half = LANES // 2
    first = mode_in_group(rows, depth) < GROUP // 2
    for g in range(diagonal.shape[0] // rows):
        span = slice(g * rows, (g + 1) * rows)
        blocks = diagonal[span, :].astype(F32)
        blocks = [jnp.where(first, blocks, 0.0), jnp.where(first, 0.0, blocks)]
        blocks = jnp.concatenate(blocks, axis=1).astype(BF16)
        out[2 * g * depth : 2 * (g + 1) * depth, :] = dot(blocks, mixed[span, 0:half], (0, 0))


def output_kernel(cells, out):
    out[...] = to_field(cells[...])


def local_grad_kernel(grad, before, after, weights, out, padded, table):
    banded_backward(weights, table)
    pad_cells(padded, grad[...], beside_layers(before[...], after[...]))

    def store(start, result):
        out[start : start + STEP, :] = result

    stencil(padded, table, True, store)


def finish_kernel(received, sums, synthesis, local, grad_out, stencil_out):
    in_slab = sums is None
    if in_slab:
        modes, terms = slab_load(received)
        terms = terms.reshape(TERM_ROWS, LANES)
    else:
        modes, terms = received[...], sums[...].astype(F32)
    cells = (dot(synthesis[...], modes.astype(BF16)) + local[...]).astype(BF16)
    grad_out[...] = to_field(cells)
    half = LANES // 2
    for k in range(OFFSETS):
        row = (k // 2) * half
        lane = (k % 2) * half
        stencil_out[k] = terms[row : row + half, lane : lane + half]


def shape(dims, dtype):
    return jax.ShapeDtypeStruct(dims, dtype)


class Staged:
    def __init__(self, source, buffer, semaphore):
        self.copy = pltpu.make_async_copy(source, buffer, semaphore)
        self.buffer = buffer
        self.copy.start()
        self.ready = False

    def load(self):
        if not self.ready:
            self.copy.wait()
            self.ready = True

    def __getitem__(self, index):
        self.load()
        return self.buffer[index]


class Sent:
    def __init__(self, target, buffer, semaphore):
        self.copy = pltpu.make_async_copy(buffer, target, semaphore)
        self.buffer = buffer

    def __setitem__(self, index, value):
        self.buffer[index] = value
        self.copy.start()

    def __getitem__(self, index):
        return self.buffer[index]

    @property
    def shape(self):
        return self.buffer.shape


def row_count(rows):
    return rows.stop - rows.start if isinstance(rows, slice) else rows


def run(
    body, outs, *operands, staged=(), sent=(), moved=(), plain=(), slots=(), scratch=(), flops=0, limit=VMEM_BYTES
):
    given = [k for k, operand in enumerate(operands) if operand is not None]
    made = [k for k, out in enumerate(outs) if out is not None]

    def rows_of(chosen, places, arrays):
        chosen = {k: chosen[k] if isinstance(chosen, dict) else None for k in places if k in chosen}
        return {k: rows or arrays[k].shape[0] for k, rows in chosen.items()}

    moved = dict(moved)
    slots = dict(slots)
    staged = rows_of(staged, given, operands)
    sent = rows_of(sent, made, outs)

    def kernel(*refs):
        refs = list(refs)

        def take(count):
            taken = refs[:count]
            del refs[:count]
            return taken

        def part(ref, rows):
            if isinstance(rows, slice):
                return ref.at[rows]
            return ref if ref.shape[0] == rows else ref.at[0:rows]

        filled = dict(zip(given, take(len(given))))
        take(len(slots))
        kept = dict(zip(made, take(len(made))))
        own = take(len(scratch))
        copies = []
        for place, (k, out) in enumerate(moved.items()):
            source, target = filled.pop(k), kept.pop(out)
            rows = min(source.shape[0], target.shape[0])
            semaphore = refs[-1].at[len(staged) + len(sent) + place]
            copies.append(
                pltpu.make_async_copy(part(source, rows), part(target, rows), semaphore)
            )
        for place, (k, buffer) in enumerate(zip(staged, take(len(staged)))):
            filled[k] = Staged(part(filled[k], staged[k]), buffer, refs[-1].at[place])
        for place, (k, buffer) in enumerate(zip(sent, take(len(sent)))):
            kept[k] = Sent(part(kept[k], sent[k]), buffer, refs[-1].at[len(staged) + place])
        for copy in copies:
            copy.start()
        body(
            *[filled.get(k) for k in range(len(operands)) if k not in moved],
            *[kept.get(k) for k in range(len(outs)) if k not in moved.values()],
            *own,
        )
        for k in staged:
            filled[k].load()
        for k in sent:
            kept[k].copy.wait()
        for copy in copies:
            copy.wait()

    arrays = [operands[k] for k in given]
    results = [outs[k] for k in made]
    size = sum(x.size * x.dtype.itemsize for x in (*arrays, *results))
    in_vmem = pl.BlockSpec(memory_space=pltpu.VMEM)
    in_hbm = pl.BlockSpec(memory_space=pltpu.HBM)
    buffers = [(operands[k], rows) for k, rows in staged.items()]
    buffers += [(outs[k], rows) for k, rows in sent.items()]
    buffers = [pltpu.VMEM((row_count(rows), *x.shape[1:]), x.dtype) for x, rows in buffers]
    if len(buffers) + len(moved) > 0:
        buffers.append(pltpu.SemaphoreType.DMA((len(buffers) + len(moved),)))
    results = pl.pallas_call(
        kernel,
        out_shape=results,
        in_specs=[in_hbm if k in staged or k in moved else in_vmem for k in given]
        + [in_hbm] * len(slots),
        out_specs=[in_hbm if k in sent or k in plain else in_vmem for k in made],
        input_output_aliases={len(given) + at: made.index(k) for at, k in enumerate(slots)},
        scratch_shapes=[*scratch, *buffers],
        compiler_params=pltpu.CompilerParams(vmem_limit_bytes=limit),
        cost_estimate=pl.CostEstimate(flops=flops, bytes_accessed=size, transcendentals=0),
        name=body.__name__ if hasattr(body, "__name__") else body.func.__name__,
    )(*arrays, *slots.values())
    results = dict(zip(made, results))
    return [results.get(k) for k in range(len(outs))]


def exchange(values):
    return lax.all_to_all(values, ("space", "batch"), split_axis=0, concat_axis=0, tiled=True)


def neighbours(first, last):
    ends = lax.axis_size("space") - 1
    before = lax.ppermute(last, "space", [(i, i + 1) for i in range(ends)])
    after = lax.ppermute(first, "space", [(i + 1, i) for i in range(ends)])
    return before, after


def shards(snapshots, cotangent, mode_weight, conv_weight):
    batches = lax.axis_size("batch")
    slabs = lax.axis_size("space")
    devices = batches * slabs
    _, channels, layers, plane = snapshots.shape
    modes = mode_weight.shape[0] * mode_weight.shape[1]
    half = LANES // 2
    assert channels == half and layers == 2 and plane == CELLS
    plane_rows = devices * modes
    count = modes * 2 * KZ * batches
    in_slab = modes == 8 and devices * 32 == TERM_ROWS

    analysis, synthesis = plane_tables(batches, slabs)
    gather, scatter, gather_back, scatter_back = depth_tables(slabs, layers, modes)
    weights = mode_weight.reshape(modes * 2 * KZ * channels, channels)
    taps = conv_weight.reshape(OFFSETS, channels, channels)
    field = shape((channels, layers, plane), BF16)
    wide = shape((CELLS, LANES), BF16)
    edge = shape((CELLS // 2, LANES), BF16)
    plane_modes = shape((plane_rows, LANES), BF16)
    padded = pltpu.VMEM((CELLS + 2 * NY, 2 * LANES), BF16)

    def send(values):
        return exchange(values.reshape(devices, modes, LANES)).reshape(plane_rows, LANES)

    packed = shape((weights.shape[0] // 2, LANES), BF16)
    chunks = math.gcd(CHUNKS, weights.shape[0] // (GROUP * channels))
    share = weights.shape[0] // chunks
    cells, coef, first, last, kept_weights, slot = run(
        functools.partial(analyse_kernel, chunks),
        [
            wide,
            plane_modes,
            edge,
            edge,
            shape((HBM_BYTES // (2 * LANES), LANES), BF16),
            plane_modes,
        ],
        snapshots.reshape(field.shape),
        analysis,
        *[weights] * chunks,
        staged={0: None, 1: None} | {2 + k: slice(k * share, (k + 1) * share) for k in range(chunks)},
        sent=(0, 1, 2, 3),
        plain=(4, 5),
        scratch=[pltpu.VMEM(packed.shape, BF16), pltpu.SemaphoreType.DMA((chunks,))],
        limit=WHOLE_VMEM,
        flops=10**8,
    )
    coef = send(coef)
    (packed_weights,) = run(fetch_kernel, [packed], kept_weights, moved={0: 0})
    before, after = neighbours(first, last)
    local, lanes, outer_cells = run(
        local_kernel,
        [shape((CELLS, LANES), F32), shape((2 * LANES, CELLS), BF16), wide],
        cells,
        before,
        after,
        cotangent.reshape(field.shape),
        taps,
        scratch=[padded, pltpu.VMEM((3, 2 * LANES, 3 * LANES), BF16)],
        flops=8 * 10**9,
    )
    back, diagonal = run(
        functools.partial(mix_kernel, batches, slabs),
        [plane_modes, shape((count, GROUP * half // 2), BF16)],
        coef,
        gather,
        packed_weights,
        scatter,
        sent=(0, 1),
        slots={0: slot},
        flops=4 * 10**8,
    )
    back = send(back)
    slab = shape((devices * 8 + TERM_ROWS, LANES), BF16)
    activated, grad, first, last, back, terms = run(
        functools.partial(activate_kernel, in_slab),
        [
            wide,
            shape((HBM_BYTES // (2 * LANES), LANES), BF16),
            edge,
            edge,
            slab if in_slab else plane_modes,
            None if in_slab else shape((TERM_ROWS, LANES), BF16),
        ],
        back,
        np.ascontiguousarray(synthesis.T),
        local,
        outer_cells,
        lanes,
        sent={1: CELLS, 2: None, 3: None, 4: None},
        scratch=[pltpu.VMEM((CELLS + 2 * NY, 3 * LANES), BF16)],
        flops=10**9,
    )
    if in_slab:
        back = exchange(back.reshape(devices, -1, LANES)).reshape(-1, LANES)
    else:
        back = send(back)
        terms = exchange(terms.reshape(devices, TERM_ROWS // devices, LANES))
    before, after = neighbours(first, last)
    activated, packed_weights = run(
        output_kernel,
        [field, packed],
        activated,
        kept_weights,
        moved={1: 1},
        flops=10**8,
    )
    back, before, after, activated, packed_weights = lax.optimization_barrier(
        (back, before, after, activated, packed_weights)
    )
    scale = 1.0 / math.sqrt(batches * slabs * layers * plane)
    grad_modes, mixed_grad, sums = run(
        functools.partial(unmix_kernel, batches, slabs, scale),
        [
            slab if in_slab else plane_modes,
            shape((count, LANES), BF16),
            None if in_slab else shape((TERM_ROWS // devices, LANES), F32),
        ],
        back,
        None if in_slab else terms,
        gather_back,
        packed_weights,
        scatter_back,
        sent=(0,),
        flops=4 * 10**8,
    )
    if in_slab:
        grad_modes = exchange(grad_modes.reshape(devices, -1, LANES)).reshape(-1, LANES)
    else:
        grad_modes = send(grad_modes)
        sums = lax.all_gather(sums, ("space", "batch"), axis=0, tiled=True)
    (local,) = run(
        local_grad_kernel,
        [shape((CELLS, LANES), F32)],
        grad,
        before,
        after,
        taps,
        staged={0: CELLS},
        scratch=[padded, pltpu.VMEM((3, 3 * LANES, 2 * LANES), BF16)],
        flops=7 * 10**8,
    )
    (mode_gradient,) = run(
        functools.partial(weight_kernel, batches),
        [shape((modes * 2 * KZ * channels, channels), F32)],
        diagonal,
        mixed_grad,
        flops=4 * 10**8,
    )
    input_gradient, conv_gradient = run(
        finish_kernel,
        [field, shape((OFFSETS, channels, channels), F32)],
        grad_modes,
        sums,
        np.ascontiguousarray(analysis.T),
        local,
        flops=10**8,
    )
    return (
        activated.reshape(snapshots.shape),
        input_gradient.reshape(snapshots.shape),
        mode_gradient.reshape(mode_weight.shape),
        conv_gradient.reshape(conv_weight.shape),
    )


def solution(mesh):
    in_specs = (
        P("batch", None, "space", None),
        P("batch", None, "space", None),
        P("batch", "space", None, None, None),
        P(),
    )
    out_specs = (
        P("batch", None, "space", None),
        P("batch", None, "space", None),
        P("batch", "space", None, None, None),
        P(),
    )
    return jax.shard_map(shards, mesh=mesh, in_specs=in_specs, out_specs=out_specs, check_vma=False)
```
